32 devices in a mesh: grp: 2 (over y), col: 4 (over z), row: 2 (over x), gz: 2 (over core).
Axes of the slice: x: 2, y: 2, z: 4, core: 2. Of those that a mesh axis runs over, the one named last changes fastest.
Arguments:
- electric: float32 [3, 64, 16, 1024], P(None, 'gz', 'row', ('grp', 'col')), parts along dimension 3, may hold values from -6 to 6
- magnetic: float32 [3, 64, 16, 1024], P(None, 'gz', 'row', ('grp', 'col')), parts along dimension 3, may hold values from -6 to 6
- material: int32 [64, 16, 1024], P('gz', 'row', ('grp', 'col')), parts along dimension 2, may hold values from 0 to 7
- eps_table: float32 [8], replicated, may hold values from 1.5 to 12
- mode_table: float32 [8, 64, 64], P(None, 'gz'), may hold values from -0.09375 to 0.09375
- port_row: int32 [4, 4, 4], P(('grp', 'row'), 'col'), parts along dimension 0, may hold values from 0 to 7
- port_col: int32 [4, 4, 4], P(('grp', 'row'), 'col'), parts along dimension 0, may hold values from 0 to 64
- port_mode: int32 [4, 4, 4], P(('grp', 'row'), 'col'), parts along dimension 0, may hold values from 0 to 7
- port_ids: int32 [4, 4, 4], P(('grp', 'row'), 'col'), parts along dimension 0, may hold values from 0 to 31, as said below
Outputs:
- electric_out: float32 [3, 64, 16, 1024], P(None, 'gz', 'row', ('grp', 'col')), parts along dimension 3
- magnetic_out: float32 [3, 64, 16, 1024], P(None, 'gz', 'row', ('grp', 'col')), parts along dimension 3
- intersections: float32 [64, 16], P(('grp', 'col', 'row', 'gz')), parts along dimension 0
The draws below stay inside these ranges and needn't reach their ends.
There are 2 independent parts, one for each index of `grp`. The reference program is written for one: setup_inputs(seed, part) draws one part's arguments, and reference() takes and returns one part's arrays. A program takes and returns all parts, laid end to end along the dimension named above; an argument that names none is the same for every part. Nothing has to cross between parts.
Inputs may be any that keep to these rules, and one draw needn't show every extreme that they name: port_ids names every port number exactly once.
All inputs are finite; a program needn't handle non-finite values.
Results may differ from the reference program's by a relative error of at most 0.0003.
Values sent between devices are 32-bit elements; how exact they have to be, the bound alone decides.
No kernel may reach another device: no remote copies, remote signals or barrier semaphores. Data moves between devices by JAX's collectives and lax.ppermute only.
A program may use at most 64 MiB of HBM per device.

```python
import math
import jax
import jax.numpy as jnp
from jax import lax

CX = 8
CY = 128
STEPS = 4
FREQ = 8
MATS = 8
MODES = 8
PLEN = 64
PORT_TILE = 4
TILES_R = 2
TILES_C = 4
NZ = 64
NX = 16
NY = 512
PORTS = 32


def draw_port_ids(key, part):
    key = jax.random.fold_in(key, 11)
    order = jax.random.permutation(key, PORTS).astype(jnp.int32)
    return order.reshape(NX // CX, NY // CY, PORT_TILE)


def with_ends(drawn, stream_key, low, top_value):
    dims = drawn.shape
    place = [jax.random.randint(jax.random.fold_in(stream_key, axis), (), 0, dims[axis]) for axis in range(len(dims))]
    drawn = drawn.at[tuple(place)].set(low)
    longest = dims.index(max(dims))
    place[longest] = (place[longest] + 1) % dims[longest]
    return drawn.at[tuple(place)].set(top_value)


def block_scale(rng, dims, pieces, smallest, high):
    loudness, own = 1.0, jax.random.fold_in(rng, 6)
    for position, parts in pieces:
        draws = jnp.exp(jax.random.uniform(jax.random.fold_in(own, position), (parts,), jnp.float32, smallest / len(pieces), high / len(pieces)))
        loudness = loudness * jnp.repeat(draws, dims[position] // parts).reshape([-1 if axis == position else 1 for axis in range(len(dims))])
    return loudness


def normal_values(stream_key, extent, width, bound, split=(), held_as=jnp.bfloat16):
    gain = block_scale(stream_key, extent, split, -0.22, 0.18) if split else 1.0
    entries = jax.random.normal(stream_key, extent, jnp.float32) * width * gain
    return jnp.minimum(jnp.maximum(entries, -bound), bound).astype(held_as)


def setup_inputs(seed: int = 0, part: int = 0) -> dict:
    seeds = jax.random.split(jax.random.key(seed), 10)
    own_keys = jax.random.split(jax.random.fold_in(seeds[9], part), 10)
    electric = normal_values(own_keys[0], (3, NZ, NX, NY), 1.0, 6.0, ((1, 2), (2, 2), (3, 4)), jnp.float32)
    magnetic = normal_values(own_keys[1], (3, NZ, NX, NY), 1.0, 6.0, ((1, 2), (2, 2), (3, 4)), jnp.float32)
    material = with_ends(jax.random.randint(own_keys[2], (NZ, NX, NY), 0, MATS), jax.random.fold_in(own_keys[2], 1), 0, MATS - 1).astype(jnp.int32)
    eps_table = jnp.clip(jnp.exp(jax.random.uniform(seeds[3], (MATS,), jnp.float32, math.log(1.5), math.log(12.0))), 1.5, 12.0)
    mode_table = normal_values(seeds[4], (MODES, NZ, PLEN), (NZ * PLEN) ** -0.5, 0.09375, ((1, 2),), jnp.float32)
    port_row = with_ends(jax.random.randint(own_keys[5], (TILES_R, TILES_C, PORT_TILE), 0, CX), jax.random.fold_in(own_keys[5], 1), 0, CX - 1).astype(jnp.int32)
    port_col = with_ends(jax.random.randint(own_keys[6], (TILES_R, TILES_C, PORT_TILE), 0, CY - PLEN + 1), jax.random.fold_in(own_keys[6], 1), 0, CY - PLEN).astype(jnp.int32)
    port_mode = with_ends(jax.random.randint(own_keys[7], (TILES_R, TILES_C, PORT_TILE), 0, MODES), jax.random.fold_in(own_keys[7], 1), 0, MODES - 1).astype(jnp.int32)
    port_ids = draw_port_ids(jax.random.fold_in(jax.random.fold_in(seeds[9], part), 71), part)
    return {"electric": electric, "magnetic": magnetic, "material": material, "eps_table": eps_table, "mode_table": mode_table, "port_row": port_row, "port_col": port_col, "port_mode": port_mode, "port_ids": port_ids}


time_step = 0.5


def forward_diff(field, axis):
    return jnp.diff(field, axis=axis, append=0.0)


def backward_diff(field, axis):
    return jnp.diff(field, axis=axis, prepend=0.0)


def dft_basis():
    times = (jnp.arange(STEPS, dtype=jnp.float32) + 1.0) * time_step
    omegas = jnp.pi * (jnp.arange(FREQ, dtype=jnp.float32) + 1.0) / FREQ
    angle = times[:, None] * omegas[None, :]
    return jnp.concatenate([jnp.cos(angle), -jnp.sin(angle)], axis=1)


def port_samples(elec_z, rows_pos, cols_pos, modes_pos, mode_table):
    zero_index = jnp.zeros((), jnp.int32)

    def single(row_at, col_at, mode_at):
        strip = lax.dynamic_slice(elec_z, (zero_index, row_at.astype(jnp.int32), col_at.astype(jnp.int32)), (elec_z.shape[0], 1, PLEN))[:, 0, :]
        return jnp.sum(strip * mode_table[mode_at])

    return jax.vmap(single)(rows_pos, cols_pos, modes_pos)


def reference(electric, magnetic, material, eps_table, mode_table, port_row, port_col, port_mode, port_ids):
    coefficient = time_step * (1.0 / eps_table)[material]
    elec_x, elec_y, elec_z = electric[0], electric[1], electric[2]
    magn_x, magn_y, magn_z = magnetic[0], magnetic[1], magnetic[2]
    tile_r = jnp.arange(TILES_R, dtype=jnp.int32)[:, None, None]
    tile_c = jnp.arange(TILES_C, dtype=jnp.int32)[None, :, None]
    rows_pos = (tile_r * CX + port_row).reshape(-1).astype(jnp.int32)
    cols_pos = (tile_c * CY + port_col).reshape(-1).astype(jnp.int32)
    modes_pos = port_mode.reshape(-1)
    samples = []
    for counter in range(STEPS):
        magn_x = magn_x - time_step * (forward_diff(elec_z, 2) - forward_diff(elec_y, 0))
        magn_y = magn_y - time_step * (forward_diff(elec_x, 0) - forward_diff(elec_z, 1))
        magn_z = magn_z - time_step * (forward_diff(elec_y, 1) - forward_diff(elec_x, 2))
        elec_x = elec_x + coefficient * (backward_diff(magn_z, 2) - backward_diff(magn_y, 0))
        elec_y = elec_y + coefficient * (backward_diff(magn_x, 0) - backward_diff(magn_z, 1))
        elec_z = elec_z + coefficient * (backward_diff(magn_y, 1) - backward_diff(magn_x, 2))
        samples.append(port_samples(elec_z, rows_pos, cols_pos, modes_pos, mode_table))
    sampled = jnp.stack(samples)
    transform = jnp.dot(sampled.T, dft_basis(), precision=lax.Precision.HIGHEST)
    intersections = jnp.zeros((PORTS, 2 * FREQ), jnp.float32).at[port_ids.reshape(-1)].set(transform)
    return jnp.stack([elec_x, elec_y, elec_z]), jnp.stack([magn_x, magn_y, magn_z]), intersections
```

```python
import functools

import jax
import jax.numpy as jnp
import numpy as np
from jax import lax
from jax.experimental import pallas as pl
from jax.experimental.pallas import tpu as pltpu
from jax.sharding import PartitionSpec as P

STEPS = 4
FREQ = 8
MATS = 8
PLEN = 64
PORT_TILE = 4
FIELDS = 7
DEPTH = STEPS

time_step = 0.5

VMEM = pl.BlockSpec(memory_space=pltpu.VMEM)
SMEM = pl.BlockSpec(memory_space=pltpu.SMEM)
PARAMS = pltpu.CompilerParams(vmem_limit_bytes=48 * 1024 * 1024)


def dft_basis():
    times = (np.arange(STEPS) + 1.0) * time_step
    omegas = np.pi * (np.arange(FREQ) + 1.0) / FREQ
    angle = times[:, None] * omegas[None, :]
    basis = np.zeros((8, 128), np.float32)
    basis[:STEPS, : 2 * FREQ] = np.concatenate([np.cos(angle), -np.sin(angle)], axis=1)
    return basis


def iota(shape, axis):
    return lax.broadcasted_iota(jnp.int32, shape, axis)


def pack_pair(first, second, up):
    low = iota((8, 128), 0) < DEPTH
    if up:
        return jnp.where(low, pltpu.roll(first, DEPTH, 0), second)
    return jnp.where(low, first, pltpu.roll(second, DEPTH, 0))


def pack_rows(pairs, row_size, out_refs):
    if row_size == 2:
        row = lax.axis_index("row")
        for up in (True, False):

            @pl.when(row == (0 if up else 1))
            def _(up=up):
                for i, (first, second) in enumerate(pairs):
                    out_refs[0][i] = pack_pair(first(), second(), up)
    else:
        for i, (first, second) in enumerate(pairs):
            out_refs[0][i] = pack_pair(first(), second(), True)
            out_refs[1][i] = pack_pair(first(), second(), False)


def unpack_pair(refs, i, row_size):
    low = iota((8, 128), 0) < DEPTH
    if row_size == 2:
        row = lax.axis_index("row")
        packed = refs[0][i]
        mine = (iota((8, 128), 0) < DEPTH) == (row == 0)
        turned = pltpu.roll(packed, DEPTH, 0)
        first = jnp.where(row == 0, packed, turned)
        second = jnp.where(row == 0, turned, packed)
        zero = jnp.zeros_like(packed)
        return jnp.where(mine, first, zero), jnp.where(mine, second, zero)
    below, above = refs[0][i], refs[1][i]
    first = jnp.where(low, above, pltpu.roll(below, DEPTH, 0))
    second = jnp.where(low, pltpu.roll(above, DEPTH, 0), below)
    return first, second


def pack_kernel(row_size, eps_ref, elec_ref, magn_ref, mat_ref, coef_ref, z_ref, up_ref, down_ref, *x_refs):
    layers = elec_ref.shape[1]
    gz = lax.axis_index("gz")
    for z in range(layers):
        material = mat_ref[z]
        eps = jnp.full((8, 128), eps_ref[0], jnp.float32)
        for which in range(1, MATS):
            eps = jnp.where(material == which, eps_ref[which], eps)
        coef_ref[z] = time_step * (1.0 / eps)

    def tile(field, z):
        if field < 3:
            return elec_ref[field, z]
        if field < 6:
            return magn_ref[field - 3, z]
        return coef_ref[z]

    start = jnp.where(gz == 0, layers - DEPTH, 0)
    for field in range(FIELDS):
        for k in range(DEPTH):
            z_ref[field * DEPTH + k] = tile(field, start + k)
    group = iota((8, 128), 1) // DEPTH
    for field in range(FIELDS):
        up = jnp.zeros((8, 128), jnp.float32)
        down = jnp.zeros((8, 128), jnp.float32)
        for z in range(layers):
            turned = pltpu.roll(tile(field, z), (DEPTH * (z + 1)) % 128, 1)
            up = jnp.where(group == z, turned, up)
            down = jnp.where(group == (z + 1) % layers, turned, down)
        up_ref[field] = up
        down_ref[field] = pltpu.roll(down, 128 - DEPTH, 1)
    pairs = [
        (functools.partial(tile, c, z), functools.partial(tile, c + 3, z))
        for c in range(3)
        for z in range(layers)
    ]
    pairs += [(functools.partial(tile, 6, z), functools.partial(tile, 6, z + layers // 2)) for z in range(layers // 2)]
    pack_rows(pairs, row_size, x_refs)


def corner_kernel(row_size, z_ref, y_ref, yz_ref, *x_refs):
    half = FIELDS * 2
    pairs = []
    for i in range(FIELDS * DEPTH):
        other = (y_ref, i) if i < half else (yz_ref, i - half)
        pairs.append((functools.partial(z_ref.__getitem__, i), functools.partial(other[0].__getitem__, other[1])))
    pack_rows(pairs, row_size, x_refs)


def fwd_y(main, side):
    last = iota((8, 128), 1) == 127
    a, b = pltpu.roll(main, 127, 1), pltpu.roll(side, 127, 1)
    return jnp.where(last, b, a) - main, jnp.where(last, a, b) - side


def bwd_y(main, side):
    first = iota((8, 128), 1) == 0
    a, b = pltpu.roll(main, 1, 1), pltpu.roll(side, 1, 1)
    return main - jnp.where(first, b, a), side - jnp.where(first, a, b)


def fwd_x(main, side):
    last = iota((8, 128), 0) == 7
    a, b = pltpu.roll(main, 7, 0), pltpu.roll(side, 7, 0)
    return jnp.where(last, b, a) - main, jnp.where(last, a, b) - side


def bwd_x(main, side):
    first = iota((8, 128), 0) == 0
    a, b = pltpu.roll(main, 1, 0), pltpu.roll(side, 1, 0)
    return main - jnp.where(first, b, a), side - jnp.where(first, a, b)


TILES = ((0, 0), (0, 1), (1, 0), (1, 1))


def diff(kind, tiles):
    out = {}
    if kind in (fwd_y, bwd_y):
        for r in range(2):
            out[r, 0], out[r, 1] = kind(tiles[r, 0], tiles[r, 1])
    else:
        for c in range(2):
            out[0, c], out[1, c] = kind(tiles[0, c], tiles[1, c])
    return out


def step_kernel(
    row_size, mode_ref, basis_ref, prow_ref, pcol_ref, pmode_ref, pid_ref,
    elec_ref, magn_ref, coef_ref, z_ref, y_ref, yz_ref, *rest,
):
    n_x = 1 if row_size == 2 else 2
    x_refs, corner_refs = rest[:n_x], rest[n_x : 2 * n_x]
    eout_ref, hout_ref, term_ref, field_ref, weight_ref, strip_ref, sum_ref = rest[2 * n_x :]
    layers = elec_ref.shape[1]
    extended = layers + DEPTH
    gz, row, col = (lax.axis_index(name) for name in ("gz", "row", "col"))
    lane, sub = iota((8, 128), 1), iota((8, 128), 0)

    def put(field, r, c, where, value):
        field_ref[field, where, 8 * r : 8 * r + 8, 128 * c : 128 * c + 128] = value

    def get(field, r, c, where):
        return field_ref[field, where, 8 * r : 8 * r + 8, 128 * c : 128 * c + 128]

    def assemble(gz_is):
        base = 1 + DEPTH * gz_is
        halo = 1 + layers * (1 - gz_is)
        far = 0 if gz_is == 0 else layers - DEPTH

        def side(low_tile, high_tile, z):
            low = pltpu.roll(low_tile, (128 - DEPTH - DEPTH * z) % 128, 1)
            high = pltpu.roll(high_tile, (128 - DEPTH * z) % 128, 1)
            return jnp.where(lane < 64, high, low)

        corner = {}
        for i in range(FIELDS * DEPTH):
            first, second = unpack_pair(corner_refs, i, row_size)
            corner["z", i] = first
            corner["y" if i < 2 * FIELDS else "yz", i % (2 * FIELDS)] = second
        for field in range(FIELDS):
            for c in (0, 1):
                put(field, 0, c, 0, jnp.zeros((8, 128), jnp.float32))
                put(field, 1, c, 0, jnp.zeros((8, 128), jnp.float32))
                put(field, 0, c, extended + 1, jnp.zeros((8, 128), jnp.float32))
                put(field, 1, c, extended + 1, jnp.zeros((8, 128), jnp.float32))
            for z in range(layers):
                if field < 3:
                    main = elec_ref[field, z]
                elif field < 6:
                    main = magn_ref[field - 3, z]
                else:
                    main = coef_ref[z]
                put(field, 0, 0, base + z, main)
                put(field, 0, 1, base + z, side(y_ref[field], y_ref[FIELDS + field], z))
                put(field, 1, 1, base + z, side(corner["y", field], corner["y", FIELDS + field], z))
            for k in range(DEPTH):
                i = field * DEPTH + k
                put(field, 0, 0, halo + k, z_ref[i])
                put(field, 0, 1, halo + k, side(yz_ref[field], yz_ref[FIELDS + field], far + k))
                put(field, 1, 0, halo + k, corner["z", i])
                put(field, 1, 1, halo + k, side(corner["yz", field], corner["yz", FIELDS + field], far + k))
        for c in range(3):
            for z in range(layers):
                first, second = unpack_pair(x_refs, c * layers + z, row_size)
                put(c, 1, 0, base + z, first)
                put(c + 3, 1, 0, base + z, second)
        for z in range(layers // 2):
            first, second = unpack_pair(x_refs, 3 * layers + z, row_size)
            put(6, 1, 0, base + z, first)
            put(6, 1, 0, base + z + layers // 2, second)
        for k in range(PORT_TILE):
            weight_ref[k] = jnp.zeros(weight_ref.shape[1:], jnp.float32)
            strip_ref[...] = jnp.zeros(strip_ref.shape, jnp.float32)
            strip_ref[:, :PLEN] = mode_ref[pmode_ref[0, 0, k]]
            moved = pltpu.roll(strip_ref[...], pcol_ref[0, 0, k], 1)
            weight_ref[k, DEPTH * gz_is : DEPTH * gz_is + layers, :] = moved

    for gz_is in (0, 1):
        pl.when(gz == gz_is)(functools.partial(assemble, gz_is))

    half = jnp.full((8, 128), time_step, jnp.float32)
    below = jnp.where((sub >= 4) & (row == 0), 0.0, half)
    before = jnp.where((lane >= 64) & (col == 0), 0.0, half)
    ch = {(0, 0): half, (0, 1): before, (1, 0): below, (1, 1): jnp.minimum(below, before)}

    def step(n, carry):
        hx_prev = {t: jnp.zeros((8, 128), jnp.float32) for t in TILES}
        hy_prev = dict(hx_prev)
        ex = {t: get(0, *t, 1) for t in TILES}
        ey = {t: get(1, *t, 1) for t in TILES}
        acc = [jnp.zeros((8, 128), jnp.float32) for _ in range(PORT_TILE)]
        for j in range(extended):
            at = j + 1
            ez = {t: get(2, *t, at) for t in TILES}
            ex_next = {t: get(0, *t, at + 1) for t in TILES}
            ey_next = {t: get(1, *t, at + 1) for t in TILES}
            dy_ez, dx_ez = diff(fwd_y, ez), diff(fwd_x, ez)
            dx_ey, dy_ex = diff(fwd_x, ey), diff(fwd_y, ex)
            hx, hy, hz = {}, {}, {}
            for t in TILES:
                hx[t] = get(3, *t, at) - ch[t] * (dy_ez[t] - (ey_next[t] - ey[t]))
                hy[t] = get(4, *t, at) - ch[t] * ((ex_next[t] - ex[t]) - dx_ez[t])
                hz[t] = get(5, *t, at) - ch[t] * (dx_ey[t] - dy_ex[t])
                put(3, *t, at, hx[t])
                put(4, *t, at, hy[t])
                put(5, *t, at, hz[t])
            dy_hz, dx_hz = diff(bwd_y, hz), diff(bwd_x, hz)
            dx_hy, dy_hx = diff(bwd_x, hy), diff(bwd_y, hx)
            for t in TILES:
                ce = get(6, *t, at)
                put(0, *t, at, ex[t] + ce * (dy_hz[t] - (hy[t] - hy_prev[t])))
                put(1, *t, at, ey[t] + ce * ((hx[t] - hx_prev[t]) - dx_hz[t]))
                new = ez[t] + ce * (dx_hy[t] - dy_hx[t])
                put(2, *t, at, new)
                if t == (0, 0):
                    acc = [acc[k] + new * weight_ref[k, j : j + 1, :] for k in range(PORT_TILE)]
            hx_prev, hy_prev, ex, ey = hx, hy, ex_next, ey_next
        for k in range(PORT_TILE):
            chosen = jnp.where(sub == prow_ref[0, 0, k], acc[k], 0.0)
            sum_ref[n, k : k + 1, :] = jnp.sum(chosen, axis=0, keepdims=True)
        return carry

    lax.fori_loop(0, STEPS, step, 0)

    transform = jnp.zeros((8, 128), jnp.float32)
    for n in range(STEPS):
        sampled = jnp.sum(sum_ref[n], axis=1, keepdims=True)
        transform = transform + sampled * basis_ref[n : n + 1, :]
    per_row = 128 // (2 * FREQ)
    place = iota(term_ref.shape, 0)
    term = jnp.zeros(term_ref.shape, jnp.float32)
    for k in range(PORT_TILE):
        port = pid_ref[0, 0, k]
        spread = jnp.broadcast_to(transform[k : k + 1, :], (8, 128))
        spread = pltpu.roll(spread, (port % per_row) * (2 * FREQ), 1)
        spread = jnp.concatenate([spread] * (term_ref.shape[0] // 8), axis=0)
        term = term + jnp.where(place == port // per_row, spread, 0.0)
    term_ref[...] = term

    for gz_is in (0, 1):

        @pl.when(gz == gz_is)
        def _(gz_is=gz_is):
            base = 1 + DEPTH * gz_is
            for c in range(3):
                eout_ref[c] = field_ref[c, base : base + layers, 0:8, 0:128]
                hout_ref[c] = field_ref[c + 3, base : base + layers, 0:8, 0:128]


def shifted(block, axis, size, distance):
    route = [(i - distance, i) for i in range(size) if 0 <= i - distance < size]
    return lax.ppermute(block, axis, route)


def swapped(block, axis, size, bit=1):
    return lax.ppermute(block, axis, [(i, i ^ bit) for i in range(size)])


def solution(mesh):
    sizes = dict(mesh.shape)
    row_size, col_size, gz_size = sizes["row"], sizes["col"], sizes["gz"]

    def across_rows(blocks):
        if row_size == 2:
            return (swapped(blocks[0], "row", 2),)
        return (shifted(blocks[0], "row", row_size, 1), shifted(blocks[1], "row", row_size, -1))

    def per_device(
        electric, magnetic, material, eps_table, mode_table, port_row, port_col, port_mode, port_ids
    ):
        layers, rows_dev, cols_dev = material.shape
        f32 = jnp.float32
        n_x = 1 if row_size == 2 else 2
        n_pairs = 3 * layers + layers // 2
        n_corner = FIELDS * DEPTH
        packed = pl.pallas_call(
            functools.partial(pack_kernel, row_size),
            out_shape=[
                jax.ShapeDtypeStruct(material.shape, f32),
                jax.ShapeDtypeStruct((FIELDS * DEPTH, 8, 128), f32),
                jax.ShapeDtypeStruct((FIELDS, 8, 128), f32),
                jax.ShapeDtypeStruct((FIELDS, 8, 128), f32),
            ]
            + [jax.ShapeDtypeStruct((n_pairs, 8, 128), f32)] * n_x,
            in_specs=[SMEM, VMEM, VMEM, VMEM],
            out_specs=[VMEM] * (4 + n_x),
            compiler_params=PARAMS,
            name="pack",
        )(eps_table, electric, magnetic, material)
        coef, z_send, up_send, down_send = packed[:4]
        x_halo = across_rows(packed[4:])
        low = shifted(up_send, "col", col_size, 1)
        high = shifted(down_send, "col", col_size, -1)
        z_halo = swapped(z_send, "gz", gz_size)
        y_halo = jnp.concatenate([low, high])
        yz_halo = swapped(y_halo, "gz", gz_size)
        corner_send = pl.pallas_call(
            functools.partial(corner_kernel, row_size),
            out_shape=[jax.ShapeDtypeStruct((n_corner, 8, 128), f32)] * n_x,
            in_specs=[VMEM] * 3,
            out_specs=[VMEM] * n_x,
            compiler_params=PARAMS,
            name="corners",
        )(z_halo, y_halo, yz_halo)
        corner = across_rows(corner_send)
        total_ports = PORT_TILE * col_size * row_size
        term_rows = max(8, total_ports * 2 * FREQ // 128)
        electric_out, magnetic_out, term = pl.pallas_call(
            functools.partial(step_kernel, row_size),
            out_shape=[
                jax.ShapeDtypeStruct(electric.shape, f32),
                jax.ShapeDtypeStruct(magnetic.shape, f32),
                jax.ShapeDtypeStruct((term_rows, 128), f32),
            ],
            in_specs=[VMEM] * 2 + [SMEM] * 4 + [VMEM] * (6 + 2 * n_x),
            out_specs=[VMEM] * 3,
            scratch_shapes=[
                pltpu.VMEM((FIELDS, layers + DEPTH + 2, 16, 256), f32),
                pltpu.VMEM((PORT_TILE, layers + 8, 128), f32),
                pltpu.VMEM((layers, 128), f32),
                pltpu.VMEM((STEPS, 8, 128), f32),
            ],
            compiler_params=PARAMS,
            name="steps",
        )(
            mode_table, jnp.asarray(dft_basis()), port_row, port_col, port_mode, port_ids,
            electric, magnetic, coef, z_halo, y_halo, yz_halo, *x_halo, *corner,
        )
        for axis in ("gz", "row", "col"):
            bit = 1
            while bit < sizes[axis]:
                term = term + swapped(term, axis, sizes[axis], bit)
                bit *= 2
        mine = (lax.axis_index("col") * row_size + lax.axis_index("row")) * gz_size + lax.axis_index("gz")
        own = total_ports // (col_size * row_size * gz_size)
        per_row = 128 // (own * 2 * FREQ)
        cut = lax.dynamic_slice(
            term, (mine // per_row, (mine % per_row) * own * 2 * FREQ), (1, own * 2 * FREQ)
        )
        return (electric_out, magnetic_out, cut.reshape(own, 2 * FREQ))

    in_specs = (
        P(None, "gz", "row", ("grp", "col")),
        P(None, "gz", "row", ("grp", "col")),
        P("gz", "row", ("grp", "col")),
        P(),
        P(None, "gz", None),
        P(("grp", "row"), "col", None),
        P(("grp", "row"), "col", None),
        P(("grp", "row"), "col", None),
        P(("grp", "row"), "col", None),
    )
    out_specs = (
        P(None, "gz", "row", ("grp", "col")),
        P(None, "gz", "row", ("grp", "col")),
        P(("grp", "col", "row", "gz"), None),
    )
    return jax.shard_map(
        per_device, mesh=mesh, in_specs=in_specs, out_specs=out_specs, check_vma=False
    )
```

```python
import functools

import jax
import jax.numpy as jnp
import numpy as np
from jax import lax
from jax.experimental import pallas as pl
from jax.experimental.pallas import tpu as pltpu
from jax.sharding import PartitionSpec as P

STEPS = 4
FREQ = 8
MATS = 8
PLEN = 64
PORT_TILE = 4
FIELDS = 7
DEPTH = STEPS

time_step = 0.5

VMEM = pl.BlockSpec(memory_space=pltpu.VMEM)
SMEM = pl.BlockSpec(memory_space=pltpu.SMEM)
PARAMS = pltpu.CompilerParams(vmem_limit_bytes=48 * 1024 * 1024)


def dft_basis():
    times = (np.arange(STEPS) + 1.0) * time_step
    omegas = np.pi * (np.arange(FREQ) + 1.0) / FREQ
    angle = times[:, None] * omegas[None, :]
    basis = np.zeros((8, 128), np.float32)
    basis[:STEPS, : 2 * FREQ] = np.concatenate([np.cos(angle), -np.sin(angle)], axis=1)
    return basis


def iota(shape, axis):
    return lax.broadcasted_iota(jnp.int32, shape, axis)


def pack_pair(first, second, up):
    low = iota((8, 128), 0) < DEPTH
    if up:
        return jnp.where(low, pltpu.roll(first, DEPTH, 0), second)
    return jnp.where(low, first, pltpu.roll(second, DEPTH, 0))


def pack_rows(pairs, row_size, out_refs):
    if row_size == 2:
        row = lax.axis_index("row")
        for up in (True, False):

            @pl.when(row == (0 if up else 1))
            def _(up=up):
                for i, (first, second) in enumerate(pairs):
                    out_refs[0][i] = pack_pair(first(), second(), up)
    else:
        for i, (first, second) in enumerate(pairs):
            out_refs[0][i] = pack_pair(first(), second(), True)
            out_refs[1][i] = pack_pair(first(), second(), False)


def unpack_pair(refs, i, row_size):
    low = iota((8, 128), 0) < DEPTH
    if row_size == 2:
        row = lax.axis_index("row")
        packed = refs[0][i]
        mine = (iota((8, 128), 0) < DEPTH) == (row == 0)
        turned = pltpu.roll(packed, DEPTH, 0)
        first = jnp.where(row == 0, packed, turned)
        second = jnp.where(row == 0, turned, packed)
        zero = jnp.zeros_like(packed)
        return jnp.where(mine, first, zero), jnp.where(mine, second, zero)
    below, above = refs[0][i], refs[1][i]
    first = jnp.where(low, above, pltpu.roll(below, DEPTH, 0))
    second = jnp.where(low, pltpu.roll(above, DEPTH, 0), below)
    return first, second


def pack_kernel(row_size, *refs):
    inputs, outputs, (scratch, sems) = refs[:4], refs[4:-5], (refs[-5:-1], refs[-1])
    coef_ref, z_ref, up_ref, down_ref, *x_refs = outputs
    copies = [pltpu.make_async_copy(inputs[i], scratch[i], sems.at[i]) for i in range(4)]
    for copy in copies:
        copy.start()
    for copy in copies:
        copy.wait()
    eps_ref, elec_ref, magn_ref, mat_ref = scratch
    layers = elec_ref.shape[1]
    gz = lax.axis_index("gz")
    for z in range(layers):
        material = mat_ref[z]
        eps = jnp.full((8, 128), eps_ref[0], jnp.float32)
        for which in range(1, MATS):
            eps = jnp.where(material == which, eps_ref[which], eps)
        coef_ref[z] = time_step * (1.0 / eps)

    def tile(field, z):
        if field < 3:
            return elec_ref[field, z]
        if field < 6:
            return magn_ref[field - 3, z]
        return coef_ref[z]

    start = jnp.where(gz == 0, layers - DEPTH, 0)
    for field in range(FIELDS):
        for k in range(DEPTH):
            z_ref[field * DEPTH + k] = tile(field, start + k)
    group = iota((8, 128), 1) // DEPTH
    for field in range(FIELDS):
        up = jnp.zeros((8, 128), jnp.float32)
        down = jnp.zeros((8, 128), jnp.float32)
        for z in range(layers):
            turned = pltpu.roll(tile(field, z), (DEPTH * (z + 1)) % 128, 1)
            up = jnp.where(group == z, turned, up)
            down = jnp.where(group == (z + 1) % layers, turned, down)
        up_ref[field] = up
        down_ref[field] = pltpu.roll(down, 128 - DEPTH, 1)
    pairs = [
        (functools.partial(tile, c, z), functools.partial(tile, c + 3, z))
        for c in range(3)
        for z in range(layers)
    ]
    pairs += [(functools.partial(tile, 6, z), functools.partial(tile, 6, z + layers // 2)) for z in range(layers // 2)]
    pack_rows(pairs, row_size, x_refs)


def corner_kernel(row_size, z_ref, y_ref, yz_ref, *x_refs):
    half = FIELDS * 2
    pairs = []
    for i in range(FIELDS * DEPTH):
        other = (y_ref, i) if i < half else (yz_ref, i - half)
        pairs.append((functools.partial(z_ref.__getitem__, i), functools.partial(other[0].__getitem__, other[1])))
    pack_rows(pairs, row_size, x_refs)


def fwd_y(main, side):
    last = iota((8, 128), 1) == 127
    a, b = pltpu.roll(main, 127, 1), pltpu.roll(side, 127, 1)
    return jnp.where(last, b, a) - main, jnp.where(last, a, b) - side


def bwd_y(main, side):
    first = iota((8, 128), 1) == 0
    a, b = pltpu.roll(main, 1, 1), pltpu.roll(side, 1, 1)
    return main - jnp.where(first, b, a), side - jnp.where(first, a, b)


def fwd_x(main, side):
    last = iota((8, 128), 0) == 7
    a, b = pltpu.roll(main, 7, 0), pltpu.roll(side, 7, 0)
    return jnp.where(last, b, a) - main, jnp.where(last, a, b) - side


def bwd_x(main, side):
    first = iota((8, 128), 0) == 0
    a, b = pltpu.roll(main, 1, 0), pltpu.roll(side, 1, 0)
    return main - jnp.where(first, b, a), side - jnp.where(first, a, b)


TILES = ((0, 0), (0, 1), (1, 0), (1, 1))


def diff(kind, tiles):
    out = {}
    if kind in (fwd_y, bwd_y):
        for r in range(2):
            out[r, 0], out[r, 1] = kind(tiles[r, 0], tiles[r, 1])
    else:
        for c in range(2):
            out[0, c], out[1, c] = kind(tiles[0, c], tiles[1, c])
    return out


def step_kernel(
    row_size, ports_each, mode_ref, basis_ref, prow_ref, pcol_ref, pmode_ref, pid_ref,
    elec_ref, magn_ref, coef_ref, z_ref, y_ref, yz_ref, *rest,
):
    n_x = 1 if row_size == 2 else 2
    x_refs, corner_refs = rest[:n_x], rest[n_x : 2 * n_x]
    eout_ref, hout_ref, term_ref, field_ref, weight_ref, strip_ref, sum_ref = rest[2 * n_x :]
    layers = elec_ref.shape[1]
    extended = layers + DEPTH
    gz, row, col = (lax.axis_index(name) for name in ("gz", "row", "col"))
    lane, sub = iota((8, 128), 1), iota((8, 128), 0)

    def put(field, r, c, where, value):
        field_ref[field, where, 8 * r : 8 * r + 8, 128 * c : 128 * c + 128] = value

    def get(field, r, c, where):
        return field_ref[field, where, 8 * r : 8 * r + 8, 128 * c : 128 * c + 128]

    def assemble(gz_is):
        base = 1 + DEPTH * gz_is
        halo = 1 + layers * (1 - gz_is)
        far = 0 if gz_is == 0 else layers - DEPTH

        def side(low_tile, high_tile, z):
            low = pltpu.roll(low_tile, (128 - DEPTH - DEPTH * z) % 128, 1)
            high = pltpu.roll(high_tile, (128 - DEPTH * z) % 128, 1)
            return jnp.where(lane < 64, high, low)

        corner = {}
        for i in range(FIELDS * DEPTH):
            first, second = unpack_pair(corner_refs, i, row_size)
            corner["z", i] = first
            corner["y" if i < 2 * FIELDS else "yz", i % (2 * FIELDS)] = second
        for field in range(FIELDS):
            for c in (0, 1):
                put(field, 0, c, 0, jnp.zeros((8, 128), jnp.float32))
                put(field, 1, c, 0, jnp.zeros((8, 128), jnp.float32))
                put(field, 0, c, extended + 1, jnp.zeros((8, 128), jnp.float32))
                put(field, 1, c, extended + 1, jnp.zeros((8, 128), jnp.float32))
            for z in range(layers):
                if field < 3:
                    main = elec_ref[field, z]
                elif field < 6:
                    main = magn_ref[field - 3, z]
                else:
                    main = coef_ref[z]
                put(field, 0, 0, base + z, main)
                put(field, 0, 1, base + z, side(y_ref[field], y_ref[FIELDS + field], z))
                put(field, 1, 1, base + z, side(corner["y", field], corner["y", FIELDS + field], z))
            for k in range(DEPTH):
                i = field * DEPTH + k
                put(field, 0, 0, halo + k, z_ref[i])
                put(field, 0, 1, halo + k, side(yz_ref[field], yz_ref[FIELDS + field], far + k))
                put(field, 1, 0, halo + k, corner["z", i])
                put(field, 1, 1, halo + k, side(corner["yz", field], corner["yz", FIELDS + field], far + k))
        for c in range(3):
            for z in range(layers):
                first, second = unpack_pair(x_refs, c * layers + z, row_size)
                put(c, 1, 0, base + z, first)
                put(c + 3, 1, 0, base + z, second)
        for z in range(layers // 2):
            first, second = unpack_pair(x_refs, 3 * layers + z, row_size)
            put(6, 1, 0, base + z, first)
            put(6, 1, 0, base + z + layers // 2, second)
        for k in range(PORT_TILE):
            weight_ref[k] = jnp.zeros(weight_ref.shape[1:], jnp.float32)
            strip_ref[...] = jnp.zeros(strip_ref.shape, jnp.float32)
            strip_ref[:, :PLEN] = mode_ref[pmode_ref[0, 0, k]]
            moved = pltpu.roll(strip_ref[...], pcol_ref[0, 0, k], 1)
            weight_ref[k, DEPTH * gz_is : DEPTH * gz_is + layers, :] = moved

    for gz_is in (0, 1):
        pl.when(gz == gz_is)(functools.partial(assemble, gz_is))

    half = jnp.full((8, 128), time_step, jnp.float32)
    below = jnp.where((sub >= 4) & (row == 0), 0.0, half)
    before = jnp.where((lane >= 64) & (col == 0), 0.0, half)
    ch = {(0, 0): half, (0, 1): before, (1, 0): below, (1, 1): jnp.minimum(below, before)}

    def step(n, carry):
        hx_prev = {t: jnp.zeros((8, 128), jnp.float32) for t in TILES}
        hy_prev = dict(hx_prev)
        ex = {t: get(0, *t, 1) for t in TILES}
        ey = {t: get(1, *t, 1) for t in TILES}
        acc = [jnp.zeros((8, 128), jnp.float32) for _ in range(PORT_TILE)]
        for j in range(extended):
            at = j + 1
            ez = {t: get(2, *t, at) for t in TILES}
            ex_next = {t: get(0, *t, at + 1) for t in TILES}
            ey_next = {t: get(1, *t, at + 1) for t in TILES}
            dy_ez, dx_ez = diff(fwd_y, ez), diff(fwd_x, ez)
            dx_ey, dy_ex = diff(fwd_x, ey), diff(fwd_y, ex)
            hx, hy, hz = {}, {}, {}
            for t in TILES:
                hx[t] = get(3, *t, at) - ch[t] * (dy_ez[t] - (ey_next[t] - ey[t]))
                hy[t] = get(4, *t, at) - ch[t] * ((ex_next[t] - ex[t]) - dx_ez[t])
                hz[t] = get(5, *t, at) - ch[t] * (dx_ey[t] - dy_ex[t])
                put(3, *t, at, hx[t])
                put(4, *t, at, hy[t])
                put(5, *t, at, hz[t])
            dy_hz, dx_hz = diff(bwd_y, hz), diff(bwd_x, hz)
            dx_hy, dy_hx = diff(bwd_x, hy), diff(bwd_y, hx)
            for t in TILES:
                ce = get(6, *t, at)
                put(0, *t, at, ex[t] + ce * (dy_hz[t] - (hy[t] - hy_prev[t])))
                put(1, *t, at, ey[t] + ce * ((hx[t] - hx_prev[t]) - dx_hz[t]))
                new = ez[t] + ce * (dx_hy[t] - dy_hx[t])
                put(2, *t, at, new)
                if t == (0, 0):
                    acc = [acc[k] + new * weight_ref[k, j : j + 1, :] for k in range(PORT_TILE)]
            hx_prev, hy_prev, ex, ey = hx, hy, ex_next, ey_next
        for k in range(PORT_TILE):
            chosen = jnp.where(sub == prow_ref[0, 0, k], acc[k], 0.0)
            sum_ref[n, k : k + 1, :] = jnp.sum(chosen, axis=0, keepdims=True)
        return carry

    lax.fori_loop(0, STEPS, step, 0)

    transform = jnp.zeros((8, 128), jnp.float32)
    for n in range(STEPS):
        sampled = jnp.sum(sum_ref[n], axis=1, keepdims=True)
        transform = transform + sampled * basis_ref[n : n + 1, :]
    place = iota(term_ref.shape, 0)
    term = jnp.zeros(term_ref.shape, jnp.float32)
    for k in range(PORT_TILE):
        port = pid_ref[0, 0, k]
        spread = jnp.broadcast_to(transform[k : k + 1, :], (8, 128))
        spread = pltpu.roll(spread, (port % ports_each) * (2 * FREQ), 1)
        spread = jnp.concatenate([spread] * (term_ref.shape[0] // 8), axis=0)
        term = term + jnp.where(place == port // ports_each, spread, 0.0)
    term_ref[...] = term

    for gz_is in (0, 1):

        @pl.when(gz == gz_is)
        def _(gz_is=gz_is):
            base = 1 + DEPTH * gz_is
            for c in range(3):
                eout_ref[c] = field_ref[c, base : base + layers, 0:8, 0:128]
                hout_ref[c] = field_ref[c + 3, base : base + layers, 0:8, 0:128]


def shifted(block, axis, size, distance):
    route = [(i - distance, i) for i in range(size) if 0 <= i - distance < size]
    return lax.ppermute(block, axis, route)


def swapped(block, axis, size, bit=1):
    return lax.ppermute(block, axis, [(i, i ^ bit) for i in range(size)])


def solution(mesh):
    sizes = dict(mesh.shape)
    row_size, col_size, gz_size = sizes["row"], sizes["col"], sizes["gz"]

    def across_rows(blocks):
        if row_size == 2:
            return (swapped(blocks[0], "row", 2),)
        return (shifted(blocks[0], "row", row_size, 1), shifted(blocks[1], "row", row_size, -1))

    def per_device(
        electric, magnetic, material, eps_table, mode_table, port_row, port_col, port_mode, port_ids
    ):
        layers, rows_dev, cols_dev = material.shape
        f32 = jnp.float32
        n_x = 1 if row_size == 2 else 2
        n_pairs = 3 * layers + layers // 2
        n_corner = FIELDS * DEPTH
        packed = pl.pallas_call(
            functools.partial(pack_kernel, row_size),
            out_shape=[
                jax.ShapeDtypeStruct(material.shape, f32),
                jax.ShapeDtypeStruct((FIELDS * DEPTH, 8, 128), f32),
                jax.ShapeDtypeStruct((FIELDS, 8, 128), f32),
                jax.ShapeDtypeStruct((FIELDS, 8, 128), f32),
            ]
            + [jax.ShapeDtypeStruct((n_pairs, 8, 128), f32)] * n_x,
            in_specs=[pl.BlockSpec(memory_space=pl.ANY)] * 4,
            out_specs=[VMEM] * (4 + n_x),
            scratch_shapes=[
                pltpu.SMEM(eps_table.shape, f32),
                pltpu.VMEM(electric.shape, f32),
                pltpu.VMEM(magnetic.shape, f32),
                pltpu.VMEM(material.shape, jnp.int32),
                pltpu.SemaphoreType.DMA((4,)),
            ],
            compiler_params=PARAMS,
            name="pack",
        )(eps_table, electric, magnetic, material)
        coef, z_send, up_send, down_send = packed[:4]
        x_halo = across_rows(packed[4:])
        low = shifted(up_send, "col", col_size, 1)
        high = shifted(down_send, "col", col_size, -1)
        z_halo = swapped(z_send, "gz", gz_size)
        y_halo = jnp.concatenate([low, high])
        yz_halo = swapped(y_halo, "gz", gz_size)
        corner_send = pl.pallas_call(
            functools.partial(corner_kernel, row_size),
            out_shape=[jax.ShapeDtypeStruct((n_corner, 8, 128), f32)] * n_x,
            in_specs=[VMEM] * 3,
            out_specs=[VMEM] * n_x,
            compiler_params=PARAMS,
            name="corners",
        )(z_halo, y_halo, yz_halo)
        corner = across_rows(corner_send)
        devices = col_size * row_size * gz_size
        ports_each = PORT_TILE * col_size * row_size // devices
        electric_out, magnetic_out, term = pl.pallas_call(
            functools.partial(step_kernel, row_size, ports_each),
            out_shape=[
                jax.ShapeDtypeStruct(electric.shape, f32),
                jax.ShapeDtypeStruct(magnetic.shape, f32),
                jax.ShapeDtypeStruct((devices, 128), f32),
            ],
            in_specs=[VMEM] * 2 + [SMEM] * 4 + [VMEM] * (6 + 2 * n_x),
            out_specs=[VMEM] * 3,
            scratch_shapes=[
                pltpu.VMEM((FIELDS, layers + DEPTH + 2, 16, 256), f32),
                pltpu.VMEM((PORT_TILE, layers + 8, 128), f32),
                pltpu.VMEM((layers, 128), f32),
                pltpu.VMEM((STEPS, 8, 128), f32),
            ],
            compiler_params=PARAMS,
            name="steps",
        )(
            mode_table, jnp.asarray(dft_basis()), port_row, port_col, port_mode, port_ids,
            electric, magnetic, coef, z_halo, y_halo, yz_halo, *x_halo, *corner,
        )
        terms = lax.all_to_all(term, ("col", "row", "gz"), 0, 0, tiled=True)
        mine = jnp.sum(terms, axis=0)[: ports_each * 2 * FREQ]
        return (electric_out, magnetic_out, mine.reshape(ports_each, 2 * FREQ))

    in_specs = (
        P(None, "gz", "row", ("grp", "col")),
        P(None, "gz", "row", ("grp", "col")),
        P("gz", "row", ("grp", "col")),
        P(),
        P(None, "gz", None),
        P(("grp", "row"), "col", None),
        P(("grp", "row"), "col", None),
        P(("grp", "row"), "col", None),
        P(("grp", "row"), "col", None),
    )
    out_specs = (
        P(None, "gz", "row", ("grp", "col")),
        P(None, "gz", "row", ("grp", "col")),
        P(("grp", "col", "row", "gz"), None),
    )
    return jax.shard_map(
        per_device, mesh=mesh, in_specs=in_specs, out_specs=out_specs, check_vma=False
    )
```

```python
import functools

import jax
import jax.numpy as jnp
import numpy as np
from jax import lax
from jax.experimental import pallas as pl
from jax.experimental.pallas import tpu as pltpu
from jax.sharding import PartitionSpec as P

STEPS = 4
FREQ = 8
MATS = 8
PLEN = 64
PORT_TILE = 4
FIELDS = 7
DEPTH = STEPS
ROWS = 8
LAYERS = 32
CHUNK = 5
GROUP = 32

time_step = 0.5

UP_PLANES = [(f, 4) for f in (0, 1, 2, 4, 5)] + [(f, x) for x in (5, 6, 7) for f in range(FIELDS)]
DOWN_PLANES = [(f, x) for x in (0, 1, 2) for f in range(FIELDS)] + [(1, 3), (2, 3)]
PLANES = max(len(UP_PLANES), len(DOWN_PLANES))
PAIRS = (PLANES + 1) // 2

VMEM = pl.BlockSpec(memory_space=pltpu.VMEM)
SMEM = pl.BlockSpec(memory_space=pltpu.SMEM)
HBM = pl.BlockSpec(memory_space=pltpu.HBM)


def dft_basis():
    times = (np.arange(STEPS) + 1.0) * time_step
    omegas = np.pi * (np.arange(FREQ) + 1.0) / FREQ
    angle = times[:, None] * omegas[None, :]
    basis = np.zeros((8, 128), np.float32)
    basis[:STEPS, : 2 * FREQ] = np.concatenate([np.cos(angle), -np.sin(angle)], axis=1)
    return basis


def iota(axis):
    return lax.broadcasted_iota(jnp.int32, (8, 128), axis)


def turn(tile, shift, axis):
    return pltpu.roll(tile, shift % tile.shape[axis], axis)


def directions(row_size, body):
    if row_size == 2:
        row = lax.axis_index("row")
        pl.when(row == 0)(functools.partial(body, True, 0))
        pl.when(row == 1)(functools.partial(body, False, 0))
    else:
        body(True, 0)
        body(False, 1)


def pack_kernel(row_size, eps_hbm, elec_hbm, magn_hbm, mat_hbm, main_ref, z_ref, *rest):
    x_refs, (eps_ref, mat_ref, sems) = rest[:-3], rest[-3:]
    block = LAYERS * ROWS
    copies = [pltpu.make_async_copy(eps_hbm, eps_ref, sems.at[0]), pltpu.make_async_copy(mat_hbm, mat_ref, sems.at[1])]
    copies.append(pltpu.make_async_copy(elec_hbm, main_ref.at[pl.ds(0, 3)], sems.at[2]))
    copies.append(pltpu.make_async_copy(magn_hbm, main_ref.at[pl.ds(3, 3)], sems.at[3]))
    for copy in copies:
        copy.start()
    copies[0].wait()
    copies[1].wait()
    for z in range(LAYERS):
        material = mat_ref[z]
        eps = jnp.full((8, 128), eps_ref[0], jnp.float32)
        for which in range(1, MATS):
            eps = jnp.where(material == which, eps_ref[which], eps)
        main_ref[6, z] = time_step * (1.0 / eps)
    copies[2].wait()
    copies[3].wait()
    flat = main_ref.reshape(FIELDS * block, 128)

    def send(up, slot):
        for i, (f, x) in enumerate(UP_PLANES if up else DOWN_PLANES):
            x_refs[slot][i] = flat[pl.ds(f * block + x, LAYERS, stride=ROWS), :]

    directions(row_size, send)
    start = jnp.where(lax.axis_index("gz") == 0, LAYERS - DEPTH, 0)
    for f in range(FIELDS):
        z_ref[f] = main_ref[f, pl.ds(start, DEPTH)]


def edge_kernel(main_ref, z_ref, mode_ref, prow_ref, pcol_ref, pmode_ref,
                state_ref, own_ref, up_ref, down_ref, ext_ref, weight_ref, stage_ref, strip_ref):
    lane = iota(1)
    group = lane // GROUP
    place = lane % GROUP
    gz = lax.axis_index("gz")
    block = LAYERS * ROWS
    for f in range(FIELDS):
        stage_ref[f, 0:block] = main_ref[f].reshape(block, 128)
        halo = z_ref[f].reshape(DEPTH * ROWS, 128)
        nothing = jnp.zeros_like(halo)
        stage_ref[f, block : block + DEPTH * ROWS] = jnp.where(gz == 0, halo, nothing)
        stage_ref[f, block + DEPTH * ROWS :] = jnp.where(gz == 0, nothing, halo)
        ext_ref[f] = stage_ref[f, block:]
    for b in range(2):
        for zz in range(CHUNK):
            up = jnp.zeros((8, 128), jnp.float32)
            down = jnp.zeros((8, 128), jnp.float32)
            for f in range(FIELDS):
                own = None
                for r in range(4):
                    x = 4 * b + r
                    tile = stage_ref[f, pl.ds(zz * ROWS + x, 8, stride=CHUNK * ROWS), :]
                    state_ref[f, x, zz] = tile
                    moved = turn(tile, GROUP * r + 8, 1)
                    own = moved if own is None else jnp.where(group == r, moved, own)
                own_ref[f, b, zz] = own
                up = jnp.where(place // DEPTH == f, turn(own, DEPTH * f - 4, 1), up)
                down = jnp.where(place // DEPTH == f, turn(own, DEPTH * f - 8, 1), down)
            up_ref[b, zz] = up
            down_ref[b, zz] = down
    for k in range(PORT_TILE):
        strip_ref[...] = jnp.zeros(strip_ref.shape, jnp.float32)
        strip_ref[0:LAYERS, 0:PLEN] = mode_ref[pmode_ref[0, 0, k]]
        strip_ref[...] = pltpu.roll(strip_ref[...], pcol_ref[0, 0, k], 1)
        at = lane - GROUP * (prow_ref[0, 0, k] % 4)
        for zz in range(CHUNK):
            tile = strip_ref[pl.ds(zz, 8, stride=CHUNK), :]
            weight_ref[k, 0, zz] = jnp.where((lane >= DEPTH) & (lane < 128 - DEPTH), tile, 0.0)
            own = pltpu.roll(tile, GROUP * (prow_ref[0, 0, k] % 4) + 8, 1)
            edge = jnp.where((at >= 4) & (at < 8), own, 0.0)
            weight_ref[k, 1, zz] = jnp.where((at >= 16) & (at < 20), turn(own, 8, 1), edge)


def corner_kernel(row_size, ext_ref, low_ref, high_ref, *x_refs):
    def send(up, slot):
        planes = UP_PLANES if up else DOWN_PLANES

        def tile(i):
            f, x = planes[i]
            return ext_ref[f, pl.ds(x, 8, stride=ROWS), :]

        for i in range(PAIRS):
            first = tile(i)
            if i + PAIRS < len(planes):
                first = first + turn(tile(i + PAIRS), 4, 0)
            x_refs[slot][i] = first
        b = 1 if up else 0
        for zz in range(CHUNK):
            x_refs[slot][PAIRS + zz] = low_ref[b, zz]
            x_refs[slot][PAIRS + CHUNK + zz] = high_ref[b, zz]

    directions(row_size, send)


def edge_tile(own, low, high, f):
    place = iota(1) % GROUP
    out = jnp.where(place < 16, turn(low, 12 - DEPTH * f, 1), turn(own, 8, 1))
    out = jnp.where(place < 12, turn(high, 8 - DEPTH * f, 1), out)
    return jnp.where(place < 8, own, out)


def step_kernel(row_size, ports_each, basis_ref, prow_ref, pid_ref, state_ref, own_ref, low_ref, high_ref, weight_ref, *rest):
    n_x = 1 if row_size == 2 else 2
    x_refs, corner_refs = rest[:n_x], rest[n_x : 2 * n_x]
    eout_hbm, hout_hbm, term_ref, main, edge, plane_ref, sum_ref, out_ref, sems = rest[2 * n_x :]
    gz, row, col = (lax.axis_index(name) for name in ("gz", "row", "col"))
    lane, sub = iota(1), iota(0)
    place, group = lane % GROUP, lane // GROUP
    zeros = jnp.zeros((8, 128), jnp.float32)
    last_group, first_group = group == 3, group == 0

    def run(has_below, has_above):
        for f in range(FIELDS):
            for x in range(ROWS):
                for zz in range(CHUNK):
                    main[f, DEPTH + x, zz] = state_ref[f, x, zz]
            for b in range(2):
                for zz in range(CHUNK):
                    edge[f, 1 + b, zz] = edge_tile(own_ref[f, b, zz], low_ref[b, zz], high_ref[b, zz], f)

        def halo_rows(planes, slot, offset, b):
            valid = (sub < 4) == (gz == 0)
            got = set(planes)
            for i, (f, x) in enumerate(planes):
                packed = corner_refs[slot][i % PAIRS]
                if i >= PAIRS:
                    packed = turn(packed, 4, 0)
                plane_ref[slot, i, 0:LAYERS] = x_refs[slot][i]
                plane_ref[slot, i, LAYERS:] = jnp.where(valid, packed, 0.0)
            for i, (f, x) in enumerate(planes):
                for zz in range(CHUNK):
                    main[f, DEPTH + x + offset, zz] = plane_ref[slot, i, pl.ds(zz, 8, stride=CHUNK), :]
            for f in range(FIELDS):
                for zz in range(CHUNK):
                    own = zeros
                    for r in range(4):
                        x = 4 * b + r
                        if (f, x - offset) in got:
                            own = jnp.where(group == r, turn(main[f, DEPTH + x, zz], GROUP * r + 8, 1), own)
                    low = corner_refs[slot][PAIRS + zz]
                    high = corner_refs[slot][PAIRS + CHUNK + zz]
                    edge[f, 1 + b, zz] = edge_tile(own, low, high, f)

        if has_below:
            halo_rows(UP_PLANES, 0, -ROWS, -1)
        if has_above:
            halo_rows(DOWN_PLANES, n_x - 1, ROWS, 2)

        below_layers = (sub == 7) & (gz == 0)
        half = [jnp.where(below_layers, 0.0, time_step) if zz else jnp.full((8, 128), time_step) for zz in range(CHUNK)]
        outside = (place >= 12) & (place < 16) & (col == 0)
        edge_half = [jnp.where(outside, 0.0, half[zz]) for zz in range(CHUNK)]
        lowest = jnp.where(row == 0, 0.0, 1.0) if row_size > 2 else None

        def above(tiles, zz):
            return tiles[zz + 1] if zz + 1 < CHUNK else turn(tiles[0], -1, 0)

        def beneath(tiles, zz):
            return tiles[zz - 1] if zz else turn(tiles[CHUNK - 1], 1, 0)

        def update(keep, i, h, with_e, with_hx, carry, next_x, prev_x):
            every = range(CHUNK)
            ex, ey, ez = ([keep[f, i, zz] for zz in every] for f in range(3))
            ey_up, ez_up = next_x(1, ey, i), next_x(2, ez, i)
            hx, hy, hz = [], [], []
            for zz in every:
                if with_hx:
                    curl = (turn(ez[zz], -1, 1) - ez[zz]) - (above(ey, zz) - ey[zz])
                    hx.append(keep[3, i, zz] - h[zz] * curl)
                    keep[3, i, zz] = hx[zz]
                curl = (above(ex, zz) - ex[zz]) - (ez_up[zz] - ez[zz])
                hy.append(keep[4, i, zz] - h[zz] * curl)
                keep[4, i, zz] = hy[zz]
                curl = (ey_up[zz] - ey[zz]) - (turn(ex[zz], -1, 1) - ex[zz])
                hz.append(keep[5, i, zz] - h[zz] * curl)
                keep[5, i, zz] = hz[zz]
            if with_e:
                hy_down, hz_down = prev_x(hy, carry and carry[0]), prev_x(hz, carry and carry[1])
                for zz in every:
                    c = keep[6, i, zz]
                    curl = (hz[zz] - turn(hz[zz], 1, 1)) - (hy[zz] - beneath(hy, zz))
                    keep[0, i, zz] = ex[zz] + c * curl
                    curl = (hx[zz] - beneath(hx, zz)) - (hz[zz] - hz_down[zz])
                    keep[1, i, zz] = ey[zz] + c * curl
                    curl = (hy[zz] - hy_down[zz]) - (hx[zz] - turn(hx[zz], 1, 1))
                    keep[2, i, zz] = ez[zz] + c * curl
            return hy, hz

        blank = [zeros] * CHUNK

        for n in range(1, STEPS + 1):
            first = n - 5 if has_below else 0
            last = 11 - n if has_above else 7
            final = DEPTH + 11 if has_above else DEPTH + 7

            def next_row(f, own, i):
                return [main[f, i + 1, zz] for zz in range(CHUNK)] if i < final else blank

            def prev_row(own, carry):
                return carry or blank

            carry = None
            for x in range(first, last + 1):
                h = half if lowest is None or x >= 0 else [v * lowest for v in half]
                with_e = not (has_below and x == first)
                carry = update(main, DEPTH + x, h, with_e, with_e, carry, next_row, prev_row)

            top = 3 if has_above else 2

            def next_block(f, own, i):
                turned = [turn(v, -GROUP, 1) for v in own]
                other = [turn(edge[f, i + 1, zz], -GROUP, 1) for zz in range(CHUNK)] if i < top else blank
                return [jnp.where(last_group, o, v) for o, v in zip(other, turned)]

            def prev_block(own, carry):
                turned = [turn(v, GROUP, 1) for v in own]
                other = [turn(v, GROUP, 1) for v in carry] if carry else blank
                return [jnp.where(first_group, o, v) for o, v in zip(other, turned)]

            carry = None
            for i in range(0 if has_below else 1, top + 1):
                h = edge_half if lowest is None or i else [v * lowest for v in edge_half]
                carry = update(edge, i, h, True, True, carry, next_block, prev_block)

            for k in range(PORT_TILE):
                at = prow_ref[0, 0, k]
                total = zeros
                for zz in range(CHUNK):
                    total = total + main[2, DEPTH + at, zz] * weight_ref[k, 0, zz]
                    total = total + edge[2, 1 + at // 4, zz] * weight_ref[k, 1, zz]
                sum_ref[n - 1, k : k + 1, :] = jnp.sum(total, axis=0, keepdims=True)

    if row_size == 2:
        pl.when(row == 0)(functools.partial(run, False, True))
        pl.when(row == 1)(functools.partial(run, True, False))
    else:
        run(True, True)

    copies = []
    for f in range(6):
        for b in range(2):
            for zz in range(CHUNK):
                tile = edge[f, 1 + b, zz]
                near = jnp.where(place < 8, tile, turn(tile, -8, 1))
                for r in range(4):
                    x = 4 * b + r
                    sides = turn(near, -(GROUP * r + 8), 1)
                    tile = jnp.where((lane < DEPTH) | (lane >= 128 - DEPTH), sides, main[f, DEPTH + x, zz])
                    out_ref[f, pl.ds(zz * ROWS + x, 8, stride=CHUNK * ROWS), :] = tile
        dest = eout_hbm if f < 3 else hout_hbm
        copies.append(pltpu.make_async_copy(out_ref.at[f, pl.ds(0, LAYERS * ROWS)], dest.at[f % 3], sems.at[f]))
        copies[-1].start()

    transform = zeros
    for n in range(STEPS):
        sampled = jnp.sum(sum_ref[n], axis=1, keepdims=True)
        transform = transform + sampled * basis_ref[n : n + 1, :]
    target = lax.broadcasted_iota(jnp.int32, term_ref.shape, 0)
    term = jnp.zeros(term_ref.shape, jnp.float32)
    for k in range(PORT_TILE):
        port = pid_ref[0, 0, k]
        spread = jnp.broadcast_to(transform[k : k + 1, :], (8, 128))
        spread = pltpu.roll(spread, (port % ports_each) * (2 * FREQ), 1)
        spread = jnp.concatenate([spread] * (term_ref.shape[0] // 8), axis=0)
        term = term + jnp.where(target == port // ports_each, spread, 0.0)
    term_ref[...] = term
    for copy in copies:
        copy.wait()


def shifted(block, axis, size, distance):
    route = [(i - distance, i) for i in range(size) if 0 <= i - distance < size]
    return lax.ppermute(block, axis, route)


def swapped(block, axis, size):
    return lax.ppermute(block, axis, [(i, i ^ 1) for i in range(size)])


def solution(mesh):
    sizes = dict(mesh.shape)
    row_size, col_size, gz_size = sizes["row"], sizes["col"], sizes["gz"]
    n_x = 1 if row_size == 2 else 2

    def across_rows(blocks):
        if row_size == 2:
            return (swapped(blocks[0], "row", 2),)
        return (shifted(blocks[0], "row", row_size, 1), shifted(blocks[1], "row", row_size, -1))

    def per_device(
        electric, magnetic, material, eps_table, mode_table, port_row, port_col, port_mode, port_ids
    ):
        f32 = jnp.float32

        def array(*shape):
            return jax.ShapeDtypeStruct(shape, f32)

        main, z_send, *x_send = pl.pallas_call(
            functools.partial(pack_kernel, row_size),
            out_shape=[array(FIELDS, LAYERS, ROWS, 128), array(FIELDS, DEPTH, ROWS, 128)]
            + [array(PLANES, LAYERS, 128)] * n_x,
            in_specs=[HBM] * 4,
            out_specs=[VMEM] * (2 + n_x),
            scratch_shapes=[
                pltpu.SMEM(eps_table.shape, f32),
                pltpu.VMEM(material.shape, jnp.int32),
                pltpu.SemaphoreType.DMA((4,)),
            ],
            name="pack",
        )(eps_table, electric, magnetic, material)
        x_halo = across_rows(x_send)
        z_halo = swapped(z_send, "gz", gz_size)
        state, own, up_send, down_send, ext, weights = pl.pallas_call(
            edge_kernel,
            out_shape=[
                array(FIELDS, ROWS, CHUNK, 8, 128),
                array(FIELDS, 2, CHUNK, 8, 128),
                array(2, CHUNK, 8, 128),
                array(2, CHUNK, 8, 128),
                array(FIELDS, 2 * DEPTH * ROWS, 128),
                array(PORT_TILE, 2, CHUNK, 8, 128),
            ],
            in_specs=[VMEM] * 3 + [SMEM] * 3,
            out_specs=[VMEM] * 6,
            scratch_shapes=[
                pltpu.VMEM((FIELDS, 8 * CHUNK * ROWS, 128), f32),
                pltpu.VMEM((8 * CHUNK, 128), f32),
            ],
            name="edges",
        )(main, z_halo, mode_table, port_row, port_col, port_mode)
        low = shifted(up_send, "col", col_size, 1)
        high = shifted(down_send, "col", col_size, -1)
        corner_send = pl.pallas_call(
            functools.partial(corner_kernel, row_size),
            out_shape=[array(PAIRS + 2 * CHUNK, 8, 128)] * n_x,
            in_specs=[VMEM] * 3,
            out_specs=[VMEM] * n_x,
            name="corners",
        )(ext, low, high)
        corner = across_rows(corner_send)
        devices = col_size * row_size * gz_size
        ports_each = PORT_TILE * col_size * row_size // devices
        electric_out, magnetic_out, term = pl.pallas_call(
            functools.partial(step_kernel, row_size, ports_each),
            out_shape=[array(3, LAYERS * ROWS, 128), array(3, LAYERS * ROWS, 128), array(devices, 128)],
            in_specs=[VMEM] + [SMEM] * 2 + [VMEM] * (5 + 2 * n_x),
            out_specs=[HBM, HBM, VMEM],
            scratch_shapes=[
                pltpu.VMEM((FIELDS, ROWS + 2 * DEPTH, CHUNK, 8, 128), f32),
                pltpu.VMEM((FIELDS, 4, CHUNK, 8, 128), f32),
                pltpu.VMEM((n_x, PLANES, 8 * CHUNK, 128), f32),
                pltpu.VMEM((STEPS, 8, 128), f32),
                pltpu.VMEM((6, 8 * CHUNK * ROWS, 128), f32),
                pltpu.SemaphoreType.DMA((6,)),
            ],
            name="steps",
        )(jnp.asarray(dft_basis()), port_row, port_ids, state, own, low, high, weights, *x_halo, *corner)
        terms = lax.all_to_all(term, ("col", "row", "gz"), 0, 0, tiled=True)
        mine = jnp.sum(terms, axis=0)[: ports_each * 2 * FREQ]
        return (
            electric_out.reshape(electric.shape),
            magnetic_out.reshape(magnetic.shape),
            mine.reshape(ports_each, 2 * FREQ),
        )

    in_specs = (
        P(None, "gz", "row", ("grp", "col")),
        P(None, "gz", "row", ("grp", "col")),
        P("gz", "row", ("grp", "col")),
        P(),
        P(None, "gz", None),
        P(("grp", "row"), "col", None),
        P(("grp", "row"), "col", None),
        P(("grp", "row"), "col", None),
        P(("grp", "row"), "col", None),
    )
    out_specs = (
        P(None, "gz", "row", ("grp", "col")),
        P(None, "gz", "row", ("grp", "col")),
        P(("grp", "col", "row", "gz"), None),
    )
    return jax.shard_map(
        per_device, mesh=mesh, in_specs=in_specs, out_specs=out_specs, check_vma=False
    )
```

```python
import functools

import jax
import jax.numpy as jnp
import numpy as np
from jax import lax
from jax.experimental import pallas as pl
from jax.experimental.pallas import tpu as pltpu
from jax.sharding import PartitionSpec as P

STEPS = 4
FREQ = 8
MATS = 8
PLEN = 64
PORT_TILE = 4
FIELDS = 7
DEPTH = STEPS
ROWS = 8
LAYERS = 32
CHUNK = 5
GROUP = 32

time_step = 0.5

UP_PLANES = [(f, 4) for f in (0, 1, 2, 4, 5)] + [(f, x) for x in (5, 6, 7) for f in range(FIELDS)]
DOWN_PLANES = [(f, x) for x in (0, 1, 2) for f in range(FIELDS)] + [(1, 3), (2, 3)]
PLANES = max(len(UP_PLANES), len(DOWN_PLANES))
PAIRS = (PLANES + 1) // 2

VMEM = pl.BlockSpec(memory_space=pltpu.VMEM)
SMEM = pl.BlockSpec(memory_space=pltpu.SMEM)
HBM = pl.BlockSpec(memory_space=pltpu.HBM)
PARAMS = pltpu.CompilerParams(vmem_limit_bytes=16 * 1024 * 1024)


def dft_basis():
    times = (np.arange(STEPS) + 1.0) * time_step
    omegas = np.pi * (np.arange(FREQ) + 1.0) / FREQ
    angle = times[:, None] * omegas[None, :]
    basis = np.zeros((8, 128), np.float32)
    basis[:STEPS, : 2 * FREQ] = np.concatenate([np.cos(angle), -np.sin(angle)], axis=1)
    return basis


def iota(axis):
    return lax.broadcasted_iota(jnp.int32, (8, 128), axis)


def turn(tile, shift, axis):
    return pltpu.roll(tile, shift % tile.shape[axis], axis)


def directions(row_size, body):
    if row_size == 2:
        row = lax.axis_index("row")
        pl.when(row == 0)(functools.partial(body, True, 0))
        pl.when(row == 1)(functools.partial(body, False, 0))
    else:
        body(True, 0)
        body(False, 1)


def pack_kernel(row_size, eps_hbm, elec_hbm, magn_hbm, mat_hbm, main_ref, z_ref, *rest):
    x_refs, (eps_ref, mat_ref, sems) = rest[:-3], rest[-3:]
    block = LAYERS * ROWS
    copies = [pltpu.make_async_copy(eps_hbm, eps_ref, sems.at[0]), pltpu.make_async_copy(mat_hbm, mat_ref, sems.at[1])]
    copies.append(pltpu.make_async_copy(elec_hbm, main_ref.at[pl.ds(0, 3)], sems.at[2]))
    copies.append(pltpu.make_async_copy(magn_hbm, main_ref.at[pl.ds(3, 3)], sems.at[3]))
    for copy in copies:
        copy.start()
    copies[0].wait()
    copies[1].wait()
    for z in range(LAYERS):
        material = mat_ref[z]
        eps = jnp.full((8, 128), eps_ref[0], jnp.float32)
        for which in range(1, MATS):
            eps = jnp.where(material == which, eps_ref[which], eps)
        main_ref[6, z] = time_step * (1.0 / eps)
    copies[2].wait()
    copies[3].wait()
    flat = main_ref.reshape(FIELDS * block, 128)

    def send(up, slot):
        for i, (f, x) in enumerate(UP_PLANES if up else DOWN_PLANES):
            x_refs[slot][i] = flat[pl.ds(f * block + x, LAYERS, stride=ROWS), :]

    directions(row_size, send)
    start = jnp.where(lax.axis_index("gz") == 0, LAYERS - DEPTH, 0)
    for f in range(FIELDS):
        z_ref[f] = main_ref[f, pl.ds(start, DEPTH)]


def edge_kernel(main_ref, z_ref, mode_ref, prow_ref, pcol_ref, pmode_ref,
                state_ref, own_ref, up_ref, down_ref, ext_ref, weight_ref, stage_ref, strip_ref):
    lane = iota(1)
    group = lane // GROUP
    place = lane % GROUP
    gz = lax.axis_index("gz")
    block = LAYERS * ROWS
    for f in range(FIELDS):
        stage_ref[f, 0:block] = main_ref[f].reshape(block, 128)
        halo = z_ref[f].reshape(DEPTH * ROWS, 128)
        nothing = jnp.zeros_like(halo)
        stage_ref[f, block : block + DEPTH * ROWS] = jnp.where(gz == 0, halo, nothing)
        stage_ref[f, block + DEPTH * ROWS :] = jnp.where(gz == 0, nothing, halo)
        ext_ref[f] = stage_ref[f, block:]
    for b in range(2):
        for zz in range(CHUNK):
            tiles = [
                [stage_ref[f, pl.ds(zz * ROWS + 4 * b + r, 8, stride=CHUNK * ROWS), :] for r in range(4)]
                for f in range(FIELDS)
            ]
            up = jnp.zeros((8, 128), jnp.float32)
            down = jnp.zeros((8, 128), jnp.float32)
            owns = []
            for f in range(FIELDS):
                own = turn(tiles[f][0], 8, 1)
                for r in range(1, 4):
                    own = jnp.where(group == r, turn(tiles[f][r], GROUP * r + 8, 1), own)
                up = jnp.where(place // DEPTH == f, turn(own, DEPTH * f - 4, 1), up)
                down = jnp.where(place // DEPTH == f, turn(own, DEPTH * f - 8, 1), down)
                owns.append(own)
            for f in range(FIELDS):
                for r in range(4):
                    state_ref[f, 4 * b + r, zz] = tiles[f][r]
                own_ref[f, b, zz] = owns[f]
            up_ref[b, zz] = up
            down_ref[b, zz] = down
    for k in range(PORT_TILE):
        strip_ref[...] = jnp.zeros(strip_ref.shape, jnp.float32)
        strip_ref[0:LAYERS, 0:PLEN] = mode_ref[pmode_ref[0, 0, k]]
        strip_ref[...] = pltpu.roll(strip_ref[...], pcol_ref[0, 0, k], 1)
        at = lane - GROUP * (prow_ref[0, 0, k] % 4)
        for zz in range(CHUNK):
            tile = strip_ref[pl.ds(zz, 8, stride=CHUNK), :]
            weight_ref[k, 0, zz] = jnp.where((lane >= DEPTH) & (lane < 128 - DEPTH), tile, 0.0)
            own = pltpu.roll(tile, GROUP * (prow_ref[0, 0, k] % 4) + 8, 1)
            edge = jnp.where((at >= 4) & (at < 8), own, 0.0)
            weight_ref[k, 1, zz] = jnp.where((at >= 16) & (at < 20), turn(own, 8, 1), edge)


def corner_kernel(row_size, ext_ref, low_ref, high_ref, *x_refs):
    def send(up, slot):
        planes = UP_PLANES if up else DOWN_PLANES

        def tile(i):
            f, x = planes[i]
            return ext_ref[f, pl.ds(x, 8, stride=ROWS), :]

        for i in range(PAIRS):
            first = tile(i)
            if i + PAIRS < len(planes):
                first = first + turn(tile(i + PAIRS), 4, 0)
            x_refs[slot][i] = first
        b = 1 if up else 0
        for zz in range(CHUNK):
            x_refs[slot][PAIRS + zz] = low_ref[b, zz]
            x_refs[slot][PAIRS + CHUNK + zz] = high_ref[b, zz]

    directions(row_size, send)


def edge_tile(own, low, high, f):
    place = iota(1) % GROUP
    out = jnp.where(place < 16, turn(low, 12 - DEPTH * f, 1), turn(own, 8, 1))
    out = jnp.where(place < 12, turn(high, 8 - DEPTH * f, 1), out)
    return jnp.where(place < 8, own, out)


def join_kernel(own_ref, low_ref, high_ref, edge_ref):
    for b in range(2):
        for zz in range(CHUNK):
            low, high = low_ref[b, zz], high_ref[b, zz]
            tiles = [edge_tile(own_ref[f, b, zz], low, high, f) for f in range(FIELDS)]
            for f in range(FIELDS):
                edge_ref[f, b, zz] = tiles[f]


def step_kernel(row_size, ports_each, basis_ref, prow_ref, pid_ref, state_ref, joined_ref, weight_ref, *rest):
    n_x = 1 if row_size == 2 else 2
    x_refs, corner_refs = rest[:n_x], rest[n_x : 2 * n_x]
    eout_hbm, hout_hbm, keep_ref, send_ref, main_e, main_h, main_c, edge_e, edge_h, edge_c, plane_ref, sum_ref, out_ref, sems = rest[2 * n_x :]
    gz, row, col = (lax.axis_index(name) for name in ("gz", "row", "col"))
    lane, sub = iota(1), iota(0)
    place, group = lane % GROUP, lane // GROUP
    zeros = jnp.zeros((8, 128), jnp.float32)
    last_group, first_group = group == 3, group == 0

    def at_main(f, i, zz, n):
        if DEPTH <= i < DEPTH + ROWS and (n == 1 or f == 6):
            return state_ref[f, i - DEPTH, zz]
        if f == 6:
            return main_c[i, zz]
        return main_e[f, i, zz] if f < 3 else main_h[f - 3, i, zz]

    def at_edge(f, i, zz, n):
        if 1 <= i < 3 and (n == 1 or f == 6):
            return joined_ref[f, i - 1, zz]
        if f == 6:
            return edge_c[i, zz]
        return edge_e[f, i, zz] if f < 3 else edge_h[f - 3, i, zz]

    def put(e, h, c, f, i, zz, tile):
        if f == 6:
            c[i, zz] = tile
        elif f < 3:
            e[f, i, zz] = tile
        else:
            h[f - 3, i, zz] = tile

    def run(has_below, has_above):
        def halo_rows(planes, slot, offset, b):
            valid = (sub < 4) == (gz == 0)
            got = set(planes)
            for i, (f, x) in enumerate(planes):
                packed = corner_refs[slot][i % PAIRS]
                if i >= PAIRS:
                    packed = turn(packed, 4, 0)
                plane_ref[slot, i, 0:LAYERS] = x_refs[slot][i]
                plane_ref[slot, i, LAYERS:] = jnp.where(valid, packed, 0.0)
            rows = {}
            for i, (f, x) in enumerate(planes):
                for zz in range(CHUNK):
                    rows[f, x, zz] = plane_ref[slot, i, pl.ds(zz, 8, stride=CHUNK), :]
                for zz in range(CHUNK):
                    put(main_e, main_h, main_c, f, DEPTH + x + offset, zz, rows[f, x, zz])
            for zz in range(CHUNK):
                low = corner_refs[slot][PAIRS + zz]
                high = corner_refs[slot][PAIRS + CHUNK + zz]
                tiles = []
                for f in range(FIELDS):
                    own = zeros
                    for r in range(4):
                        x = 4 * b + r - offset
                        if (f, x) in got:
                            tile = at_main(f, DEPTH + x + offset, zz, 0)
                            own = jnp.where(group == r, turn(tile, GROUP * r + 8, 1), own)
                    tiles.append(edge_tile(own, low, high, f))
                for f in range(FIELDS):
                    put(edge_e, edge_h, edge_c, f, 1 + b, zz, tiles[f])

        if has_below:
            halo_rows(UP_PLANES, 0, -ROWS, -1)
        if has_above:
            halo_rows(DOWN_PLANES, n_x - 1, ROWS, 2)

        below_layers = (sub == 7) & (gz == 0)
        half = [jnp.where(below_layers, 0.0, time_step) if zz else jnp.full((8, 128), time_step) for zz in range(CHUNK)]
        outside = (place >= 12) & (place < 16) & (col == 0)
        edge_half = [jnp.where(outside, 0.0, half[zz]) for zz in range(CHUNK)]
        lowest = jnp.where(row == 0, 0.0, 1.0) if row_size > 2 else None

        def above(tiles, zz):
            return tiles[zz + 1] if zz + 1 < CHUNK else turn(tiles[0], -1, 0)

        def beneath(tiles, zz):
            return tiles[zz - 1] if zz else turn(tiles[CHUNK - 1], 1, 0)

        blank = [zeros] * CHUNK
        every = range(CHUNK)

        def sweep(items, load, work):
            loaded = {items[0]: load(items[0])}
            for i in items:
                if i + 1 in items:
                    loaded[i + 1] = load(i + 1)
                work(i, loaded)

        def phases(n, items, final, at, keep_e, keep_h, across, half_of, only_h):
            def load_e(i):
                ex, ey, ez = ([at(f, i, zz, n) for zz in every] for f in range(3))
                return ex, ey, ez, [turn(v, -1, 1) for v in ex], [turn(v, -1, 1) for v in ez], across(ey, -1), across(ez, -1)

            def work_h(i, loaded):
                ex, ey, ez, ex_right, ez_right, ey_own, ez_own = loaded[i]
                old = [[at(f, i, zz, n) for zz in every] for f in (3, 4, 5)]
                h = half_of(i)
                if i + 1 in loaded:
                    after = loaded[i + 1]
                elif i < final:
                    after = load_e(i + 1)
                else:
                    after = [blank] * 7
                ey_up, ez_up = across.pick(ey_own, after[5]), across.pick(ez_own, after[6])
                new = []
                for zz in every:
                    hx = (ez_right[zz] - ez[zz]) - (above(ey, zz) - ey[zz])
                    hy = (above(ex, zz) - ex[zz]) - (ez_up[zz] - ez[zz])
                    hz = (ey_up[zz] - ey[zz]) - (ex_right[zz] - ex[zz])
                    new.append([old[c][zz] - h[zz] * v for c, v in enumerate((hx, hy, hz))])
                for zz in every:
                    for c in range(3):
                        if c or i not in only_h:
                            keep_h[c, i, zz] = new[zz][c]

            def load_h(i):
                hy, hz = ([keep_h[c, i, zz] for zz in every] for c in (1, 2))
                shifted_h = across(hy, 1), across(hz, 1)
                if i in only_h:
                    return None, hy, hz, None, None, *shifted_h
                hx = [keep_h[0, i, zz] for zz in every]
                return hx, hy, hz, [turn(v, 1, 1) for v in hx], [turn(v, 1, 1) for v in hz], *shifted_h

            def work_e(i, loaded):
                if i in only_h:
                    return
                hx, hy, hz, hx_left, hz_left, hy_own, hz_own = loaded[i]
                old = [[at(f, i, zz, n) for zz in every] for f in range(3)]
                coef = [at(6, i, zz, n) for zz in every]
                before = loaded.get(i - 1, [blank] * 7)
                hy_down, hz_down = across.pick(hy_own, before[5]), across.pick(hz_own, before[6])
                new = []
                for zz in every:
                    ex = (hz[zz] - hz_left[zz]) - (hy[zz] - beneath(hy, zz))
                    ey = (hx[zz] - beneath(hx, zz)) - (hz[zz] - hz_down[zz])
                    ez = (hy[zz] - hy_down[zz]) - (hx[zz] - hx_left[zz])
                    new.append([old[c][zz] + coef[zz] * v for c, v in enumerate((ex, ey, ez))])
                for zz in every:
                    for c in range(3):
                        keep_e[c, i, zz] = new[zz][c]

            sweep(items, load_e, work_h)
            yield
            sweep(items, load_h, work_e)

        class RowAcross:
            def __call__(self, tiles, way):
                return tiles

            def pick(self, own, other):
                return other

        class BlockAcross:
            def __call__(self, tiles, way):
                self.edge = last_group if way < 0 else first_group
                return [turn(v, way * GROUP, 1) for v in tiles]

            def pick(self, own, other):
                return [jnp.where(self.edge, o, v) for o, v in zip(other, own)]

        for n in range(1, STEPS + 1):
            first = n - 5 if has_below else 0
            last = 11 - n if has_above else 7
            final = DEPTH + 11 if has_above else DEPTH + 7
            top = 3 if has_above else 2

            def half_of(i, limit, values):
                return values if lowest is None or i >= limit else [v * lowest for v in values]

            rows = phases(
                n, list(range(DEPTH + first, DEPTH + last + 1)), final, at_main, main_e, main_h, RowAcross(),
                lambda i: half_of(i, DEPTH, half), [DEPTH + first] if has_below else [],
            )
            blocks = phases(
                n, list(range(0 if has_below else 1, top + 1)), top, at_edge, edge_e, edge_h, BlockAcross(),
                lambda i: half_of(i, 1, edge_half), [],
            )
            for part in (rows, blocks):
                next(part)
            for part in (rows, blocks):
                next(part, None)

            for k in range(PORT_TILE):
                at = prow_ref[0, 0, k]
                total = zeros
                for zz in range(CHUNK):
                    total = total + main_e[2, DEPTH + at, zz] * weight_ref[k, 0, zz]
                    total = total + edge_e[2, 1 + at // 4, zz] * weight_ref[k, 1, zz]
                sum_ref[n - 1, k : k + 1, :] = jnp.sum(total, axis=0, keepdims=True)

    if row_size == 2:
        pl.when(row == 0)(functools.partial(run, False, True))
        pl.when(row == 1)(functools.partial(run, True, False))
    else:
        run(True, True)

    copies = []
    for f in range(6):
        main, edge = (main_e, edge_e) if f < 3 else (main_h, edge_h)
        for b in range(2):
            tiles = [edge[f % 3, 1 + b, zz] for zz in range(CHUNK)]
            near = [jnp.where(place < 8, tile, turn(tile, -8, 1)) for tile in tiles]
            done = {}
            for r in range(4):
                for zz in range(CHUNK):
                    sides = turn(near[zz], -(GROUP * r + 8), 1)
                    own = main[f % 3, DEPTH + 4 * b + r, zz]
                    done[r, zz] = jnp.where((lane < DEPTH) | (lane >= 128 - DEPTH), sides, own)
            for (r, zz), tile in done.items():
                out_ref[f, pl.ds(zz * ROWS + 4 * b + r, 8, stride=CHUNK * ROWS), :] = tile
        dest = eout_hbm if f < 3 else hout_hbm
        copies.append(pltpu.make_async_copy(out_ref.at[f, pl.ds(0, LAYERS * ROWS)], dest.at[f % 3], sems.at[f]))
        copies[-1].start()

    transform = zeros
    for n in range(STEPS):
        sampled = jnp.sum(sum_ref[n], axis=1, keepdims=True)
        transform = transform + sampled * basis_ref[n : n + 1, :]
    keep_ref[...] = jnp.zeros(keep_ref.shape, jnp.float32)
    send_ref[...] = jnp.zeros(send_ref.shape, jnp.float32)
    for k in range(PORT_TILE):
        port = pid_ref[0, 0, k]
        device = port // ports_each

        def place_in(ref, k=k, port=port, device=device):
            ref[device // 2, pl.ds(port % ports_each, 1), :] = transform[k : k + 1, : 2 * FREQ]

        pl.when(device % 2 == gz)(functools.partial(place_in, keep_ref))
        pl.when(device % 2 != gz)(functools.partial(place_in, send_ref))
    for copy in copies:
        copy.wait()


def shifted(block, axis, size, distance):
    route = [(i - distance, i) for i in range(size) if 0 <= i - distance < size]
    return lax.ppermute(block, axis, route)


def swapped(block, axis, size):
    return lax.ppermute(block, axis, [(i, i ^ 1) for i in range(size)])


def solution(mesh):
    sizes = dict(mesh.shape)
    row_size, col_size, gz_size = sizes["row"], sizes["col"], sizes["gz"]
    n_x = 1 if row_size == 2 else 2

    def across_rows(blocks):
        if row_size == 2:
            return (swapped(blocks[0], "row", 2),)
        return (shifted(blocks[0], "row", row_size, 1), shifted(blocks[1], "row", row_size, -1))

    def per_device(
        electric, magnetic, material, eps_table, mode_table, port_row, port_col, port_mode, port_ids
    ):
        f32 = jnp.float32

        def array(*shape):
            return jax.ShapeDtypeStruct(shape, f32)

        main, z_send, *x_send = pl.pallas_call(
            functools.partial(pack_kernel, row_size),
            out_shape=[array(FIELDS, LAYERS, ROWS, 128), array(FIELDS, DEPTH, ROWS, 128)]
            + [array(PLANES, LAYERS, 128)] * n_x,
            in_specs=[HBM] * 4,
            out_specs=[VMEM] * (2 + n_x),
            scratch_shapes=[
                pltpu.SMEM(eps_table.shape, f32),
                pltpu.VMEM(material.shape, jnp.int32),
                pltpu.SemaphoreType.DMA((4,)),
            ],
            compiler_params=PARAMS,
            name="pack",
        )(eps_table, electric, magnetic, material)
        x_halo = across_rows(x_send)
        z_halo = swapped(z_send, "gz", gz_size)
        state, own, up_send, down_send, ext, weights = pl.pallas_call(
            edge_kernel,
            out_shape=[
                array(FIELDS, ROWS, CHUNK, 8, 128),
                array(FIELDS, 2, CHUNK, 8, 128),
                array(2, CHUNK, 8, 128),
                array(2, CHUNK, 8, 128),
                array(FIELDS, 2 * DEPTH * ROWS, 128),
                array(PORT_TILE, 2, CHUNK, 8, 128),
            ],
            in_specs=[VMEM] * 3 + [SMEM] * 3,
            out_specs=[VMEM] * 6,
            scratch_shapes=[
                pltpu.VMEM((FIELDS, 8 * CHUNK * ROWS, 128), f32),
                pltpu.VMEM((8 * CHUNK, 128), f32),
            ],
            compiler_params=PARAMS,
            name="edges",
        )(main, z_halo, mode_table, port_row, port_col, port_mode)
        low = shifted(up_send, "col", col_size, 1)
        high = shifted(down_send, "col", col_size, -1)
        corner_send = pl.pallas_call(
            functools.partial(corner_kernel, row_size),
            out_shape=[array(PAIRS + 2 * CHUNK, 8, 128)] * n_x,
            in_specs=[VMEM] * 3,
            out_specs=[VMEM] * n_x,
            compiler_params=PARAMS,
            name="corners",
        )(ext, low, high)
        corner = across_rows(corner_send)
        devices = col_size * row_size * gz_size
        ports_each = PORT_TILE * col_size * row_size // devices
        edges = pl.pallas_call(
            join_kernel,
            out_shape=array(FIELDS, 2, CHUNK, 8, 128),
            in_specs=[VMEM] * 3,
            out_specs=VMEM,
            compiler_params=PARAMS,
            name="joins",
        )(own, low, high)
        electric_out, magnetic_out, keep, send = pl.pallas_call(
            functools.partial(step_kernel, row_size, ports_each),
            out_shape=[array(3, LAYERS * ROWS, 128)] * 2 + [array(devices // 2, ports_each, 2 * FREQ)] * 2,
            in_specs=[VMEM] + [SMEM] * 2 + [VMEM] * (3 + 2 * n_x),
            out_specs=[HBM, HBM, VMEM, VMEM],
            scratch_shapes=[
                pltpu.VMEM((3, ROWS + 2 * DEPTH, CHUNK, 8, 128), f32),
                pltpu.VMEM((3, ROWS + 2 * DEPTH, CHUNK, 8, 128), f32),
                pltpu.VMEM((ROWS + 2 * DEPTH, CHUNK, 8, 128), f32),
                pltpu.VMEM((3, 4, CHUNK, 8, 128), f32),
                pltpu.VMEM((3, 4, CHUNK, 8, 128), f32),
                pltpu.VMEM((4, CHUNK, 8, 128), f32),
                pltpu.VMEM((n_x, PLANES, 8 * CHUNK, 128), f32),
                pltpu.VMEM((STEPS, 8, 128), f32),
                pltpu.VMEM((6, 8 * CHUNK * ROWS, 128), f32),
                pltpu.SemaphoreType.DMA((6,)),
            ],
            compiler_params=PARAMS,
            name="steps",
        )(jnp.asarray(dft_basis()), port_row, port_ids, state, edges, weights, *x_halo, *corner)
        terms = keep + swapped(send, "gz", gz_size)
        terms = lax.all_to_all(terms, ("col", "row"), 0, 0, tiled=True)
        mine = jnp.sum(terms, axis=0)
        return (
            electric_out.reshape(electric.shape),
            magnetic_out.reshape(magnetic.shape),
            mine,
        )

    in_specs = (
        P(None, "gz", "row", ("grp", "col")),
        P(None, "gz", "row", ("grp", "col")),
        P("gz", "row", ("grp", "col")),
        P(),
        P(None, "gz", None),
        P(("grp", "row"), "col", None),
        P(("grp", "row"), "col", None),
        P(("grp", "row"), "col", None),
        P(("grp", "row"), "col", None),
    )
    out_specs = (
        P(None, "gz", "row", ("grp", "col")),
        P(None, "gz", "row", ("grp", "col")),
        P(("grp", "col", "row", "gz"), None),
    )
    return jax.shard_map(
        per_device, mesh=mesh, in_specs=in_specs, out_specs=out_specs, check_vma=False
    )
```

```python
import functools

import jax
import jax.numpy as jnp
import numpy as np
from jax import lax
from jax.experimental import pallas as pl
from jax.experimental.pallas import tpu as pltpu
from jax.sharding import PartitionSpec as P

STEPS = 4
FREQ = 8
MATS = 8
PLEN = 64
PORT_TILE = 4
FIELDS = 7
DEPTH = STEPS
ROWS = 8
LAYERS = 32
CHUNK = 5
GROUP = 32

time_step = 0.5

UP_PLANES = [(f, 4) for f in (0, 1, 2, 4, 5)] + [(f, x) for x in (5, 6, 7) for f in range(FIELDS)]
DOWN_PLANES = [(f, x) for x in (0, 1, 2) for f in range(FIELDS)] + [(1, 3), (2, 3)]
PLANES = max(len(UP_PLANES), len(DOWN_PLANES))
PAIRS = (PLANES + 1) // 2

VMEM = pl.BlockSpec(memory_space=pltpu.VMEM)
SMEM = pl.BlockSpec(memory_space=pltpu.SMEM)
HBM = pl.BlockSpec(memory_space=pltpu.HBM)
PARAMS = pltpu.CompilerParams(vmem_limit_bytes=16 * 1024 * 1024)


def dft_basis():
    times = (np.arange(STEPS) + 1.0) * time_step
    omegas = np.pi * (np.arange(FREQ) + 1.0) / FREQ
    angle = times[:, None] * omegas[None, :]
    basis = np.zeros((8, 128), np.float32)
    basis[:STEPS, : 2 * FREQ] = np.concatenate([np.cos(angle), -np.sin(angle)], axis=1)
    return basis


def iota(axis):
    return lax.broadcasted_iota(jnp.int32, (8, 128), axis)


def turn(tile, shift, axis):
    return pltpu.roll(tile, shift % tile.shape[axis], axis)


def directions(row_size, body):
    if row_size == 2:
        row = lax.axis_index("row")
        pl.when(row == 0)(functools.partial(body, True, 0))
        pl.when(row == 1)(functools.partial(body, False, 0))
    else:
        body(True, 0)
        body(False, 1)


def pack_kernel(eps_hbm, elec_hbm, magn_hbm, mat_hbm, main_ref, z_ref, eps_ref, mat_ref, sems):
    copies = [pltpu.make_async_copy(eps_hbm, eps_ref, sems.at[0]), pltpu.make_async_copy(mat_hbm, mat_ref, sems.at[1])]
    copies.append(pltpu.make_async_copy(elec_hbm, main_ref.at[pl.ds(0, 3)], sems.at[2]))
    copies.append(pltpu.make_async_copy(magn_hbm, main_ref.at[pl.ds(3, 3)], sems.at[3]))
    for copy in copies:
        copy.start()
    copies[0].wait()
    copies[1].wait()
    for z in range(LAYERS):
        material = mat_ref[z]
        eps = jnp.full((8, 128), eps_ref[0], jnp.float32)
        for which in range(1, MATS):
            eps = jnp.where(material == which, eps_ref[which], eps)
        main_ref[6, z] = time_step * (1.0 / eps)
    copies[2].wait()
    copies[3].wait()
    start = jnp.where(lax.axis_index("gz") == 0, LAYERS - DEPTH, 0)
    for f in range(FIELDS):
        z_ref[f] = main_ref[f, pl.ds(start, DEPTH)]


def edge_kernel(main_ref, z_ref, state_ref, own_ref, up_ref, down_ref, ext_ref):
    lane = iota(1)
    group, place = lane // GROUP, lane % GROUP
    gz = lax.axis_index("gz")
    block = LAYERS * ROWS
    flat = main_ref.reshape(FIELDS * block, 128)
    for f in range(FIELDS):
        halo = z_ref[f].reshape(DEPTH * ROWS, 128)
        nothing = jnp.zeros_like(halo)
        ext_ref[f, : DEPTH * ROWS] = jnp.where(gz == 0, halo, nothing)
        ext_ref[f, DEPTH * ROWS :] = jnp.where(gz == 0, nothing, halo)

    def tile(f, x, zz):
        if zz == CHUNK - 1:
            return ext_ref[f, pl.ds(x, 8, stride=ROWS), :]
        return flat[pl.ds(f * block + zz * 8 * ROWS + x, 8, stride=ROWS), :]

    for b in range(2):
        for zz in range(CHUNK):
            tiles = [[tile(f, 4 * b + r, zz) for r in range(4)] for f in range(FIELDS)]
            up = jnp.zeros((8, 128), jnp.float32)
            down = jnp.zeros((8, 128), jnp.float32)
            owns = []
            for f in range(FIELDS):
                own = turn(tiles[f][0], 8, 1)
                for r in range(1, 4):
                    own = jnp.where(group == r, turn(tiles[f][r], GROUP * r + 8, 1), own)
                up = jnp.where(place // DEPTH == f, turn(own, DEPTH * f - 4, 1), up)
                down = jnp.where(place // DEPTH == f, turn(own, DEPTH * f - 8, 1), down)
                owns.append(own)
            for f in range(FIELDS):
                for r in range(4):
                    state_ref[f, 4 * b + r, zz] = tiles[f][r]
                own_ref[f, b, zz] = owns[f]
            up_ref[b, zz] = up
            down_ref[b, zz] = down


def plane_kernel(row_size, state_ref, *x_refs):
    def send(up, slot):
        planes = UP_PLANES if up else DOWN_PLANES
        for i, (f, x) in enumerate(planes):
            for zz in range(CHUNK - 1):
                x_refs[slot][i * (CHUNK - 1) + zz] = state_ref[f, x, zz]
        for i in range(PAIRS):
            f, x = planes[i]
            pair = state_ref[f, x, CHUNK - 1]
            if i + PAIRS < len(planes):
                f, x = planes[i + PAIRS]
                pair = pair + turn(state_ref[f, x, CHUNK - 1], 4, 0)
            x_refs[slot][PLANES * (CHUNK - 1) + i] = pair

    directions(row_size, send)


def corner_kernel(row_size, low_ref, high_ref, *x_refs):
    def send(up, slot):
        b = 1 if up else 0
        for zz in range(CHUNK):
            x_refs[slot][zz] = low_ref[b, zz]
            x_refs[slot][CHUNK + zz] = high_ref[b, zz]

    directions(row_size, send)


def edge_tile(own, low, high, f):
    place = iota(1) % GROUP
    out = jnp.where(place < 16, turn(low, 12 - DEPTH * f, 1), turn(own, 8, 1))
    out = jnp.where(place < 12, turn(high, 8 - DEPTH * f, 1), out)
    return jnp.where(place < 8, own, out)


def join_kernel(own_ref, low_ref, high_ref, mode_ref, prow_ref, pcol_ref, pmode_ref, edge_ref, weight_ref, strip_ref):
    for b in range(2):
        for zz in range(CHUNK):
            low, high = low_ref[b, zz], high_ref[b, zz]
            tiles = [edge_tile(own_ref[f, b, zz], low, high, f) for f in range(FIELDS)]
            for f in range(FIELDS):
                edge_ref[f, b, zz] = tiles[f]
    lane = iota(1)
    for k in range(PORT_TILE):
        strip_ref[k] = jnp.zeros(strip_ref.shape[1:], jnp.float32)
        strip_ref[k, :, 0:PLEN] = mode_ref[pmode_ref[0, 0, k]]
        turned = GROUP * (prow_ref[0, 0, k] % 4)
        at = lane - turned
        for zz in range(CHUNK - 1):
            tile = pltpu.roll(strip_ref[k, 8 * zz : 8 * zz + 8, :], pcol_ref[0, 0, k], 1)
            weight_ref[k, 0, zz] = jnp.where((lane >= DEPTH) & (lane < 128 - DEPTH), tile, 0.0)
            own = pltpu.roll(tile, turned + 8, 1)
            edge = jnp.where((at >= 4) & (at < 8), own, 0.0)
            weight_ref[k, 1, zz] = jnp.where((at >= 16) & (at < 20), turn(own, 8, 1), edge)


def step_kernel(row_size, basis_ref, prow_ref, pid_ref, state_ref, joined_ref, weight_ref, *rest):
    n_x = 1 if row_size == 2 else 2
    x_refs, corner_refs = rest[:n_x], rest[n_x : 2 * n_x]
    eout_hbm, hout_hbm, term_ref, main_e, main_h, main_c, edge_e, edge_h, edge_c, sum_ref, out_ref, sems = rest[2 * n_x :]
    gz, row, col = (lax.axis_index(name) for name in ("gz", "row", "col"))
    lane, sub = iota(1), iota(0)
    place, group = lane % GROUP, lane // GROUP
    zeros = jnp.zeros((8, 128), jnp.float32)
    last_group, first_group = group == 3, group == 0

    def at_main(f, i, zz, n):
        if DEPTH <= i < DEPTH + ROWS and (n == 1 or f == 6):
            return state_ref[f, i - DEPTH, zz]
        if f == 6:
            return main_c[i, zz]
        return main_e[f, i, zz] if f < 3 else main_h[f - 3, i, zz]

    def at_edge(f, i, zz, n):
        if 1 <= i < 3 and (n == 1 or f == 6):
            return joined_ref[f, i - 1, zz]
        if f == 6:
            return edge_c[i, zz]
        return edge_e[f, i, zz] if f < 3 else edge_h[f - 3, i, zz]

    def put(e, h, c, f, i, zz, tile):
        if f == 6:
            c[i, zz] = tile
        elif f < 3:
            e[f, i, zz] = tile
        else:
            h[f - 3, i, zz] = tile

    def run(has_below, has_above):
        def halo_rows(planes, slot, offset, b):
            valid = (sub < 4) == (gz == 0)
            got = set(planes)
            for i, (f, x) in enumerate(planes):
                rows = [x_refs[slot][i * (CHUNK - 1) + zz] for zz in range(CHUNK - 1)]
                packed = x_refs[slot][PLANES * (CHUNK - 1) + i % PAIRS]
                if i >= PAIRS:
                    packed = turn(packed, 4, 0)
                rows.append(jnp.where(valid, packed, 0.0))
                for zz in range(CHUNK):
                    put(main_e, main_h, main_c, f, DEPTH + x + offset, zz, rows[zz])
            for zz in range(CHUNK):
                low = corner_refs[slot][zz]
                high = corner_refs[slot][CHUNK + zz]
                tiles = []
                for f in range(FIELDS):
                    own = zeros
                    for r in range(4):
                        x = 4 * b + r - offset
                        if (f, x) in got:
                            tile = at_main(f, DEPTH + x + offset, zz, 0)
                            own = jnp.where(group == r, turn(tile, GROUP * r + 8, 1), own)
                    tiles.append(edge_tile(own, low, high, f))
                for f in range(FIELDS):
                    put(edge_e, edge_h, edge_c, f, 1 + b, zz, tiles[f])

        if has_below:
            halo_rows(UP_PLANES, 0, -ROWS, -1)
        if has_above:
            halo_rows(DOWN_PLANES, n_x - 1, ROWS, 2)

        half = [jnp.full((8, 128), time_step)] * (CHUNK - 1)
        half.append(jnp.where((sub >= 4) & (gz == 0), 0.0, time_step))
        outside = (place >= 12) & (place < 16) & (col == 0)
        edge_half = [jnp.where(outside, 0.0, half[zz]) for zz in range(CHUNK)]
        lowest = jnp.where(row == 0, 0.0, 1.0) if row_size > 2 else None

        def above(tiles):
            turned = [turn(v, -1, 0) for v in tiles]
            return [jnp.where(sub == 7, turned[(zz + 1) % CHUNK], turned[zz]) for zz in range(CHUNK)]

        def beneath(tiles):
            turned = [turn(v, 1, 0) for v in tiles]
            return [jnp.where(sub == 0, turned[zz - 1], turned[zz]) for zz in range(CHUNK)]

        blank = [zeros] * CHUNK
        every = range(CHUNK)

        def sweep(items, load, work):
            loaded = {items[0]: load(items[0])}
            for i in items:
                if i + 1 in items:
                    loaded[i + 1] = load(i + 1)
                work(i, loaded)

        def phases(n, items, final, at, keep_e, keep_h, across, half_of, only_h):
            def load_e(i):
                ex, ey, ez = ([at(f, i, zz, n) for zz in every] for f in range(3))
                return ex, ey, ez, [turn(v, -1, 1) for v in ex], [turn(v, -1, 1) for v in ez], across(ey, -1), across(ez, -1), above(ex), above(ey)

            def work_h(i, loaded):
                ex, ey, ez, ex_right, ez_right, ey_own, ez_own, ex_above, ey_above = loaded[i]
                old = [[at(f, i, zz, n) for zz in every] for f in (3, 4, 5)]
                h = half_of(i)
                if i + 1 in loaded:
                    after = loaded[i + 1]
                elif i < final:
                    after = load_e(i + 1)
                else:
                    after = [blank] * 7
                ey_up, ez_up = across.pick(ey_own, after[5]), across.pick(ez_own, after[6])
                new = []
                for zz in every:
                    hx = (ez_right[zz] - ez[zz]) - (ey_above[zz] - ey[zz])
                    hy = (ex_above[zz] - ex[zz]) - (ez_up[zz] - ez[zz])
                    hz = (ey_up[zz] - ey[zz]) - (ex_right[zz] - ex[zz])
                    new.append([old[c][zz] - h[zz] * v for c, v in enumerate((hx, hy, hz))])
                for zz in every:
                    for c in range(3):
                        if c or i not in only_h:
                            keep_h[c, i, zz] = new[zz][c]

            def load_h(i):
                hy, hz = ([keep_h[c, i, zz] for zz in every] for c in (1, 2))
                shifted_h = across(hy, 1), across(hz, 1)
                if i in only_h:
                    return None, hy, hz, None, None, *shifted_h, None, None
                hx = [keep_h[0, i, zz] for zz in every]
                return hx, hy, hz, [turn(v, 1, 1) for v in hx], [turn(v, 1, 1) for v in hz], *shifted_h, beneath(hx), beneath(hy)

            def work_e(i, loaded):
                if i in only_h:
                    return
                hx, hy, hz, hx_left, hz_left, hy_own, hz_own, hx_beneath, hy_beneath = loaded[i]
                old = [[at(f, i, zz, n) for zz in every] for f in range(3)]
                coef = [at(6, i, zz, n) for zz in every]
                before = loaded.get(i - 1, [blank] * 7)
                hy_down, hz_down = across.pick(hy_own, before[5]), across.pick(hz_own, before[6])
                new = []
                for zz in every:
                    ex = (hz[zz] - hz_left[zz]) - (hy[zz] - hy_beneath[zz])
                    ey = (hx[zz] - hx_beneath[zz]) - (hz[zz] - hz_down[zz])
                    ez = (hy[zz] - hy_down[zz]) - (hx[zz] - hx_left[zz])
                    new.append([old[c][zz] + coef[zz] * v for c, v in enumerate((ex, ey, ez))])
                for zz in every:
                    for c in range(3):
                        keep_e[c, i, zz] = new[zz][c]

            sweep(items, load_e, work_h)
            yield
            sweep(items, load_h, work_e)

        class RowAcross:
            def __call__(self, tiles, way):
                return tiles

            def pick(self, own, other):
                return other

        class BlockAcross:
            def __call__(self, tiles, way):
                self.edge = last_group if way < 0 else first_group
                return [turn(v, way * GROUP, 1) for v in tiles]

            def pick(self, own, other):
                return [jnp.where(self.edge, o, v) for o, v in zip(other, own)]

        for n in range(1, STEPS + 1):
            first = n - 5 if has_below else 0
            last = 11 - n if has_above else 7
            final = DEPTH + 11 if has_above else DEPTH + 7
            top = 3 if has_above else 2

            def half_of(i, limit, values):
                return values if lowest is None or i >= limit else [v * lowest for v in values]

            rows = phases(
                n, list(range(DEPTH + first, DEPTH + last + 1)), final, at_main, main_e, main_h, RowAcross(),
                lambda i: half_of(i, DEPTH, half), [DEPTH + first] if has_below else [],
            )
            blocks = phases(
                n, list(range(0 if has_below else 1, top + 1)), top, at_edge, edge_e, edge_h, BlockAcross(),
                lambda i: half_of(i, 1, edge_half), [],
            )
            for part in (rows, blocks):
                next(part)
            for part in (rows, blocks):
                next(part, None)

            for k in range(PORT_TILE):
                at = prow_ref[0, 0, k]
                total = zeros
                for zz in range(CHUNK - 1):
                    total = total + main_e[2, DEPTH + at, zz] * weight_ref[k, 0, zz]
                    total = total + edge_e[2, 1 + at // 4, zz] * weight_ref[k, 1, zz]
                sum_ref[n - 1, k : k + 1, :] = jnp.sum(total, axis=0, keepdims=True)

    if row_size == 2:
        pl.when(row == 0)(functools.partial(run, False, True))
        pl.when(row == 1)(functools.partial(run, True, False))
    else:
        run(True, True)

    copies = []
    for f in range(6):
        main, edge = (main_e, edge_e) if f < 3 else (main_h, edge_h)
        for b in range(2):
            tiles = [edge[f % 3, 1 + b, zz] for zz in range(CHUNK - 1)]
            near = [jnp.where(place < 8, tile, turn(tile, -8, 1)) for tile in tiles]
            done = {}
            for r in range(4):
                for zz in range(CHUNK - 1):
                    sides = turn(near[zz], -(GROUP * r + 8), 1)
                    own = main[f % 3, DEPTH + 4 * b + r, zz]
                    done[r, zz] = jnp.where((lane < DEPTH) | (lane >= 128 - DEPTH), sides, own)
            for (r, zz), tile in done.items():
                out_ref[f, pl.ds(zz * 8 * ROWS + 4 * b + r, 8, stride=ROWS), :] = tile
        dest = eout_hbm if f < 3 else hout_hbm
        copies.append(pltpu.make_async_copy(out_ref.at[f], dest.at[f % 3], sems.at[f]))
        copies[-1].start()

    transform = zeros
    for n in range(STEPS):
        sampled = jnp.sum(sum_ref[n], axis=1, keepdims=True)
        transform = transform + sampled * basis_ref[n : n + 1, :]
    term_ref[...] = transform[:PORT_TILE, : 4 * FREQ]
    for k in range(PORT_TILE):
        port = jnp.full((1, 2 * FREQ), pid_ref[0, 0, k]).astype(jnp.float32)
        term_ref[k : k + 1, 2 * FREQ :] = port
    for copy in copies:
        copy.wait()


def shifted(block, axis, size, distance):
    route = [(i - distance, i) for i in range(size) if 0 <= i - distance < size]
    return lax.ppermute(block, axis, route)


def swapped(block, axis, size):
    return lax.ppermute(block, axis, [(i, i ^ 1) for i in range(size)])


def solution(mesh):
    sizes = dict(mesh.shape)
    row_size, col_size, gz_size = sizes["row"], sizes["col"], sizes["gz"]
    n_x = 1 if row_size == 2 else 2

    def across_rows(blocks):
        if row_size == 2:
            return (swapped(blocks[0], "row", 2),)
        return (shifted(blocks[0], "row", row_size, 1), shifted(blocks[1], "row", row_size, -1))

    def per_device(
        electric, magnetic, material, eps_table, mode_table, port_row, port_col, port_mode, port_ids
    ):
        f32 = jnp.float32

        def array(*shape):
            return jax.ShapeDtypeStruct(shape, f32)

        main, z_send = pl.pallas_call(
            pack_kernel,
            out_shape=[array(FIELDS, LAYERS, ROWS, 128), array(FIELDS, DEPTH, ROWS, 128)],
            in_specs=[HBM] * 4,
            out_specs=[VMEM] * 2,
            scratch_shapes=[
                pltpu.SMEM(eps_table.shape, f32),
                pltpu.VMEM(material.shape, jnp.int32),
                pltpu.SemaphoreType.DMA((4,)),
            ],
            name="pack",
        )(eps_table, electric, magnetic, material)
        z_halo = swapped(z_send, "gz", gz_size)
        state, own, up_send, down_send = pl.pallas_call(
            edge_kernel,
            out_shape=[
                array(FIELDS, ROWS, CHUNK, 8, 128),
                array(FIELDS, 2, CHUNK, 8, 128),
                array(2, CHUNK, 8, 128),
                array(2, CHUNK, 8, 128),
            ],
            in_specs=[VMEM] * 2,
            out_specs=[VMEM] * 4,
            scratch_shapes=[pltpu.VMEM((FIELDS, 8 * ROWS, 128), f32)],
            compiler_params=PARAMS,
            name="edges",
        )(main, z_halo)
        low = shifted(up_send, "col", col_size, 1)
        high = shifted(down_send, "col", col_size, -1)
        x_send = pl.pallas_call(
            functools.partial(plane_kernel, row_size),
            out_shape=[array(PLANES * (CHUNK - 1) + PAIRS, 8, 128)] * n_x,
            in_specs=[VMEM],
            out_specs=[VMEM] * n_x,
            compiler_params=PARAMS,
            name="planes",
        )(state)
        x_halo = across_rows(x_send)
        corner_send = pl.pallas_call(
            functools.partial(corner_kernel, row_size),
            out_shape=[array(2 * CHUNK, 8, 128)] * n_x,
            in_specs=[VMEM] * 2,
            out_specs=[VMEM] * n_x,
            compiler_params=PARAMS,
            name="corners",
        )(low, high)
        corner = across_rows(corner_send)
        devices = col_size * row_size * gz_size
        ports_each = PORT_TILE * col_size * row_size // devices
        edges, weights = pl.pallas_call(
            join_kernel,
            out_shape=[array(FIELDS, 2, CHUNK, 8, 128), array(PORT_TILE, 2, CHUNK - 1, 8, 128)],
            in_specs=[VMEM] * 4 + [SMEM] * 3,
            out_specs=[VMEM] * 2,
            scratch_shapes=[pltpu.VMEM((PORT_TILE, LAYERS, 128), f32)],
            compiler_params=PARAMS,
            name="joins",
        )(own, low, high, mode_table, port_row, port_col, port_mode)
        electric_out, magnetic_out, term = pl.pallas_call(
            functools.partial(step_kernel, row_size),
            out_shape=[array(3, LAYERS * ROWS, 128)] * 2 + [array(PORT_TILE, 4 * FREQ)],
            in_specs=[VMEM] + [SMEM] * 2 + [VMEM] * (3 + 2 * n_x),
            out_specs=[HBM, HBM, VMEM],
            scratch_shapes=[
                pltpu.VMEM((3, ROWS + 2 * DEPTH, CHUNK, 8, 128), f32),
                pltpu.VMEM((3, ROWS + 2 * DEPTH, CHUNK, 8, 128), f32),
                pltpu.VMEM((ROWS + 2 * DEPTH, CHUNK, 8, 128), f32),
                pltpu.VMEM((3, 4, CHUNK, 8, 128), f32),
                pltpu.VMEM((3, 4, CHUNK, 8, 128), f32),
                pltpu.VMEM((4, CHUNK, 8, 128), f32),
                pltpu.VMEM((STEPS, 8, 128), f32),
                pltpu.VMEM((6, LAYERS * ROWS, 128), f32),
                pltpu.SemaphoreType.DMA((6,)),
            ],
            compiler_params=PARAMS,
            name="steps",
        )(jnp.asarray(dft_basis()), port_row, port_ids, state, edges, weights, *x_halo, *corner)
        names = ("col", "row", "gz")
        terms = lax.all_gather(term, names, axis=0, tiled=True)
        first = lax.axis_index(names) * ports_each
        mine = jnp.stack(
            [
                jnp.sum(jnp.where(terms[:, 2 * FREQ :] == first + j, terms[:, : 2 * FREQ], 0.0), axis=0)
                for j in range(ports_each)
            ]
        )
        return (
            electric_out.reshape(electric.shape),
            magnetic_out.reshape(magnetic.shape),
            mine,
        )

    in_specs = (
        P(None, "gz", "row", ("grp", "col")),
        P(None, "gz", "row", ("grp", "col")),
        P("gz", "row", ("grp", "col")),
        P(),
        P(None, "gz", None),
        P(("grp", "row"), "col", None),
        P(("grp", "row"), "col", None),
        P(("grp", "row"), "col", None),
        P(("grp", "row"), "col", None),
    )
    out_specs = (
        P(None, "gz", "row", ("grp", "col")),
        P(None, "gz", "row", ("grp", "col")),
        P(("grp", "col", "row", "gz"), None),
    )
    return jax.shard_map(
        per_device, mesh=mesh, in_specs=in_specs, out_specs=out_specs, check_vma=False
    )
```

```python
import functools

import jax
import jax.numpy as jnp
import numpy as np
from jax import lax
from jax.experimental import pallas as pl
from jax.experimental.pallas import tpu as pltpu
from jax.sharding import PartitionSpec as P

STEPS = 4
FREQ = 8
MATS = 8
PLEN = 64
PORT_TILE = 4
FIELDS = 7
DEPTH = STEPS
ROWS = 8
LAYERS = 32
OWN = 4
CHUNK = 5
GROUP = 32

time_step = 0.5

UP_PLANES = [(f, 4) for f in (0, 1, 2, 4, 5)] + [(f, x) for x in (5, 6, 7) for f in range(FIELDS)]
DOWN_PLANES = [(f, x) for x in (0, 1, 2) for f in range(FIELDS)] + [(1, 3), (2, 3)]
PLANES = max(len(UP_PLANES), len(DOWN_PLANES))
PAIRS = (PLANES + 1) // 2

VMEM = pl.BlockSpec(memory_space=pltpu.VMEM)
SMEM = pl.BlockSpec(memory_space=pltpu.SMEM)
HBM = pl.BlockSpec(memory_space=pltpu.HBM)
PARAMS = pltpu.CompilerParams(vmem_limit_bytes=16 * 1024 * 1024)


def dft_basis():
    times = (np.arange(STEPS) + 1.0) * time_step
    omegas = np.pi * (np.arange(FREQ) + 1.0) / FREQ
    angle = times[:, None] * omegas[None, :]
    basis = np.zeros((8, 128), np.float32)
    basis[:STEPS, : 2 * FREQ] = np.concatenate([np.cos(angle), -np.sin(angle)], axis=1)
    return basis


def iota(axis):
    return lax.broadcasted_iota(jnp.int32, (8, 128), axis)


def turn(tile, shift, axis):
    return pltpu.roll(tile, shift % tile.shape[axis], axis)


def directions(row_size, body):
    if row_size == 2:
        row = lax.axis_index("row")
        pl.when(row == 0)(functools.partial(body, True, 0))
        pl.when(row == 1)(functools.partial(body, False, 0))
    else:
        body(True, 0)
        body(False, 1)


def pack_kernel(row_size, eps_hbm, elec_hbm, magn_hbm, mat_hbm, main_ref, z_ref, *rest):
    x_refs, (eps_ref, mat_ref, sems) = rest[:-3], rest[-3:]
    block = LAYERS * ROWS
    copies = [pltpu.make_async_copy(eps_hbm, eps_ref, sems.at[0]), pltpu.make_async_copy(mat_hbm, mat_ref, sems.at[1])]
    copies.append(pltpu.make_async_copy(elec_hbm, main_ref.at[pl.ds(0, 3)], sems.at[2]))
    copies.append(pltpu.make_async_copy(magn_hbm, main_ref.at[pl.ds(3, 3)], sems.at[3]))
    for copy in copies:
        copy.start()
    copies[0].wait()
    copies[1].wait()
    for z in range(LAYERS):
        material = mat_ref[z]
        eps = jnp.full((8, 128), eps_ref[0], jnp.float32)
        for which in range(1, MATS):
            eps = jnp.where(material == which, eps_ref[which], eps)
        main_ref[6, z] = time_step * (1.0 / eps)
    copies[2].wait()
    copies[3].wait()
    flat = main_ref.reshape(FIELDS * block, 128)

    def send(up, slot):
        for i, (f, x) in enumerate(UP_PLANES if up else DOWN_PLANES):
            x_refs[slot][i] = flat[pl.ds(f * block + x, LAYERS, stride=ROWS), :]

    directions(row_size, send)
    start = jnp.where(lax.axis_index("gz") == 0, LAYERS - DEPTH, 0)
    for f in range(FIELDS):
        z_ref[f] = main_ref[f, pl.ds(start, DEPTH)]


def gather_edges(tiles, groups):
    own = None
    for r, tile in enumerate(tiles):
        if tile is not None:
            moved = turn(tile, GROUP * r + 8, 1)
            own = moved if own is None else jnp.where(groups[r], moved, own)
    return own


def edge_kernel(main_ref, own_ref, up_ref, down_ref):
    lane = iota(1)
    groups = [(lane >> 5) == r for r in range(4)]
    slots = [((lane & (GROUP - 1)) >> 2) == f for f in range(FIELDS)]
    block = LAYERS * ROWS
    flat = main_ref.reshape(FIELDS * block, 128)
    for b in range(2):
        for zz in range(OWN):
            up = down = jnp.zeros((8, 128), jnp.float32)
            for f in range(FIELDS):
                at = f * block + zz * 8 * ROWS + 4 * b
                tiles = [flat[pl.ds(at + r, 8, stride=ROWS), :] for r in range(4)]
                own = gather_edges(tiles, groups)
                up = jnp.where(slots[f], turn(own, DEPTH * f - 4, 1), up)
                down = jnp.where(slots[f], turn(own, DEPTH * f - 8, 1), down)
                own_ref[f, b, zz] = own
            up_ref[b, zz] = up
            down_ref[b, zz] = down


def halo_layers(valid, gz, side_ref, b):
    return jnp.where(valid, jnp.where(gz == 0, side_ref[b, 0], side_ref[b, OWN - 1]), 0.0)


def spread_layers(gz, z_ref, ext_ref):
    for f in range(FIELDS):
        halo = z_ref[f].reshape(DEPTH * ROWS, 128)
        nothing = jnp.zeros_like(halo)
        ext_ref[f, : DEPTH * ROWS] = jnp.where(gz == 0, halo, nothing)
        ext_ref[f, DEPTH * ROWS :] = jnp.where(gz == 0, nothing, halo)


def corner_kernel(row_size, z_ref, low_ref, high_ref, low_z_ref, high_z_ref, *rest):
    x_refs, ext_ref = rest[:-1], rest[-1]
    gz = lax.axis_index("gz")
    valid = (iota(0) < 4) == (gz == 0)
    spread_layers(gz, z_ref, ext_ref)

    def send(up, slot):
        planes = UP_PLANES if up else DOWN_PLANES

        def tile(i):
            f, x = planes[i]
            return ext_ref[f, pl.ds(x, 8, stride=ROWS), :]

        for i in range(PAIRS):
            pair = tile(i)
            if i + PAIRS < len(planes):
                pair = pair + turn(tile(i + PAIRS), 4, 0)
            x_refs[slot][i] = pair
        b = 1 if up else 0
        for zz in range(OWN):
            x_refs[slot][PAIRS + zz] = low_ref[b, zz]
            x_refs[slot][PAIRS + CHUNK + zz] = high_ref[b, zz]
        x_refs[slot][PAIRS + OWN] = halo_layers(valid, gz, low_z_ref, b)
        x_refs[slot][PAIRS + CHUNK + OWN] = halo_layers(valid, gz, high_z_ref, b)

    directions(row_size, send)


def edge_tile(own, low, high, f, place):
    out = jnp.where(place < 16, turn(low, 12 - DEPTH * f, 1), turn(own, 8, 1))
    out = jnp.where(place < 12, turn(high, 8 - DEPTH * f, 1), out)
    return jnp.where(place < 8, own, out)


class Tiles:
    def __init__(self, first, e_ref, h_ref, shift):
        self.first, self.e_ref, self.h_ref, self.shift = first, e_ref, h_ref, shift
        self.written = set()

    def get(self, f, i, zz):
        if (f, i) not in self.written:
            return self.first(f, i, zz)
        return self.e_ref[f, i - self.shift, zz] if f < 3 else self.h_ref[f - 3, i - self.shift, zz]

    def put(self, f, i, zz, tile):
        if f < 3:
            self.e_ref[f, i - self.shift, zz] = tile
        else:
            self.h_ref[f - 3, i - self.shift, zz] = tile

    def keep(self, fields, i):
        self.written |= {(f, i) for f in fields}


def leapfrog(tiles, exists, h_rows, e_rows, across, h_of, c_of, h_layers, e_layers, skip_hx):
    sub = iota(0)
    every = range(CHUNK)
    blank = [jnp.zeros((8, 128), jnp.float32)] * CHUNK

    def above(values):
        turned = [turn(v, -1, 0) for v in values]
        return [jnp.where(sub == 7, turned[(zz + 1) % CHUNK], turned[zz]) for zz in every]

    def beneath(values):
        turned = [turn(v, 1, 0) for v in values]
        return [jnp.where(sub == 0, turned[zz - 1], turned[zz]) for zz in every]

    def row(f, i):
        return [tiles.get(f, i, zz) for zz in every]

    def load_e(i):
        ey, ez = row(1, i), row(2, i)
        out = dict(ey=ey, ez=ez, ey_x=across.turned(ey, -1), ez_x=across.turned(ez, -1))
        if i in h_rows:
            ex = row(0, i)
            out.update(ex=ex, ex_y=[turn(v, -1, 1) for v in ex], ex_z=above(ex))
            if i not in skip_hx:
                out.update(ez_y=[turn(v, -1, 1) for v in ez], ey_z=above(ey))
        return out

    def work_h(i, loaded):
        e, after, h = loaded[i], loaded.get(i + 1), h_of(i)
        ey_x = across.pick(e["ey_x"], after["ey_x"] if after else blank, -1)
        ez_x = across.pick(e["ez_x"], after["ez_x"] if after else blank, -1)
        new = {}
        for zz in h_layers:
            if i not in skip_hx:
                curl = (e["ez_y"][zz] - e["ez"][zz]) - (e["ey_z"][zz] - e["ey"][zz])
                new[3, zz] = tiles.get(3, i, zz) - h[zz] * curl
            curl = (e["ex_z"][zz] - e["ex"][zz]) - (ez_x[zz] - e["ez"][zz])
            new[4, zz] = tiles.get(4, i, zz) - h[zz] * curl
            curl = (ey_x[zz] - e["ey"][zz]) - (e["ex_y"][zz] - e["ex"][zz])
            new[5, zz] = tiles.get(5, i, zz) - h[zz] * curl
        for (f, zz), tile in new.items():
            tiles.put(f, i, zz, tile)
        tiles.keep((4, 5) if i in skip_hx else (3, 4, 5), i)

    def load_h(i):
        hy, hz = row(4, i), row(5, i)
        out = dict(hy=hy, hz=hz, hy_x=across.turned(hy, 1), hz_x=across.turned(hz, 1))
        if i in e_rows:
            hx = row(3, i)
            out.update(hx=hx, hx_y=[turn(v, 1, 1) for v in hx], hz_y=[turn(v, 1, 1) for v in hz])
            out.update(hx_z=beneath(hx), hy_z=beneath(hy))
        return out

    def work_e(i, loaded):
        h, before, c = loaded[i], loaded.get(i - 1), c_of(i)
        hy_x = across.pick(h["hy_x"], before["hy_x"] if before else blank, 1)
        hz_x = across.pick(h["hz_x"], before["hz_x"] if before else blank, 1)
        new = {}
        for zz in e_layers:
            curl = (h["hz"][zz] - h["hz_y"][zz]) - (h["hy"][zz] - h["hy_z"][zz])
            new[0, zz] = tiles.get(0, i, zz) + c[zz] * curl
            curl = (h["hx"][zz] - h["hx_z"][zz]) - (h["hz"][zz] - hz_x[zz])
            new[1, zz] = tiles.get(1, i, zz) + c[zz] * curl
            curl = (h["hy"][zz] - hy_x[zz]) - (h["hx"][zz] - h["hx_y"][zz])
            new[2, zz] = tiles.get(2, i, zz) + c[zz] * curl
        for (f, zz), tile in new.items():
            tiles.put(f, i, zz, tile)
        tiles.keep((0, 1, 2), i)

    def sweep(rows, load, work):
        loaded = {}

        def want(i):
            if i not in loaded and i in exists:
                loaded[i] = load(i)

        for i in rows:
            for j in (i - 1, i, i + 1):
                if j in rows or j == i + (1 if load is load_e else -1):
                    want(j)
            work(i, loaded)

    sweep(h_rows, load_e, work_h)
    yield
    sweep(e_rows, load_h, work_e)


class Rows:
    def turned(self, values, way):
        return values

    def pick(self, own, other, way):
        return other


class Blocks:
    def __init__(self, groups):
        self.groups = groups

    def turned(self, values, way):
        return [turn(v, way * GROUP, 1) for v in values]

    def pick(self, own, other, way):
        edge = self.groups[3] if way < 0 else self.groups[0]
        return [jnp.where(edge, o, v) for o, v in zip(other, own)]


def spans_inner(n, has_below, has_above):
    last = 7 - n if has_above else 7
    return (n - 1 if has_below else 0, last), (n if has_below else 0, last)


def spans_below(n):
    return (n - 5, n - 2), (n - 4, n - 1)


def spans_above(n):
    return (8 - n, 11 - n), (8 - n, 11 - n)


def advance(n, spans, main, edge, main_exists, edge_exists, values, skip_hx):
    row_size, gz, row, col = values
    lane, sub = iota(1), iota(0)
    place, group = lane & (GROUP - 1), lane >> 5
    groups = [group == r for r in range(4)]
    full = jnp.full((8, 128), time_step, jnp.float32)
    layer_half = [full] * OWN + [jnp.where((sub >= 4) & (gz == 0), 0.0, full)]
    outside = (place >= 12) & (place < 16) & (col == 0)
    edge_half = [jnp.where(outside, 0.0, v) for v in layer_half]
    lowest = jnp.where(row == 0, 0.0, 1.0) if row_size > 2 else None

    def cover(block, span):
        low, high = max(span[0] - 4 * block, 0), min(span[1] - 4 * block, 3)
        if low == 0 and high == 3:
            return None
        return (group >= low) & (group <= high)

    def blocks_of(span):
        return [b + 1 for b in range(-1, 3) if span[0] <= 4 * b + 3 and span[1] >= 4 * b]

    def main_h(i):
        return layer_half if lowest is None or i >= DEPTH else [v * lowest for v in layer_half]

    def main_c(i):
        return [main.get(6, i, zz) for zz in range(CHUNK)]

    def edge_h(i, span):
        h = edge_half if lowest is None or i else [v * lowest for v in edge_half]
        mask = cover(i - 1, span)
        return h if mask is None else [jnp.where(mask, v, 0.0) for v in h]

    def edge_c(i, span):
        c = [edge.get(6, i, zz) for zz in range(CHUNK)]
        mask = cover(i - 1, span)
        return c if mask is None else [jnp.where(mask, v, 0.0) for v in c]

    layers = range(CHUNK)
    last = range(OWN) if n == STEPS else layers
    parts = []
    for h_span, e_span in spans:
        h_rows = list(range(DEPTH + h_span[0], DEPTH + h_span[1] + 1))
        e_rows = list(range(DEPTH + e_span[0], DEPTH + e_span[1] + 1))
        skip = h_rows[:1] if skip_hx and h_span[0] < e_span[0] else []
        parts.append(leapfrog(main, main_exists, h_rows, e_rows, Rows(), main_h, main_c, layers, last, skip))
        h_of, c_of = functools.partial(edge_h, span=h_span), functools.partial(edge_c, span=e_span)
        parts.append(
            leapfrog(edge, edge_exists, blocks_of(h_span), blocks_of(e_span), Blocks(groups), h_of, c_of, layers, last, [])
        )
    for part in parts:
        next(part)
    for part in parts:
        next(part, None)


def port_sums(n, reached, prow_ref, weight_ref, e_ref, edge_ref, shift, edge_shift, sum_ref, add_ref):
    for k in range(PORT_TILE):
        at = prow_ref[0, 0, k]
        total = jnp.zeros((8, 128), jnp.float32)
        for zz in range(OWN):
            total = total + e_ref[2, at + shift, zz] * weight_ref[k, 0, zz]
            total = total + edge_ref[2, (at >> 2) + edge_shift, zz] * weight_ref[k, 1, zz]
        total = jnp.sum(jnp.where(reached(n, at), total, 0.0), axis=0, keepdims=True)
        if add_ref is not None:
            total = total + add_ref[n - 1, k : k + 1, :]
        sum_ref[n - 1, k : k + 1, :] = total


def finished(f, b, main, edge):
    lane = iota(1)
    place = lane & (GROUP - 1)
    sides = (lane < DEPTH) | (lane >= 128 - DEPTH)
    out = {}
    for zz in range(OWN):
        tile = edge.get(f, b + 1, zz)
        near = jnp.where(place < 8, tile, turn(tile, -8, 1))
        for r in range(4):
            own = main.get(f, DEPTH + 4 * b + r, zz)
            out[r, zz] = jnp.where(sides, turn(near, -(GROUP * r + 8), 1), own)
    return out


def inner_kernel(
    row_size, main_ref, z_ref, own_ref, low_ref, high_ref, low_z_ref, high_z_ref, mode_ref, prow_ref, pcol_ref, pmode_ref,
    e_ref, h_ref, c_ref, edge_e_ref, edge_h_ref, edge_c_ref, done_ref, weight_ref, sum_ref, ext_ref, strip_ref, joined_ref,
):
    gz, row, col = (lax.axis_index(name) for name in ("gz", "row", "col"))
    lane, sub = iota(1), iota(0)
    place = lane & (GROUP - 1)
    groups = [(lane >> 5) == r for r in range(4)]
    valid = (sub < 4) == (gz == 0)
    block = LAYERS * ROWS
    flat = main_ref.reshape(FIELDS * block, 128)
    spread_layers(gz, z_ref, ext_ref)

    def first(f, i, zz):
        x = i - DEPTH
        if zz == OWN:
            return ext_ref[f, pl.ds(x, 8, stride=ROWS), :]
        return flat[pl.ds(f * block + zz * 8 * ROWS + x, 8, stride=ROWS), :]

    for b in range(2):
        for zz in range(CHUNK):
            if zz < OWN:
                low, high = low_ref[b, zz], high_ref[b, zz]
            else:
                low, high = (halo_layers(valid, gz, ref, b) for ref in (low_z_ref, high_z_ref))
            for f in range(FIELDS):
                if zz < OWN:
                    own = own_ref[f, b, zz]
                else:
                    own = gather_edges([first(f, DEPTH + 4 * b + r, zz) for r in range(4)], groups)
                tile = edge_tile(own, low, high, f, place)
                joined_ref[f, b, zz] = tile
                if f == 6:
                    edge_c_ref[b, zz] = tile
    for k in range(PORT_TILE):
        strip_ref[k] = jnp.zeros(strip_ref.shape[1:], jnp.float32)
        strip_ref[k, :, 0:PLEN] = mode_ref[pmode_ref[0, 0, k]]
    for k in range(PORT_TILE):
        turned = GROUP * (prow_ref[0, 0, k] & 3)
        at = lane - turned
        for zz in range(OWN):
            tile = pltpu.roll(strip_ref[k, 8 * zz : 8 * zz + 8, :], pcol_ref[0, 0, k], 1)
            weight_ref[k, 0, zz] = jnp.where((lane >= DEPTH) & (lane < 128 - DEPTH), tile, 0.0)
            own = pltpu.roll(tile, turned + 8, 1)
            edge = jnp.where((at >= 4) & (at < 8), own, 0.0)
            weight_ref[k, 1, zz] = jnp.where((at >= 16) & (at < 20), turn(own, 8, 1), edge)
    sum_ref[...] = jnp.zeros(sum_ref.shape, jnp.float32)
    for x in range(ROWS):
        for zz in range(CHUNK):
            c_ref[x, zz] = first(6, DEPTH + x, zz)

    def run(has_below, has_above):
        main = Tiles(first, e_ref, h_ref, DEPTH)
        edge = Tiles(lambda f, i, zz: joined_ref[f, i - 1, zz], edge_e_ref, edge_h_ref, 1)

        def reached(n, at):
            low, high = spans_inner(n, has_below, has_above)[1]
            return (at >= low) & (at <= high)

        for n in range(1, STEPS + 1):
            spans = [spans_inner(n, has_below, has_above)]
            advance(n, spans, main, edge, range(4, 12), (1, 2), (row_size, gz, row, col), False)
            port_sums(n, reached, prow_ref, weight_ref, e_ref, edge_e_ref, 0, 0, sum_ref, None)
        for f in range(6):
            for i in range(4, 12):
                if (f, i) not in main.written:
                    for zz in range(CHUNK):
                        main.put(f, i, zz, main.get(f, i, zz))
            for i in (1, 2):
                if (f, i) not in edge.written:
                    for zz in range(CHUNK):
                        edge.put(f, i, zz, edge.get(f, i, zz))
        if has_below != has_above:
            for f in range(6):
                for (r, zz), tile in finished(f, 0 if has_above else 1, main, edge).items():
                    done_ref[f, r, zz] = tile

    if row_size == 2:
        pl.when(row == 0)(functools.partial(run, False, True))
        pl.when(row == 1)(functools.partial(run, True, False))
    else:
        run(True, True)


def outer_kernel(
    row_size, ports_each, basis_ref, prow_ref, pid_ref, e_in, h_in, c_in, edge_e_in, edge_h_in, edge_c_in, done_ref, weight_ref,
    sum_in, *rest,
):
    n_x = 1 if row_size == 2 else 2
    x_refs, corner_refs = rest[:n_x], rest[n_x : 2 * n_x]
    eout_hbm, hout_hbm, term_ref, e_ref, h_ref, c_ref, edge_e_ref, edge_h_ref, edge_c_ref, sum_ref, out_ref, sems = rest[2 * n_x :]
    gz, row, col = (lax.axis_index(name) for name in ("gz", "row", "col"))
    lane, sub = iota(1), iota(0)
    place = lane & (GROUP - 1)
    groups = [(lane >> 5) == r for r in range(4)]
    valid = (sub < 4) == (gz == 0)
    zeros = jnp.zeros((8, 128), jnp.float32)

    def first_main(f, i, zz):
        own = 4 <= i < 12
        if f == 6:
            return c_in[i - DEPTH, zz] if own else c_ref[i, zz]
        return e_in[f, i - DEPTH, zz] if f < 3 else h_in[f - 3, i - DEPTH, zz]

    def first_edge(f, i, zz):
        own = i in (1, 2)
        if f == 6:
            return edge_c_in[i - 1, zz] if own else edge_c_ref[i, zz]
        return edge_e_in[f, i - 1, zz] if f < 3 else edge_h_in[f - 3, i - 1, zz]

    def run(has_below, has_above):
        main = Tiles(first_main, e_ref, h_ref, 0)
        edge = Tiles(first_edge, edge_e_ref, edge_h_ref, 0)

        def halo_rows(planes, slot, offset, b):
            got = {}
            for i, (f, x) in enumerate(planes):
                packed = corner_refs[slot][i % PAIRS]
                if i >= PAIRS:
                    packed = turn(packed, 4, 0)
                tiles = [x_refs[slot][i, 8 * zz : 8 * zz + 8, :] for zz in range(OWN)]
                tiles.append(jnp.where(valid, packed, 0.0))
                for zz in range(CHUNK):
                    if f == 6:
                        c_ref[DEPTH + x + offset, zz] = tiles[zz]
                    else:
                        main.put(f, DEPTH + x + offset, zz, tiles[zz])
                    got[f, x + offset - 4 * b, zz] = tiles[zz]
                main.keep((f,), DEPTH + x + offset)
            main.written -= {(6, i) for i in range(16)}
            for zz in range(CHUNK):
                low = corner_refs[slot][PAIRS + zz]
                high = corner_refs[slot][PAIRS + CHUNK + zz]
                for f in range(FIELDS):
                    tiles = [got.get((f, r, zz)) for r in range(4)]
                    own = gather_edges(tiles, groups)
                    tile = edge_tile(zeros if own is None else own, low, high, f, place)
                    if f == 6:
                        edge_c_ref[1 + b, zz] = tile
                    else:
                        edge.put(f, 1 + b, zz, tile)
            edge.keep(range(6), 1 + b)

        if has_below:
            halo_rows(UP_PLANES, 0, -ROWS, -1)
        if has_above:
            halo_rows(DOWN_PLANES, n_x - 1, ROWS, 2)

        def reached(n, at):
            out = None
            for wanted, span in ((has_below, spans_below(n)[1]), (has_above, spans_above(n)[1])):
                if wanted:
                    part = (at >= span[0]) & (at <= span[1])
                    out = part if out is None else out | part
            return out

        rows = range(0 if has_below else 4, 16 if has_above else 12)
        blocks = range(0 if has_below else 1, 4 if has_above else 3)
        for n in range(1, STEPS + 1):
            spans = ([spans_below(n)] if has_below else []) + ([spans_above(n)] if has_above else [])
            advance(n, spans, main, edge, rows, blocks, (row_size, gz, row, col), True)
            port_sums(n, reached, prow_ref, weight_ref, e_ref, edge_e_ref, DEPTH, 1, sum_ref, sum_in)
        for f in range(6):
            for b in range(2):
                if has_below and has_above or b == (1 if has_above else 0):
                    tiles = finished(f, b, main, edge)
                else:
                    tiles = {(r, zz): done_ref[f, r, zz] for r in range(4) for zz in range(OWN)}
                for (r, zz), tile in tiles.items():
                    out_ref[f, pl.ds(zz * 8 * ROWS + 4 * b + r, 8, stride=ROWS), :] = tile

    if row_size == 2:
        pl.when(row == 0)(functools.partial(run, False, True))
        pl.when(row == 1)(functools.partial(run, True, False))
    else:
        run(True, True)

    copies = []
    for part, dest in ((0, eout_hbm), (1, hout_hbm)):
        copies.append(pltpu.make_async_copy(out_ref.at[pl.ds(3 * part, 3)], dest, sems.at[part]))
        copies[-1].start()
    transform = zeros
    for n in range(STEPS):
        sampled = jnp.sum(sum_ref[n], axis=1, keepdims=True)
        transform = transform + sampled * basis_ref[n : n + 1, :]
    term_ref[...] = jnp.zeros(term_ref.shape, jnp.float32)
    for k in range(PORT_TILE):
        port = pid_ref[0, 0, k]
        term_ref[port // ports_each, pl.ds(port % ports_each, 1), :] = transform[k : k + 1, : 2 * FREQ]
    for copy in copies:
        copy.wait()


def shifted(block, axis, size, distance):
    route = [(i - distance, i) for i in range(size) if 0 <= i - distance < size]
    return lax.ppermute(block, axis, route)


def swapped(block, axis, size):
    return lax.ppermute(block, axis, [(i, i ^ 1) for i in range(size)])


def solution(mesh):
    sizes = dict(mesh.shape)
    row_size, col_size, gz_size = sizes["row"], sizes["col"], sizes["gz"]
    n_x = 1 if row_size == 2 else 2

    def across_rows(blocks):
        if row_size == 2:
            return (swapped(blocks[0], "row", 2),)
        return (shifted(blocks[0], "row", row_size, 1), shifted(blocks[1], "row", row_size, -1))

    def per_device(
        electric, magnetic, material, eps_table, mode_table, port_row, port_col, port_mode, port_ids
    ):
        f32 = jnp.float32

        def array(*shape):
            return jax.ShapeDtypeStruct(shape, f32)

        def scratch(*shape):
            return pltpu.VMEM(shape, f32)

        main, z_send, *x_send = pl.pallas_call(
            functools.partial(pack_kernel, row_size),
            out_shape=[array(FIELDS, LAYERS, ROWS, 128), array(FIELDS, DEPTH, ROWS, 128)]
            + [array(PLANES, LAYERS, 128)] * n_x,
            in_specs=[HBM] * 4,
            out_specs=[VMEM] * (2 + n_x),
            scratch_shapes=[
                pltpu.SMEM(eps_table.shape, f32),
                pltpu.VMEM(material.shape, jnp.int32),
                pltpu.SemaphoreType.DMA((4,)),
            ],
            name="pack",
        )(eps_table, electric, magnetic, material)
        x_halo = across_rows(x_send)
        own, up_send, down_send = pl.pallas_call(
            edge_kernel,
            out_shape=[array(FIELDS, 2, OWN, 8, 128), array(2, OWN, 8, 128), array(2, OWN, 8, 128)],
            in_specs=[VMEM],
            out_specs=[VMEM] * 3,
            compiler_params=PARAMS,
            name="edges",
        )(main)
        low = shifted(up_send, "col", col_size, 1)
        high = shifted(down_send, "col", col_size, -1)
        z_halo = swapped(z_send, "gz", gz_size)
        low_z = swapped(low, "gz", gz_size)
        high_z = swapped(high, "gz", gz_size)
        corner_send = pl.pallas_call(
            functools.partial(corner_kernel, row_size),
            out_shape=[array(PAIRS + 2 * CHUNK, 8, 128)] * n_x,
            in_specs=[VMEM] * 5,
            out_specs=[VMEM] * n_x,
            scratch_shapes=[scratch(FIELDS, 8 * ROWS, 128)],
            compiler_params=PARAMS,
            name="corners",
        )(z_halo, low, high, low_z, high_z)
        corner = across_rows(corner_send)
        inner = pl.pallas_call(
            functools.partial(inner_kernel, row_size),
            out_shape=[
                array(3, ROWS, CHUNK, 8, 128),
                array(3, ROWS, CHUNK, 8, 128),
                array(ROWS, CHUNK, 8, 128),
                array(3, 2, CHUNK, 8, 128),
                array(3, 2, CHUNK, 8, 128),
                array(2, CHUNK, 8, 128),
                array(6, 4, OWN, 8, 128),
                array(PORT_TILE, 2, OWN, 8, 128),
                array(STEPS, 8, 128),
            ],
            in_specs=[VMEM] * 8 + [SMEM] * 3,
            out_specs=[VMEM] * 9,
            scratch_shapes=[
                scratch(FIELDS, 8 * ROWS, 128),
                scratch(PORT_TILE, LAYERS, 128),
                scratch(FIELDS, 2, CHUNK, 8, 128),
            ],
            compiler_params=PARAMS,
            name="inner",
        )(main, z_halo, own, low, high, low_z, high_z, mode_table, port_row, port_col, port_mode)
        devices = col_size * row_size * gz_size
        ports_each = PORT_TILE * col_size * row_size // devices
        electric_out, magnetic_out, term = pl.pallas_call(
            functools.partial(outer_kernel, row_size, ports_each),
            out_shape=[array(3, LAYERS * ROWS, 128)] * 2 + [array(devices, ports_each, 2 * FREQ)],
            in_specs=[VMEM] + [SMEM] * 2 + [VMEM] * (9 + 2 * n_x),
            out_specs=[HBM, HBM, VMEM],
            scratch_shapes=[
                scratch(3, 16, CHUNK, 8, 128),
                scratch(3, 16, CHUNK, 8, 128),
                scratch(16, CHUNK, 8, 128),
                scratch(3, 4, CHUNK, 8, 128),
                scratch(3, 4, CHUNK, 8, 128),
                scratch(4, CHUNK, 8, 128),
                scratch(STEPS, 8, 128),
                scratch(6, LAYERS * ROWS, 128),
                pltpu.SemaphoreType.DMA((2,)),
            ],
            compiler_params=PARAMS,
            name="outer",
        )(jnp.asarray(dft_basis()), port_row, port_ids, *inner, *x_halo, *corner)
        terms = lax.all_to_all(term, ("col", "row", "gz"), 0, 0, tiled=True)
        return (
            electric_out.reshape(electric.shape),
            magnetic_out.reshape(magnetic.shape),
            jnp.sum(terms, axis=0),
        )

    in_specs = (
        P(None, "gz", "row", ("grp", "col")),
        P(None, "gz", "row", ("grp", "col")),
        P("gz", "row", ("grp", "col")),
        P(),
        P(None, "gz", None),
        P(("grp", "row"), "col", None),
        P(("grp", "row"), "col", None),
        P(("grp", "row"), "col", None),
        P(("grp", "row"), "col", None),
    )
    out_specs = (
        P(None, "gz", "row", ("grp", "col")),
        P(None, "gz", "row", ("grp", "col")),
        P(("grp", "col", "row", "gz"), None),
    )
    return jax.shard_map(
        per_device, mesh=mesh, in_specs=in_specs, out_specs=out_specs, check_vma=False
    )
```

```python
import functools

import jax
import jax.numpy as jnp
import numpy as np
from jax import lax
from jax.experimental import pallas as pl
from jax.experimental.pallas import tpu as pltpu
from jax.sharding import PartitionSpec as P

STEPS = 4
FREQ = 8
MATS = 8
PLEN = 64
PORT_TILE = 4
FIELDS = 7
DEPTH = STEPS
ROWS = 8
LAYERS = 32
OWN = 4
CHUNK = 5
GROUP = 32

time_step = 0.5

UP_PLANES = [(f, 4) for f in (0, 1, 2, 4, 5)] + [(f, x) for x in (5, 6, 7) for f in range(FIELDS)]
DOWN_PLANES = [(f, x) for x in (0, 1, 2) for f in range(FIELDS)] + [(1, 3), (2, 3)]
PLANES = max(len(UP_PLANES), len(DOWN_PLANES))
PAIRS = (PLANES + 1) // 2

VMEM = pl.BlockSpec(memory_space=pltpu.VMEM)
SMEM = pl.BlockSpec(memory_space=pltpu.SMEM)
HBM = pl.BlockSpec(memory_space=pltpu.HBM)
PARAMS = pltpu.CompilerParams(vmem_limit_bytes=16 * 1024 * 1024)


def dft_basis():
    times = (np.arange(STEPS) + 1.0) * time_step
    omegas = np.pi * (np.arange(FREQ) + 1.0) / FREQ
    angle = times[:, None] * omegas[None, :]
    return np.concatenate([np.cos(angle), -np.sin(angle)], axis=1)


BASIS = dft_basis()


def iota(axis):
    return lax.broadcasted_iota(jnp.int32, (8, 128), axis)


def turn(tile, shift, axis):
    return pltpu.roll(tile, shift % tile.shape[axis], axis)


def directions(row_size, body):
    if row_size == 2:
        row = lax.axis_index("row")
        pl.when(row == 0)(functools.partial(body, True, 0))
        pl.when(row == 1)(functools.partial(body, False, 0))
    else:
        body(True, 0)
        body(False, 1)


def pack_kernel(eps_hbm, elec_hbm, magn_hbm, mat_hbm, main_ref, z_ref, own_ref, up_ref, down_ref, eps_ref, mat_ref, sems):
    copies = [pltpu.make_async_copy(eps_hbm, eps_ref, sems.at[0]), pltpu.make_async_copy(mat_hbm, mat_ref, sems.at[1])]
    copies.append(pltpu.make_async_copy(elec_hbm, main_ref.at[pl.ds(0, 3)], sems.at[2]))
    copies.append(pltpu.make_async_copy(magn_hbm, main_ref.at[pl.ds(3, 3)], sems.at[3]))
    for copy in copies:
        copy.start()
    copies[0].wait()
    copies[1].wait()
    for z in range(LAYERS):
        material = mat_ref[z]
        eps = jnp.full((8, 128), eps_ref[0], jnp.float32)
        for which in range(1, MATS):
            eps = jnp.where(material == which, eps_ref[which], eps)
        main_ref[6, z] = time_step * (1.0 / eps)
    copies[2].wait()
    copies[3].wait()
    start = jnp.where(lax.axis_index("gz") == 0, LAYERS - DEPTH, 0)
    for f in range(FIELDS):
        z_ref[f] = main_ref[f, pl.ds(start, DEPTH)]
    pack_edges(main_ref, own_ref, up_ref, down_ref)


def gather_edges(tiles, groups):
    own = None
    for r, tile in enumerate(tiles):
        if tile is not None:
            moved = turn(tile, GROUP * r + 8, 1)
            own = moved if own is None else jnp.where(groups[r], moved, own)
    return own


def pack_edges(main_ref, own_ref, up_ref, down_ref):
    lane = iota(1)
    groups = [(lane >> 5) == r for r in range(4)]
    slots = [((lane & (GROUP - 1)) >> 2) == f for f in range(FIELDS)]
    block = LAYERS * ROWS
    flat = main_ref.reshape(FIELDS * block, 128)
    values = []
    for b in range(2):
        for zz in range(OWN):
            up = down = jnp.zeros((8, 128), jnp.float32)
            for f in range(FIELDS):
                at = f * block + zz * 8 * ROWS + 4 * b
                own = gather_edges([flat[pl.ds(at + r, 8, stride=ROWS), :] for r in range(4)], groups)
                up = jnp.where(slots[f], turn(own, DEPTH * f - 4, 1), up)
                down = jnp.where(slots[f], turn(own, DEPTH * f - 8, 1), down)
                values.append((own_ref, (f, b, zz), own))
            values += [(up_ref, (b, zz), up), (down_ref, (b, zz), down)]
    for ref, where, value in values:
        ref[where] = value


def plane_kernel(row_size, main_ref, low_ref, high_ref, *x_refs):
    block = LAYERS * ROWS
    flat = main_ref.reshape(FIELDS * block, 128)

    def send(up, slot):
        planes = UP_PLANES if up else DOWN_PLANES
        for start in range(0, len(planes), 8):
            part = [flat[pl.ds(f * block + x, LAYERS, stride=ROWS), :] for f, x in planes[start : start + 8]]
            for i, plane in enumerate(part):
                x_refs[slot][start + i] = plane

    directions(row_size, send)


def halo_layers(valid, gz, side_ref, b):
    return jnp.where(valid, jnp.where(gz == 0, side_ref[b, 0], side_ref[b, OWN - 1]), 0.0)


def spread_layers(gz, z_ref, ext_ref):
    for f in range(FIELDS):
        halo = z_ref[f].reshape(DEPTH * ROWS, 128)
        nothing = jnp.zeros_like(halo)
        ext_ref[f, : DEPTH * ROWS] = jnp.where(gz == 0, halo, nothing)
        ext_ref[f, DEPTH * ROWS :] = jnp.where(gz == 0, nothing, halo)


def corner_kernel(row_size, z_ref, low_ref, high_ref, low_z_ref, high_z_ref, *rest):
    x_refs, ext_ref = rest[:-1], rest[-1]
    gz = lax.axis_index("gz")
    valid = (iota(0) < 4) == (gz == 0)
    spread_layers(gz, z_ref, ext_ref)

    def send(up, slot):
        planes = UP_PLANES if up else DOWN_PLANES

        def tile(i):
            f, x = planes[i]
            return ext_ref[f, pl.ds(x, 8, stride=ROWS), :]

        for i in range(PAIRS):
            pair = tile(i)
            if i + PAIRS < len(planes):
                pair = pair + turn(tile(i + PAIRS), 4, 0)
            x_refs[slot][i] = pair
        b = 1 if up else 0
        for zz in range(OWN):
            x_refs[slot][PAIRS + zz] = low_ref[b, zz]
            x_refs[slot][PAIRS + CHUNK + zz] = high_ref[b, zz]
        x_refs[slot][PAIRS + OWN] = halo_layers(valid, gz, low_z_ref, b)
        x_refs[slot][PAIRS + CHUNK + OWN] = halo_layers(valid, gz, high_z_ref, b)

    directions(row_size, send)


def edge_tile(own, low, high, f, place):
    out = jnp.where(place < 16, turn(low, 12 - DEPTH * f, 1), turn(own, 8, 1))
    out = jnp.where(place < 12, turn(high, 8 - DEPTH * f, 1), out)
    return jnp.where(place < 8, own, out)


class Tiles:
    def __init__(self, first, ez_ref, shift):
        self.first, self.ez_ref, self.shift = first, ez_ref, shift
        self.values = {}

    def get(self, f, i, zz):
        value = self.values.get((f, i, zz))
        return self.first(f, i, zz) if value is None else value

    def put(self, f, i, zz, tile):
        self.values[f, i, zz] = tile
        at = i - self.shift
        if f == 2 and zz < OWN and 0 <= at < self.ez_ref.shape[0]:
            self.ez_ref[at, zz] = tile


def leapfrog(tiles, exists, h_rows, e_rows, across, h_of, c_of, h_layers, e_layers, skip_hx):
    sub = iota(0)
    every = range(CHUNK)
    blank = [jnp.zeros((8, 128), jnp.float32)] * CHUNK

    def above(values):
        turned = [turn(v, -1, 0) for v in values]
        return [jnp.where(sub == 7, turned[(zz + 1) % CHUNK], turned[zz]) for zz in every]

    def beneath(values):
        turned = [turn(v, 1, 0) for v in values]
        return [jnp.where(sub == 0, turned[zz - 1], turned[zz]) for zz in every]

    def row(f, i):
        return [tiles.get(f, i, zz) for zz in every]

    def load_e(i):
        ey, ez = row(1, i), row(2, i)
        out = dict(ey=ey, ez=ez, ey_x=across.turned(ey, -1), ez_x=across.turned(ez, -1))
        if i in h_rows:
            ex = row(0, i)
            out.update(ex=ex, ex_y=[turn(v, -1, 1) for v in ex], ex_z=above(ex))
            if i not in skip_hx:
                out.update(ez_y=[turn(v, -1, 1) for v in ez], ey_z=above(ey))
        return out

    def work_h(i, loaded):
        e, after, h = loaded[i], loaded.get(i + 1), h_of(i)
        ey_x = across.pick(e["ey_x"], after["ey_x"] if after else blank, -1)
        ez_x = across.pick(e["ez_x"], after["ez_x"] if after else blank, -1)
        new = {}
        for zz in h_layers:
            if i not in skip_hx:
                curl = (e["ez_y"][zz] - e["ez"][zz]) - (e["ey_z"][zz] - e["ey"][zz])
                new[3, zz] = tiles.get(3, i, zz) - h[zz] * curl
            curl = (e["ex_z"][zz] - e["ex"][zz]) - (ez_x[zz] - e["ez"][zz])
            new[4, zz] = tiles.get(4, i, zz) - h[zz] * curl
            curl = (ey_x[zz] - e["ey"][zz]) - (e["ex_y"][zz] - e["ex"][zz])
            new[5, zz] = tiles.get(5, i, zz) - h[zz] * curl
        for (f, zz), tile in new.items():
            tiles.put(f, i, zz, tile)

    def load_h(i):
        hy, hz = row(4, i), row(5, i)
        out = dict(hy=hy, hz=hz, hy_x=across.turned(hy, 1), hz_x=across.turned(hz, 1))
        if i in e_rows:
            hx = row(3, i)
            out.update(hx=hx, hx_y=[turn(v, 1, 1) for v in hx], hz_y=[turn(v, 1, 1) for v in hz])
            out.update(hx_z=beneath(hx), hy_z=beneath(hy))
        return out

    def work_e(i, loaded):
        h, before, c = loaded[i], loaded.get(i - 1), c_of(i)
        hy_x = across.pick(h["hy_x"], before["hy_x"] if before else blank, 1)
        hz_x = across.pick(h["hz_x"], before["hz_x"] if before else blank, 1)
        new = {}
        for zz in e_layers:
            curl = (h["hz"][zz] - h["hz_y"][zz]) - (h["hy"][zz] - h["hy_z"][zz])
            new[0, zz] = tiles.get(0, i, zz) + c[zz] * curl
            curl = (h["hx"][zz] - h["hx_z"][zz]) - (h["hz"][zz] - hz_x[zz])
            new[1, zz] = tiles.get(1, i, zz) + c[zz] * curl
            curl = (h["hy"][zz] - hy_x[zz]) - (h["hx"][zz] - h["hx_y"][zz])
            new[2, zz] = tiles.get(2, i, zz) + c[zz] * curl
        for (f, zz), tile in new.items():
            tiles.put(f, i, zz, tile)

    def sweep(rows, load, work):
        loaded = {}

        def want(i):
            if i not in loaded and i in exists:
                loaded[i] = load(i)

        for i in rows:
            for j in (i - 1, i, i + 1):
                if j in rows or j == i + (1 if load is load_e else -1):
                    want(j)
            work(i, loaded)

    sweep(h_rows, load_e, work_h)
    yield
    sweep(e_rows, load_h, work_e)


class Rows:
    def turned(self, values, way):
        return values

    def pick(self, own, other, way):
        return other


class Blocks:
    def __init__(self, groups):
        self.groups = groups

    def turned(self, values, way):
        return [turn(v, way * GROUP, 1) for v in values]

    def pick(self, own, other, way):
        edge = self.groups[3] if way < 0 else self.groups[0]
        return [jnp.where(edge, o, v) for o, v in zip(other, own)]


def spans_inner(n, has_below, has_above):
    last = 7 - n if has_above else 7
    return (n - 1 if has_below else 0, last), (n if has_below else 0, last)


def spans_below(n):
    return (n - 5, n - 2), (n - 4, n - 1)


def spans_above(n):
    return (8 - n, 11 - n), (8 - n, 11 - n)


class Stepper:
    def __init__(self, row_size, main, edge, main_exists, edge_exists, skip_hx):
        gz, row, col = (lax.axis_index(name) for name in ("gz", "row", "col"))
        lane, sub = iota(1), iota(0)
        place, self.group = lane & (GROUP - 1), lane >> 5
        full = jnp.full((8, 128), time_step, jnp.float32)
        self.layer_half = [full] * OWN + [jnp.where((sub >= 4) & (gz == 0), 0.0, full)]
        outside = (place >= 12) & (place < 16) & (col == 0)
        self.edge_half = [jnp.where(outside, 0.0, v) for v in self.layer_half]
        self.lowest = jnp.where(row == 0, 0.0, 1.0) if row_size > 2 else None
        self.main, self.edge, self.skip_hx = main, edge, skip_hx
        self.main_exists, self.edge_exists = main_exists, edge_exists
        self.blocks = Blocks([self.group == r for r in range(4)])

    def masked(self, values, block, span):
        low, high = max(span[0] - 4 * block, 0), min(span[1] - 4 * block, 3)
        if low == 0 and high == 3:
            return values
        mask = (self.group >= low) & (self.group <= high)
        return [jnp.where(mask, v, 0.0) for v in values]

    def main_h(self, i):
        return self.layer_half if self.lowest is None or i >= DEPTH else [v * self.lowest for v in self.layer_half]

    def main_c(self, i):
        return [self.main.get(6, i, zz) for zz in range(CHUNK)]

    def edge_h(self, i, span):
        h = self.edge_half if self.lowest is None or i else [v * self.lowest for v in self.edge_half]
        return self.masked(h, i - 1, span)

    def edge_c(self, i, span):
        return self.masked([self.edge.get(6, i, zz) for zz in range(CHUNK)], i - 1, span)

    def step(self, n, spans):
        def blocks_of(span):
            return [b + 1 for b in range(-1, 3) if span[0] <= 4 * b + 3 and span[1] >= 4 * b]

        layers = range(CHUNK)
        last = range(OWN) if n == STEPS else layers
        parts = []
        for h_span, e_span in spans:
            h_rows = list(range(DEPTH + h_span[0], DEPTH + h_span[1] + 1))
            e_rows = list(range(DEPTH + e_span[0], DEPTH + e_span[1] + 1))
            skip = h_rows[:1] if self.skip_hx and h_span[0] < e_span[0] else []
            parts.append(
                leapfrog(self.main, self.main_exists, h_rows, e_rows, Rows(), self.main_h, self.main_c, layers, last, skip)
            )
            h_of, c_of = functools.partial(self.edge_h, span=h_span), functools.partial(self.edge_c, span=e_span)
            parts.append(
                leapfrog(
                    self.edge, self.edge_exists, blocks_of(h_span), blocks_of(e_span), self.blocks, h_of, c_of, layers, last, []
                )
            )
        for part in parts:
            next(part)
        for part in parts:
            next(part, None)


def port_sums(n, reached, prow_ref, weight_ref, ez_ref, edge_ref, sum_ref, add_ref):
    for k in range(PORT_TILE):
        at = prow_ref[0, 0, k]
        total = jnp.zeros((8, 128), jnp.float32)
        for zz in range(OWN):
            total = total + ez_ref[at, zz] * weight_ref[k, 0, zz]
            total = total + edge_ref[at >> 2, zz] * weight_ref[k, 1, zz]
        total = jnp.sum(jnp.where(reached(n, at), total, 0.0), axis=0, keepdims=True)
        if add_ref is not None:
            total = total + add_ref[n - 1, k : k + 1, :]
        sum_ref[n - 1, k : k + 1, :] = total


def finished(f, b, main, edge):
    lane = iota(1)
    place = lane & (GROUP - 1)
    sides = (lane < DEPTH) | (lane >= 128 - DEPTH)
    out = {}
    for zz in range(OWN):
        tile = edge.get(f, b + 1, zz)
        near = jnp.where(place < 8, tile, turn(tile, -8, 1))
        for r in range(4):
            own = main.get(f, DEPTH + 4 * b + r, zz)
            out[r, zz] = jnp.where(sides, turn(near, -(GROUP * r + 8), 1), own)
    return out


def inner_kernel(
    row_size, main_ref, z_ref, own_ref, low_ref, high_ref, low_z_ref, high_z_ref, mode_ref, prow_ref, pcol_ref, pmode_ref,
    e_ref, h_ref, c_ref, edge_e_ref, edge_h_ref, edge_c_ref, done_ref, weight_ref, sum_ref, ext_ref, strip_ref, ez_ref, edge_ez_ref,
):
    gz, row = lax.axis_index("gz"), lax.axis_index("row")
    lane, sub = iota(1), iota(0)
    place = lane & (GROUP - 1)
    groups = [(lane >> 5) == r for r in range(4)]
    valid = (sub < 4) == (gz == 0)
    block = LAYERS * ROWS
    flat = main_ref.reshape(FIELDS * block, 128)
    spread_layers(gz, z_ref, ext_ref)

    def first(f, i, zz):
        x = i - DEPTH
        if zz == OWN:
            return ext_ref[f, pl.ds(x, 8, stride=ROWS), :]
        return flat[pl.ds(f * block + zz * 8 * ROWS + x, 8, stride=ROWS), :]

    joined = {}
    for b in range(2):
        for zz in range(CHUNK):
            if zz < OWN:
                low, high = low_ref[b, zz], high_ref[b, zz]
            else:
                low, high = (halo_layers(valid, gz, ref, b) for ref in (low_z_ref, high_z_ref))
            for f in range(FIELDS):
                if zz < OWN:
                    own = own_ref[f, b, zz]
                else:
                    own = gather_edges([first(f, DEPTH + 4 * b + r, zz) for r in range(4)], groups)
                joined[f, b + 1, zz] = edge_tile(own, low, high, f, place)
    for k in range(PORT_TILE):
        strip_ref[k] = jnp.zeros(strip_ref.shape[1:], jnp.float32)
        strip_ref[k, :, 0:PLEN] = mode_ref[pmode_ref[0, 0, k]]
    for k in range(PORT_TILE):
        turned = GROUP * (prow_ref[0, 0, k] & 3)
        at = lane - turned
        for zz in range(OWN):
            tile = pltpu.roll(strip_ref[k, 8 * zz : 8 * zz + 8, :], pcol_ref[0, 0, k], 1)
            weight_ref[k, 0, zz] = jnp.where((lane >= DEPTH) & (lane < 128 - DEPTH), tile, 0.0)
            own = pltpu.roll(tile, turned + 8, 1)
            edge = jnp.where((at >= 4) & (at < 8), own, 0.0)
            weight_ref[k, 1, zz] = jnp.where((at >= 16) & (at < 20), turn(own, 8, 1), edge)

    def run(has_below, has_above):
        main = Tiles(first, ez_ref, DEPTH)
        edge = Tiles(lambda f, i, zz: joined[f, i, zz], edge_ez_ref, 1)
        stepper = Stepper(row_size, main, edge, range(4, 12), (1, 2), False)

        def reached(n, at):
            low, high = spans_inner(n, has_below, has_above)[1]
            return (at >= low) & (at <= high)

        for n in range(1, STEPS + 1):
            stepper.step(n, [spans_inner(n, has_below, has_above)])
            port_sums(n, reached, prow_ref, weight_ref, ez_ref, edge_ez_ref, sum_ref, None)
        for tiles, base, count, refs in (
            (main, DEPTH, ROWS, (e_ref, h_ref, c_ref)),
            (edge, 1, 2, (edge_e_ref, edge_h_ref, edge_c_ref)),
        ):
            for i in range(count):
                for zz in range(CHUNK):
                    for f in range(6):
                        refs[f // 3][f % 3, i, zz] = tiles.get(f, base + i, zz)
                    refs[2][i, zz] = tiles.get(6, base + i, zz)
        if has_below != has_above:
            for f in range(6):
                for (r, zz), tile in finished(f, 0 if has_above else 1, main, edge).items():
                    done_ref[f, r, zz] = tile

    if row_size == 2:
        pl.when(row == 0)(functools.partial(run, False, True))
        pl.when(row == 1)(functools.partial(run, True, False))
    else:
        run(True, True)


def outer_kernel(
    row_size, ports_each, prow_ref, pid_ref, e_in, h_in, c_in, edge_e_in, edge_h_in, edge_c_in, done_ref, weight_ref,
    sum_in, *rest,
):
    n_x = 1 if row_size == 2 else 2
    x_refs, corner_refs = rest[:n_x], rest[n_x : 2 * n_x]
    eout_hbm, hout_hbm, term_ref, ez_ref, edge_ez_ref, sum_ref, out_ref, sems = rest[2 * n_x :]
    gz, row = lax.axis_index("gz"), lax.axis_index("row")
    lane, sub = iota(1), iota(0)
    place = lane & (GROUP - 1)
    groups = [(lane >> 5) == r for r in range(4)]
    valid = (sub < 4) == (gz == 0)
    zeros = jnp.zeros((8, 128), jnp.float32)

    def first_main(f, i, zz):
        if f == 6:
            return c_in[i - DEPTH, zz]
        return e_in[f, i - DEPTH, zz] if f < 3 else h_in[f - 3, i - DEPTH, zz]

    def first_edge(f, i, zz):
        if f == 6:
            return edge_c_in[i - 1, zz]
        return edge_e_in[f, i - 1, zz] if f < 3 else edge_h_in[f - 3, i - 1, zz]

    def run(has_below, has_above):
        main = Tiles(first_main, ez_ref, DEPTH)
        edge = Tiles(first_edge, edge_ez_ref, 1)

        def halo_rows(planes, slot, offset, b):
            got = {}
            for i, (f, x) in enumerate(planes):
                packed = corner_refs[slot][i % PAIRS]
                if i >= PAIRS:
                    packed = turn(packed, 4, 0)
                tiles = [x_refs[slot][i, 8 * zz : 8 * zz + 8, :] for zz in range(OWN)]
                tiles.append(jnp.where(valid, packed, 0.0))
                for zz in range(CHUNK):
                    main.put(f, DEPTH + x + offset, zz, tiles[zz])
                    got[f, x + offset - 4 * b, zz] = tiles[zz]
            for zz in range(CHUNK):
                low = corner_refs[slot][PAIRS + zz]
                high = corner_refs[slot][PAIRS + CHUNK + zz]
                for f in range(FIELDS):
                    tiles = [got.get((f, r, zz)) for r in range(4)]
                    own = gather_edges(tiles, groups)
                    tile = edge_tile(zeros if own is None else own, low, high, f, place)
                    edge.put(f, 1 + b, zz, tile)

        if has_below:
            halo_rows(UP_PLANES, 0, -ROWS, -1)
        if has_above:
            halo_rows(DOWN_PLANES, n_x - 1, ROWS, 2)

        def reached(n, at):
            out = None
            for wanted, span in ((has_below, spans_below(n)[1]), (has_above, spans_above(n)[1])):
                if wanted:
                    part = (at >= span[0]) & (at <= span[1])
                    out = part if out is None else out | part
            return out

        rows = range(0 if has_below else 4, 16 if has_above else 12)
        blocks = range(0 if has_below else 1, 4 if has_above else 3)
        stepper = Stepper(row_size, main, edge, rows, blocks, True)
        for n in range(1, STEPS + 1):
            spans = ([spans_below(n)] if has_below else []) + ([spans_above(n)] if has_above else [])
            stepper.step(n, spans)
            port_sums(n, reached, prow_ref, weight_ref, ez_ref, edge_ez_ref, sum_ref, sum_in)
        for f in range(6):
            for b in range(2):
                if has_below and has_above or b == (1 if has_above else 0):
                    tiles = finished(f, b, main, edge)
                else:
                    tiles = {(r, zz): done_ref[f, r, zz] for r in range(4) for zz in range(OWN)}
                for (r, zz), tile in tiles.items():
                    out_ref[f, pl.ds(zz * 8 * ROWS + 4 * b + r, 8, stride=ROWS), :] = tile

    if row_size == 2:
        pl.when(row == 0)(functools.partial(run, False, True))
        pl.when(row == 1)(functools.partial(run, True, False))
    else:
        run(True, True)

    copies = []
    for part, dest in ((0, eout_hbm), (1, hout_hbm)):
        copies.append(pltpu.make_async_copy(out_ref.at[pl.ds(3 * part, 3)], dest, sems.at[part]))
        copies[-1].start()
    basis = zeros
    for n in range(STEPS):
        for f in range(2 * FREQ):
            basis = jnp.where((sub == n) & (lane == f), float(BASIS[n, f]), basis)
    transform = zeros
    for n in range(STEPS):
        sampled = jnp.sum(sum_ref[n], axis=1, keepdims=True)
        transform = transform + sampled * basis[n : n + 1, :]
    term_ref[...] = jnp.zeros(term_ref.shape, jnp.float32)
    for k in range(PORT_TILE):
        port = pid_ref[0, 0, k]
        term_ref[port // ports_each, pl.ds(port % ports_each, 1), :] = transform[k : k + 1, : 2 * FREQ]
    for copy in copies:
        copy.wait()


def shifted(block, axis, size, distance):
    route = [(i - distance, i) for i in range(size) if 0 <= i - distance < size]
    return lax.ppermute(block, axis, route)


def swapped(block, axis, size):
    return lax.ppermute(block, axis, [(i, i ^ 1) for i in range(size)])


def solution(mesh):
    sizes = dict(mesh.shape)
    row_size, col_size, gz_size = sizes["row"], sizes["col"], sizes["gz"]
    n_x = 1 if row_size == 2 else 2

    def across_rows(blocks):
        if row_size == 2:
            return (swapped(blocks[0], "row", 2),)
        return (shifted(blocks[0], "row", row_size, 1), shifted(blocks[1], "row", row_size, -1))

    def per_device(
        electric, magnetic, material, eps_table, mode_table, port_row, port_col, port_mode, port_ids
    ):
        f32 = jnp.float32

        def array(*shape):
            return jax.ShapeDtypeStruct(shape, f32)

        def scratch(*shape):
            return pltpu.VMEM(shape, f32)

        main, z_send, own, up_send, down_send = pl.pallas_call(
            pack_kernel,
            out_shape=[
                array(FIELDS, LAYERS, ROWS, 128),
                array(FIELDS, DEPTH, ROWS, 128),
                array(FIELDS, 2, OWN, 8, 128),
                array(2, OWN, 8, 128),
                array(2, OWN, 8, 128),
            ],
            in_specs=[HBM] * 4,
            out_specs=[VMEM] * 5,
            scratch_shapes=[
                pltpu.SMEM(eps_table.shape, f32),
                pltpu.VMEM(material.shape, jnp.int32),
                pltpu.SemaphoreType.DMA((4,)),
            ],
            name="pack",
        )(eps_table, electric, magnetic, material)
        low = shifted(up_send, "col", col_size, 1)
        high = shifted(down_send, "col", col_size, -1)
        z_halo = swapped(z_send, "gz", gz_size)
        x_send = pl.pallas_call(
            functools.partial(plane_kernel, row_size),
            out_shape=[array(PLANES, LAYERS, 128)] * n_x,
            in_specs=[VMEM] + [pl.BlockSpec(memory_space=pl.ANY)] * 2,
            out_specs=[VMEM] * n_x,
            compiler_params=PARAMS,
            name="planes",
        )(main, low, high)
        x_halo = across_rows(x_send)
        low_z = swapped(low, "gz", gz_size)
        high_z = swapped(high, "gz", gz_size)
        corner_send = pl.pallas_call(
            functools.partial(corner_kernel, row_size),
            out_shape=[array(PAIRS + 2 * CHUNK, 8, 128)] * n_x,
            in_specs=[VMEM] * 5,
            out_specs=[VMEM] * n_x,
            scratch_shapes=[scratch(FIELDS, 8 * ROWS, 128)],
            compiler_params=PARAMS,
            name="corners",
        )(z_halo, low, high, low_z, high_z)
        corner = across_rows(corner_send)
        inner = pl.pallas_call(
            functools.partial(inner_kernel, row_size),
            out_shape=[
                array(3, ROWS, CHUNK, 8, 128),
                array(3, ROWS, CHUNK, 8, 128),
                array(ROWS, CHUNK, 8, 128),
                array(3, 2, CHUNK, 8, 128),
                array(3, 2, CHUNK, 8, 128),
                array(2, CHUNK, 8, 128),
                array(6, 4, OWN, 8, 128),
                array(PORT_TILE, 2, OWN, 8, 128),
                array(STEPS, 8, 128),
            ],
            in_specs=[VMEM] * 8 + [SMEM] * 3,
            out_specs=[VMEM] * 9,
            scratch_shapes=[
                scratch(FIELDS, 8 * ROWS, 128),
                scratch(PORT_TILE, LAYERS, 128),
                scratch(ROWS, OWN, 8, 128),
                scratch(2, OWN, 8, 128),
            ],
            compiler_params=PARAMS,
            name="inner",
        )(main, z_halo, own, low, high, low_z, high_z, mode_table, port_row, port_col, port_mode)
        devices = col_size * row_size * gz_size
        ports_each = PORT_TILE * col_size * row_size // devices
        electric_out, magnetic_out, term = pl.pallas_call(
            functools.partial(outer_kernel, row_size, ports_each),
            out_shape=[array(3, LAYERS * ROWS, 128)] * 2 + [array(devices, ports_each, 2 * FREQ)],
            in_specs=[SMEM] * 2 + [VMEM] * (9 + 2 * n_x),
            out_specs=[HBM, HBM, VMEM],
            scratch_shapes=[
                scratch(ROWS, OWN, 8, 128),
                scratch(2, OWN, 8, 128),
                scratch(STEPS, 8, 128),
                scratch(6, LAYERS * ROWS, 128),
                pltpu.SemaphoreType.DMA((2,)),
            ],
            compiler_params=PARAMS,
            name="outer",
        )(port_row, port_ids, *inner, *x_halo, *corner)
        terms = lax.all_to_all(term, ("col", "row", "gz"), 0, 0, tiled=True)
        return (
            electric_out.reshape(electric.shape),
            magnetic_out.reshape(magnetic.shape),
            jnp.sum(terms, axis=0),
        )

    in_specs = (
        P(None, "gz", "row", ("grp", "col")),
        P(None, "gz", "row", ("grp", "col")),
        P("gz", "row", ("grp", "col")),
        P(),
        P(None, "gz", None),
        P(("grp", "row"), "col", None),
        P(("grp", "row"), "col", None),
        P(("grp", "row"), "col", None),
        P(("grp", "row"), "col", None),
    )
    out_specs = (
        P(None, "gz", "row", ("grp", "col")),
        P(None, "gz", "row", ("grp", "col")),
        P(("grp", "col", "row", "gz"), None),
    )
    return jax.shard_map(
        per_device, mesh=mesh, in_specs=in_specs, out_specs=out_specs, check_vma=False
    )
```

```python
import functools

import jax
import jax.numpy as jnp
import numpy as np
from jax import lax
from jax.experimental import pallas as pl
from jax.experimental.pallas import tpu as pltpu
from jax.sharding import PartitionSpec as P

STEPS = 4
FREQ = 8
MATS = 8
PLEN = 64
PORT_TILE = 4
FIELDS = 7
DEPTH = STEPS
ROWS = 8
LAYERS = 32
OWN = 4
CHUNK = 5
GROUP = 32

time_step = 0.5

UP_PLANES = [(f, 4) for f in (0, 1, 2, 4, 5)] + [(f, x) for x in (5, 6, 7) for f in range(FIELDS)]
DOWN_PLANES = [(f, x) for x in (0, 1, 2) for f in range(FIELDS)] + [(1, 3), (2, 3)]
PLANES = max(len(UP_PLANES), len(DOWN_PLANES))
PAIRS = (PLANES + 1) // 2

VMEM = pl.BlockSpec(memory_space=pltpu.VMEM)
SMEM = pl.BlockSpec(memory_space=pltpu.SMEM)
HBM = pl.BlockSpec(memory_space=pltpu.HBM)
PARAMS = pltpu.CompilerParams(vmem_limit_bytes=16 * 1024 * 1024)


def dft_basis():
    times = (np.arange(STEPS) + 1.0) * time_step
    omegas = np.pi * (np.arange(FREQ) + 1.0) / FREQ
    angle = times[:, None] * omegas[None, :]
    return np.concatenate([np.cos(angle), -np.sin(angle)], axis=1)


BASIS = dft_basis()


def iota(axis):
    return lax.broadcasted_iota(jnp.int32, (8, 128), axis)


def turn(tile, shift, axis):
    return pltpu.roll(tile, shift % tile.shape[axis], axis)


def directions(row_size, body):
    if row_size == 2:
        row = lax.axis_index("row")
        pl.when(row == 0)(functools.partial(body, True, 0))
        pl.when(row == 1)(functools.partial(body, False, 0))
    else:
        body(True, 0)
        body(False, 1)


def pack_kernel(row_size, eps_hbm, elec_hbm, magn_hbm, mat_hbm, state_ref, z_ref, own_ref, even_ref, odd_ref, *rest):
    x_refs, (main_ref, eps_ref, mat_ref, sems) = rest[:-4], rest[-4:]
    copies = [pltpu.make_async_copy(eps_hbm, eps_ref, sems.at[0]), pltpu.make_async_copy(mat_hbm, mat_ref, sems.at[1])]
    copies.append(pltpu.make_async_copy(elec_hbm, main_ref.at[pl.ds(0, 3)], sems.at[2]))
    copies.append(pltpu.make_async_copy(magn_hbm, main_ref.at[pl.ds(3, 3)], sems.at[3]))
    for copy in copies:
        copy.start()
    copies[0].wait()
    copies[1].wait()
    for z in range(LAYERS):
        material = mat_ref[z]
        eps = jnp.full((8, 128), eps_ref[0], jnp.float32)
        for which in range(1, MATS):
            eps = jnp.where(material == which, eps_ref[which], eps)
        main_ref[6, z] = time_step * (1.0 / eps)
    copies[2].wait()
    copies[3].wait()
    start = jnp.where(lax.axis_index("gz") == 0, LAYERS - DEPTH, 0)
    for f in range(FIELDS):
        z_ref[f] = main_ref[f, pl.ds(start, DEPTH)]
    block = LAYERS * ROWS
    flat = main_ref.reshape(FIELDS * block, 128)
    for f in range(FIELDS):
        for x in range(ROWS):
            state_ref[f, x] = flat[pl.ds(f * block + x, LAYERS, stride=ROWS), :].reshape(OWN, 8, 128)

    def send(up, slot):
        for i, (f, x) in enumerate(UP_PLANES if up else DOWN_PLANES):
            x_refs[slot][i] = state_ref[f, x]

    directions(row_size, send)
    pack_edges(state_ref, own_ref, even_ref, odd_ref)


def gather_edges(tiles, groups):
    own = None
    for r, tile in enumerate(tiles):
        if tile is not None:
            moved = turn(tile, GROUP * r + 8, 1)
            own = moved if own is None else jnp.where(groups[r], moved, own)
    return own


def pack_edges(state_ref, own_ref, even_ref, odd_ref):
    lane = iota(1)
    groups = [(lane >> 5) == r for r in range(4)]
    slots = [((lane & (GROUP - 1)) >> 2) == f for f in range(FIELDS)]
    even = (lax.axis_index("col") & 1) == 0
    for b in range(2):
        for zz in range(OWN):
            up = down = jnp.zeros((8, 128), jnp.float32)
            owns = []
            for f in range(FIELDS):
                own = gather_edges([state_ref[f, 4 * b + r, zz] for r in range(4)], groups)
                up = jnp.where(slots[f], turn(own, DEPTH * f - 4, 1), up)
                down = jnp.where(slots[f], turn(own, DEPTH * f - 8, 1), down)
                owns.append(own)
            for f in range(FIELDS):
                own_ref[f, b, zz] = owns[f]
            even_ref[b, zz] = jnp.where(even, up, down)
            odd_ref[b, zz] = jnp.where(even, down, up)


def low_and_high(even_ref, odd_ref):
    even = (lax.axis_index("col") & 1) == 0

    def low(*at):
        return jnp.where(even, odd_ref[at], even_ref[at])

    def high(*at):
        return jnp.where(even, even_ref[at], odd_ref[at])

    return low, high


def halo_layers(valid, gz, side, b):
    return jnp.where(valid, jnp.where(gz == 0, side(b, 0), side(b, OWN - 1)), 0.0)


def spread_layers(gz, z_ref, ext_ref):
    for f in range(FIELDS):
        halo = z_ref[f].reshape(DEPTH * ROWS, 128)
        nothing = jnp.zeros_like(halo)
        ext_ref[f, : DEPTH * ROWS] = jnp.where(gz == 0, halo, nothing)
        ext_ref[f, DEPTH * ROWS :] = jnp.where(gz == 0, nothing, halo)


def corner_kernel(row_size, z_ref, even_ref, odd_ref, even_z_ref, odd_z_ref, *rest):
    x_refs, ext_ref = rest[:-1], rest[-1]
    gz = lax.axis_index("gz")
    valid = (iota(0) < 4) == (gz == 0)
    spread_layers(gz, z_ref, ext_ref)
    low, high = low_and_high(even_ref, odd_ref)
    low_z, high_z = low_and_high(even_z_ref, odd_z_ref)

    def send(up, slot):
        planes = UP_PLANES if up else DOWN_PLANES

        def tile(i):
            f, x = planes[i]
            return ext_ref[f, pl.ds(x, 8, stride=ROWS), :]

        for i in range(PAIRS):
            pair = tile(i)
            if i + PAIRS < len(planes):
                pair = pair + turn(tile(i + PAIRS), 4, 0)
            x_refs[slot][i] = pair
        b = 1 if up else 0
        for zz in range(OWN):
            x_refs[slot][PAIRS + zz] = low(b, zz)
            x_refs[slot][PAIRS + CHUNK + zz] = high(b, zz)
        x_refs[slot][PAIRS + OWN] = halo_layers(valid, gz, low_z, b)
        x_refs[slot][PAIRS + CHUNK + OWN] = halo_layers(valid, gz, high_z, b)

    directions(row_size, send)


def edge_tile(own, low, high, f, place):
    out = jnp.where(place < 16, turn(low, 12 - DEPTH * f, 1), turn(own, 8, 1))
    out = jnp.where(place < 12, turn(high, 8 - DEPTH * f, 1), out)
    return jnp.where(place < 8, own, out)


class Tiles:
    def __init__(self, first, ez_ref, shift):
        self.first, self.ez_ref, self.shift = first, ez_ref, shift
        self.values = {}

    def get(self, f, i, zz):
        value = self.values.get((f, i, zz))
        return self.first(f, i, zz) if value is None else value

    def put(self, f, i, zz, tile):
        self.values[f, i, zz] = tile
        at = i - self.shift
        if f == 2 and zz < OWN and 0 <= at < self.ez_ref.shape[0]:
            self.ez_ref[at, zz] = tile


def leapfrog(tiles, exists, h_rows, e_rows, across, h_of, c_of, h_layers, e_layers, skip_hx):
    sub = iota(0)
    every = range(CHUNK)
    blank = [jnp.zeros((8, 128), jnp.float32)] * CHUNK

    def above(values):
        turned = [turn(v, -1, 0) for v in values]
        return [jnp.where(sub == 7, turned[(zz + 1) % CHUNK], turned[zz]) for zz in every]

    def beneath(values):
        turned = [turn(v, 1, 0) for v in values]
        return [jnp.where(sub == 0, turned[zz - 1], turned[zz]) for zz in every]

    def row(f, i):
        return [tiles.get(f, i, zz) for zz in every]

    def load_e(i):
        ey, ez = row(1, i), row(2, i)
        out = dict(ey=ey, ez=ez, ey_x=across.turned(ey, -1), ez_x=across.turned(ez, -1))
        if i in h_rows:
            ex = row(0, i)
            out.update(ex=ex, ex_y=[turn(v, -1, 1) for v in ex], ex_z=above(ex))
            if i not in skip_hx:
                out.update(ez_y=[turn(v, -1, 1) for v in ez], ey_z=above(ey))
        return out

    def work_h(i, loaded):
        e, after, h = loaded[i], loaded.get(i + 1), h_of(i)
        ey_x = across.pick(e["ey_x"], after["ey_x"] if after else blank, -1)
        ez_x = across.pick(e["ez_x"], after["ez_x"] if after else blank, -1)
        new = {}
        for zz in h_layers:
            if i not in skip_hx:
                curl = (e["ez_y"][zz] - e["ez"][zz]) - (e["ey_z"][zz] - e["ey"][zz])
                new[3, zz] = tiles.get(3, i, zz) - h[zz] * curl
            curl = (e["ex_z"][zz] - e["ex"][zz]) - (ez_x[zz] - e["ez"][zz])
            new[4, zz] = tiles.get(4, i, zz) - h[zz] * curl
            curl = (ey_x[zz] - e["ey"][zz]) - (e["ex_y"][zz] - e["ex"][zz])
            new[5, zz] = tiles.get(5, i, zz) - h[zz] * curl
        for (f, zz), tile in new.items():
            tiles.put(f, i, zz, tile)

    def load_h(i):
        hy, hz = row(4, i), row(5, i)
        out = dict(hy=hy, hz=hz, hy_x=across.turned(hy, 1), hz_x=across.turned(hz, 1))
        if i in e_rows:
            hx = row(3, i)
            out.update(hx=hx, hx_y=[turn(v, 1, 1) for v in hx], hz_y=[turn(v, 1, 1) for v in hz])
            out.update(hx_z=beneath(hx), hy_z=beneath(hy))
        return out

    def work_e(i, loaded):
        h, before, c = loaded[i], loaded.get(i - 1), c_of(i)
        hy_x = across.pick(h["hy_x"], before["hy_x"] if before else blank, 1)
        hz_x = across.pick(h["hz_x"], before["hz_x"] if before else blank, 1)
        new = {}
        for zz in e_layers:
            curl = (h["hz"][zz] - h["hz_y"][zz]) - (h["hy"][zz] - h["hy_z"][zz])
            new[0, zz] = tiles.get(0, i, zz) + c[zz] * curl
            curl = (h["hx"][zz] - h["hx_z"][zz]) - (h["hz"][zz] - hz_x[zz])
            new[1, zz] = tiles.get(1, i, zz) + c[zz] * curl
            curl = (h["hy"][zz] - hy_x[zz]) - (h["hx"][zz] - h["hx_y"][zz])
            new[2, zz] = tiles.get(2, i, zz) + c[zz] * curl
        for (f, zz), tile in new.items():
            tiles.put(f, i, zz, tile)

    def sweep(rows, load, work):
        loaded = {}

        def want(i):
            if i not in loaded and i in exists:
                loaded[i] = load(i)

        for i in rows:
            for j in (i - 1, i, i + 1):
                if j in rows or j == i + (1 if load is load_e else -1):
                    want(j)
            work(i, loaded)

    sweep(h_rows, load_e, work_h)
    yield
    sweep(e_rows, load_h, work_e)


class Rows:
    def turned(self, values, way):
        return values

    def pick(self, own, other, way):
        return other


class Blocks:
    def __init__(self, groups):
        self.groups = groups

    def turned(self, values, way):
        return [turn(v, way * GROUP, 1) for v in values]

    def pick(self, own, other, way):
        edge = self.groups[3] if way < 0 else self.groups[0]
        return [jnp.where(edge, o, v) for o, v in zip(other, own)]


def spans_inner(n, has_below, has_above):
    last = 7 - n if has_above else 7
    return (n - 1 if has_below else 0, last), (n if has_below else 0, last)


def spans_below(n):
    return (n - 5, n - 2), (n - 4, n - 1)


def spans_above(n):
    return (8 - n, 11 - n), (8 - n, 11 - n)


class Stepper:
    def __init__(self, row_size, main, edge, main_exists, edge_exists, skip_hx):
        gz, row, col = (lax.axis_index(name) for name in ("gz", "row", "col"))
        lane, sub = iota(1), iota(0)
        place, self.group = lane & (GROUP - 1), lane >> 5
        full = jnp.full((8, 128), time_step, jnp.float32)
        self.layer_half = [full] * OWN + [jnp.where((sub >= 4) & (gz == 0), 0.0, full)]
        outside = (place >= 12) & (place < 16) & (col == 0)
        self.edge_half = [jnp.where(outside, 0.0, v) for v in self.layer_half]
        self.lowest = jnp.where(row == 0, 0.0, 1.0) if row_size > 2 else None
        self.main, self.edge, self.skip_hx = main, edge, skip_hx
        self.main_exists, self.edge_exists = main_exists, edge_exists
        self.blocks = Blocks([self.group == r for r in range(4)])

    def masked(self, values, block, span):
        low, high = max(span[0] - 4 * block, 0), min(span[1] - 4 * block, 3)
        if low == 0 and high == 3:
            return values
        mask = (self.group >= low) & (self.group <= high)
        return [jnp.where(mask, v, 0.0) for v in values]

    def main_h(self, i):
        return self.layer_half if self.lowest is None or i >= DEPTH else [v * self.lowest for v in self.layer_half]

    def main_c(self, i):
        return [self.main.get(6, i, zz) for zz in range(CHUNK)]

    def edge_h(self, i, span):
        h = self.edge_half if self.lowest is None or i else [v * self.lowest for v in self.edge_half]
        return self.masked(h, i - 1, span)

    def edge_c(self, i, span):
        return self.masked([self.edge.get(6, i, zz) for zz in range(CHUNK)], i - 1, span)

    def step(self, n, spans):
        def blocks_of(span):
            return [b + 1 for b in range(-1, 3) if span[0] <= 4 * b + 3 and span[1] >= 4 * b]

        layers = range(CHUNK)
        last = range(OWN) if n == STEPS else layers
        parts = []
        for h_span, e_span in spans:
            h_rows = list(range(DEPTH + h_span[0], DEPTH + h_span[1] + 1))
            e_rows = list(range(DEPTH + e_span[0], DEPTH + e_span[1] + 1))
            skip = h_rows[:1] if self.skip_hx and h_span[0] < e_span[0] else []
            parts.append(
                leapfrog(self.main, self.main_exists, h_rows, e_rows, Rows(), self.main_h, self.main_c, layers, last, skip)
            )
            h_of, c_of = functools.partial(self.edge_h, span=h_span), functools.partial(self.edge_c, span=e_span)
            parts.append(
                leapfrog(
                    self.edge, self.edge_exists, blocks_of(h_span), blocks_of(e_span), self.blocks, h_of, c_of, layers, last, []
                )
            )
        for part in parts:
            next(part)
        for part in parts:
            next(part, None)


def port_sums(n, reached, prow_ref, weight_ref, ez_ref, edge_ref, sum_ref, add_ref):
    for k in range(PORT_TILE):
        at = prow_ref[0, 0, k]
        total = jnp.zeros((8, 128), jnp.float32)
        for zz in range(OWN):
            total = total + ez_ref[at, zz] * weight_ref[k, 0, zz]
            total = total + edge_ref[at >> 2, zz] * weight_ref[k, 1, zz]
        total = jnp.sum(jnp.where(reached(n, at), total, 0.0), axis=0, keepdims=True)
        if add_ref is not None:
            total = total + add_ref[n - 1, k : k + 1, :]
        sum_ref[n - 1, k : k + 1, :] = total


def finished(f, b, main, edge):
    lane = iota(1)
    place = lane & (GROUP - 1)
    sides = (lane < DEPTH) | (lane >= 128 - DEPTH)
    out = {}
    for zz in range(OWN):
        tile = edge.get(f, b + 1, zz)
        near = jnp.where(place < 8, tile, turn(tile, -8, 1))
        for r in range(4):
            own = main.get(f, DEPTH + 4 * b + r, zz)
            out[r, zz] = jnp.where(sides, turn(near, -(GROUP * r + 8), 1), own)
    return out


def inner_kernel(
    row_size, state_ref, z_ref, own_ref, even_ref, odd_ref, even_z_ref, odd_z_ref, mode_ref, prow_ref, pcol_ref, pmode_ref, pid_ref,
    e_ref, h_ref, c_ref, edge_e_ref, edge_h_ref, edge_c_ref, done_ref, weight_ref, sum_ref, ext_ref, halo_ref, strip_ref, ez_ref, edge_ez_ref,
):
    gz, row = lax.axis_index("gz"), lax.axis_index("row")
    lane, sub = iota(1), iota(0)
    place = lane & (GROUP - 1)
    groups = [(lane >> 5) == r for r in range(4)]
    valid = (sub < 4) == (gz == 0)
    spread_layers(gz, z_ref, ext_ref)
    low_of, high_of = low_and_high(even_ref, odd_ref)
    low_z, high_z = low_and_high(even_z_ref, odd_z_ref)
    for f in range(FIELDS):
        for x in range(ROWS):
            halo_ref[f, x] = ext_ref[f, pl.ds(x, 8, stride=ROWS), :]

    def first(f, i, zz):
        return halo_ref[f, i - DEPTH] if zz == OWN else state_ref[f, i - DEPTH, zz]

    joined = {}
    for b in range(2):
        for zz in range(CHUNK):
            if zz < OWN:
                low, high = low_of(b, zz), high_of(b, zz)
            else:
                low, high = (halo_layers(valid, gz, side, b) for side in (low_z, high_z))
            for f in range(FIELDS):
                if zz < OWN:
                    own = own_ref[f, b, zz]
                else:
                    own = gather_edges([first(f, DEPTH + 4 * b + r, zz) for r in range(4)], groups)
                joined[f, b + 1, zz] = edge_tile(own, low, high, f, place)
    for k in range(PORT_TILE):
        strip_ref[k] = jnp.zeros(strip_ref.shape[1:], jnp.float32)
        strip_ref[k, :, 0:PLEN] = mode_ref[pmode_ref[0, 0, k]]
    for k in range(PORT_TILE):
        turned = GROUP * (prow_ref[0, 0, k] & 3)
        at = lane - turned
        for zz in range(OWN):
            tile = pltpu.roll(strip_ref[k, 8 * zz : 8 * zz + 8, :], pcol_ref[0, 0, k], 1)
            weight_ref[k, 0, zz] = jnp.where((lane >= DEPTH) & (lane < 128 - DEPTH), tile, 0.0)
            own = pltpu.roll(tile, turned + 8, 1)
            edge = jnp.where((at >= 4) & (at < 8), own, 0.0)
            weight_ref[k, 1, zz] = jnp.where((at >= 16) & (at < 20), turn(own, 8, 1), edge)

    def run(has_below, has_above):
        main = Tiles(first, ez_ref, DEPTH)
        edge = Tiles(lambda f, i, zz: joined[f, i, zz], edge_ez_ref, 1)
        stepper = Stepper(row_size, main, edge, range(4, 12), (1, 2), False)

        def reached(n, at):
            low, high = spans_inner(n, has_below, has_above)[1]
            return (at >= low) & (at <= high)

        for n in range(1, STEPS + 1):
            stepper.step(n, [spans_inner(n, has_below, has_above)])
            port_sums(n, reached, prow_ref, weight_ref, ez_ref, edge_ez_ref, sum_ref, None)
        for tiles, base, count, refs in (
            (main, DEPTH, ROWS, (e_ref, h_ref, c_ref)),
            (edge, 1, 2, (edge_e_ref, edge_h_ref, edge_c_ref)),
        ):
            for i in range(count):
                for zz in range(CHUNK):
                    for f in range(6):
                        refs[f // 3][f % 3, i, zz] = tiles.get(f, base + i, zz)
                    refs[2][i, zz] = tiles.get(6, base + i, zz)
        if has_below != has_above:
            for f in range(6):
                for (r, zz), tile in finished(f, 0 if has_above else 1, main, edge).items():
                    done_ref[f, r, zz] = tile

    if row_size == 2:
        pl.when(row == 0)(functools.partial(run, False, True))
        pl.when(row == 1)(functools.partial(run, True, False))
    else:
        run(True, True)


def outer_kernel(
    row_size, ports_each, prow_ref, pid_ref, e_in, h_in, c_in, edge_e_in, edge_h_in, edge_c_in, done_ref, weight_ref,
    sum_in, *rest,
):
    n_x = 1 if row_size == 2 else 2
    x_refs, corner_refs = rest[:n_x], rest[n_x : 2 * n_x]
    eout_hbm, hout_hbm, term_ref, ez_ref, edge_ez_ref, sum_ref, turned_ref, out_ref, sems = rest[2 * n_x :]
    gz, row = lax.axis_index("gz"), lax.axis_index("row")
    lane, sub = iota(1), iota(0)
    place = lane & (GROUP - 1)
    groups = [(lane >> 5) == r for r in range(4)]
    valid = (sub < 4) == (gz == 0)
    zeros = jnp.zeros((8, 128), jnp.float32)

    def first_main(f, i, zz):
        if f == 6:
            return c_in[i - DEPTH, zz]
        return e_in[f, i - DEPTH, zz] if f < 3 else h_in[f - 3, i - DEPTH, zz]

    def first_edge(f, i, zz):
        if f == 6:
            return edge_c_in[i - 1, zz]
        return edge_e_in[f, i - 1, zz] if f < 3 else edge_h_in[f - 3, i - 1, zz]

    def run(has_below, has_above):
        main = Tiles(first_main, ez_ref, DEPTH)
        edge = Tiles(first_edge, edge_ez_ref, 1)

        def halo_rows(planes, slot, offset, b):
            got = {}
            for i, (f, x) in enumerate(planes):
                packed = corner_refs[slot][i % PAIRS]
                if i >= PAIRS:
                    packed = turn(packed, 4, 0)
                tiles = [x_refs[slot][i, zz] for zz in range(OWN)]
                tiles.append(jnp.where(valid, packed, 0.0))
                for zz in range(CHUNK):
                    main.put(f, DEPTH + x + offset, zz, tiles[zz])
                    got[f, x + offset - 4 * b, zz] = tiles[zz]
            for zz in range(CHUNK):
                low = corner_refs[slot][PAIRS + zz]
                high = corner_refs[slot][PAIRS + CHUNK + zz]
                for f in range(FIELDS):
                    tiles = [got.get((f, r, zz)) for r in range(4)]
                    own = gather_edges(tiles, groups)
                    tile = edge_tile(zeros if own is None else own, low, high, f, place)
                    edge.put(f, 1 + b, zz, tile)

        if has_below:
            halo_rows(UP_PLANES, 0, -ROWS, -1)
        if has_above:
            halo_rows(DOWN_PLANES, n_x - 1, ROWS, 2)

        def reached(n, at):
            out = None
            for wanted, span in ((has_below, spans_below(n)[1]), (has_above, spans_above(n)[1])):
                if wanted:
                    part = (at >= span[0]) & (at <= span[1])
                    out = part if out is None else out | part
            return out

        rows = range(0 if has_below else 4, 16 if has_above else 12)
        blocks = range(0 if has_below else 1, 4 if has_above else 3)
        stepper = Stepper(row_size, main, edge, rows, blocks, True)
        for n in range(1, STEPS + 1):
            spans = ([spans_below(n)] if has_below else []) + ([spans_above(n)] if has_above else [])
            stepper.step(n, spans)
            port_sums(n, reached, prow_ref, weight_ref, ez_ref, edge_ez_ref, sum_ref, sum_in)
        for f in range(6):
            for b in range(2):
                if has_below and has_above or b == (1 if has_above else 0):
                    tiles = finished(f, b, main, edge)
                else:
                    tiles = {(r, zz): done_ref[f, r, zz] for r in range(4) for zz in range(OWN)}
                for (r, zz), tile in tiles.items():
                    turned_ref[f, 4 * b + r, 8 * zz : 8 * zz + 8, :] = tile

    if row_size == 2:
        pl.when(row == 0)(functools.partial(run, False, True))
        pl.when(row == 1)(functools.partial(run, True, False))
    else:
        run(True, True)

    copies = []
    flat = turned_ref.reshape(6 * ROWS * LAYERS, 128)
    for part, dest in ((0, eout_hbm), (1, hout_hbm)):
        for f in range(3 * part, 3 * part + 3):
            for z in range(LAYERS):
                out_ref[f, z] = flat[pl.ds(f * ROWS * LAYERS + z, ROWS, stride=LAYERS), :]
        copies.append(pltpu.make_async_copy(out_ref.at[pl.ds(3 * part, 3)], dest, sems.at[part]))
        copies[-1].start()
    basis = zeros
    for n in range(STEPS):
        for f in range(2 * FREQ):
            basis = jnp.where((sub == n) & (lane == f), float(BASIS[n, f]), basis)
    transform = zeros
    for n in range(STEPS):
        sampled = jnp.sum(sum_ref[n], axis=1, keepdims=True)
        transform = transform + sampled * basis[n : n + 1, :]
    term_ref[...] = jnp.zeros(term_ref.shape, jnp.float32)
    for k in range(PORT_TILE):
        port = pid_ref[0, 0, k]
        term_ref[port // ports_each, pl.ds(port % ports_each, 1), :] = transform[k : k + 1, : 2 * FREQ]
    for copy in copies:
        copy.wait()


def shifted(block, axis, size, distance):
    route = [(i - distance, i) for i in range(size) if 0 <= i - distance < size]
    return lax.ppermute(block, axis, route)


def swapped(block, axis, size, start=0):
    pairs = [(i, i + 1) for i in range(start, size - 1, 2)]
    return lax.ppermute(block, axis, pairs + [(j, i) for i, j in pairs])


def solution(mesh):
    sizes = dict(mesh.shape)
    row_size, col_size, gz_size = sizes["row"], sizes["col"], sizes["gz"]
    n_x = 1 if row_size == 2 else 2

    def across_rows(blocks):
        if row_size == 2:
            return (swapped(blocks[0], "row", 2),)
        return (shifted(blocks[0], "row", row_size, 1), shifted(blocks[1], "row", row_size, -1))

    def per_device(
        electric, magnetic, material, eps_table, mode_table, port_row, port_col, port_mode, port_ids
    ):
        f32 = jnp.float32

        def array(*shape):
            return jax.ShapeDtypeStruct(shape, f32)

        def scratch(*shape):
            return pltpu.VMEM(shape, f32)

        state, z_send, own, even_send, odd_send, *x_send = pl.pallas_call(
            functools.partial(pack_kernel, row_size),
            out_shape=[
                array(FIELDS, ROWS, OWN, 8, 128),
                array(FIELDS, DEPTH, ROWS, 128),
                array(FIELDS, 2, OWN, 8, 128),
                array(2, OWN, 8, 128),
                array(2, OWN, 8, 128),
            ]
            + [array(PLANES, OWN, 8, 128)] * n_x,
            in_specs=[HBM] * 4,
            out_specs=[VMEM] * (5 + n_x),
            scratch_shapes=[
                scratch(FIELDS, LAYERS, ROWS, 128),
                pltpu.SMEM(eps_table.shape, f32),
                pltpu.VMEM(material.shape, jnp.int32),
                pltpu.SemaphoreType.DMA((4,)),
            ],
            name="pack",
        )(eps_table, electric, magnetic, material)
        x_halo = across_rows(x_send)
        even = swapped(even_send, "col", col_size)
        odd = swapped(odd_send, "col", col_size, 1)
        z_halo = swapped(z_send, "gz", gz_size)
        even_z = swapped(even, "gz", gz_size)
        odd_z = swapped(odd, "gz", gz_size)
        corner_send = pl.pallas_call(
            functools.partial(corner_kernel, row_size),
            out_shape=[array(PAIRS + 2 * CHUNK, 8, 128)] * n_x,
            in_specs=[VMEM] * 5,
            out_specs=[VMEM] * n_x,
            scratch_shapes=[scratch(FIELDS, 8 * ROWS, 128)],
            compiler_params=PARAMS,
            name="corners",
        )(z_halo, even, odd, even_z, odd_z)
        corner = across_rows(corner_send)
        inner = pl.pallas_call(
            functools.partial(inner_kernel, row_size),
            out_shape=[
                array(3, ROWS, CHUNK, 8, 128),
                array(3, ROWS, CHUNK, 8, 128),
                array(ROWS, CHUNK, 8, 128),
                array(3, 2, CHUNK, 8, 128),
                array(3, 2, CHUNK, 8, 128),
                array(2, CHUNK, 8, 128),
                array(6, 4, OWN, 8, 128),
                array(PORT_TILE, 2, OWN, 8, 128),
                array(STEPS, 8, 128),
            ],
            in_specs=[VMEM] * 8 + [SMEM] * 4,
            out_specs=[VMEM] * 9,
            scratch_shapes=[
                scratch(FIELDS, 8 * ROWS, 128),
                scratch(FIELDS, ROWS, 8, 128),
                scratch(PORT_TILE, LAYERS, 128),
                scratch(ROWS, OWN, 8, 128),
                scratch(2, OWN, 8, 128),
            ],
            compiler_params=PARAMS,
            name="inner",
        )(state, z_halo, own, even, odd, even_z, odd_z, mode_table, port_row, port_col, port_mode, port_ids)
        devices = col_size * row_size * gz_size
        ports_each = PORT_TILE * col_size * row_size // devices
        electric_out, magnetic_out, term = pl.pallas_call(
            functools.partial(outer_kernel, row_size, ports_each),
            out_shape=[array(3, LAYERS, ROWS, 128)] * 2 + [array(devices, ports_each, 2 * FREQ)],
            in_specs=[SMEM] * 2 + [VMEM] * (9 + 2 * n_x),
            out_specs=[HBM, HBM, VMEM],
            scratch_shapes=[
                scratch(ROWS, OWN, 8, 128),
                scratch(2, OWN, 8, 128),
                scratch(STEPS, 8, 128),
                scratch(6, ROWS, LAYERS, 128),
                scratch(6, LAYERS, ROWS, 128),
                pltpu.SemaphoreType.DMA((2,)),
            ],
            compiler_params=PARAMS,
            name="outer",
        )(port_row, port_ids, *inner, *x_halo, *corner)
        terms = lax.all_to_all(term, ("col", "row", "gz"), 0, 0, tiled=True)
        return (
            electric_out,
            magnetic_out,
            jnp.sum(terms, axis=0),
        )

    in_specs = (
        P(None, "gz", "row", ("grp", "col")),
        P(None, "gz", "row", ("grp", "col")),
        P("gz", "row", ("grp", "col")),
        P(),
        P(None, "gz", None),
        P(("grp", "row"), "col", None),
        P(("grp", "row"), "col", None),
        P(("grp", "row"), "col", None),
        P(("grp", "row"), "col", None),
    )
    out_specs = (
        P(None, "gz", "row", ("grp", "col")),
        P(None, "gz", "row", ("grp", "col")),
        P(("grp", "col", "row", "gz"), None),
    )
    return jax.shard_map(
        per_device, mesh=mesh, in_specs=in_specs, out_specs=out_specs, check_vma=False
    )
```

```python
import functools

import jax
import jax.numpy as jnp
import numpy as np
from jax import lax
from jax.experimental import pallas as pl
from jax.experimental.pallas import tpu as pltpu
from jax.sharding import PartitionSpec as P

STEPS = 4
FREQ = 8
MATS = 8
PLEN = 64
PORT_TILE = 4
FIELDS = 7
DEPTH = STEPS
ROWS = 8
LAYERS = 32
OWN = 4
CHUNK = 5
GROUP = 32

time_step = 0.5

UP_PLANES = [(f, 4) for f in (0, 1, 2, 4, 5)] + [(f, x) for x in (5, 6, 7) for f in range(FIELDS)]
DOWN_PLANES = [(f, x) for x in (0, 1, 2) for f in range(FIELDS)] + [(1, 3), (2, 3)]
PLANES = max(len(UP_PLANES), len(DOWN_PLANES))
PAIRS = (PLANES + 1) // 2

VMEM = pl.BlockSpec(memory_space=pltpu.VMEM)
SMEM = pl.BlockSpec(memory_space=pltpu.SMEM)
HBM = pl.BlockSpec(memory_space=pltpu.HBM)
PARAMS = pltpu.CompilerParams(vmem_limit_bytes=16 * 1024 * 1024)


def dft_basis():
    times = (np.arange(STEPS) + 1.0) * time_step
    omegas = np.pi * (np.arange(FREQ) + 1.0) / FREQ
    angle = times[:, None] * omegas[None, :]
    return np.concatenate([np.cos(angle), -np.sin(angle)], axis=1)


BASIS = dft_basis()


def iota(axis):
    return lax.broadcasted_iota(jnp.int32, (8, 128), axis)


def turn(tile, shift, axis):
    return pltpu.roll(tile, shift % tile.shape[axis], axis)


def directions(row_size, body):
    if row_size == 2:
        row = lax.axis_index("row")
        pl.when(row == 0)(functools.partial(body, True, 0))
        pl.when(row == 1)(functools.partial(body, False, 0))
    else:
        body(True, 0)
        body(False, 1)


def pack_kernel(row_size, eps_hbm, elec_hbm, magn_hbm, mat_hbm, state_ref, z_ref, own_ref, even_ref, odd_ref, *rest):
    x_refs, (main_ref, eps_ref, mat_ref, sems) = rest[:-4], rest[-4:]
    copies = [pltpu.make_async_copy(eps_hbm, eps_ref, sems.at[0]), pltpu.make_async_copy(mat_hbm, mat_ref, sems.at[1])]
    copies.append(pltpu.make_async_copy(elec_hbm, main_ref.at[pl.ds(0, 3)], sems.at[2]))
    copies.append(pltpu.make_async_copy(magn_hbm, main_ref.at[pl.ds(3, 3)], sems.at[3]))
    for copy in copies:
        copy.start()
    copies[0].wait()
    copies[1].wait()
    for z in range(LAYERS):
        material = mat_ref[z]
        eps = jnp.full((8, 128), eps_ref[0], jnp.float32)
        for which in range(1, MATS):
            eps = jnp.where(material == which, eps_ref[which], eps)
        main_ref[6, z] = time_step * (1.0 / eps)
    copies[2].wait()
    copies[3].wait()
    start = jnp.where(lax.axis_index("gz") == 0, LAYERS - DEPTH, 0)
    for f in range(FIELDS):
        z_ref[f] = main_ref[f, pl.ds(start, DEPTH)]
    block = LAYERS * ROWS
    flat = main_ref.reshape(FIELDS * block, 128)
    for f in range(FIELDS):
        for x in range(ROWS):
            state_ref[f, x] = flat[pl.ds(f * block + x, LAYERS, stride=ROWS), :].reshape(OWN, 8, 128)

    def send(up, slot):
        for i, (f, x) in enumerate(UP_PLANES if up else DOWN_PLANES):
            x_refs[slot][i] = state_ref[f, x]

    directions(row_size, send)
    pack_edges(state_ref, own_ref, even_ref, odd_ref)


def lane_groups():
    group = iota(1) >> 5
    return [jnp.where(group == r, 1.0, 0.0) for r in range(4)]


def gather_edges(tiles, groups):
    own = None
    for r, tile in enumerate(tiles):
        if tile is not None:
            moved = turn(tile, GROUP * r + 8, 1) * groups[r]
            own = moved if own is None else own + moved
    return own


def pack_edges(state_ref, own_ref, even_ref, odd_ref):
    lane = iota(1)
    groups = lane_groups()
    slots = [jnp.where(((lane & (GROUP - 1)) >> 2) == f, 1.0, 0.0) for f in range(FIELDS)]
    even = (lax.axis_index("col") & 1) == 0
    for b in range(2):
        for zz in range(OWN):
            up = down = jnp.zeros((8, 128), jnp.float32)
            owns = []
            for f in range(FIELDS):
                own = gather_edges([state_ref[f, 4 * b + r, zz] for r in range(4)], groups)
                up = up + turn(own, DEPTH * f - 4, 1) * slots[f]
                down = down + turn(own, DEPTH * f - 8, 1) * slots[f]
                owns.append(own)
            for f in range(FIELDS):
                own_ref[f, b, zz] = owns[f]
            even_ref[b, zz] = jnp.where(even, up, down)
            odd_ref[b, zz] = jnp.where(even, down, up)


def low_and_high(even_ref, odd_ref):
    even = (lax.axis_index("col") & 1) == 0

    def low(*at):
        return jnp.where(even, odd_ref[at], even_ref[at])

    def high(*at):
        return jnp.where(even, even_ref[at], odd_ref[at])

    return low, high


def halo_layers(valid, gz, side, b):
    return jnp.where(valid, jnp.where(gz == 0, side(b, 0), side(b, OWN - 1)), 0.0)


def spread_layers(gz, z_ref, ext_ref):
    for f in range(FIELDS):
        halo = z_ref[f].reshape(DEPTH * ROWS, 128)
        nothing = jnp.zeros_like(halo)
        ext_ref[f, : DEPTH * ROWS] = jnp.where(gz == 0, halo, nothing)
        ext_ref[f, DEPTH * ROWS :] = jnp.where(gz == 0, nothing, halo)


def corner_kernel(row_size, prep_ref, z_ref, even_ref, odd_ref, even_z_ref, odd_z_ref, *rest):
    x_refs, ext_ref = rest[:-1], rest[-1]
    gz = lax.axis_index("gz")
    valid = (iota(0) < 4) == (gz == 0)
    spread_layers(gz, z_ref, ext_ref)
    low, high = low_and_high(even_ref, odd_ref)
    low_z, high_z = low_and_high(even_z_ref, odd_z_ref)

    def send(up, slot):
        planes = UP_PLANES if up else DOWN_PLANES

        def tile(i):
            f, x = planes[i]
            return ext_ref[f, pl.ds(x, 8, stride=ROWS), :]

        for i in range(PAIRS):
            pair = tile(i)
            if i + PAIRS < len(planes):
                pair = pair + turn(tile(i + PAIRS), 4, 0)
            x_refs[slot][i] = pair
        b = 1 if up else 0
        for zz in range(OWN):
            x_refs[slot][PAIRS + zz] = low(b, zz)
            x_refs[slot][PAIRS + CHUNK + zz] = high(b, zz)
        x_refs[slot][PAIRS + OWN] = halo_layers(valid, gz, low_z, b)
        x_refs[slot][PAIRS + CHUNK + OWN] = halo_layers(valid, gz, high_z, b)

    directions(row_size, send)


def edge_tile(own, low, high, f, place):
    out = jnp.where(place < 16, turn(low, 12 - DEPTH * f, 1), turn(own, 8, 1))
    out = jnp.where(place < 12, turn(high, 8 - DEPTH * f, 1), out)
    return jnp.where(place < 8, own, out)


class Tiles:
    def __init__(self, first, ez_ref, shift):
        self.first, self.ez_ref, self.shift = first, ez_ref, shift
        self.values = {}

    def get(self, f, i, zz):
        value = self.values.get((f, i, zz))
        return self.first(f, i, zz) if value is None else value

    def put(self, f, i, zz, tile):
        self.values[f, i, zz] = tile
        at = i - self.shift
        if f == 2 and zz < OWN and 0 <= at < self.ez_ref.shape[0]:
            self.ez_ref[at, zz] = tile


def leapfrog(tiles, exists, h_rows, e_rows, across, h_of, c_of, h_layers, e_layers, skip_hx):
    sub = iota(0)
    every = range(CHUNK)
    blank = [jnp.zeros((8, 128), jnp.float32)] * CHUNK

    def above(values):
        turned = [turn(v, -1, 0) for v in values]
        return [jnp.where(sub == 7, turned[(zz + 1) % CHUNK], turned[zz]) for zz in every]

    def beneath(values):
        turned = [turn(v, 1, 0) for v in values]
        return [jnp.where(sub == 0, turned[zz - 1], turned[zz]) for zz in every]

    def row(f, i):
        return [tiles.get(f, i, zz) for zz in every]

    def load_e(i):
        ey, ez = row(1, i), row(2, i)
        out = dict(ey=ey, ez=ez, ey_x=across.turned(ey, -1), ez_x=across.turned(ez, -1))
        if i in h_rows:
            ex = row(0, i)
            out.update(ex=ex, ex_y=[turn(v, -1, 1) for v in ex], ex_z=above(ex))
            if i not in skip_hx:
                out.update(ez_y=[turn(v, -1, 1) for v in ez], ey_z=above(ey))
        return out

    def work_h(i, loaded):
        e, after, h = loaded[i], loaded.get(i + 1), h_of(i)
        ey_x = across.pick(e["ey_x"], after["ey_x"] if after else blank, -1)
        ez_x = across.pick(e["ez_x"], after["ez_x"] if after else blank, -1)
        new = {}
        for zz in h_layers:
            if i not in skip_hx:
                curl = (e["ez_y"][zz] - e["ez"][zz]) - (e["ey_z"][zz] - e["ey"][zz])
                new[3, zz] = tiles.get(3, i, zz) - h[zz] * curl
            curl = (e["ex_z"][zz] - e["ex"][zz]) - (ez_x[zz] - e["ez"][zz])
            new[4, zz] = tiles.get(4, i, zz) - h[zz] * curl
            curl = (ey_x[zz] - e["ey"][zz]) - (e["ex_y"][zz] - e["ex"][zz])
            new[5, zz] = tiles.get(5, i, zz) - h[zz] * curl
        for (f, zz), tile in new.items():
            tiles.put(f, i, zz, tile)

    def load_h(i):
        hy, hz = row(4, i), row(5, i)
        out = dict(hy=hy, hz=hz, hy_x=across.turned(hy, 1), hz_x=across.turned(hz, 1))
        if i in e_rows:
            hx = row(3, i)
            out.update(hx=hx, hx_y=[turn(v, 1, 1) for v in hx], hz_y=[turn(v, 1, 1) for v in hz])
            out.update(hx_z=beneath(hx), hy_z=beneath(hy))
        return out

    def work_e(i, loaded):
        h, before, c = loaded[i], loaded.get(i - 1), c_of(i)
        hy_x = across.pick(h["hy_x"], before["hy_x"] if before else blank, 1)
        hz_x = across.pick(h["hz_x"], before["hz_x"] if before else blank, 1)
        new = {}
        for zz in e_layers:
            curl = (h["hz"][zz] - h["hz_y"][zz]) - (h["hy"][zz] - h["hy_z"][zz])
            new[0, zz] = tiles.get(0, i, zz) + c[zz] * curl
            curl = (h["hx"][zz] - h["hx_z"][zz]) - (h["hz"][zz] - hz_x[zz])
            new[1, zz] = tiles.get(1, i, zz) + c[zz] * curl
            curl = (h["hy"][zz] - hy_x[zz]) - (h["hx"][zz] - h["hx_y"][zz])
            new[2, zz] = tiles.get(2, i, zz) + c[zz] * curl
        for (f, zz), tile in new.items():
            tiles.put(f, i, zz, tile)

    def sweep(rows, load, work):
        loaded = {}

        def want(i):
            if i not in loaded and i in exists:
                loaded[i] = load(i)

        for i in rows:
            for j in (i - 1, i, i + 1):
                if j in rows or j == i + (1 if load is load_e else -1):
                    want(j)
            work(i, loaded)

    sweep(h_rows, load_e, work_h)
    yield
    sweep(e_rows, load_h, work_e)


class Rows:
    def turned(self, values, way):
        return values

    def pick(self, own, other, way):
        return other


class Blocks:
    def __init__(self, groups):
        self.groups = groups

    def turned(self, values, way):
        return [turn(v, way * GROUP, 1) for v in values]

    def pick(self, own, other, way):
        edge = self.groups[3] if way < 0 else self.groups[0]
        return [jnp.where(edge, o, v) for o, v in zip(other, own)]


def spans_inner(n, has_below, has_above):
    last = 7 - n if has_above else 7
    return (n - 1 if has_below else 0, last), (n if has_below else 0, last)


def spans_below(n):
    return (n - 5, n - 2), (n - 4, n - 1)


def spans_above(n):
    return (8 - n, 11 - n), (8 - n, 11 - n)


class Stepper:
    def __init__(self, row_size, main, edge, main_exists, edge_exists, skip_hx):
        gz, row, col = (lax.axis_index(name) for name in ("gz", "row", "col"))
        lane, sub = iota(1), iota(0)
        place, self.group = lane & (GROUP - 1), lane >> 5
        full = jnp.full((8, 128), time_step, jnp.float32)
        self.layer_half = [full] * OWN + [jnp.where((sub >= 4) & (gz == 0), 0.0, full)]
        outside = (place >= 12) & (place < 16) & (col == 0)
        self.edge_half = [jnp.where(outside, 0.0, v) for v in self.layer_half]
        self.lowest = jnp.where(row == 0, 0.0, 1.0) if row_size > 2 else None
        self.main, self.edge, self.skip_hx = main, edge, skip_hx
        self.main_exists, self.edge_exists = main_exists, edge_exists
        self.blocks = Blocks([self.group == r for r in range(4)])

    def masked(self, values, block, span):
        low, high = max(span[0] - 4 * block, 0), min(span[1] - 4 * block, 3)
        if low == 0 and high == 3:
            return values
        mask = (self.group >= low) & (self.group <= high)
        return [jnp.where(mask, v, 0.0) for v in values]

    def main_h(self, i):
        return self.layer_half if self.lowest is None or i >= DEPTH else [v * self.lowest for v in self.layer_half]

    def main_c(self, i):
        return [self.main.get(6, i, zz) for zz in range(CHUNK)]

    def edge_h(self, i, span):
        h = self.edge_half if self.lowest is None or i else [v * self.lowest for v in self.edge_half]
        return self.masked(h, i - 1, span)

    def edge_c(self, i, span):
        return self.masked([self.edge.get(6, i, zz) for zz in range(CHUNK)], i - 1, span)

    def step(self, n, spans):
        def blocks_of(span):
            return [b + 1 for b in range(-1, 3) if span[0] <= 4 * b + 3 and span[1] >= 4 * b]

        layers = range(CHUNK)
        last = range(OWN) if n == STEPS else layers
        parts = []
        for h_span, e_span in spans:
            h_rows = list(range(DEPTH + h_span[0], DEPTH + h_span[1] + 1))
            e_rows = list(range(DEPTH + e_span[0], DEPTH + e_span[1] + 1))
            skip = h_rows[:1] if self.skip_hx and h_span[0] < e_span[0] else []
            parts.append(
                leapfrog(self.main, self.main_exists, h_rows, e_rows, Rows(), self.main_h, self.main_c, layers, last, skip)
            )
            h_of, c_of = functools.partial(self.edge_h, span=h_span), functools.partial(self.edge_c, span=e_span)
            parts.append(
                leapfrog(
                    self.edge, self.edge_exists, blocks_of(h_span), blocks_of(e_span), self.blocks, h_of, c_of, layers, last, []
                )
            )
        for part in parts:
            next(part)
        for part in parts:
            next(part, None)


def port_sums(n, reached, prow_ref, weight_ref, ez_ref, edge_ref, sum_ref, add_ref):
    for k in range(PORT_TILE):
        at = prow_ref[0, 0, k]
        total = jnp.zeros((8, 128), jnp.float32)
        for zz in range(OWN):
            total = total + ez_ref[at, zz] * weight_ref[k, 0, zz]
            total = total + edge_ref[at >> 2, zz] * weight_ref[k, 1, zz]
        total = jnp.sum(jnp.where(reached(n, at), total, 0.0), axis=0, keepdims=True)
        if add_ref is not None:
            total = total + add_ref[n - 1, k : k + 1, :]
        sum_ref[n - 1, k : k + 1, :] = total


def finished(f, b, main, edge):
    lane = iota(1)
    place = lane & (GROUP - 1)
    sides = (lane < DEPTH) | (lane >= 128 - DEPTH)
    out = {}
    for zz in range(OWN):
        tile = edge.get(f, b + 1, zz)
        near = jnp.where(place < 8, tile, turn(tile, -8, 1))
        for r in range(4):
            own = main.get(f, DEPTH + 4 * b + r, zz)
            out[r, zz] = jnp.where(sides, turn(near, -(GROUP * r + 8), 1), own)
    return out


def prep_kernel(state_hbm, even_ref, mode_ref, prow_ref, pcol_ref, pmode_ref, pid_ref, state_ref, weight_ref, strip_ref, sem):
    copy = pltpu.make_async_copy(state_hbm, state_ref, sem)
    copy.start()
    lane = iota(1)
    for k in range(PORT_TILE):
        strip_ref[k] = jnp.zeros(strip_ref.shape[1:], jnp.float32)
        strip_ref[k, :, 0:PLEN] = mode_ref[pmode_ref[0, 0, k]]
    for k in range(PORT_TILE):
        turned = GROUP * (prow_ref[0, 0, k] & 3)
        at = lane - turned
        for zz in range(OWN):
            tile = pltpu.roll(strip_ref[k, 8 * zz : 8 * zz + 8, :], pcol_ref[0, 0, k], 1)
            weight_ref[k, 0, zz] = jnp.where((lane >= DEPTH) & (lane < 128 - DEPTH), tile, 0.0)
            own = pltpu.roll(tile, turned + 8, 1)
            edge = jnp.where((at >= 4) & (at < 8), own, 0.0)
            weight_ref[k, 1, zz] = jnp.where((at >= 16) & (at < 20), turn(own, 8, 1), edge)

    copy.wait()


def inner_kernel(
    row_size, state_ref, z_ref, own_ref, even_ref, odd_ref, even_z_ref, odd_z_ref, weight_ref, prow_ref,
    e_ref, h_ref, c_ref, edge_e_ref, edge_h_ref, edge_c_ref, done_ref, sum_ref, ext_ref, halo_ref, ez_ref, edge_ez_ref,
):
    gz, row = lax.axis_index("gz"), lax.axis_index("row")
    lane, sub = iota(1), iota(0)
    place = lane & (GROUP - 1)
    groups = lane_groups()
    valid = (sub < 4) == (gz == 0)
    spread_layers(gz, z_ref, ext_ref)
    low_of, high_of = low_and_high(even_ref, odd_ref)
    low_z, high_z = low_and_high(even_z_ref, odd_z_ref)
    for f in range(FIELDS):
        for x in range(ROWS):
            halo_ref[f, x] = ext_ref[f, pl.ds(x, 8, stride=ROWS), :]

    def first(f, i, zz):
        return halo_ref[f, i - DEPTH] if zz == OWN else state_ref[f, i - DEPTH, zz]

    joined = {}
    for b in range(2):
        for zz in range(CHUNK):
            if zz < OWN:
                low, high = low_of(b, zz), high_of(b, zz)
            else:
                low, high = (halo_layers(valid, gz, side, b) for side in (low_z, high_z))
            for f in range(FIELDS):
                if zz < OWN:
                    own = own_ref[f, b, zz]
                else:
                    own = gather_edges([first(f, DEPTH + 4 * b + r, zz) for r in range(4)], groups)
                joined[f, b + 1, zz] = edge_tile(own, low, high, f, place)
    def run(has_below, has_above):
        main = Tiles(first, ez_ref, DEPTH)
        edge = Tiles(lambda f, i, zz: joined[f, i, zz], edge_ez_ref, 1)
        stepper = Stepper(row_size, main, edge, range(4, 12), (1, 2), False)

        def reached(n, at):
            low, high = spans_inner(n, has_below, has_above)[1]
            return (at >= low) & (at <= high)

        for n in range(1, STEPS + 1):
            stepper.step(n, [spans_inner(n, has_below, has_above)])
            port_sums(n, reached, prow_ref, weight_ref, ez_ref, edge_ez_ref, sum_ref, None)
        for tiles, base, count, refs in (
            (main, DEPTH, ROWS, (e_ref, h_ref, c_ref)),
            (edge, 1, 2, (edge_e_ref, edge_h_ref, edge_c_ref)),
        ):
            for i in range(count):
                for zz in range(CHUNK):
                    for f in range(6):
                        refs[f // 3][f % 3, i, zz] = tiles.get(f, base + i, zz)
                    refs[2][i, zz] = tiles.get(6, base + i, zz)
        if has_below != has_above:
            for f in range(6):
                for (r, zz), tile in finished(f, 0 if has_above else 1, main, edge).items():
                    done_ref[f, r, zz] = tile

    if row_size == 2:
        pl.when(row == 0)(functools.partial(run, False, True))
        pl.when(row == 1)(functools.partial(run, True, False))
    else:
        run(True, True)


def outer_kernel(
    row_size, ports_each, prow_ref, pid_ref, e_in, h_in, c_in, edge_e_in, edge_h_in, edge_c_in, done_ref, sum_in, weight_ref,
    *rest,
):
    n_x = 1 if row_size == 2 else 2
    x_refs, corner_refs = rest[:n_x], rest[n_x : 2 * n_x]
    eout_hbm, hout_hbm, term_ref, ez_ref, edge_ez_ref, sum_ref, turned_ref, out_ref, sems = rest[2 * n_x :]
    gz, row = lax.axis_index("gz"), lax.axis_index("row")
    lane, sub = iota(1), iota(0)
    place = lane & (GROUP - 1)
    groups = lane_groups()
    valid = (sub < 4) == (gz == 0)
    zeros = jnp.zeros((8, 128), jnp.float32)

    def first_main(f, i, zz):
        if f == 6:
            return c_in[i - DEPTH, zz]
        return e_in[f, i - DEPTH, zz] if f < 3 else h_in[f - 3, i - DEPTH, zz]

    def first_edge(f, i, zz):
        if f == 6:
            return edge_c_in[i - 1, zz]
        return edge_e_in[f, i - 1, zz] if f < 3 else edge_h_in[f - 3, i - 1, zz]

    def run(has_below, has_above):
        main = Tiles(first_main, ez_ref, DEPTH)
        edge = Tiles(first_edge, edge_ez_ref, 1)

        def halo_rows(planes, slot, offset, b):
            got = {}
            for i, (f, x) in enumerate(planes):
                packed = corner_refs[slot][i % PAIRS]
                if i >= PAIRS:
                    packed = turn(packed, 4, 0)
                tiles = [x_refs[slot][i, zz] for zz in range(OWN)]
                tiles.append(jnp.where(valid, packed, 0.0))
                for zz in range(CHUNK):
                    main.put(f, DEPTH + x + offset, zz, tiles[zz])
                    got[f, x + offset - 4 * b, zz] = tiles[zz]
            for zz in range(CHUNK):
                low = corner_refs[slot][PAIRS + zz]
                high = corner_refs[slot][PAIRS + CHUNK + zz]
                for f in range(FIELDS):
                    tiles = [got.get((f, r, zz)) for r in range(4)]
                    own = gather_edges(tiles, groups)
                    tile = edge_tile(zeros if own is None else own, low, high, f, place)
                    edge.put(f, 1 + b, zz, tile)

        if has_below:
            halo_rows(UP_PLANES, 0, -ROWS, -1)
        if has_above:
            halo_rows(DOWN_PLANES, n_x - 1, ROWS, 2)

        def reached(n, at):
            out = None
            for wanted, span in ((has_below, spans_below(n)[1]), (has_above, spans_above(n)[1])):
                if wanted:
                    part = (at >= span[0]) & (at <= span[1])
                    out = part if out is None else out | part
            return out

        rows = range(0 if has_below else 4, 16 if has_above else 12)
        blocks = range(0 if has_below else 1, 4 if has_above else 3)
        stepper = Stepper(row_size, main, edge, rows, blocks, True)
        for n in range(1, STEPS + 1):
            spans = ([spans_below(n)] if has_below else []) + ([spans_above(n)] if has_above else [])
            stepper.step(n, spans)
            port_sums(n, reached, prow_ref, weight_ref, ez_ref, edge_ez_ref, sum_ref, sum_in)
        for f in range(6):
            for b in range(2):
                if has_below and has_above or b == (1 if has_above else 0):
                    tiles = finished(f, b, main, edge)
                else:
                    tiles = {(r, zz): done_ref[f, r, zz] for r in range(4) for zz in range(OWN)}
                for (r, zz), tile in tiles.items():
                    turned_ref[f, 4 * b + r, 8 * zz : 8 * zz + 8, :] = tile

    if row_size == 2:
        pl.when(row == 0)(functools.partial(run, False, True))
        pl.when(row == 1)(functools.partial(run, True, False))
    else:
        run(True, True)

    copies = []
    flat = turned_ref.reshape(6 * ROWS * LAYERS, 128)
    for part, dest in ((0, eout_hbm), (1, hout_hbm)):
        for f in range(3 * part, 3 * part + 3):
            for z in range(LAYERS):
                out_ref[f, z] = flat[pl.ds(f * ROWS * LAYERS + z, ROWS, stride=LAYERS), :]
        copies.append(pltpu.make_async_copy(out_ref.at[pl.ds(3 * part, 3)], dest, sems.at[part]))
        copies[-1].start()
    basis = zeros
    for n in range(STEPS):
        for f in range(2 * FREQ):
            basis = jnp.where((sub == n) & (lane == f), float(BASIS[n, f]), basis)
    transform = zeros
    for n in range(STEPS):
        sampled = jnp.sum(sum_ref[n], axis=1, keepdims=True)
        transform = transform + sampled * basis[n : n + 1, :]
    term_ref[...] = jnp.zeros(term_ref.shape, jnp.float32)
    for k in range(PORT_TILE):
        port = pid_ref[0, 0, k]
        term_ref[port // ports_each, pl.ds(port % ports_each, 1), :] = transform[k : k + 1, : 2 * FREQ]
    for copy in copies:
        copy.wait()


def shifted(block, axis, size, distance):
    route = [(i - distance, i) for i in range(size) if 0 <= i - distance < size]
    return lax.ppermute(block, axis, route)


def swapped(block, axis, size, start=0):
    pairs = [(i, i + 1) for i in range(start, size - 1, 2)]
    return lax.ppermute(block, axis, pairs + [(j, i) for i, j in pairs])


def solution(mesh):
    sizes = dict(mesh.shape)
    row_size, col_size, gz_size = sizes["row"], sizes["col"], sizes["gz"]
    n_x = 1 if row_size == 2 else 2

    def across_rows(blocks):
        if row_size == 2:
            return (swapped(blocks[0], "row", 2),)
        return (shifted(blocks[0], "row", row_size, 1), shifted(blocks[1], "row", row_size, -1))

    def per_device(
        electric, magnetic, material, eps_table, mode_table, port_row, port_col, port_mode, port_ids
    ):
        f32 = jnp.float32

        def array(*shape):
            return jax.ShapeDtypeStruct(shape, f32)

        def scratch(*shape):
            return pltpu.VMEM(shape, f32)

        state, z_send, own, even_send, odd_send, *x_send = pl.pallas_call(
            functools.partial(pack_kernel, row_size),
            out_shape=[
                array(FIELDS, ROWS, OWN, 8, 128),
                array(FIELDS, DEPTH, ROWS, 128),
                array(FIELDS, 2, OWN, 8, 128),
                array(2, OWN, 8, 128),
                array(2, OWN, 8, 128),
            ]
            + [array(PLANES, OWN, 8, 128)] * n_x,
            in_specs=[HBM] * 4,
            out_specs=[VMEM] * (5 + n_x),
            scratch_shapes=[
                scratch(FIELDS, LAYERS, ROWS, 128),
                pltpu.SMEM(eps_table.shape, f32),
                pltpu.VMEM(material.shape, jnp.int32),
                pltpu.SemaphoreType.DMA((4,)),
            ],
            name="pack",
        )(eps_table, electric, magnetic, material)
        x_halo = across_rows(x_send)
        even = swapped(even_send, "col", col_size)
        odd = swapped(odd_send, "col", col_size, 1)
        z_halo = swapped(z_send, "gz", gz_size)
        even_z = swapped(even, "gz", gz_size)
        odd_z = swapped(odd, "gz", gz_size)
        state, weights = pl.pallas_call(
            prep_kernel,
            out_shape=[array(FIELDS, ROWS, OWN, 8, 128), array(PORT_TILE, 2, OWN, 8, 128)],
            in_specs=[HBM, pl.BlockSpec(memory_space=pl.ANY), VMEM] + [SMEM] * 4,
            out_specs=[VMEM] * 2,
            scratch_shapes=[scratch(PORT_TILE, LAYERS, 128), pltpu.SemaphoreType.DMA],
            compiler_params=PARAMS,
            name="prep",
        )(state, even, mode_table, port_row, port_col, port_mode, port_ids)
        corner_send = pl.pallas_call(
            functools.partial(corner_kernel, row_size),
            out_shape=[array(PAIRS + 2 * CHUNK, 8, 128)] * n_x,
            in_specs=[pl.BlockSpec(memory_space=pl.ANY)] + [VMEM] * 5,
            out_specs=[VMEM] * n_x,
            scratch_shapes=[scratch(FIELDS, 8 * ROWS, 128)],
            compiler_params=PARAMS,
            name="corners",
        )(weights, z_halo, even, odd, even_z, odd_z)
        corner = across_rows(corner_send)
        inner = pl.pallas_call(
            functools.partial(inner_kernel, row_size),
            out_shape=[
                array(3, ROWS, CHUNK, 8, 128),
                array(3, ROWS, CHUNK, 8, 128),
                array(ROWS, CHUNK, 8, 128),
                array(3, 2, CHUNK, 8, 128),
                array(3, 2, CHUNK, 8, 128),
                array(2, CHUNK, 8, 128),
                array(6, 4, OWN, 8, 128),
                array(STEPS, 8, 128),
            ],
            in_specs=[VMEM] * 8 + [SMEM],
            out_specs=[VMEM] * 8,
            scratch_shapes=[
                scratch(FIELDS, 8 * ROWS, 128),
                scratch(FIELDS, ROWS, 8, 128),
                scratch(ROWS, OWN, 8, 128),
                scratch(2, OWN, 8, 128),
            ],
            compiler_params=PARAMS,
            name="inner",
        )(state, z_halo, own, even, odd, even_z, odd_z, weights, port_row)
        devices = col_size * row_size * gz_size
        ports_each = PORT_TILE * col_size * row_size // devices
        electric_out, magnetic_out, term = pl.pallas_call(
            functools.partial(outer_kernel, row_size, ports_each),
            out_shape=[array(3, LAYERS, ROWS, 128)] * 2 + [array(devices, ports_each, 2 * FREQ)],
            in_specs=[SMEM] * 2 + [VMEM] * (9 + 2 * n_x),
            out_specs=[HBM, HBM, VMEM],
            scratch_shapes=[
                scratch(ROWS, OWN, 8, 128),
                scratch(2, OWN, 8, 128),
                scratch(STEPS, 8, 128),
                scratch(6, ROWS, LAYERS, 128),
                scratch(6, LAYERS, ROWS, 128),
                pltpu.SemaphoreType.DMA((2,)),
            ],
            compiler_params=PARAMS,
            name="outer",
        )(port_row, port_ids, *inner, weights, *x_halo, *corner)
        terms = lax.all_to_all(term, ("col", "row", "gz"), 0, 0, tiled=True)
        return (
            electric_out,
            magnetic_out,
            jnp.sum(terms, axis=0),
        )

    in_specs = (
        P(None, "gz", "row", ("grp", "col")),
        P(None, "gz", "row", ("grp", "col")),
        P("gz", "row", ("grp", "col")),
        P(),
        P(None, "gz", None),
        P(("grp", "row"), "col", None),
        P(("grp", "row"), "col", None),
        P(("grp", "row"), "col", None),
        P(("grp", "row"), "col", None),
    )
    out_specs = (
        P(None, "gz", "row", ("grp", "col")),
        P(None, "gz", "row", ("grp", "col")),
        P(("grp", "col", "row", "gz"), None),
    )
    return jax.shard_map(
        per_device, mesh=mesh, in_specs=in_specs, out_specs=out_specs, check_vma=False
    )
```

```python
import functools

import jax
import jax.numpy as jnp
import numpy as np
from jax import lax
from jax.experimental import pallas as pl
from jax.experimental.pallas import tpu as pltpu
from jax.sharding import PartitionSpec as P

STEPS = 4
FREQ = 8
MATS = 8
PLEN = 64
PORT_TILE = 4
FIELDS = 7
DEPTH = STEPS
ROWS = 8
LAYERS = 32
OWN = 4
CHUNK = 5
GROUP = 32

time_step = 0.5

UP_PLANES = [(f, 4) for f in (0, 1, 2, 4, 5)] + [(f, x) for x in (5, 6, 7) for f in range(FIELDS)]
DOWN_PLANES = [(f, x) for x in (0, 1, 2) for f in range(FIELDS)] + [(1, 3), (2, 3)]
PLANES = max(len(UP_PLANES), len(DOWN_PLANES))
PAIRS = (PLANES + 1) // 2

VMEM = pl.BlockSpec(memory_space=pltpu.VMEM)
SMEM = pl.BlockSpec(memory_space=pltpu.SMEM)
HBM = pl.BlockSpec(memory_space=pltpu.HBM)
PARAMS = pltpu.CompilerParams(vmem_limit_bytes=16 * 1024 * 1024)


def dft_basis():
    times = (np.arange(STEPS) + 1.0) * time_step
    omegas = np.pi * (np.arange(FREQ) + 1.0) / FREQ
    angle = times[:, None] * omegas[None, :]
    return np.concatenate([np.cos(angle), -np.sin(angle)], axis=1)


BASIS = dft_basis()


def iota(axis):
    return lax.broadcasted_iota(jnp.int32, (8, 128), axis)


def turn(tile, shift, axis):
    return pltpu.roll(tile, shift % tile.shape[axis], axis)


def directions(row_size, body):
    if row_size == 2:
        row = lax.axis_index("row")
        pl.when(row == 0)(functools.partial(body, True, 0))
        pl.when(row == 1)(functools.partial(body, False, 0))
    else:
        body(True, 0)
        body(False, 1)


def pack_kernel(row_size, eps_hbm, elec_hbm, magn_hbm, mat_hbm, state_ref, z_ref, own_ref, even_ref, odd_ref, *rest):
    x_refs, (main_ref, eps_ref, mat_ref, sems) = rest[:-4], rest[-4:]
    copies = [pltpu.make_async_copy(eps_hbm, eps_ref, sems.at[0]), pltpu.make_async_copy(mat_hbm, mat_ref, sems.at[1])]
    copies.append(pltpu.make_async_copy(elec_hbm, main_ref.at[pl.ds(0, 3)], sems.at[2]))
    copies.append(pltpu.make_async_copy(magn_hbm, main_ref.at[pl.ds(3, 3)], sems.at[3]))
    for copy in copies:
        copy.start()
    copies[0].wait()
    copies[1].wait()
    for z in range(LAYERS):
        material = mat_ref[z]
        eps = jnp.full((8, 128), eps_ref[0], jnp.float32)
        for which in range(1, MATS):
            eps = jnp.where(material == which, eps_ref[which], eps)
        main_ref[6, z] = time_step * (1.0 / eps)
    copies[2].wait()
    copies[3].wait()
    start = jnp.where(lax.axis_index("gz") == 0, LAYERS - DEPTH, 0)
    for f in range(FIELDS):
        z_ref[f] = main_ref[f, pl.ds(start, DEPTH)]
    block = LAYERS * ROWS
    flat = main_ref.reshape(FIELDS * block, 128)
    for f in range(FIELDS):
        for x in range(ROWS):
            state_ref[f, x] = flat[pl.ds(f * block + x, LAYERS, stride=ROWS), :].reshape(OWN, 8, 128)

    def send(up, slot):
        for i, (f, x) in enumerate(UP_PLANES if up else DOWN_PLANES):
            x_refs[slot][i] = state_ref[f, x]

    directions(row_size, send)
    pack_edges(state_ref, own_ref, even_ref, odd_ref)


def lane_groups():
    group = iota(1) >> 5
    return [jnp.where(group == r, 1.0, 0.0) for r in range(4)]


def gather_edges(rows_of, groups):
    moved = [[tile if tile is None else turn(tile, GROUP * r + 8, 1) for r, tile in enumerate(rows)] for rows in rows_of]
    out = []
    for rows in moved:
        parts = [tile * groups[r] for r, tile in enumerate(rows) if tile is not None]
        out.append(functools.reduce(lambda a, b: a + b, parts) if parts else jnp.zeros((8, 128), jnp.float32))
    return out


def staged(items, first, second):
    waiting = None
    for item in items:
        made = first(item)
        if waiting is not None:
            second(*waiting)
        waiting = (item, made)
    second(*waiting)


def pack_edges(state_ref, own_ref, even_ref, odd_ref):
    lane = iota(1)
    groups = lane_groups()
    slots = [jnp.where(((lane & (GROUP - 1)) >> 2) == f, 1.0, 0.0) for f in range(FIELDS)]
    even = (lax.axis_index("col") & 1) == 0

    def first(at):
        b, zz = at
        return gather_edges([[state_ref[f, 4 * b + r, zz] for r in range(4)] for f in range(FIELDS)], groups)

    def second(at, owns):
        b, zz = at
        ups = [turn(own, DEPTH * f - 4, 1) for f, own in enumerate(owns)]
        downs = [turn(own, DEPTH * f - 8, 1) for f, own in enumerate(owns)]
        up = functools.reduce(lambda a, b: a + b, [v * m for v, m in zip(ups, slots)])
        down = functools.reduce(lambda a, b: a + b, [v * m for v, m in zip(downs, slots)])
        for f in range(FIELDS):
            own_ref[f, b, zz] = owns[f]
        even_ref[b, zz] = jnp.where(even, up, down)
        odd_ref[b, zz] = jnp.where(even, down, up)

    staged([(b, zz) for b in range(2) for zz in range(OWN)], first, second)


def low_and_high(even_ref, odd_ref):
    even = (lax.axis_index("col") & 1) == 0

    def low(*at):
        return jnp.where(even, odd_ref[at], even_ref[at])

    def high(*at):
        return jnp.where(even, even_ref[at], odd_ref[at])

    return low, high


def layer_edge_kernel(even_ref, odd_ref, inner_ref, out_ref):
    gz = lax.axis_index("gz")
    for i, ref in enumerate((even_ref, odd_ref)):
        for b in range(2):
            out_ref[i, b] = jnp.where(gz == 0, ref[b, OWN - 1], ref[b, 0])


def spread_layers(gz, z_ref, ext_ref):
    for f in range(FIELDS):
        halo = z_ref[f].reshape(DEPTH * ROWS, 128)
        nothing = jnp.zeros_like(halo)
        ext_ref[f, : DEPTH * ROWS] = jnp.where(gz == 0, halo, nothing)
        ext_ref[f, DEPTH * ROWS :] = jnp.where(gz == 0, nothing, halo)


def corner_kernel(row_size, z_ref, even_ref, odd_ref, layer_ref, *rest):
    x_refs, ext_ref = rest[:-1], rest[-1]
    gz = lax.axis_index("gz")
    valid = (iota(0) < 4) == (gz == 0)
    spread_layers(gz, z_ref, ext_ref)
    low, high = low_and_high(even_ref, odd_ref)
    low_z, high_z = low_and_high(layer_ref.at[0], layer_ref.at[1])

    def send(up, slot):
        planes = UP_PLANES if up else DOWN_PLANES

        def tile(i):
            f, x = planes[i]
            return ext_ref[f, pl.ds(x, 8, stride=ROWS), :]

        for i in range(PAIRS):
            pair = tile(i)
            if i + PAIRS < len(planes):
                pair = pair + turn(tile(i + PAIRS), 4, 0)
            x_refs[slot][i] = pair
        b = 1 if up else 0
        for zz in range(OWN):
            x_refs[slot][PAIRS + zz] = low(b, zz)
            x_refs[slot][PAIRS + CHUNK + zz] = high(b, zz)
        x_refs[slot][PAIRS + OWN] = jnp.where(valid, low_z(b), 0.0)
        x_refs[slot][PAIRS + CHUNK + OWN] = jnp.where(valid, high_z(b), 0.0)

    directions(row_size, send)


def turn_sides(low, high):
    lows = [turn(low, 12 - DEPTH * f, 1) for f in range(FIELDS)]
    return lows, [turn(high, 8 - DEPTH * f, 1) for f in range(FIELDS)]


def edge_tiles(owns, sides, place):
    turned = [turn(own, 8, 1) for own in owns]
    out = []
    for own, own_turned, low, high in zip(owns, turned, *sides):
        tile = jnp.where(place < 16, low, own_turned)
        tile = jnp.where(place < 12, high, tile)
        out.append(jnp.where(place < 8, own, tile))
    return out


class Tiles:
    def __init__(self, first, ez_ref, shift):
        self.first, self.ez_ref, self.shift = first, ez_ref, shift
        self.values = {}

    def get(self, f, i, zz):
        value = self.values.get((f, i, zz))
        return self.first(f, i, zz) if value is None else value

    def put(self, f, i, zz, tile):
        self.values[f, i, zz] = tile
        at = i - self.shift
        if f == 2 and zz < OWN and 0 <= at < self.ez_ref.shape[0]:
            self.ez_ref[at, zz] = tile


def leapfrog(tiles, exists, h_rows, e_rows, across, h_of, c_of, h_layers, e_layers, skip_hx):
    sub = iota(0)
    every = range(CHUNK)
    blank = [jnp.zeros((8, 128), jnp.float32)] * CHUNK

    def above(values):
        turned = [turn(v, -1, 0) for v in values]
        return [jnp.where(sub == 7, turned[(zz + 1) % CHUNK], turned[zz]) for zz in every]

    def beneath(values):
        turned = [turn(v, 1, 0) for v in values]
        return [jnp.where(sub == 0, turned[zz - 1], turned[zz]) for zz in every]

    def row(f, i):
        return [tiles.get(f, i, zz) for zz in every]

    def load_e(i):
        ey, ez = row(1, i), row(2, i)
        out = dict(ey=ey, ez=ez, ey_x=across.turned(ey, -1), ez_x=across.turned(ez, -1))
        if i in h_rows:
            ex = row(0, i)
            out.update(ex=ex, ex_y=[turn(v, -1, 1) for v in ex], ex_z=above(ex))
            if i not in skip_hx:
                out.update(ez_y=[turn(v, -1, 1) for v in ez], ey_z=above(ey))
        return out

    def work_h(i, loaded):
        e, after, h = loaded[i], loaded.get(i + 1), h_of(i)
        ey_x = across.pick(e["ey_x"], after["ey_x"] if after else blank, -1)
        ez_x = across.pick(e["ez_x"], after["ez_x"] if after else blank, -1)
        new = {}
        for zz in h_layers:
            if i not in skip_hx:
                curl = (e["ez_y"][zz] - e["ez"][zz]) - (e["ey_z"][zz] - e["ey"][zz])
                new[3, zz] = tiles.get(3, i, zz) - h[zz] * curl
            curl = (e["ex_z"][zz] - e["ex"][zz]) - (ez_x[zz] - e["ez"][zz])
            new[4, zz] = tiles.get(4, i, zz) - h[zz] * curl
            curl = (ey_x[zz] - e["ey"][zz]) - (e["ex_y"][zz] - e["ex"][zz])
            new[5, zz] = tiles.get(5, i, zz) - h[zz] * curl
        for (f, zz), tile in new.items():
            tiles.put(f, i, zz, tile)

    def load_h(i):
        hy, hz = row(4, i), row(5, i)
        out = dict(hy=hy, hz=hz, hy_x=across.turned(hy, 1), hz_x=across.turned(hz, 1))
        if i in e_rows:
            hx = row(3, i)
            out.update(hx=hx, hx_y=[turn(v, 1, 1) for v in hx], hz_y=[turn(v, 1, 1) for v in hz])
            out.update(hx_z=beneath(hx), hy_z=beneath(hy))
        return out

    def work_e(i, loaded):
        h, before, c = loaded[i], loaded.get(i - 1), c_of(i)
        hy_x = across.pick(h["hy_x"], before["hy_x"] if before else blank, 1)
        hz_x = across.pick(h["hz_x"], before["hz_x"] if before else blank, 1)
        new = {}
        for zz in e_layers:
            curl = (h["hz"][zz] - h["hz_y"][zz]) - (h["hy"][zz] - h["hy_z"][zz])
            new[0, zz] = tiles.get(0, i, zz) + c[zz] * curl
            curl = (h["hx"][zz] - h["hx_z"][zz]) - (h["hz"][zz] - hz_x[zz])
            new[1, zz] = tiles.get(1, i, zz) + c[zz] * curl
            curl = (h["hy"][zz] - hy_x[zz]) - (h["hx"][zz] - h["hx_y"][zz])
            new[2, zz] = tiles.get(2, i, zz) + c[zz] * curl
        for (f, zz), tile in new.items():
            tiles.put(f, i, zz, tile)

    def sweep(rows, load, work):
        loaded = {}

        def want(i):
            if i not in loaded and i in exists:
                loaded[i] = load(i)

        for i in rows:
            for j in (i - 1, i, i + 1):
                if j in rows or j == i + (1 if load is load_e else -1):
                    want(j)
            work(i, loaded)

    sweep(h_rows, load_e, work_h)
    yield
    sweep(e_rows, load_h, work_e)


class Rows:
    def turned(self, values, way):
        return values

    def pick(self, own, other, way):
        return other


class Blocks:
    def __init__(self, groups):
        self.groups = groups

    def turned(self, values, way):
        return [turn(v, way * GROUP, 1) for v in values]

    def pick(self, own, other, way):
        edge = self.groups[3] if way < 0 else self.groups[0]
        return [jnp.where(edge, o, v) for o, v in zip(other, own)]


def spans_inner(n, has_below, has_above):
    last = 7 - n if has_above else 7
    return (n - 1 if has_below else 0, last), (n if has_below else 0, last)


def spans_below(n):
    return (n - 5, n - 2), (n - 4, n - 1)


def spans_above(n):
    return (8 - n, 11 - n), (8 - n, 11 - n)


class Stepper:
    def __init__(self, row_size, main, edge, main_exists, edge_exists, skip_hx):
        gz, row, col = (lax.axis_index(name) for name in ("gz", "row", "col"))
        lane, sub = iota(1), iota(0)
        place, self.group = lane & (GROUP - 1), lane >> 5
        full = jnp.full((8, 128), time_step, jnp.float32)
        self.layer_half = [full] * OWN + [jnp.where((sub >= 4) & (gz == 0), 0.0, full)]
        outside = (place >= 12) & (place < 16) & (col == 0)
        self.edge_half = [jnp.where(outside, 0.0, v) for v in self.layer_half]
        self.lowest = jnp.where(row == 0, 0.0, 1.0) if row_size > 2 else None
        self.main, self.edge, self.skip_hx = main, edge, skip_hx
        self.main_exists, self.edge_exists = main_exists, edge_exists
        self.blocks = Blocks([self.group == r for r in range(4)])

    def masked(self, values, block, span):
        low, high = max(span[0] - 4 * block, 0), min(span[1] - 4 * block, 3)
        if low == 0 and high == 3:
            return values
        mask = (self.group >= low) & (self.group <= high)
        return [jnp.where(mask, v, 0.0) for v in values]

    def main_h(self, i):
        return self.layer_half if self.lowest is None or i >= DEPTH else [v * self.lowest for v in self.layer_half]

    def main_c(self, i):
        return [self.main.get(6, i, zz) for zz in range(CHUNK)]

    def edge_h(self, i, span):
        h = self.edge_half if self.lowest is None or i else [v * self.lowest for v in self.edge_half]
        return self.masked(h, i - 1, span)

    def edge_c(self, i, span):
        return self.masked([self.edge.get(6, i, zz) for zz in range(CHUNK)], i - 1, span)

    def step(self, n, spans):
        def blocks_of(span):
            return [b + 1 for b in range(-1, 3) if span[0] <= 4 * b + 3 and span[1] >= 4 * b]

        layers = range(CHUNK)
        last = range(OWN) if n == STEPS else layers
        parts = []
        for h_span, e_span in spans:
            h_rows = list(range(DEPTH + h_span[0], DEPTH + h_span[1] + 1))
            e_rows = list(range(DEPTH + e_span[0], DEPTH + e_span[1] + 1))
            skip = h_rows[:1] if self.skip_hx and h_span[0] < e_span[0] else []
            if self.main is not None:
                parts.append(
                    leapfrog(self.main, self.main_exists, h_rows, e_rows, Rows(), self.main_h, self.main_c, layers, last, skip)
                )
            if self.edge is None:
                continue
            h_of, c_of = functools.partial(self.edge_h, span=h_span), functools.partial(self.edge_c, span=e_span)
            parts.append(
                leapfrog(
                    self.edge, self.edge_exists, blocks_of(h_span), blocks_of(e_span), self.blocks, h_of, c_of, layers, last, []
                )
            )
        for part in parts:
            next(part)
        for part in parts:
            next(part, None)


def rows_cases(row_size, row, run):
    if row_size == 2:
        pl.when(row == 0)(functools.partial(run, False, True))
        pl.when(row == 1)(functools.partial(run, True, False))
    else:
        run(True, True)


def port_sums(n, reached, prow_ref, weight_ref, ez_ref, edge_ref, sum_ref, add_ref):
    for k in range(PORT_TILE):
        at = prow_ref[0, 0, k]
        total = jnp.zeros((8, 128), jnp.float32)
        for zz in range(OWN):
            if ez_ref is not None:
                total = total + ez_ref[at, zz] * weight_ref[k, 0, zz]
            if edge_ref is not None:
                total = total + edge_ref[at >> 2, zz] * weight_ref[k, 1, zz]
        total = jnp.sum(jnp.where(reached(n, at), total, 0.0), axis=0, keepdims=True)
        if add_ref is not None:
            total = total + add_ref[n - 1, k : k + 1, :]
        sum_ref[n - 1, k : k + 1, :] = total


def finish(fields, b, main, edge, write):
    lane = iota(1)
    place = lane & (GROUP - 1)
    sides = (lane < DEPTH) | (lane >= 128 - DEPTH)

    def first(f):
        tiles = [edge.get(f, b + 1, zz) for zz in range(OWN)]
        turned = [turn(tile, -8, 1) for tile in tiles]
        return [jnp.where(place < 8, tile, other) for tile, other in zip(tiles, turned)]

    def second(f, near):
        turned = {(r, zz): turn(near[zz], -(GROUP * r + 8), 1) for r in range(4) for zz in range(OWN)}
        made = {(r, zz): jnp.where(sides, tile, main.get(f, DEPTH + 4 * b + r, zz)) for (r, zz), tile in turned.items()}
        for (r, zz), tile in made.items():
            write(f, r, zz, tile)

    staged(fields, first, second)


def port_weights(mode_ref, prow_ref, pcol_ref, pmode_ref, weight_ref, strip_ref):
    lane = iota(1)
    for k in range(PORT_TILE):
        strip_ref[k] = jnp.zeros(strip_ref.shape[1:], jnp.float32)
        strip_ref[k, :, 0:PLEN] = mode_ref[pmode_ref[0, 0, k]]
    for k in range(PORT_TILE):
        turned = GROUP * (prow_ref[0, 0, k] & 3)
        at = lane - turned
        for zz in range(OWN):
            tile = pltpu.roll(strip_ref[k, 8 * zz : 8 * zz + 8, :], pcol_ref[0, 0, k], 1)
            weight_ref[k, 0, zz] = jnp.where((lane >= DEPTH) & (lane < 128 - DEPTH), tile, 0.0)
            own = pltpu.roll(tile, turned + 8, 1)
            edge = jnp.where((at >= 4) & (at < 8), own, 0.0)
            weight_ref[k, 1, zz] = jnp.where((at >= 16) & (at < 20), turn(own, 8, 1), edge)


def inner_kernel(
    row_size, state_ref, z_ref, mode_ref, prow_ref, pcol_ref, pmode_ref, pid_ref,
    e_ref, h_ref, c_ref, sum_ref, weight_ref, ext_ref, halo_ref, ez_ref, strip_ref,
):
    gz, row = lax.axis_index("gz"), lax.axis_index("row")
    spread_layers(gz, z_ref, ext_ref)
    for f in range(FIELDS):
        for x in range(ROWS):
            halo_ref[f, x] = ext_ref[f, pl.ds(x, 8, stride=ROWS), :]
    port_weights(mode_ref, prow_ref, pcol_ref, pmode_ref, weight_ref, strip_ref)

    def first(f, i, zz):
        return halo_ref[f, i - DEPTH] if zz == OWN else state_ref[f, i - DEPTH, zz]

    def run(has_below, has_above):
        main = Tiles(first, ez_ref, DEPTH)
        stepper = Stepper(row_size, main, None, range(4, 12), (), False)

        def reached(n, at):
            low, high = spans_inner(n, has_below, has_above)[1]
            return (at >= low) & (at <= high)

        for n in range(1, STEPS + 1):
            stepper.step(n, [spans_inner(n, has_below, has_above)])
            port_sums(n, reached, prow_ref, weight_ref, ez_ref, None, sum_ref, None)
        for i in range(ROWS):
            for zz in range(CHUNK):
                for f in range(6):
                    (e_ref, h_ref)[f // 3][f % 3, i, zz] = main.get(f, DEPTH + i, zz)
                c_ref[i, zz] = main.get(6, DEPTH + i, zz)

    rows_cases(row_size, row, run)


def rim_kernel(
    row_size, z_ref, own_ref, even_ref, odd_ref, layer_ref, e_in, h_in, sum_in, weight_ref, prow_ref,
    edge_e_ref, edge_h_ref, edge_c_ref, done_ref, sum_ref, ext_ref, ez_ref,
):
    gz, row = lax.axis_index("gz"), lax.axis_index("row")
    place = iota(1) & (GROUP - 1)
    groups = lane_groups()
    valid = (iota(0) < 4) == (gz == 0)
    spread_layers(gz, z_ref, ext_ref)
    low_of, high_of = low_and_high(even_ref, odd_ref)
    low_z, high_z = low_and_high(layer_ref.at[0], layer_ref.at[1])
    joined = {}

    def first(at):
        b, zz = at
        if zz < OWN:
            return [own_ref[f, b, zz] for f in range(FIELDS)], turn_sides(low_of(b, zz), high_of(b, zz))
        rows = [[ext_ref[f, pl.ds(4 * b + r, 8, stride=ROWS), :] for r in range(4)] for f in range(FIELDS)]
        sides = turn_sides(*(jnp.where(valid, side(b), 0.0) for side in (low_z, high_z)))
        return gather_edges(rows, groups), sides

    def second(at, made):
        for f, tile in enumerate(edge_tiles(*made, place)):
            joined[f, at[0] + 1, at[1]] = tile

    staged([(b, zz) for b in range(2) for zz in range(CHUNK)], first, second)

    def run(has_below, has_above):
        main = Tiles(lambda f, i, zz: (e_in, h_in)[f // 3][f % 3, i - DEPTH, zz], None, DEPTH)
        edge = Tiles(lambda f, i, zz: joined[f, i, zz], ez_ref, 1)
        stepper = Stepper(row_size, None, edge, (), (1, 2), False)

        def reached(n, at):
            low, high = spans_inner(n, has_below, has_above)[1]
            return (at >= low) & (at <= high)

        for n in range(1, STEPS + 1):
            stepper.step(n, [spans_inner(n, has_below, has_above)])
            port_sums(n, reached, prow_ref, weight_ref, None, ez_ref, sum_ref, sum_in)
        for i in range(2):
            for zz in range(CHUNK):
                for f in range(6):
                    (edge_e_ref, edge_h_ref)[f // 3][f % 3, i, zz] = edge.get(f, 1 + i, zz)
                edge_c_ref[i, zz] = edge.get(6, 1 + i, zz)
        if has_below != has_above:

            def write(f, r, zz, tile):
                done_ref[f, r, zz] = tile

            finish(range(6), 0 if has_above else 1, main, edge, write)

    rows_cases(row_size, row, run)


def outer_kernel(
    row_size, ports_each, prow_ref, pid_ref, e_in, h_in, c_in, weight_ref, edge_e_in, edge_h_in, edge_c_in, done_ref, sum_in,
    *rest,
):
    n_x = 1 if row_size == 2 else 2
    x_refs, corner_refs = rest[:n_x], rest[n_x : 2 * n_x]
    eout_hbm, hout_hbm, term_ref, ez_ref, edge_ez_ref, sum_ref, turned_ref, out_ref, sems = rest[2 * n_x :]
    gz, row = lax.axis_index("gz"), lax.axis_index("row")
    lane, sub = iota(1), iota(0)
    place = lane & (GROUP - 1)
    groups = lane_groups()
    valid = (sub < 4) == (gz == 0)
    zeros = jnp.zeros((8, 128), jnp.float32)

    def first_main(f, i, zz):
        if f == 6:
            return c_in[i - DEPTH, zz]
        return e_in[f, i - DEPTH, zz] if f < 3 else h_in[f - 3, i - DEPTH, zz]

    def first_edge(f, i, zz):
        if f == 6:
            return edge_c_in[i - 1, zz]
        return edge_e_in[f, i - 1, zz] if f < 3 else edge_h_in[f - 3, i - 1, zz]

    def run(has_below, has_above):
        main = Tiles(first_main, ez_ref, DEPTH)
        edge = Tiles(first_edge, edge_ez_ref, 1)

        def halo_rows(planes, slot, offset, b):
            got = {}
            for i, (f, x) in enumerate(planes):
                packed = corner_refs[slot][i % PAIRS]
                if i >= PAIRS:
                    packed = turn(packed, 4, 0)
                tiles = [x_refs[slot][i, zz] for zz in range(OWN)]
                tiles.append(jnp.where(valid, packed, 0.0))
                for zz in range(CHUNK):
                    main.put(f, DEPTH + x + offset, zz, tiles[zz])
                    got[f, x + offset - 4 * b, zz] = tiles[zz]

            def first(zz):
                rows = [[got.get((f, r, zz)) for r in range(4)] for f in range(FIELDS)]
                sides = turn_sides(corner_refs[slot][PAIRS + zz], corner_refs[slot][PAIRS + CHUNK + zz])
                return gather_edges(rows, groups), sides

            def second(zz, made):
                for f, tile in enumerate(edge_tiles(*made, place)):
                    edge.put(f, 1 + b, zz, tile)

            staged(range(CHUNK), first, second)

        if has_below:
            halo_rows(UP_PLANES, 0, -ROWS, -1)
        if has_above:
            halo_rows(DOWN_PLANES, n_x - 1, ROWS, 2)

        def reached(n, at):
            out = None
            for wanted, span in ((has_below, spans_below(n)[1]), (has_above, spans_above(n)[1])):
                if wanted:
                    part = (at >= span[0]) & (at <= span[1])
                    out = part if out is None else out | part
            return out

        rows = range(0 if has_below else 4, 16 if has_above else 12)
        blocks = range(0 if has_below else 1, 4 if has_above else 3)
        stepper = Stepper(row_size, main, edge, rows, blocks, True)
        for n in range(1, STEPS + 1):
            spans = ([spans_below(n)] if has_below else []) + ([spans_above(n)] if has_above else [])
            stepper.step(n, spans)
            port_sums(n, reached, prow_ref, weight_ref, ez_ref, edge_ez_ref, sum_ref, sum_in)
        def write(f, r, zz, tile, b):
            turned_ref[f, 4 * b + r, 8 * zz : 8 * zz + 8, :] = tile

        for b in range(2):
            put = functools.partial(write, b=b)
            if has_below and has_above or b == (1 if has_above else 0):
                finish(range(6), b, main, edge, put)
            else:
                for f in range(6):
                    for r in range(4):
                        for zz in range(OWN):
                            put(f, r, zz, done_ref[f, r, zz])

    rows_cases(row_size, row, run)

    copies = []
    flat = turned_ref.reshape(6 * ROWS * LAYERS, 128)
    for part, dest in ((0, eout_hbm), (1, hout_hbm)):
        for f in range(3 * part, 3 * part + 3):
            for z in range(LAYERS):
                out_ref[f, z] = flat[pl.ds(f * ROWS * LAYERS + z, ROWS, stride=LAYERS), :]
        copies.append(pltpu.make_async_copy(out_ref.at[pl.ds(3 * part, 3)], dest, sems.at[part]))
        copies[-1].start()
    basis = zeros
    for n in range(STEPS):
        for f in range(2 * FREQ):
            basis = jnp.where((sub == n) & (lane == f), float(BASIS[n, f]), basis)
    transform = zeros
    for n in range(STEPS):
        sampled = jnp.sum(sum_ref[n], axis=1, keepdims=True)
        transform = transform + sampled * basis[n : n + 1, :]
    term_ref[...] = jnp.zeros(term_ref.shape, jnp.float32)
    for k in range(PORT_TILE):
        port = pid_ref[0, 0, k]
        term_ref[port // ports_each, pl.ds(port % ports_each, 1), :] = transform[k : k + 1, : 2 * FREQ]
    for copy in copies:
        copy.wait()


def shifted(block, axis, size, distance):
    route = [(i - distance, i) for i in range(size) if 0 <= i - distance < size]
    return lax.ppermute(block, axis, route)


def swapped(block, axis, size, start=0):
    pairs = [(i, i + 1) for i in range(start, size - 1, 2)]
    return lax.ppermute(block, axis, pairs + [(j, i) for i, j in pairs])


def solution(mesh):
    sizes = dict(mesh.shape)
    row_size, col_size, gz_size = sizes["row"], sizes["col"], sizes["gz"]
    n_x = 1 if row_size == 2 else 2

    def across_rows(blocks):
        if row_size == 2:
            return (swapped(blocks[0], "row", 2),)
        return (shifted(blocks[0], "row", row_size, 1), shifted(blocks[1], "row", row_size, -1))

    def per_device(
        electric, magnetic, material, eps_table, mode_table, port_row, port_col, port_mode, port_ids
    ):
        f32 = jnp.float32

        def array(*shape):
            return jax.ShapeDtypeStruct(shape, f32)

        def scratch(*shape):
            return pltpu.VMEM(shape, f32)

        state, z_send, own, even_send, odd_send, *x_send = pl.pallas_call(
            functools.partial(pack_kernel, row_size),
            out_shape=[
                array(FIELDS, ROWS, OWN, 8, 128),
                array(FIELDS, DEPTH, ROWS, 128),
                array(FIELDS, 2, OWN, 8, 128),
                array(2, OWN, 8, 128),
                array(2, OWN, 8, 128),
            ]
            + [array(PLANES, OWN, 8, 128)] * n_x,
            in_specs=[HBM] * 4,
            out_specs=[VMEM] * (5 + n_x),
            scratch_shapes=[
                scratch(FIELDS, LAYERS, ROWS, 128),
                pltpu.SMEM(eps_table.shape, f32),
                pltpu.VMEM(material.shape, jnp.int32),
                pltpu.SemaphoreType.DMA((4,)),
            ],
            name="pack",
        )(eps_table, electric, magnetic, material)
        x_halo = across_rows(x_send)
        even = swapped(even_send, "col", col_size)
        odd = swapped(odd_send, "col", col_size, 1)
        z_halo = swapped(z_send, "gz", gz_size)
        e_now, h_now, c_now, sums, weights = pl.pallas_call(
            functools.partial(inner_kernel, row_size),
            out_shape=[
                array(3, ROWS, CHUNK, 8, 128),
                array(3, ROWS, CHUNK, 8, 128),
                array(ROWS, CHUNK, 8, 128),
                array(STEPS, 8, 128),
                array(PORT_TILE, 2, OWN, 8, 128),
            ],
            in_specs=[VMEM] * 3 + [SMEM] * 4,
            out_specs=[VMEM] * 5,
            scratch_shapes=[
                scratch(FIELDS, 8 * ROWS, 128),
                scratch(FIELDS, ROWS, 8, 128),
                scratch(ROWS, OWN, 8, 128),
                scratch(PORT_TILE, LAYERS, 128),
            ],
            compiler_params=PARAMS,
            cost_estimate=pl.CostEstimate(flops=5_000_000, bytes_accessed=10_000_000, transcendentals=0),
            name="inner",
        )(state, z_halo, mode_table, port_row, port_col, port_mode, port_ids)
        layer_send = pl.pallas_call(
            layer_edge_kernel,
            out_shape=array(2, 2, 8, 128),
            in_specs=[VMEM] * 2 + [pl.BlockSpec(memory_space=pl.ANY)],
            out_specs=VMEM,
            compiler_params=PARAMS,
            name="layer_edges",
        )(even, odd, sums)
        layer_halo = swapped(layer_send, "gz", gz_size)
        corner_send = pl.pallas_call(
            functools.partial(corner_kernel, row_size),
            out_shape=[array(PAIRS + 2 * CHUNK, 8, 128)] * n_x,
            in_specs=[VMEM] * 4,
            out_specs=[VMEM] * n_x,
            scratch_shapes=[scratch(FIELDS, 8 * ROWS, 128)],
            compiler_params=PARAMS,
            name="corners",
        )(z_halo, even, odd, layer_halo)
        corner = across_rows(corner_send)
        edges = pl.pallas_call(
            functools.partial(rim_kernel, row_size),
            out_shape=[
                array(3, 2, CHUNK, 8, 128),
                array(3, 2, CHUNK, 8, 128),
                array(2, CHUNK, 8, 128),
                array(6, 4, OWN, 8, 128),
                array(STEPS, 8, 128),
            ],
            in_specs=[VMEM] * 9 + [SMEM],
            out_specs=[VMEM] * 5,
            scratch_shapes=[scratch(FIELDS, 8 * ROWS, 128), scratch(2, OWN, 8, 128)],
            compiler_params=PARAMS,
            name="rim",
        )(z_halo, own, even, odd, layer_halo, e_now, h_now, sums, weights, port_row)
        devices = col_size * row_size * gz_size
        ports_each = PORT_TILE * col_size * row_size // devices
        electric_out, magnetic_out, term = pl.pallas_call(
            functools.partial(outer_kernel, row_size, ports_each),
            out_shape=[array(3, LAYERS, ROWS, 128)] * 2 + [array(devices, ports_each, 2 * FREQ)],
            in_specs=[SMEM] * 2 + [VMEM] * (9 + 2 * n_x),
            out_specs=[HBM, HBM, VMEM],
            scratch_shapes=[
                scratch(ROWS, OWN, 8, 128),
                scratch(2, OWN, 8, 128),
                scratch(STEPS, 8, 128),
                scratch(6, ROWS, LAYERS, 128),
                scratch(6, LAYERS, ROWS, 128),
                pltpu.SemaphoreType.DMA((2,)),
            ],
            compiler_params=PARAMS,
            name="outer",
        )(port_row, port_ids, e_now, h_now, c_now, weights, *edges, *x_halo, *corner)
        terms = lax.all_to_all(term, ("col", "row", "gz"), 0, 0, tiled=True)
        return (
            electric_out,
            magnetic_out,
            jnp.sum(terms, axis=0),
        )

    in_specs = (
        P(None, "gz", "row", ("grp", "col")),
        P(None, "gz", "row", ("grp", "col")),
        P("gz", "row", ("grp", "col")),
        P(),
        P(None, "gz", None),
        P(("grp", "row"), "col", None),
        P(("grp", "row"), "col", None),
        P(("grp", "row"), "col", None),
        P(("grp", "row"), "col", None),
    )
    out_specs = (
        P(None, "gz", "row", ("grp", "col")),
        P(None, "gz", "row", ("grp", "col")),
        P(("grp", "col", "row", "gz"), None),
    )
    return jax.shard_map(
        per_device, mesh=mesh, in_specs=in_specs, out_specs=out_specs, check_vma=False
    )
```

```python
import functools

import jax
import jax.numpy as jnp
import numpy as np
from jax import lax
from jax.experimental import pallas as pl
from jax.experimental.pallas import tpu as pltpu
from jax.sharding import PartitionSpec as P

STEPS = 4
FREQ = 8
MATS = 8
PLEN = 64
PORT_TILE = 4
FIELDS = 7
DEPTH = STEPS
ROWS = 8
LAYERS = 32
OWN = 4
CHUNK = 5
GROUP = 32

time_step = 0.5

UP_PLANES = [(f, 4) for f in (0, 1, 2, 4, 5)] + [(f, x) for x in (5, 6, 7) for f in range(FIELDS)]
DOWN_PLANES = [(f, x) for x in (0, 1, 2) for f in range(FIELDS)] + [(1, 3), (2, 3)]
PLANES = max(len(UP_PLANES), len(DOWN_PLANES))
PAIRS = (PLANES + 1) // 2

VMEM = pl.BlockSpec(memory_space=pltpu.VMEM)
SMEM = pl.BlockSpec(memory_space=pltpu.SMEM)
HBM = pl.BlockSpec(memory_space=pltpu.HBM)
PARAMS = pltpu.CompilerParams(vmem_limit_bytes=16 * 1024 * 1024)


def dft_basis():
    times = (np.arange(STEPS) + 1.0) * time_step
    omegas = np.pi * (np.arange(FREQ) + 1.0) / FREQ
    angle = times[:, None] * omegas[None, :]
    return np.concatenate([np.cos(angle), -np.sin(angle)], axis=1)


BASIS = dft_basis()


def iota(axis):
    return lax.broadcasted_iota(jnp.int32, (8, 128), axis)


def turn(tile, shift, axis):
    return pltpu.roll(tile, shift % tile.shape[axis], axis)


def directions(row_size, body):
    if row_size == 2:
        row = lax.axis_index("row")
        pl.when(row == 0)(functools.partial(body, True, 0))
        pl.when(row == 1)(functools.partial(body, False, 0))
    else:
        body(True, 0)
        body(False, 1)


def coefficient(material, eps_ref):
    eps = jnp.full((8, 128), eps_ref[0], jnp.float32)
    for which in range(1, MATS):
        eps = jnp.where(material == which, eps_ref[which], eps)
    return time_step * (1.0 / eps)


def rows_outside(flat, f, state_ref, at):
    for x in range(ROWS):
        state_ref[at, x] = flat[pl.ds(f * LAYERS * ROWS + x, LAYERS, stride=ROWS), :].reshape(OWN, 8, 128)


def pack_kernel(row_size, eps_hbm, elec_hbm, magn_hbm, mat_hbm, z_ref, own_ref, even_ref, odd_ref, *rest):
    x_refs, (state_ref, main_ref, eps_ref, mat_ref, sems) = rest[:-5], rest[-5:]
    copies = [pltpu.make_async_copy(eps_hbm, eps_ref, sems.at[0]), pltpu.make_async_copy(mat_hbm, mat_ref, sems.at[1])]
    copies.append(pltpu.make_async_copy(elec_hbm, main_ref.at[pl.ds(0, 3)], sems.at[2]))
    copies.append(pltpu.make_async_copy(magn_hbm, main_ref.at[pl.ds(3, 3)], sems.at[3]))
    for copy in copies:
        copy.start()
    copies[0].wait()
    copies[1].wait()
    for z in range(LAYERS):
        main_ref[6, z] = coefficient(mat_ref[z], eps_ref)
    copies[2].wait()
    copies[3].wait()
    start = jnp.where(lax.axis_index("gz") == 0, LAYERS - DEPTH, 0)
    for f in range(FIELDS):
        z_ref[f] = main_ref[f, pl.ds(start, DEPTH)]
    flat = main_ref.reshape(FIELDS * LAYERS * ROWS, 128)
    for f in range(FIELDS):
        rows_outside(flat, f, state_ref, f)

    def send(up, slot):
        for i, (f, x) in enumerate(UP_PLANES if up else DOWN_PLANES):
            x_refs[slot][i] = state_ref[f, x]

    directions(row_size, send)
    pack_edges(state_ref, own_ref, even_ref, odd_ref)


def lane_groups():
    group = iota(1) >> 5
    return [jnp.where(group == r, 1.0, 0.0) for r in range(4)]


def gather_edges(rows_of, groups):
    moved = [[tile if tile is None else turn(tile, GROUP * r + 8, 1) for r, tile in enumerate(rows)] for rows in rows_of]
    out = []
    for rows in moved:
        parts = [tile * groups[r] for r, tile in enumerate(rows) if tile is not None]
        out.append(functools.reduce(lambda a, b: a + b, parts) if parts else jnp.zeros((8, 128), jnp.float32))
    return out


def staged(items, first, second):
    waiting = None
    for item in items:
        made = first(item)
        if waiting is not None:
            second(*waiting)
        waiting = (item, made)
    second(*waiting)


def pack_edges(state_ref, own_ref, even_ref, odd_ref):
    lane = iota(1)
    groups = lane_groups()
    slots = [jnp.where(((lane & (GROUP - 1)) >> 2) == f, 1.0, 0.0) for f in range(FIELDS)]
    even = (lax.axis_index("col") & 1) == 0

    def first(at):
        b, zz = at
        return gather_edges([[state_ref[f, 4 * b + r, zz] for r in range(4)] for f in range(FIELDS)], groups)

    def second(at, owns):
        b, zz = at
        ups = [turn(own, DEPTH * f - 4, 1) for f, own in enumerate(owns)]
        downs = [turn(own, DEPTH * f - 8, 1) for f, own in enumerate(owns)]
        up = functools.reduce(lambda a, b: a + b, [v * m for v, m in zip(ups, slots)])
        down = functools.reduce(lambda a, b: a + b, [v * m for v, m in zip(downs, slots)])
        for f in range(FIELDS):
            own_ref[f, b, zz] = owns[f]
        even_ref[b, zz] = jnp.where(even, up, down)
        odd_ref[b, zz] = jnp.where(even, down, up)

    staged([(b, zz) for b in range(2) for zz in range(OWN)], first, second)


def low_and_high(even_ref, odd_ref):
    even = (lax.axis_index("col") & 1) == 0

    def low(*at):
        return jnp.where(even, odd_ref[at], even_ref[at])

    def high(*at):
        return jnp.where(even, even_ref[at], odd_ref[at])

    return low, high


def layer_edge_kernel(even_ref, odd_ref, inner_ref, out_ref):
    gz = lax.axis_index("gz")
    for i, ref in enumerate((even_ref, odd_ref)):
        for b in range(2):
            out_ref[i, b] = jnp.where(gz == 0, ref[b, OWN - 1], ref[b, 0])


def spread_layers(gz, z_ref, ext_ref):
    for f in range(FIELDS):
        halo = z_ref[f].reshape(DEPTH * ROWS, 128)
        nothing = jnp.zeros_like(halo)
        ext_ref[f, : DEPTH * ROWS] = jnp.where(gz == 0, halo, nothing)
        ext_ref[f, DEPTH * ROWS :] = jnp.where(gz == 0, nothing, halo)


def layer_kernel(row_size, z_ref, *rest):
    x_refs, ext_ref = rest[:-1], rest[-1]
    spread_layers(lax.axis_index("gz"), z_ref, ext_ref)

    def send(up, slot):
        planes = UP_PLANES if up else DOWN_PLANES
        tiles = [ext_ref[f, pl.ds(x, 8, stride=ROWS), :] for f, x in planes]
        turned = [turn(tile, 4, 0) for tile in tiles[PAIRS:]]
        for i in range(PAIRS):
            x_refs[slot][i] = tiles[i] + turned[i] if i < len(turned) else tiles[i]

    directions(row_size, send)


def corner_kernel(row_size, even_ref, odd_ref, layer_ref, *x_refs):
    valid = (iota(0) < 4) == (lax.axis_index("gz") == 0)
    low, high = low_and_high(even_ref, odd_ref)
    low_z, high_z = low_and_high(layer_ref.at[0], layer_ref.at[1])

    def send(up, slot):
        b = 1 if up else 0
        for zz in range(OWN):
            x_refs[slot][zz] = low(b, zz)
            x_refs[slot][CHUNK + zz] = high(b, zz)
        x_refs[slot][OWN] = jnp.where(valid, low_z(b), 0.0)
        x_refs[slot][CHUNK + OWN] = jnp.where(valid, high_z(b), 0.0)

    directions(row_size, send)


def turn_sides(low, high):
    lows = [turn(low, 12 - DEPTH * f, 1) for f in range(FIELDS)]
    return lows, [turn(high, 8 - DEPTH * f, 1) for f in range(FIELDS)]


def edge_tiles(owns, sides, place):
    turned = [turn(own, 8, 1) for own in owns]
    out = []
    for own, own_turned, low, high in zip(owns, turned, *sides):
        tile = jnp.where(place < 16, low, own_turned)
        tile = jnp.where(place < 12, high, tile)
        out.append(jnp.where(place < 8, own, tile))
    return out


class Tiles:
    def __init__(self, first, ez_ref, shift):
        self.first, self.ez_ref, self.shift = first, ez_ref, shift
        self.values = {}

    def get(self, f, i, zz):
        value = self.values.get((f, i, zz))
        return self.first(f, i, zz) if value is None else value

    def put(self, f, i, zz, tile):
        self.values[f, i, zz] = tile
        at = i - self.shift
        if f == 2 and zz < OWN and self.ez_ref is not None and 0 <= at < self.ez_ref.shape[0]:
            self.ez_ref[at, zz] = tile


def leapfrog(tiles, exists, h_rows, e_rows, across, h_of, c_of, h_layers, e_layers, skip_hx):
    sub = iota(0)
    every = range(CHUNK)
    blank = [jnp.zeros((8, 128), jnp.float32)] * CHUNK

    def above(values):
        turned = [turn(v, -1, 0) for v in values]
        return [jnp.where(sub == 7, turned[(zz + 1) % CHUNK], turned[zz]) for zz in every]

    def beneath(values):
        turned = [turn(v, 1, 0) for v in values]
        return [jnp.where(sub == 0, turned[zz - 1], turned[zz]) for zz in every]

    def row(f, i):
        return [tiles.get(f, i, zz) for zz in every]

    def load_e(i):
        ey, ez = row(1, i), row(2, i)
        out = dict(ey=ey, ez=ez, ey_x=across.turned(ey, -1), ez_x=across.turned(ez, -1))
        if i in h_rows:
            ex = row(0, i)
            out.update(ex=ex, ex_y=[turn(v, -1, 1) for v in ex], ex_z=above(ex))
            if i not in skip_hx:
                out.update(ez_y=[turn(v, -1, 1) for v in ez], ey_z=above(ey))
        return out

    def work_h(i, loaded):
        e, after, h = loaded[i], loaded.get(i + 1), h_of(i)
        ey_x = across.pick(e["ey_x"], after["ey_x"] if after else blank, -1)
        ez_x = across.pick(e["ez_x"], after["ez_x"] if after else blank, -1)
        new = {}
        for zz in h_layers:
            if i not in skip_hx:
                curl = (e["ez_y"][zz] - e["ez"][zz]) - (e["ey_z"][zz] - e["ey"][zz])
                new[3, zz] = tiles.get(3, i, zz) - h[zz] * curl
            curl = (e["ex_z"][zz] - e["ex"][zz]) - (ez_x[zz] - e["ez"][zz])
            new[4, zz] = tiles.get(4, i, zz) - h[zz] * curl
            curl = (ey_x[zz] - e["ey"][zz]) - (e["ex_y"][zz] - e["ex"][zz])
            new[5, zz] = tiles.get(5, i, zz) - h[zz] * curl
        for (f, zz), tile in new.items():
            tiles.put(f, i, zz, tile)

    def load_h(i):
        hy, hz = row(4, i), row(5, i)
        out = dict(hy=hy, hz=hz, hy_x=across.turned(hy, 1), hz_x=across.turned(hz, 1))
        if i in e_rows:
            hx = row(3, i)
            out.update(hx=hx, hx_y=[turn(v, 1, 1) for v in hx], hz_y=[turn(v, 1, 1) for v in hz])
            out.update(hx_z=beneath(hx), hy_z=beneath(hy))
        return out

    def work_e(i, loaded):
        h, before, c = loaded[i], loaded.get(i - 1), c_of(i)
        hy_x = across.pick(h["hy_x"], before["hy_x"] if before else blank, 1)
        hz_x = across.pick(h["hz_x"], before["hz_x"] if before else blank, 1)
        new = {}
        for zz in e_layers:
            curl = (h["hz"][zz] - h["hz_y"][zz]) - (h["hy"][zz] - h["hy_z"][zz])
            new[0, zz] = tiles.get(0, i, zz) + c[zz] * curl
            curl = (h["hx"][zz] - h["hx_z"][zz]) - (h["hz"][zz] - hz_x[zz])
            new[1, zz] = tiles.get(1, i, zz) + c[zz] * curl
            curl = (h["hy"][zz] - hy_x[zz]) - (h["hx"][zz] - h["hx_y"][zz])
            new[2, zz] = tiles.get(2, i, zz) + c[zz] * curl
        for (f, zz), tile in new.items():
            tiles.put(f, i, zz, tile)

    def sweep(rows, load, work):
        loaded = {}

        def want(i):
            if i not in loaded and i in exists:
                loaded[i] = load(i)

        for i in rows:
            for j in (i - 1, i, i + 1):
                if j in rows or j == i + (1 if load is load_e else -1):
                    want(j)
            work(i, loaded)

    sweep(h_rows, load_e, work_h)
    yield
    sweep(e_rows, load_h, work_e)


class Rows:
    def turned(self, values, way):
        return values

    def pick(self, own, other, way):
        return other


class Blocks:
    def __init__(self, groups):
        self.groups = groups

    def turned(self, values, way):
        return [turn(v, way * GROUP, 1) for v in values]

    def pick(self, own, other, way):
        edge = self.groups[3] if way < 0 else self.groups[0]
        return [jnp.where(edge, o, v) for o, v in zip(other, own)]


def spans_inner(n, has_below, has_above):
    last = 7 - n if has_above else 7
    return (n - 1 if has_below else 0, last), (n if has_below else 0, last)


def spans_below(n):
    return (n - 5, n - 2), (n - 4, n - 1)


def spans_above(n):
    return (8 - n, 11 - n), (8 - n, 11 - n)


class Stepper:
    def __init__(self, row_size, main, edge, main_exists, edge_exists, skip_hx):
        gz, row, col = (lax.axis_index(name) for name in ("gz", "row", "col"))
        lane, sub = iota(1), iota(0)
        place, self.group = lane & (GROUP - 1), lane >> 5
        full = jnp.full((8, 128), time_step, jnp.float32)
        self.layer_half = [full] * OWN + [jnp.where((sub >= 4) & (gz == 0), 0.0, full)]
        outside = (place >= 12) & (place < 16) & (col == 0)
        self.edge_half = [jnp.where(outside, 0.0, v) for v in self.layer_half]
        self.lowest = jnp.where(row == 0, 0.0, 1.0) if row_size > 2 else None
        self.main, self.edge, self.skip_hx = main, edge, skip_hx
        self.main_exists, self.edge_exists = main_exists, edge_exists
        self.blocks = Blocks([self.group == r for r in range(4)])

    def masked(self, values, block, span):
        low, high = max(span[0] - 4 * block, 0), min(span[1] - 4 * block, 3)
        if low == 0 and high == 3:
            return values
        mask = (self.group >= low) & (self.group <= high)
        return [jnp.where(mask, v, 0.0) for v in values]

    def main_h(self, i):
        return self.layer_half if self.lowest is None or i >= DEPTH else [v * self.lowest for v in self.layer_half]

    def main_c(self, i):
        return [self.main.get(6, i, zz) for zz in range(CHUNK)]

    def edge_h(self, i, span):
        h = self.edge_half if self.lowest is None or i else [v * self.lowest for v in self.edge_half]
        return self.masked(h, i - 1, span)

    def edge_c(self, i, span):
        return self.masked([self.edge.get(6, i, zz) for zz in range(CHUNK)], i - 1, span)

    def step(self, n, spans):
        def blocks_of(span):
            return [b + 1 for b in range(-1, 3) if span[0] <= 4 * b + 3 and span[1] >= 4 * b]

        layers = range(CHUNK)
        last = range(OWN) if n == STEPS else layers
        parts = []
        for h_span, e_span in spans:
            h_rows = list(range(DEPTH + h_span[0], DEPTH + h_span[1] + 1))
            e_rows = list(range(DEPTH + e_span[0], DEPTH + e_span[1] + 1))
            skip = h_rows[:1] if self.skip_hx and h_span[0] < e_span[0] else []
            if self.main is not None:
                parts.append(
                    leapfrog(self.main, self.main_exists, h_rows, e_rows, Rows(), self.main_h, self.main_c, layers, last, skip)
                )
            if self.edge is None:
                continue
            h_of, c_of = functools.partial(self.edge_h, span=h_span), functools.partial(self.edge_c, span=e_span)
            parts.append(
                leapfrog(
                    self.edge, self.edge_exists, blocks_of(h_span), blocks_of(e_span), self.blocks, h_of, c_of, layers, last, []
                )
            )
        for part in parts:
            next(part)
        for part in parts:
            next(part, None)


def rows_cases(row_size, row, run):
    if row_size == 2:
        pl.when(row == 0)(functools.partial(run, False, True))
        pl.when(row == 1)(functools.partial(run, True, False))
    else:
        run(True, True)


def port_sums(n, reached, prow_ref, weight_ref, ez_ref, edge_ref, sum_ref, add_ref):
    for k in range(PORT_TILE):
        at = prow_ref[0, 0, k]
        total = jnp.zeros((8, 128), jnp.float32)
        for zz in range(OWN):
            if ez_ref is not None:
                total = total + ez_ref[at, zz] * weight_ref[k, 0, zz]
            if edge_ref is not None:
                total = total + edge_ref[at >> 2, zz] * weight_ref[k, 1, zz]
        total = jnp.sum(jnp.where(reached(n, at), total, 0.0), axis=0, keepdims=True)
        if add_ref is not None:
            total = total + add_ref[n - 1, k : k + 1, :]
        sum_ref[n - 1, k : k + 1, :] = total


def finish(fields, b, main, edge, write):
    lane = iota(1)
    place = lane & (GROUP - 1)
    sides = (lane < DEPTH) | (lane >= 128 - DEPTH)

    def first(f):
        tiles = [edge.get(f, b + 1, zz) for zz in range(OWN)]
        turned = [turn(tile, -8, 1) for tile in tiles]
        return [jnp.where(place < 8, tile, other) for tile, other in zip(tiles, turned)]

    def second(f, near):
        turned = {(r, zz): turn(near[zz], -(GROUP * r + 8), 1) for r in range(4) for zz in range(OWN)}
        made = {(r, zz): jnp.where(sides, tile, main.get(f, DEPTH + 4 * b + r, zz)) for (r, zz), tile in turned.items()}
        for (r, zz), tile in made.items():
            write(f, r, zz, tile)

    staged(fields, first, second)


def port_weights(mode_ref, prow_ref, pcol_ref, pmode_ref, weight_ref, strip_ref):
    lane = iota(1)
    for k in range(PORT_TILE):
        strip_ref[k] = jnp.zeros(strip_ref.shape[1:], jnp.float32)
        strip_ref[k, :, 0:PLEN] = mode_ref[pmode_ref[0, 0, k]]
    for k in range(PORT_TILE):
        turned = GROUP * (prow_ref[0, 0, k] & 3)
        at = lane - turned
        for zz in range(OWN):
            tile = pltpu.roll(strip_ref[k, 8 * zz : 8 * zz + 8, :], pcol_ref[0, 0, k], 1)
            weight_ref[k, 0, zz] = jnp.where((lane >= DEPTH) & (lane < 128 - DEPTH), tile, 0.0)
            own = pltpu.roll(tile, turned + 8, 1)
            edge = jnp.where((at >= 4) & (at < 8), own, 0.0)
            weight_ref[k, 1, zz] = jnp.where((at >= 16) & (at < 20), turn(own, 8, 1), edge)


def inner_kernel(
    row_size, elec_ref, magn_ref, mat_ref, z_ref, mode_ref, eps_ref, prow_ref, pcol_ref, pmode_ref, pid_ref,
    e_ref, h_ref, c_ref, sum_ref, weight_ref, state_ref, plain_ref, ext_ref, halo_ref, ez_ref, strip_ref,
):
    gz, row = lax.axis_index("gz"), lax.axis_index("row")
    spread_layers(gz, z_ref, ext_ref)
    for f in range(FIELDS):
        for x in range(ROWS):
            halo_ref[f, x] = ext_ref[f, pl.ds(x, 8, stride=ROWS), :]
    port_weights(mode_ref, prow_ref, pcol_ref, pmode_ref, weight_ref, strip_ref)
    for z in range(LAYERS):
        plain_ref[z] = coefficient(mat_ref[z], eps_ref)
    for f in range(3):
        rows_outside(elec_ref.reshape(3 * LAYERS * ROWS, 128), f, state_ref, f)
        rows_outside(magn_ref.reshape(3 * LAYERS * ROWS, 128), f, state_ref, f + 3)
    rows_outside(plain_ref.reshape(LAYERS * ROWS, 128), 0, state_ref, 6)

    def first(f, i, zz):
        return halo_ref[f, i - DEPTH] if zz == OWN else state_ref[f, i - DEPTH, zz]

    def run(has_below, has_above):
        main = Tiles(first, ez_ref, DEPTH)
        stepper = Stepper(row_size, main, None, range(4, 12), (), False)

        def reached(n, at):
            low, high = spans_inner(n, has_below, has_above)[1]
            return (at >= low) & (at <= high)

        for n in range(1, STEPS + 1):
            stepper.step(n, [spans_inner(n, has_below, has_above)])
            port_sums(n, reached, prow_ref, weight_ref, ez_ref, None, sum_ref, None)
        for i in range(ROWS):
            for zz in range(CHUNK):
                for f in range(6):
                    (e_ref, h_ref)[f // 3][f % 3, i, zz] = main.get(f, DEPTH + i, zz)
                c_ref[i, zz] = main.get(6, DEPTH + i, zz)

    rows_cases(row_size, row, run)


def rim_kernel(
    row_size, z_ref, own_ref, even_ref, odd_ref, layer_ref, e_in, h_in, sum_in, weight_ref, prow_ref,
    edge_e_ref, edge_h_ref, edge_c_ref, done_ref, sum_ref, ext_ref, ez_ref,
):
    gz, row = lax.axis_index("gz"), lax.axis_index("row")
    place = iota(1) & (GROUP - 1)
    groups = lane_groups()
    valid = (iota(0) < 4) == (gz == 0)
    spread_layers(gz, z_ref, ext_ref)
    low_of, high_of = low_and_high(even_ref, odd_ref)
    low_z, high_z = low_and_high(layer_ref.at[0], layer_ref.at[1])
    joined = {}

    def first(at):
        b, zz = at
        if zz < OWN:
            return [own_ref[f, b, zz] for f in range(FIELDS)], turn_sides(low_of(b, zz), high_of(b, zz))
        rows = [[ext_ref[f, pl.ds(4 * b + r, 8, stride=ROWS), :] for r in range(4)] for f in range(FIELDS)]
        sides = turn_sides(*(jnp.where(valid, side(b), 0.0) for side in (low_z, high_z)))
        return gather_edges(rows, groups), sides

    def second(at, made):
        for f, tile in enumerate(edge_tiles(*made, place)):
            joined[f, at[0] + 1, at[1]] = tile

    staged([(b, zz) for b in range(2) for zz in range(CHUNK)], first, second)

    def run(has_below, has_above):
        main = Tiles(lambda f, i, zz: (e_in, h_in)[f // 3][f % 3, i - DEPTH, zz], None, DEPTH)
        edge = Tiles(lambda f, i, zz: joined[f, i, zz], ez_ref, 1)
        stepper = Stepper(row_size, None, edge, (), (1, 2), False)

        def reached(n, at):
            low, high = spans_inner(n, has_below, has_above)[1]
            return (at >= low) & (at <= high)

        for n in range(1, STEPS + 1):
            stepper.step(n, [spans_inner(n, has_below, has_above)])
            port_sums(n, reached, prow_ref, weight_ref, None, ez_ref, sum_ref, sum_in)
        for i in range(2):
            for zz in range(CHUNK):
                for f in range(6):
                    (edge_e_ref, edge_h_ref)[f // 3][f % 3, i, zz] = edge.get(f, 1 + i, zz)
                edge_c_ref[i, zz] = edge.get(6, 1 + i, zz)
        if has_below != has_above:

            def write(f, r, zz, tile):
                done_ref[f, r, zz] = tile

            finish(range(6), 0 if has_above else 1, main, edge, write)

    rows_cases(row_size, row, run)


def outer_spans(n, has_below, has_above):
    return ([spans_below(n)] if has_below else []) + ([spans_above(n)] if has_above else [])


def outer_reached(has_below, has_above):
    def reached(n, at):
        parts = [(at >= span[0]) & (at <= span[1]) for _, span in outer_spans(n, has_below, has_above)]
        return functools.reduce(lambda a, b: a | b, parts)

    return reached


def outer_main_kernel(row_size, prow_ref, e_in, h_in, c_in, weight_ref, sum_in, *rest):
    n_x = 1 if row_size == 2 else 2
    x_refs, ext_refs = rest[:n_x], rest[n_x : 2 * n_x]
    fixed_ref, own_ref, sum_ref, ez_ref = rest[2 * n_x :]
    gz, row = lax.axis_index("gz"), lax.axis_index("row")
    groups = lane_groups()
    valid = (iota(0) < 4) == (gz == 0)

    def first_main(f, i, zz):
        if f == 6:
            return c_in[i - DEPTH, zz]
        return e_in[f, i - DEPTH, zz] if f < 3 else h_in[f - 3, i - DEPTH, zz]

    def run(has_below, has_above):
        main = Tiles(first_main, ez_ref, DEPTH)

        def halo_rows(planes, slot, offset, b):
            got = {}
            packed = [ext_refs[slot][i] for i in range(PAIRS)]
            packed += [turn(tile, 4, 0) for tile in packed[: len(planes) - PAIRS]]
            for i, (f, x) in enumerate(planes):
                tiles = [x_refs[slot][i, zz] for zz in range(OWN)] + [jnp.where(valid, packed[i], 0.0)]
                for zz in range(CHUNK):
                    main.put(f, DEPTH + x + offset, zz, tiles[zz])
                    got[f, x + offset - 4 * b, zz] = tiles[zz]

            def first(zz):
                return gather_edges([[got.get((f, r, zz)) for r in range(4)] for f in range(FIELDS)], groups)

            def second(zz, owns):
                for f, tile in enumerate(owns):
                    own_ref[slot, f, zz] = tile

            staged(range(CHUNK), first, second)

        if has_below:
            halo_rows(UP_PLANES, 0, -ROWS, -1)
        if has_above:
            halo_rows(DOWN_PLANES, n_x - 1, ROWS, 2)
        rows = range(0 if has_below else 4, 16 if has_above else 12)
        stepper = Stepper(row_size, main, None, rows, (), True)
        for n in range(1, STEPS + 1):
            stepper.step(n, outer_spans(n, has_below, has_above))
            port_sums(n, outer_reached(has_below, has_above), prow_ref, weight_ref, ez_ref, None, sum_ref, sum_in)
        for b in range(2):
            if has_below and has_above or b == (1 if has_above else 0):
                for f in range(6):
                    for x in range(4 * b, 4 * b + 4):
                        for zz in range(OWN):
                            fixed_ref[f, x, zz] = main.get(f, DEPTH + x, zz)

    rows_cases(row_size, row, run)


def outer_edge_kernel(
    row_size, ports_each, prow_ref, pid_ref, edge_e_in, edge_h_in, edge_c_in, done_ref, weight_ref, fixed_ref, own_ref, sum_in,
    *rest,
):
    n_x = 1 if row_size == 2 else 2
    corner_refs = rest[:n_x]
    eout_hbm, hout_hbm, term_ref, ez_ref, sum_ref, turned_ref, out_ref, sems = rest[n_x:]
    row = lax.axis_index("row")
    lane, sub = iota(1), iota(0)
    place = lane & (GROUP - 1)
    zeros = jnp.zeros((8, 128), jnp.float32)

    def first_edge(f, i, zz):
        if f == 6:
            return edge_c_in[i - 1, zz]
        return edge_e_in[f, i - 1, zz] if f < 3 else edge_h_in[f - 3, i - 1, zz]

    def run(has_below, has_above):
        main = Tiles(lambda f, i, zz: fixed_ref[f, i - DEPTH, zz], None, DEPTH)
        edge = Tiles(first_edge, ez_ref, 1)

        def halo_block(slot, b):
            def first(zz):
                owns = [own_ref[slot, f, zz] for f in range(FIELDS)]
                return owns, turn_sides(corner_refs[slot][zz], corner_refs[slot][CHUNK + zz])

            def second(zz, made):
                for f, tile in enumerate(edge_tiles(*made, place)):
                    edge.put(f, 1 + b, zz, tile)

            staged(range(CHUNK), first, second)

        if has_below:
            halo_block(0, -1)
        if has_above:
            halo_block(n_x - 1, 2)
        blocks = range(0 if has_below else 1, 4 if has_above else 3)
        stepper = Stepper(row_size, None, edge, (), blocks, True)
        for n in range(1, STEPS + 1):
            stepper.step(n, outer_spans(n, has_below, has_above))
            port_sums(n, outer_reached(has_below, has_above), prow_ref, weight_ref, None, ez_ref, sum_ref, sum_in)

        def write(f, r, zz, tile, b):
            turned_ref[f, 4 * b + r, 8 * zz : 8 * zz + 8, :] = tile

        for b in range(2):
            put = functools.partial(write, b=b)
            if has_below and has_above or b == (1 if has_above else 0):
                finish(range(6), b, main, edge, put)
            else:
                for f in range(6):
                    for r in range(4):
                        for zz in range(OWN):
                            put(f, r, zz, done_ref[f, r, zz])

    rows_cases(row_size, row, run)

    copies = []
    flat = turned_ref.reshape(6 * ROWS * LAYERS, 128)
    for part, dest in ((0, eout_hbm), (1, hout_hbm)):
        for f in range(3 * part, 3 * part + 3):
            for z in range(LAYERS):
                out_ref[f, z] = flat[pl.ds(f * ROWS * LAYERS + z, ROWS, stride=LAYERS), :]
        copies.append(pltpu.make_async_copy(out_ref.at[pl.ds(3 * part, 3)], dest, sems.at[part]))
        copies[-1].start()
    basis = zeros
    for n in range(STEPS):
        for f in range(2 * FREQ):
            basis = jnp.where((sub == n) & (lane == f), float(BASIS[n, f]), basis)
    transform = zeros
    for n in range(STEPS):
        sampled = jnp.sum(sum_ref[n], axis=1, keepdims=True)
        transform = transform + sampled * basis[n : n + 1, :]
    term_ref[...] = jnp.zeros(term_ref.shape, jnp.float32)
    for k in range(PORT_TILE):
        port = pid_ref[0, 0, k]
        term_ref[port // ports_each, pl.ds(port % ports_each, 1), :] = transform[k : k + 1, : 2 * FREQ]
    for copy in copies:
        copy.wait()


def shifted(block, axis, size, distance):
    route = [(i - distance, i) for i in range(size) if 0 <= i - distance < size]
    return lax.ppermute(block, axis, route)


def swapped(block, axis, size, start=0):
    pairs = [(i, i + 1) for i in range(start, size - 1, 2)]
    return lax.ppermute(block, axis, pairs + [(j, i) for i, j in pairs])


def solution(mesh):
    sizes = dict(mesh.shape)
    row_size, col_size, gz_size = sizes["row"], sizes["col"], sizes["gz"]
    n_x = 1 if row_size == 2 else 2

    def across_rows(blocks):
        if row_size == 2:
            return (swapped(blocks[0], "row", 2),)
        return (shifted(blocks[0], "row", row_size, 1), shifted(blocks[1], "row", row_size, -1))

    def per_device(
        electric, magnetic, material, eps_table, mode_table, port_row, port_col, port_mode, port_ids
    ):
        f32 = jnp.float32

        def array(*shape):
            return jax.ShapeDtypeStruct(shape, f32)

        def scratch(*shape):
            return pltpu.VMEM(shape, f32)

        z_send, own, even_send, odd_send, *x_send = pl.pallas_call(
            functools.partial(pack_kernel, row_size),
            out_shape=[
                array(FIELDS, DEPTH, ROWS, 128),
                array(FIELDS, 2, OWN, 8, 128),
                array(2, OWN, 8, 128),
                array(2, OWN, 8, 128),
            ]
            + [array(PLANES, OWN, 8, 128)] * n_x,
            in_specs=[HBM] * 4,
            out_specs=[VMEM] * (4 + n_x),
            scratch_shapes=[
                scratch(FIELDS, ROWS, OWN, 8, 128),
                scratch(FIELDS, LAYERS, ROWS, 128),
                pltpu.SMEM(eps_table.shape, f32),
                pltpu.VMEM(material.shape, jnp.int32),
                pltpu.SemaphoreType.DMA((4,)),
            ],
            name="pack",
        )(eps_table, electric, magnetic, material)
        x_halo = across_rows(x_send)
        even = swapped(even_send, "col", col_size)
        odd = swapped(odd_send, "col", col_size, 1)
        z_halo = swapped(z_send, "gz", gz_size)
        ext_send = pl.pallas_call(
            functools.partial(layer_kernel, row_size),
            out_shape=[array(PAIRS, 8, 128)] * n_x,
            in_specs=[VMEM],
            out_specs=[VMEM] * n_x,
            scratch_shapes=[scratch(FIELDS, 8 * ROWS, 128)],
            compiler_params=PARAMS,
            name="layers",
        )(z_halo)
        ext_halo = across_rows(ext_send)
        e_now, h_now, c_now, sums, weights = pl.pallas_call(
            functools.partial(inner_kernel, row_size),
            out_shape=[
                array(3, ROWS, CHUNK, 8, 128),
                array(3, ROWS, CHUNK, 8, 128),
                array(ROWS, CHUNK, 8, 128),
                array(STEPS, 8, 128),
                array(PORT_TILE, 2, OWN, 8, 128),
            ],
            in_specs=[VMEM] * 5 + [SMEM] * 5,
            out_specs=[VMEM] * 5,
            scratch_shapes=[
                scratch(FIELDS, ROWS, OWN, 8, 128),
                scratch(LAYERS, ROWS, 128),
                scratch(FIELDS, 8 * ROWS, 128),
                scratch(FIELDS, ROWS, 8, 128),
                scratch(ROWS, OWN, 8, 128),
                scratch(PORT_TILE, LAYERS, 128),
            ],
            compiler_params=PARAMS,
            cost_estimate=pl.CostEstimate(flops=5_000_000, bytes_accessed=10_000_000, transcendentals=0),
            name="inner",
        )(electric, magnetic, material, z_halo, mode_table, eps_table, port_row, port_col, port_mode, port_ids)
        layer_send = pl.pallas_call(
            layer_edge_kernel,
            out_shape=array(2, 2, 8, 128),
            in_specs=[VMEM] * 2 + [pl.BlockSpec(memory_space=pl.ANY)],
            out_specs=VMEM,
            compiler_params=PARAMS,
            name="layer_edges",
        )(even, odd, sums)
        layer_halo = swapped(layer_send, "gz", gz_size)
        corner_send = pl.pallas_call(
            functools.partial(corner_kernel, row_size),
            out_shape=[array(2 * CHUNK, 8, 128)] * n_x,
            in_specs=[VMEM] * 3,
            out_specs=[VMEM] * n_x,
            compiler_params=PARAMS,
            name="corners",
        )(even, odd, layer_halo)
        corner = across_rows(corner_send)
        edges = pl.pallas_call(
            functools.partial(rim_kernel, row_size),
            out_shape=[
                array(3, 2, CHUNK, 8, 128),
                array(3, 2, CHUNK, 8, 128),
                array(2, CHUNK, 8, 128),
                array(6, 4, OWN, 8, 128),
                array(STEPS, 8, 128),
            ],
            in_specs=[VMEM] * 9 + [SMEM],
            out_specs=[VMEM] * 5,
            scratch_shapes=[scratch(FIELDS, 8 * ROWS, 128), scratch(2, OWN, 8, 128)],
            compiler_params=PARAMS,
            name="rim",
        )(z_halo, own, even, odd, layer_halo, e_now, h_now, sums, weights, port_row)
        devices = col_size * row_size * gz_size
        ports_each = PORT_TILE * col_size * row_size // devices
        edge_e, edge_h, edge_c, done, sums = edges
        fixed, halo_own, sums = pl.pallas_call(
            functools.partial(outer_main_kernel, row_size),
            out_shape=[
                array(6, ROWS, OWN, 8, 128),
                array(n_x, FIELDS, CHUNK, 8, 128),
                array(STEPS, 8, 128),
            ],
            in_specs=[SMEM] + [VMEM] * (5 + 2 * n_x),
            out_specs=[VMEM] * 3,
            scratch_shapes=[scratch(ROWS, OWN, 8, 128)],
            compiler_params=PARAMS,
            name="outer_main",
        )(port_row, e_now, h_now, c_now, weights, sums, *x_halo, *ext_halo)
        electric_out, magnetic_out, term = pl.pallas_call(
            functools.partial(outer_edge_kernel, row_size, ports_each),
            out_shape=[array(3, LAYERS, ROWS, 128)] * 2 + [array(devices, ports_each, 2 * FREQ)],
            in_specs=[SMEM] * 2 + [VMEM] * (8 + n_x),
            out_specs=[HBM, HBM, VMEM],
            scratch_shapes=[
                scratch(2, OWN, 8, 128),
                scratch(STEPS, 8, 128),
                scratch(6, ROWS, LAYERS, 128),
                scratch(6, LAYERS, ROWS, 128),
                pltpu.SemaphoreType.DMA((2,)),
            ],
            compiler_params=PARAMS,
            name="outer_edge",
        )(port_row, port_ids, edge_e, edge_h, edge_c, done, weights, fixed, halo_own, sums, *corner)
        terms = lax.all_to_all(term, ("col", "row", "gz"), 0, 0, tiled=True)
        return (
            electric_out,
            magnetic_out,
            jnp.sum(terms, axis=0),
        )

    in_specs = (
        P(None, "gz", "row", ("grp", "col")),
        P(None, "gz", "row", ("grp", "col")),
        P("gz", "row", ("grp", "col")),
        P(),
        P(None, "gz", None),
        P(("grp", "row"), "col", None),
        P(("grp", "row"), "col", None),
        P(("grp", "row"), "col", None),
        P(("grp", "row"), "col", None),
    )
    out_specs = (
        P(None, "gz", "row", ("grp", "col")),
        P(None, "gz", "row", ("grp", "col")),
        P(("grp", "col", "row", "gz"), None),
    )
    return jax.shard_map(
        per_device, mesh=mesh, in_specs=in_specs, out_specs=out_specs, check_vma=False
    )
```

```python
import functools

import jax
import jax.numpy as jnp
import numpy as np
from jax import lax
from jax.experimental import pallas as pl
from jax.experimental.pallas import tpu as pltpu
from jax.sharding import PartitionSpec as P

STEPS = 4
FREQ = 8
MATS = 8
PLEN = 64
PORT_TILE = 4
FIELDS = 7
DEPTH = STEPS
ROWS = 8
LAYERS = 32
OWN = 4
CHUNK = 5
GROUP = 32

time_step = 0.5

UP_PLANES = [(f, 4) for f in (0, 1, 2, 4, 5)] + [(f, x) for x in (5, 6, 7) for f in range(FIELDS)]
DOWN_PLANES = [(f, x) for x in (0, 1, 2) for f in range(FIELDS)] + [(1, 3), (2, 3)]
PLANES = max(len(UP_PLANES), len(DOWN_PLANES))
PAIRS = (PLANES + 1) // 2

VMEM = pl.BlockSpec(memory_space=pltpu.VMEM)
SMEM = pl.BlockSpec(memory_space=pltpu.SMEM)
HBM = pl.BlockSpec(memory_space=pltpu.HBM)
ANY = pl.BlockSpec(memory_space=pl.ANY)
PARAMS = pltpu.CompilerParams(vmem_limit_bytes=16 * 1024 * 1024)


def dft_basis():
    times = (np.arange(STEPS) + 1.0) * time_step
    omegas = np.pi * (np.arange(FREQ) + 1.0) / FREQ
    angle = times[:, None] * omegas[None, :]
    return np.concatenate([np.cos(angle), -np.sin(angle)], axis=1)


BASIS = dft_basis()


def iota(axis):
    return lax.broadcasted_iota(jnp.int32, (8, 128), axis)


def turn(tile, shift, axis):
    return pltpu.roll(tile, shift % tile.shape[axis], axis)


def directions(row_size, body):
    if row_size == 2:
        row = lax.axis_index("row")
        pl.when(row == 0)(functools.partial(body, True, 0))
        pl.when(row == 1)(functools.partial(body, False, 0))
    else:
        body(True, 0)
        body(False, 1)


def coefficient(material, eps_ref):
    eps = jnp.full((8, 128), eps_ref[0], jnp.float32)
    for which in range(1, MATS):
        eps = jnp.where(material == which, eps_ref[which], eps)
    return time_step * (1.0 / eps)


def rows_outside(flat, f, state_ref, at):
    for x in range(ROWS):
        state_ref[at, x] = flat[pl.ds(f * LAYERS * ROWS + x, LAYERS, stride=ROWS), :].reshape(OWN, 8, 128)


def pack_kernel(row_size, eps_hbm, elec_hbm, magn_hbm, mat_hbm, z_ref, own_ref, even_ref, odd_ref, *rest):
    x_refs, (state_ref, main_ref, eps_ref, mat_ref, sems) = rest[:-5], rest[-5:]
    copies = [pltpu.make_async_copy(eps_hbm, eps_ref, sems.at[0]), pltpu.make_async_copy(mat_hbm, mat_ref, sems.at[1])]
    copies.append(pltpu.make_async_copy(elec_hbm, main_ref.at[pl.ds(0, 3)], sems.at[2]))
    copies.append(pltpu.make_async_copy(magn_hbm, main_ref.at[pl.ds(3, 3)], sems.at[3]))
    for copy in copies:
        copy.start()
    copies[0].wait()
    copies[1].wait()
    for z in range(LAYERS):
        main_ref[6, z] = coefficient(mat_ref[z], eps_ref)
    copies[2].wait()
    copies[3].wait()
    start = jnp.where(lax.axis_index("gz") == 0, LAYERS - DEPTH, 0)
    for f in range(FIELDS):
        z_ref[f] = main_ref[f, pl.ds(start, DEPTH)]
    flat = main_ref.reshape(FIELDS * LAYERS * ROWS, 128)
    for f in range(FIELDS):
        rows_outside(flat, f, state_ref, f)

    def send(up, slot):
        for i, (f, x) in enumerate(UP_PLANES if up else DOWN_PLANES):
            x_refs[slot][i] = state_ref[f, x]

    directions(row_size, send)
    pack_edges(state_ref, own_ref, even_ref, odd_ref)


def lane_groups():
    group = iota(1) >> 5
    return [jnp.where(group == r, 1.0, 0.0) for r in range(4)]


def gather_edges(rows_of, groups):
    moved = [[tile if tile is None else turn(tile, GROUP * r + 8, 1) for r, tile in enumerate(rows)] for rows in rows_of]
    out = []
    for rows in moved:
        parts = [tile * groups[r] for r, tile in enumerate(rows) if tile is not None]
        out.append(functools.reduce(lambda a, b: a + b, parts) if parts else jnp.zeros((8, 128), jnp.float32))
    return out


def staged(items, first, second):
    waiting = None
    for item in items:
        made = first(item)
        if waiting is not None:
            second(*waiting)
        waiting = (item, made)
    second(*waiting)


def pack_edges(state_ref, own_ref, even_ref, odd_ref):
    lane = iota(1)
    groups = lane_groups()
    slots = [jnp.where(((lane & (GROUP - 1)) >> 2) == f, 1.0, 0.0) for f in range(FIELDS)]
    even = (lax.axis_index("col") & 1) == 0

    def first(at):
        b, zz = at
        return gather_edges([[state_ref[f, 4 * b + r, zz] for r in range(4)] for f in range(FIELDS)], groups)

    def second(at, owns):
        b, zz = at
        ups = [turn(own, DEPTH * f - 4, 1) for f, own in enumerate(owns)]
        downs = [turn(own, DEPTH * f - 8, 1) for f, own in enumerate(owns)]
        up = functools.reduce(lambda a, b: a + b, [v * m for v, m in zip(ups, slots)])
        down = functools.reduce(lambda a, b: a + b, [v * m for v, m in zip(downs, slots)])
        for f in range(FIELDS):
            own_ref[f, b, zz] = owns[f]
        even_ref[b, zz] = jnp.where(even, up, down)
        odd_ref[b, zz] = jnp.where(even, down, up)

    staged([(b, zz) for b in range(2) for zz in range(OWN)], first, second)


def low_and_high(even_ref, odd_ref):
    even = (lax.axis_index("col") & 1) == 0

    def low(*at):
        return jnp.where(even, odd_ref[at], even_ref[at])

    def high(*at):
        return jnp.where(even, even_ref[at], odd_ref[at])

    return low, high


def layer_edge_kernel(even_ref, odd_ref, inner_ref, out_ref):
    gz = lax.axis_index("gz")
    for i, ref in enumerate((even_ref, odd_ref)):
        for b in range(2):
            out_ref[i, b] = jnp.where(gz == 0, ref[b, OWN - 1], ref[b, 0])


def spread_layers(gz, z_ref, ext_ref):
    for f in range(FIELDS):
        halo = z_ref[f].reshape(DEPTH * ROWS, 128)
        nothing = jnp.zeros_like(halo)
        ext_ref[f, : DEPTH * ROWS] = jnp.where(gz == 0, halo, nothing)
        ext_ref[f, DEPTH * ROWS :] = jnp.where(gz == 0, nothing, halo)


def corner_kernel(row_size, weight_ref, z_ref, even_ref, odd_ref, layer_ref, *rest):
    x_refs, ext_ref = rest[:-1], rest[-1]
    gz = lax.axis_index("gz")
    valid = (iota(0) < 4) == (gz == 0)
    spread_layers(gz, z_ref, ext_ref)
    low, high = low_and_high(even_ref, odd_ref)
    low_z, high_z = low_and_high(layer_ref.at[0], layer_ref.at[1])

    def send(up, slot):
        planes = UP_PLANES if up else DOWN_PLANES

        def tile(i):
            f, x = planes[i]
            return ext_ref[f, pl.ds(x, 8, stride=ROWS), :]

        for i in range(PAIRS):
            pair = tile(i)
            if i + PAIRS < len(planes):
                pair = pair + turn(tile(i + PAIRS), 4, 0)
            x_refs[slot][i] = pair
        b = 1 if up else 0
        for zz in range(OWN):
            x_refs[slot][PAIRS + zz] = low(b, zz)
            x_refs[slot][PAIRS + CHUNK + zz] = high(b, zz)
        x_refs[slot][PAIRS + OWN] = jnp.where(valid, low_z(b), 0.0)
        x_refs[slot][PAIRS + CHUNK + OWN] = jnp.where(valid, high_z(b), 0.0)

    directions(row_size, send)


def turn_sides(low, high):
    lows = [turn(low, 12 - DEPTH * f, 1) for f in range(FIELDS)]
    return lows, [turn(high, 8 - DEPTH * f, 1) for f in range(FIELDS)]


def edge_tiles(owns, sides, place):
    turned = [turn(own, 8, 1) for own in owns]
    out = []
    for own, own_turned, low, high in zip(owns, turned, *sides):
        tile = jnp.where(place < 16, low, own_turned)
        tile = jnp.where(place < 12, high, tile)
        out.append(jnp.where(place < 8, own, tile))
    return out


class Tiles:
    def __init__(self, first, ez_ref, shift):
        self.first, self.ez_ref, self.shift = first, ez_ref, shift
        self.values = {}

    def get(self, f, i, zz):
        value = self.values.get((f, i, zz))
        return self.first(f, i, zz) if value is None else value

    def put(self, f, i, zz, tile):
        self.values[f, i, zz] = tile
        at = i - self.shift
        if f == 2 and zz < OWN and self.ez_ref is not None and 0 <= at < self.ez_ref.shape[0]:
            self.ez_ref[at, zz] = tile


def leapfrog(tiles, exists, h_rows, e_rows, across, h_of, c_of, h_layers, e_layers, skip_hx):
    sub = iota(0)
    every = range(CHUNK)
    blank = [jnp.zeros((8, 128), jnp.float32)] * CHUNK

    def above(values):
        turned = [turn(v, -1, 0) for v in values]
        return [jnp.where(sub == 7, turned[(zz + 1) % CHUNK], turned[zz]) for zz in every]

    def beneath(values):
        turned = [turn(v, 1, 0) for v in values]
        return [jnp.where(sub == 0, turned[zz - 1], turned[zz]) for zz in every]

    def row(f, i):
        return [tiles.get(f, i, zz) for zz in every]

    def load_e(i):
        ey, ez = row(1, i), row(2, i)
        out = dict(ey=ey, ez=ez, ey_x=across.turned(ey, -1), ez_x=across.turned(ez, -1))
        if i in h_rows:
            ex = row(0, i)
            out.update(ex=ex, ex_y=[turn(v, -1, 1) for v in ex], ex_z=above(ex))
            if i not in skip_hx:
                out.update(ez_y=[turn(v, -1, 1) for v in ez], ey_z=above(ey))
        return out

    def work_h(i, loaded):
        e, after, h = loaded[i], loaded.get(i + 1), h_of(i)
        ey_x = across.pick(e["ey_x"], after["ey_x"] if after else blank, -1)
        ez_x = across.pick(e["ez_x"], after["ez_x"] if after else blank, -1)
        new = {}
        for zz in h_layers:
            if i not in skip_hx:
                curl = (e["ez_y"][zz] - e["ez"][zz]) - (e["ey_z"][zz] - e["ey"][zz])
                new[3, zz] = tiles.get(3, i, zz) - h[zz] * curl
            curl = (e["ex_z"][zz] - e["ex"][zz]) - (ez_x[zz] - e["ez"][zz])
            new[4, zz] = tiles.get(4, i, zz) - h[zz] * curl
            curl = (ey_x[zz] - e["ey"][zz]) - (e["ex_y"][zz] - e["ex"][zz])
            new[5, zz] = tiles.get(5, i, zz) - h[zz] * curl
        for (f, zz), tile in new.items():
            tiles.put(f, i, zz, tile)

    def load_h(i):
        hy, hz = row(4, i), row(5, i)
        out = dict(hy=hy, hz=hz, hy_x=across.turned(hy, 1), hz_x=across.turned(hz, 1))
        if i in e_rows:
            hx = row(3, i)
            out.update(hx=hx, hx_y=[turn(v, 1, 1) for v in hx], hz_y=[turn(v, 1, 1) for v in hz])
            out.update(hx_z=beneath(hx), hy_z=beneath(hy))
        return out

    def work_e(i, loaded):
        h, before, c = loaded[i], loaded.get(i - 1), c_of(i)
        hy_x = across.pick(h["hy_x"], before["hy_x"] if before else blank, 1)
        hz_x = across.pick(h["hz_x"], before["hz_x"] if before else blank, 1)
        new = {}
        for zz in e_layers:
            curl = (h["hz"][zz] - h["hz_y"][zz]) - (h["hy"][zz] - h["hy_z"][zz])
            new[0, zz] = tiles.get(0, i, zz) + c[zz] * curl
            curl = (h["hx"][zz] - h["hx_z"][zz]) - (h["hz"][zz] - hz_x[zz])
            new[1, zz] = tiles.get(1, i, zz) + c[zz] * curl
            curl = (h["hy"][zz] - hy_x[zz]) - (h["hx"][zz] - h["hx_y"][zz])
            new[2, zz] = tiles.get(2, i, zz) + c[zz] * curl
        for (f, zz), tile in new.items():
            tiles.put(f, i, zz, tile)

    def sweep(rows, load, work):
        loaded = {}

        def want(i):
            if i not in loaded and i in exists:
                loaded[i] = load(i)

        for i in rows:
            for j in (i - 1, i, i + 1):
                if j in rows or j == i + (1 if load is load_e else -1):
                    want(j)
            work(i, loaded)

    sweep(h_rows, load_e, work_h)
    yield
    sweep(e_rows, load_h, work_e)


class Rows:
    def turned(self, values, way):
        return values

    def pick(self, own, other, way):
        return other


class Blocks:
    def __init__(self, groups):
        self.groups = groups

    def turned(self, values, way):
        return [turn(v, way * GROUP, 1) for v in values]

    def pick(self, own, other, way):
        edge = self.groups[3] if way < 0 else self.groups[0]
        return [jnp.where(edge, o, v) for o, v in zip(other, own)]


def spans_inner(n, has_below, has_above):
    last = 7 - n if has_above else 7
    return (n - 1 if has_below else 0, last), (n if has_below else 0, last)


def spans_below(n):
    return (n - 5, n - 2), (n - 4, n - 1)


def spans_above(n):
    return (8 - n, 11 - n), (8 - n, 11 - n)


class Stepper:
    def __init__(self, row_size, main, edge, main_exists, edge_exists, skip_hx):
        gz, row, col = (lax.axis_index(name) for name in ("gz", "row", "col"))
        lane, sub = iota(1), iota(0)
        place, self.group = lane & (GROUP - 1), lane >> 5
        full = jnp.full((8, 128), time_step, jnp.float32)
        self.layer_half = [full] * OWN + [jnp.where((sub >= 4) & (gz == 0), 0.0, full)]
        outside = (place >= 12) & (place < 16) & (col == 0)
        self.edge_half = [jnp.where(outside, 0.0, v) for v in self.layer_half]
        self.lowest = jnp.where(row == 0, 0.0, 1.0) if row_size > 2 else None
        self.main, self.edge, self.skip_hx = main, edge, skip_hx
        self.main_exists, self.edge_exists = main_exists, edge_exists
        self.blocks = Blocks([self.group == r for r in range(4)])

    def masked(self, values, block, span):
        low, high = max(span[0] - 4 * block, 0), min(span[1] - 4 * block, 3)
        if low == 0 and high == 3:
            return values
        mask = (self.group >= low) & (self.group <= high)
        return [jnp.where(mask, v, 0.0) for v in values]

    def main_h(self, i):
        return self.layer_half if self.lowest is None or i >= DEPTH else [v * self.lowest for v in self.layer_half]

    def main_c(self, i):
        return [self.main.get(6, i, zz) for zz in range(CHUNK)]

    def edge_h(self, i, span):
        h = self.edge_half if self.lowest is None or i else [v * self.lowest for v in self.edge_half]
        return self.masked(h, i - 1, span)

    def edge_c(self, i, span):
        return self.masked([self.edge.get(6, i, zz) for zz in range(CHUNK)], i - 1, span)

    def step(self, n, spans):
        def blocks_of(span):
            return [b + 1 for b in range(-1, 3) if span[0] <= 4 * b + 3 and span[1] >= 4 * b]

        layers = range(CHUNK)
        last = range(OWN) if n == STEPS else layers
        parts = []
        for h_span, e_span in spans:
            h_rows = list(range(DEPTH + h_span[0], DEPTH + h_span[1] + 1))
            e_rows = list(range(DEPTH + e_span[0], DEPTH + e_span[1] + 1))
            skip = h_rows[:1] if self.skip_hx and h_span[0] < e_span[0] else []
            if self.main is not None:
                parts.append(
                    leapfrog(self.main, self.main_exists, h_rows, e_rows, Rows(), self.main_h, self.main_c, layers, last, skip)
                )
            if self.edge is None:
                continue
            h_of, c_of = functools.partial(self.edge_h, span=h_span), functools.partial(self.edge_c, span=e_span)
            parts.append(
                leapfrog(
                    self.edge, self.edge_exists, blocks_of(h_span), blocks_of(e_span), self.blocks, h_of, c_of, layers, last, []
                )
            )
        for part in parts:
            next(part)
        for part in parts:
            next(part, None)


def rows_cases(row_size, row, run):
    if row_size == 2:
        pl.when(row == 0)(functools.partial(run, False, True))
        pl.when(row == 1)(functools.partial(run, True, False))
    else:
        run(True, True)


def port_sums(n, reached, prow_ref, weight_ref, ez_ref, edge_ref, sum_ref, add_ref):
    for k in range(PORT_TILE):
        at = prow_ref[0, 0, k]
        total = jnp.zeros((8, 128), jnp.float32)
        for zz in range(OWN):
            if ez_ref is not None:
                total = total + ez_ref[at, zz] * weight_ref[k, 0, zz]
            if edge_ref is not None:
                total = total + edge_ref[at >> 2, zz] * weight_ref[k, 1, zz]
        total = jnp.sum(jnp.where(reached(n, at), total, 0.0), axis=0, keepdims=True)
        if add_ref is not None:
            total = total + add_ref[n - 1, k : k + 1, :]
        sum_ref[n - 1, k : k + 1, :] = total


def finish(fields, b, main, edge, write):
    lane = iota(1)
    place = lane & (GROUP - 1)
    sides = (lane < DEPTH) | (lane >= 128 - DEPTH)

    def first(f):
        tiles = [edge.get(f, b + 1, zz) for zz in range(OWN)]
        turned = [turn(tile, -8, 1) for tile in tiles]
        return [jnp.where(place < 8, tile, other) for tile, other in zip(tiles, turned)]

    def second(f, near):
        turned = {(r, zz): turn(near[zz], -(GROUP * r + 8), 1) for r in range(4) for zz in range(OWN)}
        made = {(r, zz): jnp.where(sides, tile, main.get(f, DEPTH + 4 * b + r, zz)) for (r, zz), tile in turned.items()}
        for (r, zz), tile in made.items():
            write(f, r, zz, tile)

    staged(fields, first, second)


def weight_kernel(mode_ref, prow_ref, pcol_ref, pmode_ref, pid_ref, order_ref, weight_ref, strip_ref):
    lane = iota(1)
    for k in range(PORT_TILE):
        strip_ref[k] = jnp.zeros(strip_ref.shape[1:], jnp.float32)
        strip_ref[k, :, 0:PLEN] = mode_ref[pmode_ref[0, 0, k]]
    for k in range(PORT_TILE):
        turned = GROUP * (prow_ref[0, 0, k] & 3)
        at = lane - turned
        for zz in range(OWN):
            tile = pltpu.roll(strip_ref[k, 8 * zz : 8 * zz + 8, :], pcol_ref[0, 0, k], 1)
            weight_ref[k, 0, zz] = jnp.where((lane >= DEPTH) & (lane < 128 - DEPTH), tile, 0.0)
            own = pltpu.roll(tile, turned + 8, 1)
            edge = jnp.where((at >= 4) & (at < 8), own, 0.0)
            weight_ref[k, 1, zz] = jnp.where((at >= 16) & (at < 20), turn(own, 8, 1), edge)


def after_kernel(order_ref, value_ref, out_ref):
    out_ref[...] = value_ref[...]


def inner_kernel(
    row_size, elec_ref, magn_ref, mat_ref, z_ref, eps_ref,
    e_ref, h_ref, c_ref, ez_ref, state_ref, plain_ref, ext_ref, halo_ref,
):
    gz, row = lax.axis_index("gz"), lax.axis_index("row")
    spread_layers(gz, z_ref, ext_ref)
    for f in range(FIELDS):
        for x in range(ROWS):
            halo_ref[f, x] = ext_ref[f, pl.ds(x, 8, stride=ROWS), :]
    for z in range(LAYERS):
        plain_ref[z] = coefficient(mat_ref[z], eps_ref)
    for f in range(3):
        rows_outside(elec_ref.reshape(3 * LAYERS * ROWS, 128), f, state_ref, f)
        rows_outside(magn_ref.reshape(3 * LAYERS * ROWS, 128), f, state_ref, f + 3)
    rows_outside(plain_ref.reshape(LAYERS * ROWS, 128), 0, state_ref, 6)

    def first(f, i, zz):
        return halo_ref[f, i - DEPTH] if zz == OWN else state_ref[f, i - DEPTH, zz]

    def run(has_below, has_above):
        main = Tiles(first, None, DEPTH)
        stepper = Stepper(row_size, main, None, range(4, 12), (), False)
        for n in range(1, STEPS + 1):
            main.ez_ref = ez_ref.at[n - 1]
            stepper.step(n, [spans_inner(n, has_below, has_above)])
        for i in range(ROWS):
            for zz in range(CHUNK):
                for f in range(6):
                    (e_ref, h_ref)[f // 3][f % 3, i, zz] = main.get(f, DEPTH + i, zz)
                c_ref[i, zz] = main.get(6, DEPTH + i, zz)

    rows_cases(row_size, row, run)


def rim_kernel(
    row_size, z_ref, own_ref, even_ref, odd_ref, layer_ref, e_in, h_in, ez_in, weight_ref, prow_ref,
    edge_e_ref, edge_h_ref, edge_c_ref, done_ref, sum_ref, ext_ref, ez_ref,
):
    gz, row = lax.axis_index("gz"), lax.axis_index("row")
    place = iota(1) & (GROUP - 1)
    groups = lane_groups()
    valid = (iota(0) < 4) == (gz == 0)
    spread_layers(gz, z_ref, ext_ref)
    low_of, high_of = low_and_high(even_ref, odd_ref)
    low_z, high_z = low_and_high(layer_ref.at[0], layer_ref.at[1])
    joined = {}

    def first(at):
        b, zz = at
        if zz < OWN:
            return [own_ref[f, b, zz] for f in range(FIELDS)], turn_sides(low_of(b, zz), high_of(b, zz))
        rows = [[ext_ref[f, pl.ds(4 * b + r, 8, stride=ROWS), :] for r in range(4)] for f in range(FIELDS)]
        sides = turn_sides(*(jnp.where(valid, side(b), 0.0) for side in (low_z, high_z)))
        return gather_edges(rows, groups), sides

    def second(at, made):
        for f, tile in enumerate(edge_tiles(*made, place)):
            joined[f, at[0] + 1, at[1]] = tile

    staged([(b, zz) for b in range(2) for zz in range(CHUNK)], first, second)

    def run(has_below, has_above):
        main = Tiles(lambda f, i, zz: (e_in, h_in)[f // 3][f % 3, i - DEPTH, zz], None, DEPTH)
        edge = Tiles(lambda f, i, zz: joined[f, i, zz], ez_ref, 1)
        stepper = Stepper(row_size, None, edge, (), (1, 2), False)

        def reached(n, at):
            low, high = spans_inner(n, has_below, has_above)[1]
            return (at >= low) & (at <= high)

        for n in range(1, STEPS + 1):
            stepper.step(n, [spans_inner(n, has_below, has_above)])
            port_sums(n, reached, prow_ref, weight_ref, ez_in.at[n - 1], ez_ref, sum_ref, None)
        for i in range(2):
            for zz in range(CHUNK):
                for f in range(6):
                    (edge_e_ref, edge_h_ref)[f // 3][f % 3, i, zz] = edge.get(f, 1 + i, zz)
                edge_c_ref[i, zz] = edge.get(6, 1 + i, zz)
        if has_below != has_above:

            def write(f, r, zz, tile):
                done_ref[f, r, zz] = tile

            finish(range(6), 0 if has_above else 1, main, edge, write)

    rows_cases(row_size, row, run)


def outer_kernel(
    row_size, ports_each, prow_ref, pid_ref, e_in, h_in, c_in, weight_ref, edge_e_in, edge_h_in, edge_c_in, done_ref, sum_in,
    *rest,
):
    n_x = 1 if row_size == 2 else 2
    x_refs, corner_refs = rest[:n_x], rest[n_x : 2 * n_x]
    eout_hbm, hout_hbm, term_ref, ez_ref, edge_ez_ref, sum_ref, turned_ref, out_ref, sems = rest[2 * n_x :]
    gz, row = lax.axis_index("gz"), lax.axis_index("row")
    lane, sub = iota(1), iota(0)
    place = lane & (GROUP - 1)
    groups = lane_groups()
    valid = (sub < 4) == (gz == 0)
    zeros = jnp.zeros((8, 128), jnp.float32)

    def first_main(f, i, zz):
        if f == 6:
            return c_in[i - DEPTH, zz]
        return e_in[f, i - DEPTH, zz] if f < 3 else h_in[f - 3, i - DEPTH, zz]

    def first_edge(f, i, zz):
        if f == 6:
            return edge_c_in[i - 1, zz]
        return edge_e_in[f, i - 1, zz] if f < 3 else edge_h_in[f - 3, i - 1, zz]

    def run(has_below, has_above):
        main = Tiles(first_main, ez_ref, DEPTH)
        edge = Tiles(first_edge, edge_ez_ref, 1)

        def halo_rows(planes, slot, offset, b):
            got = {}
            for i, (f, x) in enumerate(planes):
                packed = corner_refs[slot][i % PAIRS]
                if i >= PAIRS:
                    packed = turn(packed, 4, 0)
                tiles = [x_refs[slot][i, zz] for zz in range(OWN)]
                tiles.append(jnp.where(valid, packed, 0.0))
                for zz in range(CHUNK):
                    main.put(f, DEPTH + x + offset, zz, tiles[zz])
                    got[f, x + offset - 4 * b, zz] = tiles[zz]

            def first(zz):
                rows = [[got.get((f, r, zz)) for r in range(4)] for f in range(FIELDS)]
                sides = turn_sides(corner_refs[slot][PAIRS + zz], corner_refs[slot][PAIRS + CHUNK + zz])
                return gather_edges(rows, groups), sides

            def second(zz, made):
                for f, tile in enumerate(edge_tiles(*made, place)):
                    edge.put(f, 1 + b, zz, tile)

            staged(range(CHUNK), first, second)

        if has_below:
            halo_rows(UP_PLANES, 0, -ROWS, -1)
        if has_above:
            halo_rows(DOWN_PLANES, n_x - 1, ROWS, 2)

        def reached(n, at):
            out = None
            for wanted, span in ((has_below, spans_below(n)[1]), (has_above, spans_above(n)[1])):
                if wanted:
                    part = (at >= span[0]) & (at <= span[1])
                    out = part if out is None else out | part
            return out

        rows = range(0 if has_below else 4, 16 if has_above else 12)
        blocks = range(0 if has_below else 1, 4 if has_above else 3)
        stepper = Stepper(row_size, main, edge, rows, blocks, True)
        for n in range(1, STEPS + 1):
            spans = ([spans_below(n)] if has_below else []) + ([spans_above(n)] if has_above else [])
            stepper.step(n, spans)
            port_sums(n, reached, prow_ref, weight_ref, ez_ref, edge_ez_ref, sum_ref, sum_in)
        def write(f, r, zz, tile, b):
            turned_ref[f, 4 * b + r, 8 * zz : 8 * zz + 8, :] = tile

        for b in range(2):
            put = functools.partial(write, b=b)
            if has_below and has_above or b == (1 if has_above else 0):
                finish(range(6), b, main, edge, put)
            else:
                for f in range(6):
                    for r in range(4):
                        for zz in range(OWN):
                            put(f, r, zz, done_ref[f, r, zz])

    rows_cases(row_size, row, run)

    copies = []
    flat = turned_ref.reshape(6 * ROWS * LAYERS, 128)
    for part, dest in ((0, eout_hbm), (1, hout_hbm)):
        for f in range(3 * part, 3 * part + 3):
            for z in range(LAYERS):
                out_ref[f, z] = flat[pl.ds(f * ROWS * LAYERS + z, ROWS, stride=LAYERS), :]
        copies.append(pltpu.make_async_copy(out_ref.at[pl.ds(3 * part, 3)], dest, sems.at[part]))
        copies[-1].start()
    basis = zeros
    for n in range(STEPS):
        for f in range(2 * FREQ):
            basis = jnp.where((sub == n) & (lane == f), float(BASIS[n, f]), basis)
    transform = zeros
    for n in range(STEPS):
        sampled = jnp.sum(sum_ref[n], axis=1, keepdims=True)
        transform = transform + sampled * basis[n : n + 1, :]
    term_ref[...] = jnp.zeros(term_ref.shape, jnp.float32)
    for k in range(PORT_TILE):
        port = pid_ref[0, 0, k]
        term_ref[port // ports_each, pl.ds(port % ports_each, 1), :] = transform[k : k + 1, : 2 * FREQ]
    for copy in copies:
        copy.wait()


def shifted(block, axis, size, distance):
    route = [(i - distance, i) for i in range(size) if 0 <= i - distance < size]
    return lax.ppermute(block, axis, route)


def swapped(block, axis, size, start=0):
    pairs = [(i, i + 1) for i in range(start, size - 1, 2)]
    return lax.ppermute(block, axis, pairs + [(j, i) for i, j in pairs])


def solution(mesh):
    sizes = dict(mesh.shape)
    row_size, col_size, gz_size = sizes["row"], sizes["col"], sizes["gz"]
    n_x = 1 if row_size == 2 else 2

    def across_rows(blocks):
        if row_size == 2:
            return (swapped(blocks[0], "row", 2),)
        return (shifted(blocks[0], "row", row_size, 1), shifted(blocks[1], "row", row_size, -1))

    def per_device(
        electric, magnetic, material, eps_table, mode_table, port_row, port_col, port_mode, port_ids
    ):
        f32 = jnp.float32

        def array(*shape):
            return jax.ShapeDtypeStruct(shape, f32)

        def scratch(*shape):
            return pltpu.VMEM(shape, f32)

        z_send, own, even_send, odd_send, *x_send = pl.pallas_call(
            functools.partial(pack_kernel, row_size),
            out_shape=[
                array(FIELDS, DEPTH, ROWS, 128),
                array(FIELDS, 2, OWN, 8, 128),
                array(2, OWN, 8, 128),
                array(2, OWN, 8, 128),
            ]
            + [array(PLANES, OWN, 8, 128)] * n_x,
            in_specs=[HBM] * 4,
            out_specs=[VMEM] * (4 + n_x),
            scratch_shapes=[
                scratch(FIELDS, ROWS, OWN, 8, 128),
                scratch(FIELDS, LAYERS, ROWS, 128),
                pltpu.SMEM(eps_table.shape, f32),
                pltpu.VMEM(material.shape, jnp.int32),
                pltpu.SemaphoreType.DMA((4,)),
            ],
            name="pack",
        )(eps_table, electric, magnetic, material)
        x_halo = across_rows(x_send)
        even = swapped(even_send, "col", col_size)
        z_halo = swapped(z_send, "gz", gz_size)
        e_now, h_now, c_now, ez_now = pl.pallas_call(
            functools.partial(inner_kernel, row_size),
            out_shape=[
                array(3, ROWS, CHUNK, 8, 128),
                array(3, ROWS, CHUNK, 8, 128),
                array(ROWS, CHUNK, 8, 128),
                array(STEPS, ROWS, OWN, 8, 128),
            ],
            in_specs=[VMEM] * 4 + [SMEM],
            out_specs=[VMEM] * 4,
            scratch_shapes=[
                scratch(FIELDS, ROWS, OWN, 8, 128),
                scratch(LAYERS, ROWS, 128),
                scratch(FIELDS, 8 * ROWS, 128),
                scratch(FIELDS, ROWS, 8, 128),
            ],
            compiler_params=PARAMS,
            cost_estimate=pl.CostEstimate(flops=5_000_000, bytes_accessed=10_000_000, transcendentals=0),
            name="inner",
        )(electric, magnetic, material, z_halo, eps_table)
        odd_send = pl.pallas_call(
            after_kernel,
            out_shape=array(2, OWN, 8, 128),
            in_specs=[ANY, VMEM],
            out_specs=VMEM,
            compiler_params=PARAMS,
            name="after_inner",
        )(c_now, odd_send)
        odd = swapped(odd_send, "col", col_size, 1)
        layer_send = pl.pallas_call(
            layer_edge_kernel,
            out_shape=array(2, 2, 8, 128),
            in_specs=[VMEM] * 2 + [pl.BlockSpec(memory_space=pl.ANY)],
            out_specs=VMEM,
            compiler_params=PARAMS,
            name="layer_edges",
        )(even, odd, c_now)
        layer_halo = swapped(layer_send, "gz", gz_size)
        weights = pl.pallas_call(
            weight_kernel,
            out_shape=array(PORT_TILE, 2, OWN, 8, 128),
            in_specs=[VMEM] + [SMEM] * 4 + [ANY],
            out_specs=VMEM,
            scratch_shapes=[scratch(PORT_TILE, LAYERS, 128)],
            compiler_params=PARAMS,
            name="weights",
        )(mode_table, port_row, port_col, port_mode, port_ids, layer_send)
        corner_send = pl.pallas_call(
            functools.partial(corner_kernel, row_size),
            out_shape=[array(PAIRS + 2 * CHUNK, 8, 128)] * n_x,
            in_specs=[ANY] + [VMEM] * 4,
            out_specs=[VMEM] * n_x,
            scratch_shapes=[scratch(FIELDS, 8 * ROWS, 128)],
            compiler_params=PARAMS,
            name="corners",
        )(weights, z_halo, even, odd, layer_halo)
        corner = across_rows(corner_send)
        edges = pl.pallas_call(
            functools.partial(rim_kernel, row_size),
            out_shape=[
                array(3, 2, CHUNK, 8, 128),
                array(3, 2, CHUNK, 8, 128),
                array(2, CHUNK, 8, 128),
                array(6, 4, OWN, 8, 128),
                array(STEPS, 8, 128),
            ],
            in_specs=[VMEM] * 9 + [SMEM],
            out_specs=[VMEM] * 5,
            scratch_shapes=[scratch(FIELDS, 8 * ROWS, 128), scratch(2, OWN, 8, 128)],
            compiler_params=PARAMS,
            name="rim",
        )(z_halo, own, even, odd, layer_halo, e_now, h_now, ez_now, weights, port_row)
        devices = col_size * row_size * gz_size
        ports_each = PORT_TILE * col_size * row_size // devices
        electric_out, magnetic_out, term = pl.pallas_call(
            functools.partial(outer_kernel, row_size, ports_each),
            out_shape=[array(3, LAYERS, ROWS, 128)] * 2 + [array(devices, ports_each, 2 * FREQ)],
            in_specs=[SMEM] * 2 + [VMEM] * (9 + 2 * n_x),
            out_specs=[HBM, HBM, VMEM],
            scratch_shapes=[
                scratch(ROWS, OWN, 8, 128),
                scratch(2, OWN, 8, 128),
                scratch(STEPS, 8, 128),
                scratch(6, ROWS, LAYERS, 128),
                scratch(6, LAYERS, ROWS, 128),
                pltpu.SemaphoreType.DMA((2,)),
            ],
            compiler_params=PARAMS,
            name="outer",
        )(port_row, port_ids, e_now, h_now, c_now, weights, *edges, *x_halo, *corner)
        terms = lax.all_to_all(term, ("col", "row", "gz"), 0, 0, tiled=True)
        return (
            electric_out,
            magnetic_out,
            jnp.sum(terms, axis=0),
        )

    in_specs = (
        P(None, "gz", "row", ("grp", "col")),
        P(None, "gz", "row", ("grp", "col")),
        P("gz", "row", ("grp", "col")),
        P(),
        P(None, "gz", None),
        P(("grp", "row"), "col", None),
        P(("grp", "row"), "col", None),
        P(("grp", "row"), "col", None),
        P(("grp", "row"), "col", None),
    )
    out_specs = (
        P(None, "gz", "row", ("grp", "col")),
        P(None, "gz", "row", ("grp", "col")),
        P(("grp", "col", "row", "gz"), None),
    )
    return jax.shard_map(
        per_device, mesh=mesh, in_specs=in_specs, out_specs=out_specs, check_vma=False
    )
```

```python
import functools

import jax
import jax.numpy as jnp
import numpy as np
from jax import lax
from jax.experimental import pallas as pl
from jax.experimental.pallas import tpu as pltpu
from jax.sharding import PartitionSpec as P

STEPS = 4
FREQ = 8
MATS = 8
PLEN = 64
PORT_TILE = 4
FIELDS = 7
DEPTH = STEPS
ROWS = 8
LAYERS = 32
OWN = 4
CHUNK = 5
GROUP = 32

time_step = 0.5

UP_PLANES = [(f, 4) for f in (0, 1, 2, 4, 5)] + [(f, x) for x in (5, 6, 7) for f in range(FIELDS)]
DOWN_PLANES = [(f, x) for x in (0, 1, 2) for f in range(FIELDS)] + [(1, 3), (2, 3)]
PLANES = max(len(UP_PLANES), len(DOWN_PLANES))
PAIRS = (PLANES + 1) // 2

VMEM = pl.BlockSpec(memory_space=pltpu.VMEM)
SMEM = pl.BlockSpec(memory_space=pltpu.SMEM)
HBM = pl.BlockSpec(memory_space=pltpu.HBM)
ANY = pl.BlockSpec(memory_space=pl.ANY)
PARAMS = pltpu.CompilerParams(vmem_limit_bytes=16 * 1024 * 1024)


def dft_basis():
    times = (np.arange(STEPS) + 1.0) * time_step
    omegas = np.pi * (np.arange(FREQ) + 1.0) / FREQ
    angle = times[:, None] * omegas[None, :]
    return np.concatenate([np.cos(angle), -np.sin(angle)], axis=1)


BASIS = dft_basis()


def iota(axis):
    return lax.broadcasted_iota(jnp.int32, (8, 128), axis)


def turn(tile, shift, axis):
    return pltpu.roll(tile, shift % tile.shape[axis], axis)


def directions(row_size, body):
    if row_size == 2:
        row = lax.axis_index("row")
        pl.when(row == 0)(functools.partial(body, True, 0))
        pl.when(row == 1)(functools.partial(body, False, 0))
    else:
        body(True, 0)
        body(False, 1)


def coefficient(material, eps_ref):
    eps = jnp.full((8, 128), eps_ref[0], jnp.float32)
    for which in range(1, MATS):
        eps = jnp.where(material == which, eps_ref[which], eps)
    return time_step * (1.0 / eps)


def rows_outside(flat, f, state_ref, at):
    for x in range(ROWS):
        state_ref[at, x] = flat[pl.ds(f * LAYERS * ROWS + x, LAYERS, stride=ROWS), :].reshape(OWN, 8, 128)


def pack_kernel(row_size, eps_hbm, elec_hbm, magn_hbm, mat_hbm, z_ref, own_ref, even_ref, odd_ref, *rest):
    x_refs, (state_ref, main_ref, eps_ref, mat_ref, sems) = rest[:-5], rest[-5:]
    copies = [pltpu.make_async_copy(eps_hbm, eps_ref, sems.at[0]), pltpu.make_async_copy(mat_hbm, mat_ref, sems.at[1])]
    copies.append(pltpu.make_async_copy(elec_hbm, main_ref.at[pl.ds(0, 3)], sems.at[2]))
    copies.append(pltpu.make_async_copy(magn_hbm, main_ref.at[pl.ds(3, 3)], sems.at[3]))
    for copy in copies:
        copy.start()
    copies[0].wait()
    copies[1].wait()
    for z in range(LAYERS):
        main_ref[6, z] = coefficient(mat_ref[z], eps_ref)
    copies[2].wait()
    copies[3].wait()
    start = jnp.where(lax.axis_index("gz") == 0, LAYERS - DEPTH, 0)
    for f in range(FIELDS):
        z_ref[f] = main_ref[f, pl.ds(start, DEPTH)]
    flat = main_ref.reshape(FIELDS * LAYERS * ROWS, 128)
    for f in range(FIELDS):
        rows_outside(flat, f, state_ref, f)

    def send(up, slot):
        for i, (f, x) in enumerate(UP_PLANES if up else DOWN_PLANES):
            x_refs[slot][i] = state_ref[f, x]

    directions(row_size, send)
    pack_edges(state_ref, own_ref, even_ref, odd_ref)


def lane_groups():
    group = iota(1) >> 5
    return [jnp.where(group == r, 1.0, 0.0) for r in range(4)]


def gather_edges(rows_of, groups):
    moved = [[tile if tile is None else turn(tile, GROUP * r + 8, 1) for r, tile in enumerate(rows)] for rows in rows_of]
    out = []
    for rows in moved:
        parts = [tile * groups[r] for r, tile in enumerate(rows) if tile is not None]
        out.append(functools.reduce(lambda a, b: a + b, parts) if parts else jnp.zeros((8, 128), jnp.float32))
    return out


def staged(items, first, second):
    waiting = None
    for item in items:
        made = first(item)
        if waiting is not None:
            second(*waiting)
        waiting = (item, made)
    second(*waiting)


def pack_edges(state_ref, own_ref, even_ref, odd_ref):
    lane = iota(1)
    groups = lane_groups()
    slots = [jnp.where(((lane & (GROUP - 1)) >> 2) == f, 1.0, 0.0) for f in range(FIELDS)]
    even = (lax.axis_index("col") & 1) == 0

    def first(at):
        b, zz = at
        return gather_edges([[state_ref[f, 4 * b + r, zz] for r in range(4)] for f in range(FIELDS)], groups)

    def second(at, owns):
        b, zz = at
        ups = [turn(own, DEPTH * f - 4, 1) for f, own in enumerate(owns)]
        downs = [turn(own, DEPTH * f - 8, 1) for f, own in enumerate(owns)]
        up = functools.reduce(lambda a, b: a + b, [v * m for v, m in zip(ups, slots)])
        down = functools.reduce(lambda a, b: a + b, [v * m for v, m in zip(downs, slots)])
        for f in range(FIELDS):
            own_ref[f, b, zz] = owns[f]
        even_ref[b, zz] = jnp.where(even, up, down)
        odd_ref[b, zz] = jnp.where(even, down, up)

    staged([(b, zz) for b in range(2) for zz in range(OWN)], first, second)


def low_and_high(even_ref, odd_ref):
    even = (lax.axis_index("col") & 1) == 0

    def low(*at):
        return jnp.where(even, odd_ref[at], even_ref[at])

    def high(*at):
        return jnp.where(even, even_ref[at], odd_ref[at])

    return low, high


def layer_edge_kernel(even_ref, odd_ref, inner_ref, out_ref):
    gz = lax.axis_index("gz")
    for i, ref in enumerate((even_ref, odd_ref)):
        for b in range(2):
            out_ref[i, b] = jnp.where(gz == 0, ref[b, OWN - 1], ref[b, 0])


def spread_layers(gz, z_ref, ext_ref):
    for f in range(FIELDS):
        halo = z_ref[f].reshape(DEPTH * ROWS, 128)
        nothing = jnp.zeros_like(halo)
        ext_ref[f, : DEPTH * ROWS] = jnp.where(gz == 0, halo, nothing)
        ext_ref[f, DEPTH * ROWS :] = jnp.where(gz == 0, nothing, halo)


def corner_kernel(row_size, weight_ref, z_ref, even_ref, odd_ref, layer_ref, *rest):
    x_refs, ext_ref = rest[:-1], rest[-1]
    gz = lax.axis_index("gz")
    valid = (iota(0) < 4) == (gz == 0)
    spread_layers(gz, z_ref, ext_ref)
    low, high = low_and_high(even_ref, odd_ref)
    low_z, high_z = low_and_high(layer_ref.at[0], layer_ref.at[1])

    def send(up, slot):
        planes = UP_PLANES if up else DOWN_PLANES

        def tile(i):
            f, x = planes[i]
            return ext_ref[f, pl.ds(x, 8, stride=ROWS), :]

        for i in range(PAIRS):
            pair = tile(i)
            if i + PAIRS < len(planes):
                pair = pair + turn(tile(i + PAIRS), 4, 0)
            x_refs[slot][i] = pair
        b = 1 if up else 0
        for zz in range(OWN):
            x_refs[slot][PAIRS + zz] = low(b, zz)
            x_refs[slot][PAIRS + CHUNK + zz] = high(b, zz)
        x_refs[slot][PAIRS + OWN] = jnp.where(valid, low_z(b), 0.0)
        x_refs[slot][PAIRS + CHUNK + OWN] = jnp.where(valid, high_z(b), 0.0)

    directions(row_size, send)


def turn_sides(low, high):
    lows = [turn(low, 12 - DEPTH * f, 1) for f in range(FIELDS)]
    return lows, [turn(high, 8 - DEPTH * f, 1) for f in range(FIELDS)]


def edge_tiles(owns, sides, place):
    turned = [turn(own, 8, 1) for own in owns]
    out = []
    for own, own_turned, low, high in zip(owns, turned, *sides):
        tile = jnp.where(place < 16, low, own_turned)
        tile = jnp.where(place < 12, high, tile)
        out.append(jnp.where(place < 8, own, tile))
    return out


class Tiles:
    def __init__(self, first, ez_ref, shift):
        self.first, self.ez_ref, self.shift = first, ez_ref, shift
        self.values = {}

    def get(self, f, i, zz):
        value = self.values.get((f, i, zz))
        return self.first(f, i, zz) if value is None else value

    def put(self, f, i, zz, tile):
        self.values[f, i, zz] = tile
        at = i - self.shift
        if f == 2 and zz < OWN and self.ez_ref is not None and 0 <= at < self.ez_ref.shape[0]:
            self.ez_ref[at, zz] = tile


def leapfrog(tiles, exists, h_rows, e_rows, across, h_of, c_of, h_layers, e_layers, skip_hx):
    sub = iota(0)
    every = range(CHUNK)
    blank = [jnp.zeros((8, 128), jnp.float32)] * CHUNK

    def above(values):
        turned = [turn(v, -1, 0) for v in values]
        return [jnp.where(sub == 7, turned[(zz + 1) % CHUNK], turned[zz]) for zz in every]

    def beneath(values):
        turned = [turn(v, 1, 0) for v in values]
        return [jnp.where(sub == 0, turned[zz - 1], turned[zz]) for zz in every]

    def row(f, i):
        return [tiles.get(f, i, zz) for zz in every]

    def load_e(i):
        ey, ez = row(1, i), row(2, i)
        out = dict(ey=ey, ez=ez, ey_x=across.turned(ey, -1), ez_x=across.turned(ez, -1))
        if i in h_rows:
            ex = row(0, i)
            out.update(ex=ex, ex_y=[turn(v, -1, 1) for v in ex], ex_z=above(ex))
            if i not in skip_hx:
                out.update(ez_y=[turn(v, -1, 1) for v in ez], ey_z=above(ey))
        return out

    def work_h(i, loaded):
        e, after, h = loaded[i], loaded.get(i + 1), h_of(i)
        ey_x = across.pick(e["ey_x"], after["ey_x"] if after else blank, -1)
        ez_x = across.pick(e["ez_x"], after["ez_x"] if after else blank, -1)
        new = {}
        for zz in h_layers:
            if i not in skip_hx:
                curl = (e["ez_y"][zz] - e["ez"][zz]) - (e["ey_z"][zz] - e["ey"][zz])
                new[3, zz] = tiles.get(3, i, zz) - h[zz] * curl
            curl = (e["ex_z"][zz] - e["ex"][zz]) - (ez_x[zz] - e["ez"][zz])
            new[4, zz] = tiles.get(4, i, zz) - h[zz] * curl
            curl = (ey_x[zz] - e["ey"][zz]) - (e["ex_y"][zz] - e["ex"][zz])
            new[5, zz] = tiles.get(5, i, zz) - h[zz] * curl
        for (f, zz), tile in new.items():
            tiles.put(f, i, zz, tile)

    def load_h(i):
        hy, hz = row(4, i), row(5, i)
        out = dict(hy=hy, hz=hz, hy_x=across.turned(hy, 1), hz_x=across.turned(hz, 1))
        if i in e_rows:
            hx = row(3, i)
            out.update(hx=hx, hx_y=[turn(v, 1, 1) for v in hx], hz_y=[turn(v, 1, 1) for v in hz])
            out.update(hx_z=beneath(hx), hy_z=beneath(hy))
        return out

    def work_e(i, loaded):
        h, before, c = loaded[i], loaded.get(i - 1), c_of(i)
        hy_x = across.pick(h["hy_x"], before["hy_x"] if before else blank, 1)
        hz_x = across.pick(h["hz_x"], before["hz_x"] if before else blank, 1)
        new = {}
        for zz in e_layers:
            curl = (h["hz"][zz] - h["hz_y"][zz]) - (h["hy"][zz] - h["hy_z"][zz])
            new[0, zz] = tiles.get(0, i, zz) + c[zz] * curl
            curl = (h["hx"][zz] - h["hx_z"][zz]) - (h["hz"][zz] - hz_x[zz])
            new[1, zz] = tiles.get(1, i, zz) + c[zz] * curl
            curl = (h["hy"][zz] - hy_x[zz]) - (h["hx"][zz] - h["hx_y"][zz])
            new[2, zz] = tiles.get(2, i, zz) + c[zz] * curl
        for (f, zz), tile in new.items():
            tiles.put(f, i, zz, tile)

    def sweep(rows, load, work):
        loaded = {}

        def want(i):
            if i not in loaded and i in exists:
                loaded[i] = load(i)

        for i in rows:
            for j in (i - 1, i, i + 1):
                if j in rows or j == i + (1 if load is load_e else -1):
                    want(j)
            work(i, loaded)

    sweep(h_rows, load_e, work_h)
    yield
    sweep(e_rows, load_h, work_e)


class Rows:
    def turned(self, values, way):
        return values

    def pick(self, own, other, way):
        return other


class Blocks:
    def __init__(self, groups):
        self.groups = groups

    def turned(self, values, way):
        return [turn(v, way * GROUP, 1) for v in values]

    def pick(self, own, other, way):
        edge = self.groups[3] if way < 0 else self.groups[0]
        return [jnp.where(edge, o, v) for o, v in zip(other, own)]


def spans_inner(n, has_below, has_above):
    last = 7 - n if has_above else 7
    return (n - 1 if has_below else 0, last), (n if has_below else 0, last)


def spans_below(n):
    return (n - 5, n - 2), (n - 4, n - 1)


def spans_above(n):
    return (8 - n, 11 - n), (8 - n, 11 - n)


class Stepper:
    def __init__(self, row_size, main, edge, main_exists, edge_exists, skip_hx):
        gz, row, col = (lax.axis_index(name) for name in ("gz", "row", "col"))
        lane, sub = iota(1), iota(0)
        place, self.group = lane & (GROUP - 1), lane >> 5
        full = jnp.full((8, 128), time_step, jnp.float32)
        self.layer_half = [full] * OWN + [jnp.where((sub >= 4) & (gz == 0), 0.0, full)]
        outside = (place >= 12) & (place < 16) & (col == 0)
        self.edge_half = [jnp.where(outside, 0.0, v) for v in self.layer_half]
        self.lowest = jnp.where(row == 0, 0.0, 1.0) if row_size > 2 else None
        self.main, self.edge, self.skip_hx = main, edge, skip_hx
        self.main_exists, self.edge_exists = main_exists, edge_exists
        self.blocks = Blocks([self.group == r for r in range(4)])

    def masked(self, values, block, span):
        low, high = max(span[0] - 4 * block, 0), min(span[1] - 4 * block, 3)
        if low == 0 and high == 3:
            return values
        mask = (self.group >= low) & (self.group <= high)
        return [jnp.where(mask, v, 0.0) for v in values]

    def main_h(self, i):
        return self.layer_half if self.lowest is None or i >= DEPTH else [v * self.lowest for v in self.layer_half]

    def main_c(self, i):
        return [self.main.get(6, i, zz) for zz in range(CHUNK)]

    def edge_h(self, i, span):
        h = self.edge_half if self.lowest is None or i else [v * self.lowest for v in self.edge_half]
        return self.masked(h, i - 1, span)

    def edge_c(self, i, span):
        return self.masked([self.edge.get(6, i, zz) for zz in range(CHUNK)], i - 1, span)

    def step(self, n, spans, between=None):
        def blocks_of(span):
            return [b + 1 for b in range(-1, 3) if span[0] <= 4 * b + 3 and span[1] >= 4 * b]

        layers = range(CHUNK)
        last = range(OWN) if n == STEPS else layers
        parts = []
        for h_span, e_span in spans:
            h_rows = list(range(DEPTH + h_span[0], DEPTH + h_span[1] + 1))
            e_rows = list(range(DEPTH + e_span[0], DEPTH + e_span[1] + 1))
            skip = h_rows[:1] if self.skip_hx and h_span[0] < e_span[0] else []
            if self.main is not None:
                parts.append(
                    leapfrog(self.main, self.main_exists, h_rows, e_rows, Rows(), self.main_h, self.main_c, layers, last, skip)
                )
            if self.edge is None:
                continue
            h_of, c_of = functools.partial(self.edge_h, span=h_span), functools.partial(self.edge_c, span=e_span)
            parts.append(
                leapfrog(
                    self.edge, self.edge_exists, blocks_of(h_span), blocks_of(e_span), self.blocks, h_of, c_of, layers, last, []
                )
            )
        for part in parts:
            next(part)
        if between is not None:
            between()
        for part in parts:
            next(part, None)


def rows_cases(row_size, row, run):
    if row_size == 2:
        pl.when(row == 0)(functools.partial(run, False, True))
        pl.when(row == 1)(functools.partial(run, True, False))
    else:
        run(True, True)


def port_sums(n, reached, prow_ref, weight_ref, ez_ref, edge_ref, sum_ref, add_ref):
    for k in range(PORT_TILE):
        at = prow_ref[0, 0, k]
        total = jnp.zeros((8, 128), jnp.float32)
        for zz in range(OWN):
            if ez_ref is not None:
                total = total + ez_ref[at, zz] * weight_ref[k, 0, zz]
            if edge_ref is not None:
                total = total + edge_ref[at >> 2, zz] * weight_ref[k, 1, zz]
        total = jnp.sum(jnp.where(reached(n, at), total, 0.0), axis=0, keepdims=True)
        if add_ref is not None:
            total = total + add_ref[n - 1, k : k + 1, :]
        sum_ref[n - 1, k : k + 1, :] = total


def finish(fields, b, main, edge, write):
    lane = iota(1)
    place = lane & (GROUP - 1)
    sides = (lane < DEPTH) | (lane >= 128 - DEPTH)

    def first(f):
        tiles = [edge.get(f, b + 1, zz) for zz in range(OWN)]
        turned = [turn(tile, -8, 1) for tile in tiles]
        return [jnp.where(place < 8, tile, other) for tile, other in zip(tiles, turned)]

    def second(f, near):
        turned = {(r, zz): turn(near[zz], -(GROUP * r + 8), 1) for r in range(4) for zz in range(OWN)}
        made = {(r, zz): jnp.where(sides, tile, main.get(f, DEPTH + 4 * b + r, zz)) for (r, zz), tile in turned.items()}
        for (r, zz), tile in made.items():
            write(f, r, zz, tile)

    staged(fields, first, second)


def weight_kernel(mode_ref, prow_ref, pcol_ref, pmode_ref, pid_ref, order_ref, weight_ref, strip_ref):
    lane = iota(1)
    for k in range(PORT_TILE):
        strip_ref[k] = jnp.zeros(strip_ref.shape[1:], jnp.float32)
        strip_ref[k, :, 0:PLEN] = mode_ref[pmode_ref[0, 0, k]]
    for k in range(PORT_TILE):
        turned = GROUP * (prow_ref[0, 0, k] & 3)
        at = lane - turned
        for zz in range(OWN):
            tile = pltpu.roll(strip_ref[k, 8 * zz : 8 * zz + 8, :], pcol_ref[0, 0, k], 1)
            weight_ref[k, 0, zz] = jnp.where((lane >= DEPTH) & (lane < 128 - DEPTH), tile, 0.0)
            own = pltpu.roll(tile, turned + 8, 1)
            edge = jnp.where((at >= 4) & (at < 8), own, 0.0)
            weight_ref[k, 1, zz] = jnp.where((at >= 16) & (at < 20), turn(own, 8, 1), edge)


def inner_kernel(
    row_size, elec_ref, magn_ref, mat_ref, z_ref, eps_ref,
    e_ref, h_ref, c_ref, ez_ref, state_ref, plain_ref, ext_ref, halo_ref,
):
    gz, row = lax.axis_index("gz"), lax.axis_index("row")
    spread_layers(gz, z_ref, ext_ref)
    for f in range(FIELDS):
        for x in range(ROWS):
            halo_ref[f, x] = ext_ref[f, pl.ds(x, 8, stride=ROWS), :]
    for z in range(LAYERS):
        plain_ref[z] = coefficient(mat_ref[z], eps_ref)
    for f in range(3):
        rows_outside(elec_ref.reshape(3 * LAYERS * ROWS, 128), f, state_ref, f)
        rows_outside(magn_ref.reshape(3 * LAYERS * ROWS, 128), f, state_ref, f + 3)
    rows_outside(plain_ref.reshape(LAYERS * ROWS, 128), 0, state_ref, 6)

    def first(f, i, zz):
        return halo_ref[f, i - DEPTH] if zz == OWN else state_ref[f, i - DEPTH, zz]

    def run(has_below, has_above):
        main = Tiles(first, None, DEPTH)
        stepper = Stepper(row_size, main, None, range(4, 12), (), False)
        for n in range(1, STEPS + 1):
            main.ez_ref = ez_ref.at[n - 1]
            stepper.step(n, [spans_inner(n, has_below, has_above)])
        for i in range(ROWS):
            for zz in range(CHUNK):
                for f in range(6):
                    (e_ref, h_ref)[f // 3][f % 3, i, zz] = main.get(f, DEPTH + i, zz)
                c_ref[i, zz] = main.get(6, DEPTH + i, zz)

    rows_cases(row_size, row, run)


def rim_kernel(
    row_size, z_ref, own_ref, even_ref, odd_ref, layer_ref, e_in, h_in, ez_in, weight_ref, prow_ref,
    edge_e_ref, edge_h_ref, edge_c_ref, done_ref, sum_ref, ext_ref, ez_ref,
):
    gz, row = lax.axis_index("gz"), lax.axis_index("row")
    place = iota(1) & (GROUP - 1)
    groups = lane_groups()
    valid = (iota(0) < 4) == (gz == 0)
    spread_layers(gz, z_ref, ext_ref)
    low_of, high_of = low_and_high(even_ref, odd_ref)
    low_z, high_z = low_and_high(layer_ref.at[0], layer_ref.at[1])
    joined = {}

    def first(at):
        b, zz = at
        if zz < OWN:
            return [own_ref[f, b, zz] for f in range(FIELDS)], turn_sides(low_of(b, zz), high_of(b, zz))
        rows = [[ext_ref[f, pl.ds(4 * b + r, 8, stride=ROWS), :] for r in range(4)] for f in range(FIELDS)]
        sides = turn_sides(*(jnp.where(valid, side(b), 0.0) for side in (low_z, high_z)))
        return gather_edges(rows, groups), sides

    def second(at, made):
        for f, tile in enumerate(edge_tiles(*made, place)):
            joined[f, at[0] + 1, at[1]] = tile

    staged([(b, zz) for b in range(2) for zz in range(CHUNK)], first, second)

    def run(has_below, has_above):
        main = Tiles(lambda f, i, zz: (e_in, h_in)[f // 3][f % 3, i - DEPTH, zz], None, DEPTH)
        edge = Tiles(lambda f, i, zz: joined[f, i, zz], ez_ref, 1)
        stepper = Stepper(row_size, None, edge, (), (1, 2), False)

        def reached(n, at):
            low, high = spans_inner(n, has_below, has_above)[1]
            return (at >= low) & (at <= high)

        for n in range(1, STEPS + 1):
            stepper.step(n, [spans_inner(n, has_below, has_above)])
            port_sums(n, reached, prow_ref, weight_ref, ez_in.at[n - 1], ez_ref, sum_ref, None)
        for i in range(2):
            for zz in range(CHUNK):
                for f in range(6):
                    (edge_e_ref, edge_h_ref)[f // 3][f % 3, i, zz] = edge.get(f, 1 + i, zz)
                edge_c_ref[i, zz] = edge.get(6, 1 + i, zz)
        if has_below != has_above:

            def write(f, r, zz, tile):
                done_ref[f, r, zz] = tile

            finish(range(6), 0 if has_above else 1, main, edge, write)

    rows_cases(row_size, row, run)


def outer_kernel(
    row_size, ports_each, prow_ref, pid_ref, e_in, h_in, c_in, weight_ref, edge_e_in, edge_h_in, edge_c_in, done_ref, sum_in,
    *rest,
):
    n_x = 1 if row_size == 2 else 2
    x_refs, corner_refs = rest[:n_x], rest[n_x : 2 * n_x]
    eout_hbm, hout_hbm, term_ref, ez_ref, edge_ez_ref, sum_ref, turned_ref, out_ref, sems = rest[2 * n_x :]
    gz, row = lax.axis_index("gz"), lax.axis_index("row")
    lane, sub = iota(1), iota(0)
    place = lane & (GROUP - 1)
    groups = lane_groups()
    valid = (sub < 4) == (gz == 0)
    zeros = jnp.zeros((8, 128), jnp.float32)

    def first_main(f, i, zz):
        if f == 6:
            return c_in[i - DEPTH, zz]
        return e_in[f, i - DEPTH, zz] if f < 3 else h_in[f - 3, i - DEPTH, zz]

    def first_edge(f, i, zz):
        if f == 6:
            return edge_c_in[i - 1, zz]
        return edge_e_in[f, i - 1, zz] if f < 3 else edge_h_in[f - 3, i - 1, zz]

    def write_terms():
        basis = zeros
        for n in range(STEPS):
            for f in range(2 * FREQ):
                basis = jnp.where((sub == n) & (lane == f), float(BASIS[n, f]), basis)
        transform = zeros
        for n in range(STEPS):
            sampled = jnp.sum(sum_ref[n], axis=1, keepdims=True)
            transform = transform + sampled * basis[n : n + 1, :]
        term_ref[...] = jnp.zeros(term_ref.shape, jnp.float32)
        for k in range(PORT_TILE):
            port = pid_ref[0, 0, k]
            term_ref[port // ports_each, pl.ds(port % ports_each, 1), :] = transform[k : k + 1, : 2 * FREQ]

    def run(has_below, has_above):
        main = Tiles(first_main, ez_ref, DEPTH)
        edge = Tiles(first_edge, edge_ez_ref, 1)

        def halo_rows(planes, slot, offset, b):
            got = {}
            for i, (f, x) in enumerate(planes):
                packed = corner_refs[slot][i % PAIRS]
                if i >= PAIRS:
                    packed = turn(packed, 4, 0)
                tiles = [x_refs[slot][i, zz] for zz in range(OWN)]
                tiles.append(jnp.where(valid, packed, 0.0))
                for zz in range(CHUNK):
                    main.put(f, DEPTH + x + offset, zz, tiles[zz])
                    got[f, x + offset - 4 * b, zz] = tiles[zz]

            def first(zz):
                rows = [[got.get((f, r, zz)) for r in range(4)] for f in range(FIELDS)]
                sides = turn_sides(corner_refs[slot][PAIRS + zz], corner_refs[slot][PAIRS + CHUNK + zz])
                return gather_edges(rows, groups), sides

            def second(zz, made):
                for f, tile in enumerate(edge_tiles(*made, place)):
                    edge.put(f, 1 + b, zz, tile)

            staged(range(CHUNK), first, second)

        if has_below:
            halo_rows(UP_PLANES, 0, -ROWS, -1)
        if has_above:
            halo_rows(DOWN_PLANES, n_x - 1, ROWS, 2)

        def reached(n, at):
            out = None
            for wanted, span in ((has_below, spans_below(n)[1]), (has_above, spans_above(n)[1])):
                if wanted:
                    part = (at >= span[0]) & (at <= span[1])
                    out = part if out is None else out | part
            return out

        rows = range(0 if has_below else 4, 16 if has_above else 12)
        blocks = range(0 if has_below else 1, 4 if has_above else 3)
        copies = []

        def hand_out(part):
            fields = range(3 * part, 3 * part + 3)

            def write(f, r, zz, tile, b):
                turned_ref[f, 4 * b + r, 8 * zz : 8 * zz + 8, :] = tile

            for b in range(2):
                put = functools.partial(write, b=b)
                if has_below and has_above or b == (1 if has_above else 0):
                    finish(fields, b, main, edge, put)
                else:
                    for f in fields:
                        for r in range(4):
                            for zz in range(OWN):
                                put(f, r, zz, done_ref[f, r, zz])
            flat = turned_ref.reshape(6 * ROWS * LAYERS, 128)
            for f in fields:
                for z in range(LAYERS):
                    out_ref[f, z] = flat[pl.ds(f * ROWS * LAYERS + z, ROWS, stride=LAYERS), :]
            dest = hout_hbm if part else eout_hbm
            copies.append(pltpu.make_async_copy(out_ref.at[pl.ds(3 * part, 3)], dest, sems.at[part]))
            copies[-1].start()

        stepper = Stepper(row_size, main, edge, rows, blocks, True)
        for n in range(1, STEPS + 1):
            spans = ([spans_below(n)] if has_below else []) + ([spans_above(n)] if has_above else [])
            stepper.step(n, spans, functools.partial(hand_out, 1) if n == STEPS else None)
            port_sums(n, reached, prow_ref, weight_ref, ez_ref, edge_ez_ref, sum_ref, sum_in)
        hand_out(0)
        write_terms()
        for copy in copies:
            copy.wait()

    rows_cases(row_size, row, run)


def shifted(block, axis, size, distance):
    route = [(i - distance, i) for i in range(size) if 0 <= i - distance < size]
    return lax.ppermute(block, axis, route)


def swapped(block, axis, size, start=0):
    pairs = [(i, i + 1) for i in range(start, size - 1, 2)]
    return lax.ppermute(block, axis, pairs + [(j, i) for i, j in pairs])


def solution(mesh):
    sizes = dict(mesh.shape)
    row_size, col_size, gz_size = sizes["row"], sizes["col"], sizes["gz"]
    n_x = 1 if row_size == 2 else 2

    def across_rows(blocks):
        if row_size == 2:
            return (swapped(blocks[0], "row", 2),)
        return (shifted(blocks[0], "row", row_size, 1), shifted(blocks[1], "row", row_size, -1))

    def per_device(
        electric, magnetic, material, eps_table, mode_table, port_row, port_col, port_mode, port_ids
    ):
        f32 = jnp.float32

        def array(*shape):
            return jax.ShapeDtypeStruct(shape, f32)

        def scratch(*shape):
            return pltpu.VMEM(shape, f32)

        z_send, own, even_send, odd_send, *x_send = pl.pallas_call(
            functools.partial(pack_kernel, row_size),
            out_shape=[
                array(FIELDS, DEPTH, ROWS, 128),
                array(FIELDS, 2, OWN, 8, 128),
                array(2, OWN, 8, 128),
                array(2, OWN, 8, 128),
            ]
            + [array(PLANES, OWN, 8, 128)] * n_x,
            in_specs=[HBM] * 4,
            out_specs=[VMEM] * (4 + n_x),
            scratch_shapes=[
                scratch(FIELDS, ROWS, OWN, 8, 128),
                scratch(FIELDS, LAYERS, ROWS, 128),
                pltpu.SMEM(eps_table.shape, f32),
                pltpu.VMEM(material.shape, jnp.int32),
                pltpu.SemaphoreType.DMA((4,)),
            ],
            name="pack",
        )(eps_table, electric, magnetic, material)
        x_halo = across_rows(x_send)
        even = swapped(even_send, "col", col_size)
        odd = swapped(odd_send, "col", col_size, 1)
        z_halo = swapped(z_send, "gz", gz_size)
        e_now, h_now, c_now, ez_now = pl.pallas_call(
            functools.partial(inner_kernel, row_size),
            out_shape=[
                array(3, ROWS, CHUNK, 8, 128),
                array(3, ROWS, CHUNK, 8, 128),
                array(ROWS, CHUNK, 8, 128),
                array(STEPS, ROWS, OWN, 8, 128),
            ],
            in_specs=[VMEM] * 4 + [SMEM],
            out_specs=[VMEM] * 4,
            scratch_shapes=[
                scratch(FIELDS, ROWS, OWN, 8, 128),
                scratch(LAYERS, ROWS, 128),
                scratch(FIELDS, 8 * ROWS, 128),
                scratch(FIELDS, ROWS, 8, 128),
            ],
            compiler_params=PARAMS,
            cost_estimate=pl.CostEstimate(flops=5_000_000, bytes_accessed=10_000_000, transcendentals=0),
            name="inner",
        )(electric, magnetic, material, z_halo, eps_table)
        layer_send = pl.pallas_call(
            layer_edge_kernel,
            out_shape=array(2, 2, 8, 128),
            in_specs=[VMEM] * 2 + [pl.BlockSpec(memory_space=pl.ANY)],
            out_specs=VMEM,
            compiler_params=PARAMS,
            name="layer_edges",
        )(even, odd, c_now)
        layer_halo = swapped(layer_send, "gz", gz_size)
        weights = pl.pallas_call(
            weight_kernel,
            out_shape=array(PORT_TILE, 2, OWN, 8, 128),
            in_specs=[VMEM] + [SMEM] * 4 + [ANY],
            out_specs=VMEM,
            scratch_shapes=[scratch(PORT_TILE, LAYERS, 128)],
            compiler_params=PARAMS,
            name="weights",
        )(mode_table, port_row, port_col, port_mode, port_ids, layer_send)
        corner_send = pl.pallas_call(
            functools.partial(corner_kernel, row_size),
            out_shape=[array(PAIRS + 2 * CHUNK, 8, 128)] * n_x,
            in_specs=[ANY] + [VMEM] * 4,
            out_specs=[VMEM] * n_x,
            scratch_shapes=[scratch(FIELDS, 8 * ROWS, 128)],
            compiler_params=PARAMS,
            name="corners",
        )(weights, z_halo, even, odd, layer_halo)
        corner = across_rows(corner_send)
        edges = pl.pallas_call(
            functools.partial(rim_kernel, row_size),
            out_shape=[
                array(3, 2, CHUNK, 8, 128),
                array(3, 2, CHUNK, 8, 128),
                array(2, CHUNK, 8, 128),
                array(6, 4, OWN, 8, 128),
                array(STEPS, 8, 128),
            ],
            in_specs=[VMEM] * 9 + [SMEM],
            out_specs=[VMEM] * 5,
            scratch_shapes=[scratch(FIELDS, 8 * ROWS, 128), scratch(2, OWN, 8, 128)],
            compiler_params=PARAMS,
            name="rim",
        )(z_halo, own, even, odd, layer_halo, e_now, h_now, ez_now, weights, port_row)
        devices = col_size * row_size * gz_size
        ports_each = PORT_TILE * col_size * row_size // devices
        electric_out, magnetic_out, term = pl.pallas_call(
            functools.partial(outer_kernel, row_size, ports_each),
            out_shape=[array(3, LAYERS, ROWS, 128)] * 2 + [array(devices, ports_each, 2 * FREQ)],
            in_specs=[SMEM] * 2 + [VMEM] * (9 + 2 * n_x),
            out_specs=[HBM, HBM, VMEM],
            scratch_shapes=[
                scratch(ROWS, OWN, 8, 128),
                scratch(2, OWN, 8, 128),
                scratch(STEPS, 8, 128),
                scratch(6, ROWS, LAYERS, 128),
                scratch(6, LAYERS, ROWS, 128),
                pltpu.SemaphoreType.DMA((2,)),
            ],
            compiler_params=PARAMS,
            name="outer",
        )(port_row, port_ids, e_now, h_now, c_now, weights, *edges, *x_halo, *corner)
        terms = lax.all_to_all(term, ("col", "row", "gz"), 0, 0, tiled=True)
        return (
            electric_out,
            magnetic_out,
            jnp.sum(terms, axis=0),
        )

    in_specs = (
        P(None, "gz", "row", ("grp", "col")),
        P(None, "gz", "row", ("grp", "col")),
        P("gz", "row", ("grp", "col")),
        P(),
        P(None, "gz", None),
        P(("grp", "row"), "col", None),
        P(("grp", "row"), "col", None),
        P(("grp", "row"), "col", None),
        P(("grp", "row"), "col", None),
    )
    out_specs = (
        P(None, "gz", "row", ("grp", "col")),
        P(None, "gz", "row", ("grp", "col")),
        P(("grp", "col", "row", "gz"), None),
    )
    return jax.shard_map(
        per_device, mesh=mesh, in_specs=in_specs, out_specs=out_specs, check_vma=False
    )
```

```python
import functools

import jax
import jax.numpy as jnp
import numpy as np
from jax import lax
from jax.experimental import pallas as pl
from jax.experimental.pallas import tpu as pltpu
from jax.sharding import PartitionSpec as P

STEPS = 4
FREQ = 8
MATS = 8
PLEN = 64
PORT_TILE = 4
FIELDS = 7
DEPTH = STEPS
ROWS = 8
LAYERS = 32
OWN = 4
CHUNK = 5
GROUP = 32

time_step = 0.5

UP_PLANES = [(f, 4) for f in (0, 1, 2, 4, 5)] + [(f, x) for x in (5, 6, 7) for f in range(FIELDS)]
DOWN_PLANES = [(f, x) for x in (0, 1, 2) for f in range(FIELDS)] + [(1, 3), (2, 3)]
PLANES = max(len(UP_PLANES), len(DOWN_PLANES))
PAIRS = (PLANES + 1) // 2

VMEM = pl.BlockSpec(memory_space=pltpu.VMEM)
SMEM = pl.BlockSpec(memory_space=pltpu.SMEM)
HBM = pl.BlockSpec(memory_space=pltpu.HBM)
ANY = pl.BlockSpec(memory_space=pl.ANY)
PARAMS = pltpu.CompilerParams(vmem_limit_bytes=16 * 1024 * 1024)


def dft_basis():
    times = (np.arange(STEPS) + 1.0) * time_step
    omegas = np.pi * (np.arange(FREQ) + 1.0) / FREQ
    angle = times[:, None] * omegas[None, :]
    return np.concatenate([np.cos(angle), -np.sin(angle)], axis=1)


BASIS = dft_basis()


def iota(axis):
    return lax.broadcasted_iota(jnp.int32, (8, 128), axis)


def turn(tile, shift, axis):
    return pltpu.roll(tile, shift % tile.shape[axis], axis)


def directions(row_size, body):
    if row_size == 2:
        row = lax.axis_index("row")
        pl.when(row == 0)(functools.partial(body, True, 0))
        pl.when(row == 1)(functools.partial(body, False, 0))
    else:
        body(True, 0)
        body(False, 1)


def coefficient(material, eps_ref):
    eps = jnp.full((8, 128), eps_ref[0], jnp.float32)
    for which in range(1, MATS):
        eps = jnp.where(material == which, eps_ref[which], eps)
    return time_step * (1.0 / eps)


def rows_outside(flat, f, state_ref, at):
    for x in range(ROWS):
        state_ref[at, x] = flat[pl.ds(f * LAYERS * ROWS + x, LAYERS, stride=ROWS), :].reshape(OWN, 8, 128)


def fetch(eps_hbm, elec_hbm, magn_hbm, mat_hbm, main_ref, eps_ref, mat_ref, sems):
    copies = [pltpu.make_async_copy(eps_hbm, eps_ref, sems.at[0]), pltpu.make_async_copy(mat_hbm, mat_ref, sems.at[1])]
    copies.append(pltpu.make_async_copy(elec_hbm, main_ref.at[pl.ds(0, 3)], sems.at[2]))
    copies.append(pltpu.make_async_copy(magn_hbm, main_ref.at[pl.ds(3, 3)], sems.at[3]))
    for copy in copies:
        copy.start()
    copies[0].wait()
    copies[1].wait()
    for z in range(LAYERS):
        main_ref[6, z] = coefficient(mat_ref[z], eps_ref)
    copies[2].wait()
    copies[3].wait()


def plane_kernel(row_size, eps_hbm, elec_hbm, magn_hbm, mat_hbm, *rest):
    x_refs, (main_ref, eps_ref, mat_ref, sems) = rest[:-4], rest[-4:]
    fetch(eps_hbm, elec_hbm, magn_hbm, mat_hbm, main_ref, eps_ref, mat_ref, sems)
    flat = main_ref.reshape(FIELDS * LAYERS * ROWS, 128)

    def send(up, slot):
        for i, (f, x) in enumerate(UP_PLANES if up else DOWN_PLANES):
            plane = flat[pl.ds(f * LAYERS * ROWS + x, LAYERS, stride=ROWS), :]
            x_refs[slot][i] = plane.reshape(OWN, 8, 128)

    directions(row_size, send)


def pack_kernel(
    order_ref, eps_hbm, elec_hbm, magn_hbm, mat_hbm, z_ref, own_ref, even_ref, odd_ref, state_ref, main_ref, eps_ref, mat_ref, sems
):
    fetch(eps_hbm, elec_hbm, magn_hbm, mat_hbm, main_ref, eps_ref, mat_ref, sems)
    start = jnp.where(lax.axis_index("gz") == 0, LAYERS - DEPTH, 0)
    for f in range(FIELDS):
        z_ref[f] = main_ref[f, pl.ds(start, DEPTH)]
    flat = main_ref.reshape(FIELDS * LAYERS * ROWS, 128)
    for f in range(FIELDS):
        rows_outside(flat, f, state_ref, f)
    pack_edges(state_ref, own_ref, even_ref, odd_ref)


def lane_groups():
    group = iota(1) >> 5
    return [jnp.where(group == r, 1.0, 0.0) for r in range(4)]


def gather_edges(rows_of, groups):
    moved = [[tile if tile is None else turn(tile, GROUP * r + 8, 1) for r, tile in enumerate(rows)] for rows in rows_of]
    out = []
    for rows in moved:
        parts = [tile * groups[r] for r, tile in enumerate(rows) if tile is not None]
        out.append(functools.reduce(lambda a, b: a + b, parts) if parts else jnp.zeros((8, 128), jnp.float32))
    return out


def staged(items, first, second):
    waiting = None
    for item in items:
        made = first(item)
        if waiting is not None:
            second(*waiting)
        waiting = (item, made)
    second(*waiting)


def pack_edges(state_ref, own_ref, even_ref, odd_ref):
    lane = iota(1)
    groups = lane_groups()
    slots = [jnp.where(((lane & (GROUP - 1)) >> 2) == f, 1.0, 0.0) for f in range(FIELDS)]
    even = (lax.axis_index("col") & 1) == 0

    def first(at):
        b, zz = at
        return gather_edges([[state_ref[f, 4 * b + r, zz] for r in range(4)] for f in range(FIELDS)], groups)

    def second(at, owns):
        b, zz = at
        ups = [turn(own, DEPTH * f - 4, 1) for f, own in enumerate(owns)]
        downs = [turn(own, DEPTH * f - 8, 1) for f, own in enumerate(owns)]
        up = functools.reduce(lambda a, b: a + b, [v * m for v, m in zip(ups, slots)])
        down = functools.reduce(lambda a, b: a + b, [v * m for v, m in zip(downs, slots)])
        for f in range(FIELDS):
            own_ref[f, b, zz] = owns[f]
        even_ref[b, zz] = jnp.where(even, up, down)
        odd_ref[b, zz] = jnp.where(even, down, up)

    staged([(b, zz) for b in range(2) for zz in range(OWN)], first, second)


def low_and_high(even_ref, odd_ref):
    even = (lax.axis_index("col") & 1) == 0

    def low(*at):
        return jnp.where(even, odd_ref[at], even_ref[at])

    def high(*at):
        return jnp.where(even, even_ref[at], odd_ref[at])

    return low, high


def layer_edge_kernel(even_ref, odd_ref, inner_ref, out_ref):
    gz = lax.axis_index("gz")
    for i, ref in enumerate((even_ref, odd_ref)):
        for b in range(2):
            out_ref[i, b] = jnp.where(gz == 0, ref[b, OWN - 1], ref[b, 0])


def spread_layers(gz, z_ref, ext_ref):
    for f in range(FIELDS):
        halo = z_ref[f].reshape(DEPTH * ROWS, 128)
        nothing = jnp.zeros_like(halo)
        ext_ref[f, : DEPTH * ROWS] = jnp.where(gz == 0, halo, nothing)
        ext_ref[f, DEPTH * ROWS :] = jnp.where(gz == 0, nothing, halo)


def corner_kernel(row_size, weight_ref, z_ref, even_ref, odd_ref, layer_ref, *rest):
    x_refs, ext_ref = rest[:-1], rest[-1]
    gz = lax.axis_index("gz")
    valid = (iota(0) < 4) == (gz == 0)
    spread_layers(gz, z_ref, ext_ref)
    low, high = low_and_high(even_ref, odd_ref)
    low_z, high_z = low_and_high(layer_ref.at[0], layer_ref.at[1])

    def send(up, slot):
        planes = UP_PLANES if up else DOWN_PLANES

        def tile(i):
            f, x = planes[i]
            return ext_ref[f, pl.ds(x, 8, stride=ROWS), :]

        for i in range(PAIRS):
            pair = tile(i)
            if i + PAIRS < len(planes):
                pair = pair + turn(tile(i + PAIRS), 4, 0)
            x_refs[slot][i] = pair
        b = 1 if up else 0
        for zz in range(OWN):
            x_refs[slot][PAIRS + zz] = low(b, zz)
            x_refs[slot][PAIRS + CHUNK + zz] = high(b, zz)
        x_refs[slot][PAIRS + OWN] = jnp.where(valid, low_z(b), 0.0)
        x_refs[slot][PAIRS + CHUNK + OWN] = jnp.where(valid, high_z(b), 0.0)

    directions(row_size, send)


def turn_sides(low, high):
    lows = [turn(low, 12 - DEPTH * f, 1) for f in range(FIELDS)]
    return lows, [turn(high, 8 - DEPTH * f, 1) for f in range(FIELDS)]


def edge_tiles(owns, sides, place):
    turned = [turn(own, 8, 1) for own in owns]
    out = []
    for own, own_turned, low, high in zip(owns, turned, *sides):
        tile = jnp.where(place < 16, low, own_turned)
        tile = jnp.where(place < 12, high, tile)
        out.append(jnp.where(place < 8, own, tile))
    return out


class Tiles:
    def __init__(self, first, ez_ref, shift):
        self.first, self.ez_ref, self.shift = first, ez_ref, shift
        self.values = {}

    def get(self, f, i, zz):
        value = self.values.get((f, i, zz))
        return self.first(f, i, zz) if value is None else value

    def put(self, f, i, zz, tile):
        self.values[f, i, zz] = tile
        at = i - self.shift
        if f == 2 and zz < OWN and self.ez_ref is not None and 0 <= at < self.ez_ref.shape[0]:
            self.ez_ref[at, zz] = tile


def leapfrog(tiles, exists, h_rows, e_rows, across, h_of, c_of, h_layers, e_layers, skip_hx):
    sub = iota(0)
    every = range(CHUNK)
    blank = [jnp.zeros((8, 128), jnp.float32)] * CHUNK

    def above(values):
        turned = [turn(v, -1, 0) for v in values]
        return [jnp.where(sub == 7, turned[(zz + 1) % CHUNK], turned[zz]) for zz in every]

    def beneath(values):
        turned = [turn(v, 1, 0) for v in values]
        return [jnp.where(sub == 0, turned[zz - 1], turned[zz]) for zz in every]

    def row(f, i):
        return [tiles.get(f, i, zz) for zz in every]

    def load_e(i):
        ey, ez = row(1, i), row(2, i)
        out = dict(ey=ey, ez=ez, ey_x=across.turned(ey, -1), ez_x=across.turned(ez, -1))
        if i in h_rows:
            ex = row(0, i)
            out.update(ex=ex, ex_y=[turn(v, -1, 1) for v in ex], ex_z=above(ex))
            if i not in skip_hx:
                out.update(ez_y=[turn(v, -1, 1) for v in ez], ey_z=above(ey))
        return out

    def work_h(i, loaded):
        e, after, h = loaded[i], loaded.get(i + 1), h_of(i)
        ey_x = across.pick(e["ey_x"], after["ey_x"] if after else blank, -1)
        ez_x = across.pick(e["ez_x"], after["ez_x"] if after else blank, -1)
        new = {}
        for zz in h_layers:
            if i not in skip_hx:
                curl = (e["ez_y"][zz] - e["ez"][zz]) - (e["ey_z"][zz] - e["ey"][zz])
                new[3, zz] = tiles.get(3, i, zz) - h[zz] * curl
            curl = (e["ex_z"][zz] - e["ex"][zz]) - (ez_x[zz] - e["ez"][zz])
            new[4, zz] = tiles.get(4, i, zz) - h[zz] * curl
            curl = (ey_x[zz] - e["ey"][zz]) - (e["ex_y"][zz] - e["ex"][zz])
            new[5, zz] = tiles.get(5, i, zz) - h[zz] * curl
        for (f, zz), tile in new.items():
            tiles.put(f, i, zz, tile)

    def load_h(i):
        hy, hz = row(4, i), row(5, i)
        out = dict(hy=hy, hz=hz, hy_x=across.turned(hy, 1), hz_x=across.turned(hz, 1))
        if i in e_rows:
            hx = row(3, i)
            out.update(hx=hx, hx_y=[turn(v, 1, 1) for v in hx], hz_y=[turn(v, 1, 1) for v in hz])
            out.update(hx_z=beneath(hx), hy_z=beneath(hy))
        return out

    def work_e(i, loaded):
        h, before, c = loaded[i], loaded.get(i - 1), c_of(i)
        hy_x = across.pick(h["hy_x"], before["hy_x"] if before else blank, 1)
        hz_x = across.pick(h["hz_x"], before["hz_x"] if before else blank, 1)
        new = {}
        for zz in e_layers:
            curl = (h["hz"][zz] - h["hz_y"][zz]) - (h["hy"][zz] - h["hy_z"][zz])
            new[0, zz] = tiles.get(0, i, zz) + c[zz] * curl
            curl = (h["hx"][zz] - h["hx_z"][zz]) - (h["hz"][zz] - hz_x[zz])
            new[1, zz] = tiles.get(1, i, zz) + c[zz] * curl
            curl = (h["hy"][zz] - hy_x[zz]) - (h["hx"][zz] - h["hx_y"][zz])
            new[2, zz] = tiles.get(2, i, zz) + c[zz] * curl
        for (f, zz), tile in new.items():
            tiles.put(f, i, zz, tile)

    def sweep(rows, load, work):
        loaded = {}

        def want(i):
            if i not in loaded and i in exists:
                loaded[i] = load(i)

        for i in rows:
            for j in (i - 1, i, i + 1):
                if j in rows or j == i + (1 if load is load_e else -1):
                    want(j)
            work(i, loaded)

    sweep(h_rows, load_e, work_h)
    yield
    sweep(e_rows, load_h, work_e)


class Rows:
    def turned(self, values, way):
        return values

    def pick(self, own, other, way):
        return other


class Blocks:
    def __init__(self, groups):
        self.groups = groups

    def turned(self, values, way):
        return [turn(v, way * GROUP, 1) for v in values]

    def pick(self, own, other, way):
        edge = self.groups[3] if way < 0 else self.groups[0]
        return [jnp.where(edge, o, v) for o, v in zip(other, own)]


def spans_inner(n, has_below, has_above):
    last = 7 - n if has_above else 7
    return (n - 1 if has_below else 0, last), (n if has_below else 0, last)


def spans_below(n):
    return (n - 5, n - 2), (n - 4, n - 1)


def spans_above(n):
    return (8 - n, 11 - n), (8 - n, 11 - n)


class Stepper:
    def __init__(self, row_size, main, edge, main_exists, edge_exists, skip_hx):
        gz, row, col = (lax.axis_index(name) for name in ("gz", "row", "col"))
        lane, sub = iota(1), iota(0)
        place, self.group = lane & (GROUP - 1), lane >> 5
        full = jnp.full((8, 128), time_step, jnp.float32)
        self.layer_half = [full] * OWN + [jnp.where((sub >= 4) & (gz == 0), 0.0, full)]
        outside = (place >= 12) & (place < 16) & (col == 0)
        self.edge_half = [jnp.where(outside, 0.0, v) for v in self.layer_half]
        self.lowest = jnp.where(row == 0, 0.0, 1.0) if row_size > 2 else None
        self.main, self.edge, self.skip_hx = main, edge, skip_hx
        self.main_exists, self.edge_exists = main_exists, edge_exists
        self.blocks = Blocks([self.group == r for r in range(4)])

    def masked(self, values, block, span):
        low, high = max(span[0] - 4 * block, 0), min(span[1] - 4 * block, 3)
        if low == 0 and high == 3:
            return values
        mask = (self.group >= low) & (self.group <= high)
        return [jnp.where(mask, v, 0.0) for v in values]

    def main_h(self, i):
        return self.layer_half if self.lowest is None or i >= DEPTH else [v * self.lowest for v in self.layer_half]

    def main_c(self, i):
        return [self.main.get(6, i, zz) for zz in range(CHUNK)]

    def edge_h(self, i, span):
        h = self.edge_half if self.lowest is None or i else [v * self.lowest for v in self.edge_half]
        return self.masked(h, i - 1, span)

    def edge_c(self, i, span):
        return self.masked([self.edge.get(6, i, zz) for zz in range(CHUNK)], i - 1, span)

    def step(self, n, spans, between=None):
        def blocks_of(span):
            return [b + 1 for b in range(-1, 3) if span[0] <= 4 * b + 3 and span[1] >= 4 * b]

        layers = range(CHUNK)
        last = range(OWN) if n == STEPS else layers
        parts = []
        for h_span, e_span in spans:
            h_rows = list(range(DEPTH + h_span[0], DEPTH + h_span[1] + 1))
            e_rows = list(range(DEPTH + e_span[0], DEPTH + e_span[1] + 1))
            skip = h_rows[:1] if self.skip_hx and h_span[0] < e_span[0] else []
            if self.main is not None:
                parts.append(
                    leapfrog(self.main, self.main_exists, h_rows, e_rows, Rows(), self.main_h, self.main_c, layers, last, skip)
                )
            if self.edge is None:
                continue
            h_of, c_of = functools.partial(self.edge_h, span=h_span), functools.partial(self.edge_c, span=e_span)
            parts.append(
                leapfrog(
                    self.edge, self.edge_exists, blocks_of(h_span), blocks_of(e_span), self.blocks, h_of, c_of, layers, last, []
                )
            )
        for part in parts:
            next(part)
        if between is not None:
            between()
        for part in parts:
            next(part, None)


def rows_cases(row_size, row, run):
    if row_size == 2:
        pl.when(row == 0)(functools.partial(run, False, True))
        pl.when(row == 1)(functools.partial(run, True, False))
    else:
        run(True, True)


def port_sums(n, reached, prow_ref, weight_ref, ez_ref, edge_ref, sum_ref, add_ref):
    for k in range(PORT_TILE):
        at = prow_ref[0, 0, k]
        total = jnp.zeros((8, 128), jnp.float32)
        for zz in range(OWN):
            if ez_ref is not None:
                total = total + ez_ref[at, zz] * weight_ref[k, 0, zz]
            if edge_ref is not None:
                total = total + edge_ref[at >> 2, zz] * weight_ref[k, 1, zz]
        total = jnp.sum(jnp.where(reached(n, at), total, 0.0), axis=0, keepdims=True)
        if add_ref is not None:
            total = total + add_ref[n - 1, k : k + 1, :]
        sum_ref[n - 1, k : k + 1, :] = total


def finish(fields, b, main, edge, write):
    lane = iota(1)
    place = lane & (GROUP - 1)
    sides = (lane < DEPTH) | (lane >= 128 - DEPTH)

    def first(f):
        tiles = [edge.get(f, b + 1, zz) for zz in range(OWN)]
        turned = [turn(tile, -8, 1) for tile in tiles]
        return [jnp.where(place < 8, tile, other) for tile, other in zip(tiles, turned)]

    def second(f, near):
        turned = {(r, zz): turn(near[zz], -(GROUP * r + 8), 1) for r in range(4) for zz in range(OWN)}
        made = {(r, zz): jnp.where(sides, tile, main.get(f, DEPTH + 4 * b + r, zz)) for (r, zz), tile in turned.items()}
        for (r, zz), tile in made.items():
            write(f, r, zz, tile)

    staged(fields, first, second)


def weight_kernel(mode_ref, prow_ref, pcol_ref, pmode_ref, pid_ref, order_ref, weight_ref, strip_ref):
    lane = iota(1)
    for k in range(PORT_TILE):
        strip_ref[k] = jnp.zeros(strip_ref.shape[1:], jnp.float32)
        strip_ref[k, :, 0:PLEN] = mode_ref[pmode_ref[0, 0, k]]
    for k in range(PORT_TILE):
        turned = GROUP * (prow_ref[0, 0, k] & 3)
        at = lane - turned
        for zz in range(OWN):
            tile = pltpu.roll(strip_ref[k, 8 * zz : 8 * zz + 8, :], pcol_ref[0, 0, k], 1)
            weight_ref[k, 0, zz] = jnp.where((lane >= DEPTH) & (lane < 128 - DEPTH), tile, 0.0)
            own = pltpu.roll(tile, turned + 8, 1)
            edge = jnp.where((at >= 4) & (at < 8), own, 0.0)
            weight_ref[k, 1, zz] = jnp.where((at >= 16) & (at < 20), turn(own, 8, 1), edge)


def inner_kernel(
    row_size, elec_ref, magn_ref, mat_ref, z_ref, eps_ref,
    e_ref, h_ref, c_ref, ez_ref, state_ref, plain_ref, ext_ref, halo_ref,
):
    gz, row = lax.axis_index("gz"), lax.axis_index("row")
    spread_layers(gz, z_ref, ext_ref)
    for f in range(FIELDS):
        for x in range(ROWS):
            halo_ref[f, x] = ext_ref[f, pl.ds(x, 8, stride=ROWS), :]
    for z in range(LAYERS):
        plain_ref[z] = coefficient(mat_ref[z], eps_ref)
    for f in range(3):
        rows_outside(elec_ref.reshape(3 * LAYERS * ROWS, 128), f, state_ref, f)
        rows_outside(magn_ref.reshape(3 * LAYERS * ROWS, 128), f, state_ref, f + 3)
    rows_outside(plain_ref.reshape(LAYERS * ROWS, 128), 0, state_ref, 6)

    def first(f, i, zz):
        return halo_ref[f, i - DEPTH] if zz == OWN else state_ref[f, i - DEPTH, zz]

    def run(has_below, has_above):
        main = Tiles(first, None, DEPTH)
        stepper = Stepper(row_size, main, None, range(4, 12), (), False)
        for n in range(1, STEPS + 1):
            main.ez_ref = ez_ref.at[n - 1]
            stepper.step(n, [spans_inner(n, has_below, has_above)])
        for i in range(ROWS):
            for zz in range(CHUNK):
                for f in range(6):
                    (e_ref, h_ref)[f // 3][f % 3, i, zz] = main.get(f, DEPTH + i, zz)
                c_ref[i, zz] = main.get(6, DEPTH + i, zz)

    rows_cases(row_size, row, run)


def rim_kernel(
    row_size, z_ref, own_ref, even_ref, odd_ref, layer_ref, e_in, h_in, ez_in, weight_ref, prow_ref,
    edge_e_ref, edge_h_ref, edge_c_ref, done_ref, sum_ref, ext_ref, ez_ref,
):
    gz, row = lax.axis_index("gz"), lax.axis_index("row")
    place = iota(1) & (GROUP - 1)
    groups = lane_groups()
    valid = (iota(0) < 4) == (gz == 0)
    spread_layers(gz, z_ref, ext_ref)
    low_of, high_of = low_and_high(even_ref, odd_ref)
    low_z, high_z = low_and_high(layer_ref.at[0], layer_ref.at[1])
    joined = {}

    def first(at):
        b, zz = at
        if zz < OWN:
            return [own_ref[f, b, zz] for f in range(FIELDS)], turn_sides(low_of(b, zz), high_of(b, zz))
        rows = [[ext_ref[f, pl.ds(4 * b + r, 8, stride=ROWS), :] for r in range(4)] for f in range(FIELDS)]
        sides = turn_sides(*(jnp.where(valid, side(b), 0.0) for side in (low_z, high_z)))
        return gather_edges(rows, groups), sides

    def second(at, made):
        for f, tile in enumerate(edge_tiles(*made, place)):
            joined[f, at[0] + 1, at[1]] = tile

    staged([(b, zz) for b in range(2) for zz in range(CHUNK)], first, second)

    def run(has_below, has_above):
        main = Tiles(lambda f, i, zz: (e_in, h_in)[f // 3][f % 3, i - DEPTH, zz], None, DEPTH)
        edge = Tiles(lambda f, i, zz: joined[f, i, zz], ez_ref, 1)
        stepper = Stepper(row_size, None, edge, (), (1, 2), False)

        def reached(n, at):
            low, high = spans_inner(n, has_below, has_above)[1]
            return (at >= low) & (at <= high)

        for n in range(1, STEPS + 1):
            stepper.step(n, [spans_inner(n, has_below, has_above)])
            port_sums(n, reached, prow_ref, weight_ref, ez_in.at[n - 1], ez_ref, sum_ref, None)
        for i in range(2):
            for zz in range(CHUNK):
                for f in range(6):
                    (edge_e_ref, edge_h_ref)[f // 3][f % 3, i, zz] = edge.get(f, 1 + i, zz)
                edge_c_ref[i, zz] = edge.get(6, 1 + i, zz)
        if has_below != has_above:

            def write(f, r, zz, tile):
                done_ref[f, r, zz] = tile

            finish(range(6), 0 if has_above else 1, main, edge, write)

    rows_cases(row_size, row, run)


def outer_kernel(
    row_size, ports_each, prow_ref, pid_ref, e_in, h_in, c_in, weight_ref, edge_e_in, edge_h_in, edge_c_in, done_ref, sum_in,
    *rest,
):
    n_x = 1 if row_size == 2 else 2
    x_refs, corner_refs = rest[:n_x], rest[n_x : 2 * n_x]
    eout_hbm, hout_hbm, term_ref, ez_ref, edge_ez_ref, sum_ref, turned_ref, out_ref, sems = rest[2 * n_x :]
    gz, row = lax.axis_index("gz"), lax.axis_index("row")
    lane, sub = iota(1), iota(0)
    place = lane & (GROUP - 1)
    groups = lane_groups()
    valid = (sub < 4) == (gz == 0)
    zeros = jnp.zeros((8, 128), jnp.float32)

    def first_main(f, i, zz):
        if f == 6:
            return c_in[i - DEPTH, zz]
        return e_in[f, i - DEPTH, zz] if f < 3 else h_in[f - 3, i - DEPTH, zz]

    def first_edge(f, i, zz):
        if f == 6:
            return edge_c_in[i - 1, zz]
        return edge_e_in[f, i - 1, zz] if f < 3 else edge_h_in[f - 3, i - 1, zz]

    def write_terms():
        basis = zeros
        for n in range(STEPS):
            for f in range(2 * FREQ):
                basis = jnp.where((sub == n) & (lane == f), float(BASIS[n, f]), basis)
        transform = zeros
        for n in range(STEPS):
            sampled = jnp.sum(sum_ref[n], axis=1, keepdims=True)
            transform = transform + sampled * basis[n : n + 1, :]
        term_ref[...] = jnp.zeros(term_ref.shape, jnp.float32)
        for k in range(PORT_TILE):
            port = pid_ref[0, 0, k]
            term_ref[port // ports_each, pl.ds(port % ports_each, 1), :] = transform[k : k + 1, : 2 * FREQ]

    def run(has_below, has_above):
        main = Tiles(first_main, ez_ref, DEPTH)
        edge = Tiles(first_edge, edge_ez_ref, 1)

        def halo_rows(planes, slot, offset, b):
            got = {}
            for i, (f, x) in enumerate(planes):
                packed = corner_refs[slot][i % PAIRS]
                if i >= PAIRS:
                    packed = turn(packed, 4, 0)
                tiles = [x_refs[slot][i, zz] for zz in range(OWN)]
                tiles.append(jnp.where(valid, packed, 0.0))
                for zz in range(CHUNK):
                    main.put(f, DEPTH + x + offset, zz, tiles[zz])
                    got[f, x + offset - 4 * b, zz] = tiles[zz]

            def first(zz):
                rows = [[got.get((f, r, zz)) for r in range(4)] for f in range(FIELDS)]
                sides = turn_sides(corner_refs[slot][PAIRS + zz], corner_refs[slot][PAIRS + CHUNK + zz])
                return gather_edges(rows, groups), sides

            def second(zz, made):
                for f, tile in enumerate(edge_tiles(*made, place)):
                    edge.put(f, 1 + b, zz, tile)

            staged(range(CHUNK), first, second)

        if has_below:
            halo_rows(UP_PLANES, 0, -ROWS, -1)
        if has_above:
            halo_rows(DOWN_PLANES, n_x - 1, ROWS, 2)

        def reached(n, at):
            out = None
            for wanted, span in ((has_below, spans_below(n)[1]), (has_above, spans_above(n)[1])):
                if wanted:
                    part = (at >= span[0]) & (at <= span[1])
                    out = part if out is None else out | part
            return out

        rows = range(0 if has_below else 4, 16 if has_above else 12)
        blocks = range(0 if has_below else 1, 4 if has_above else 3)
        copies = []

        def hand_out(part):
            fields = range(3 * part, 3 * part + 3)

            def write(f, r, zz, tile, b):
                turned_ref[f, 4 * b + r, 8 * zz : 8 * zz + 8, :] = tile

            for b in range(2):
                put = functools.partial(write, b=b)
                if has_below and has_above or b == (1 if has_above else 0):
                    finish(fields, b, main, edge, put)
                else:
                    for f in fields:
                        for r in range(4):
                            for zz in range(OWN):
                                put(f, r, zz, done_ref[f, r, zz])
            flat = turned_ref.reshape(6 * ROWS * LAYERS, 128)
            for f in fields:
                for z in range(LAYERS):
                    out_ref[f, z] = flat[pl.ds(f * ROWS * LAYERS + z, ROWS, stride=LAYERS), :]
            dest = hout_hbm if part else eout_hbm
            copies.append(pltpu.make_async_copy(out_ref.at[pl.ds(3 * part, 3)], dest, sems.at[part]))
            copies[-1].start()

        stepper = Stepper(row_size, main, edge, rows, blocks, True)
        for n in range(1, STEPS + 1):
            spans = ([spans_below(n)] if has_below else []) + ([spans_above(n)] if has_above else [])
            stepper.step(n, spans, functools.partial(hand_out, 1) if n == STEPS else None)
            port_sums(n, reached, prow_ref, weight_ref, ez_ref, edge_ez_ref, sum_ref, sum_in)
        hand_out(0)
        write_terms()
        for copy in copies:
            copy.wait()

    rows_cases(row_size, row, run)


def shifted(block, axis, size, distance):
    route = [(i - distance, i) for i in range(size) if 0 <= i - distance < size]
    return lax.ppermute(block, axis, route)


def swapped(block, axis, size, start=0):
    pairs = [(i, i + 1) for i in range(start, size - 1, 2)]
    return lax.ppermute(block, axis, pairs + [(j, i) for i, j in pairs])


def solution(mesh):
    sizes = dict(mesh.shape)
    row_size, col_size, gz_size = sizes["row"], sizes["col"], sizes["gz"]
    n_x = 1 if row_size == 2 else 2

    def across_rows(blocks):
        if row_size == 2:
            return (swapped(blocks[0], "row", 2),)
        return (shifted(blocks[0], "row", row_size, 1), shifted(blocks[1], "row", row_size, -1))

    def per_device(
        electric, magnetic, material, eps_table, mode_table, port_row, port_col, port_mode, port_ids
    ):
        f32 = jnp.float32

        def array(*shape):
            return jax.ShapeDtypeStruct(shape, f32)

        def scratch(*shape):
            return pltpu.VMEM(shape, f32)

        fetched = [
            scratch(FIELDS, LAYERS, ROWS, 128),
            pltpu.SMEM(eps_table.shape, f32),
            pltpu.VMEM(material.shape, jnp.int32),
            pltpu.SemaphoreType.DMA((4,)),
        ]
        x_send = pl.pallas_call(
            functools.partial(plane_kernel, row_size),
            out_shape=[array(PLANES, OWN, 8, 128)] * n_x,
            in_specs=[HBM] * 4,
            out_specs=[VMEM] * n_x,
            scratch_shapes=fetched,
            name="planes",
        )(eps_table, electric, magnetic, material)
        x_halo = across_rows(x_send)
        z_send, own, even_send, odd_send = pl.pallas_call(
            pack_kernel,
            out_shape=[
                array(FIELDS, DEPTH, ROWS, 128),
                array(FIELDS, 2, OWN, 8, 128),
                array(2, OWN, 8, 128),
                array(2, OWN, 8, 128),
            ],
            in_specs=[ANY] + [HBM] * 4,
            out_specs=[VMEM] * 4,
            scratch_shapes=[scratch(FIELDS, ROWS, OWN, 8, 128)] + fetched,
            name="pack",
        )(x_send[0], eps_table, electric, magnetic, material)
        even = swapped(even_send, "col", col_size)
        odd = swapped(odd_send, "col", col_size, 1)
        z_halo = swapped(z_send, "gz", gz_size)
        e_now, h_now, c_now, ez_now = pl.pallas_call(
            functools.partial(inner_kernel, row_size),
            out_shape=[
                array(3, ROWS, CHUNK, 8, 128),
                array(3, ROWS, CHUNK, 8, 128),
                array(ROWS, CHUNK, 8, 128),
                array(STEPS, ROWS, OWN, 8, 128),
            ],
            in_specs=[VMEM] * 4 + [SMEM],
            out_specs=[VMEM] * 4,
            scratch_shapes=[
                scratch(FIELDS, ROWS, OWN, 8, 128),
                scratch(LAYERS, ROWS, 128),
                scratch(FIELDS, 8 * ROWS, 128),
                scratch(FIELDS, ROWS, 8, 128),
            ],
            compiler_params=PARAMS,
            cost_estimate=pl.CostEstimate(flops=5_000_000, bytes_accessed=10_000_000, transcendentals=0),
            name="inner",
        )(electric, magnetic, material, z_halo, eps_table)
        layer_send = pl.pallas_call(
            layer_edge_kernel,
            out_shape=array(2, 2, 8, 128),
            in_specs=[VMEM] * 2 + [pl.BlockSpec(memory_space=pl.ANY)],
            out_specs=VMEM,
            compiler_params=PARAMS,
            name="layer_edges",
        )(even, odd, c_now)
        layer_halo = swapped(layer_send, "gz", gz_size)
        weights = pl.pallas_call(
            weight_kernel,
            out_shape=array(PORT_TILE, 2, OWN, 8, 128),
            in_specs=[VMEM] + [SMEM] * 4 + [ANY],
            out_specs=VMEM,
            scratch_shapes=[scratch(PORT_TILE, LAYERS, 128)],
            compiler_params=PARAMS,
            name="weights",
        )(mode_table, port_row, port_col, port_mode, port_ids, layer_send)
        corner_send = pl.pallas_call(
            functools.partial(corner_kernel, row_size),
            out_shape=[array(PAIRS + 2 * CHUNK, 8, 128)] * n_x,
            in_specs=[ANY] + [VMEM] * 4,
            out_specs=[VMEM] * n_x,
            scratch_shapes=[scratch(FIELDS, 8 * ROWS, 128)],
            compiler_params=PARAMS,
            name="corners",
        )(weights, z_halo, even, odd, layer_halo)
        corner = across_rows(corner_send)
        edges = pl.pallas_call(
            functools.partial(rim_kernel, row_size),
            out_shape=[
                array(3, 2, CHUNK, 8, 128),
                array(3, 2, CHUNK, 8, 128),
                array(2, CHUNK, 8, 128),
                array(6, 4, OWN, 8, 128),
                array(STEPS, 8, 128),
            ],
            in_specs=[VMEM] * 9 + [SMEM],
            out_specs=[VMEM] * 5,
            scratch_shapes=[scratch(FIELDS, 8 * ROWS, 128), scratch(2, OWN, 8, 128)],
            compiler_params=PARAMS,
            name="rim",
        )(z_halo, own, even, odd, layer_halo, e_now, h_now, ez_now, weights, port_row)
        devices = col_size * row_size * gz_size
        ports_each = PORT_TILE * col_size * row_size // devices
        electric_out, magnetic_out, term = pl.pallas_call(
            functools.partial(outer_kernel, row_size, ports_each),
            out_shape=[array(3, LAYERS, ROWS, 128)] * 2 + [array(devices, ports_each, 2 * FREQ)],
            in_specs=[SMEM] * 2 + [VMEM] * (9 + 2 * n_x),
            out_specs=[HBM, HBM, VMEM],
            scratch_shapes=[
                scratch(ROWS, OWN, 8, 128),
                scratch(2, OWN, 8, 128),
                scratch(STEPS, 8, 128),
                scratch(6, ROWS, LAYERS, 128),
                scratch(6, LAYERS, ROWS, 128),
                pltpu.SemaphoreType.DMA((2,)),
            ],
            compiler_params=PARAMS,
            name="outer",
        )(port_row, port_ids, e_now, h_now, c_now, weights, *edges, *x_halo, *corner)
        terms = lax.all_to_all(term, ("col", "row", "gz"), 0, 0, tiled=True)
        return (
            electric_out,
            magnetic_out,
            jnp.sum(terms, axis=0),
        )

    in_specs = (
        P(None, "gz", "row", ("grp", "col")),
        P(None, "gz", "row", ("grp", "col")),
        P("gz", "row", ("grp", "col")),
        P(),
        P(None, "gz", None),
        P(("grp", "row"), "col", None),
        P(("grp", "row"), "col", None),
        P(("grp", "row"), "col", None),
        P(("grp", "row"), "col", None),
    )
    out_specs = (
        P(None, "gz", "row", ("grp", "col")),
        P(None, "gz", "row", ("grp", "col")),
        P(("grp", "col", "row", "gz"), None),
    )
    return jax.shard_map(
        per_device, mesh=mesh, in_specs=in_specs, out_specs=out_specs, check_vma=False
    )
```

```python
import functools

import jax
import jax.numpy as jnp
import numpy as np
from jax import lax
from jax.experimental import pallas as pl
from jax.experimental.pallas import tpu as pltpu
from jax.sharding import PartitionSpec as P

STEPS = 4
FREQ = 8
MATS = 8
PLEN = 64
PORT_TILE = 4
FIELDS = 7
DEPTH = STEPS
ROWS = 8
LAYERS = 32
OWN = 4
CHUNK = 5
GROUP = 32

time_step = 0.5

UP_PLANES = [(f, 4) for f in (0, 1, 2, 4, 5)] + [(f, x) for x in (5, 6, 7) for f in range(FIELDS)]
DOWN_PLANES = [(f, x) for x in (0, 1, 2) for f in range(FIELDS)] + [(1, 3), (2, 3)]
PLANES = max(len(UP_PLANES), len(DOWN_PLANES))
PAIRS = (PLANES + 1) // 2

VMEM = pl.BlockSpec(memory_space=pltpu.VMEM)
SMEM = pl.BlockSpec(memory_space=pltpu.SMEM)
HBM = pl.BlockSpec(memory_space=pltpu.HBM)
ANY = pl.BlockSpec(memory_space=pl.ANY)
PARAMS = pltpu.CompilerParams(vmem_limit_bytes=16 * 1024 * 1024)


def dft_basis():
    times = (np.arange(STEPS) + 1.0) * time_step
    omegas = np.pi * (np.arange(FREQ) + 1.0) / FREQ
    angle = times[:, None] * omegas[None, :]
    return np.concatenate([np.cos(angle), -np.sin(angle)], axis=1)


BASIS = dft_basis()


def iota(axis):
    return lax.broadcasted_iota(jnp.int32, (8, 128), axis)


def turn(tile, shift, axis):
    return pltpu.roll(tile, shift % tile.shape[axis], axis)


def directions(row_size, body):
    if row_size == 2:
        row = lax.axis_index("row")
        pl.when(row == 0)(functools.partial(body, True, 0))
        pl.when(row == 1)(functools.partial(body, False, 0))
    else:
        body(True, 0)
        body(False, 1)


def coefficient(material, eps_ref):
    eps = jnp.full((8, 128), eps_ref[0], jnp.float32)
    for which in range(1, MATS):
        eps = jnp.where(material == which, eps_ref[which], eps)
    return time_step * (1.0 / eps)


def rows_outside(flat, f, state_ref, at):
    for x in range(ROWS):
        state_ref[at, x] = flat[pl.ds(f * LAYERS * ROWS + x, LAYERS, stride=ROWS), :].reshape(OWN, 8, 128)


def pack_kernel(row_size, eps_hbm, elec_hbm, magn_hbm, mat_hbm, z_ref, own_ref, even_ref, odd_ref, *rest):
    x_refs, (state_ref, main_ref, eps_ref, mat_ref, sems) = rest[:-5], rest[-5:]
    copies = [pltpu.make_async_copy(eps_hbm, eps_ref, sems.at[0]), pltpu.make_async_copy(mat_hbm, mat_ref, sems.at[1])]
    copies.append(pltpu.make_async_copy(elec_hbm, main_ref.at[pl.ds(0, 3)], sems.at[2]))
    copies.append(pltpu.make_async_copy(magn_hbm, main_ref.at[pl.ds(3, 3)], sems.at[3]))
    for copy in copies:
        copy.start()
    copies[0].wait()
    copies[1].wait()
    for z in range(LAYERS):
        main_ref[6, z] = coefficient(mat_ref[z], eps_ref)
    copies[2].wait()
    copies[3].wait()
    start = jnp.where(lax.axis_index("gz") == 0, LAYERS - DEPTH, 0)
    for f in range(FIELDS):
        z_ref[f] = main_ref[f, pl.ds(start, DEPTH)]
    flat = main_ref.reshape(FIELDS * LAYERS * ROWS, 128)
    for f in range(FIELDS):
        rows_outside(flat, f, state_ref, f)

    def send(up, slot):
        for i, (f, x) in enumerate(UP_PLANES if up else DOWN_PLANES):
            x_refs[slot][i] = state_ref[f, x]

    directions(row_size, send)
    pack_edges(state_ref, own_ref, even_ref, odd_ref)


def lane_groups():
    group = iota(1) >> 5
    return [jnp.where(group == r, 1.0, 0.0) for r in range(4)]


def gather_edges(rows_of, groups):
    moved = [[tile if tile is None else turn(tile, GROUP * r + 8, 1) for r, tile in enumerate(rows)] for rows in rows_of]
    out = []
    for rows in moved:
        parts = [tile * groups[r] for r, tile in enumerate(rows) if tile is not None]
        out.append(functools.reduce(lambda a, b: a + b, parts) if parts else jnp.zeros((8, 128), jnp.float32))
    return out


def staged(items, first, second):
    waiting = None
    for item in items:
        made = first(item)
        if waiting is not None:
            second(*waiting)
        waiting = (item, made)
    second(*waiting)


def pack_edges(state_ref, own_ref, even_ref, odd_ref):
    lane = iota(1)
    groups = lane_groups()
    slots = [jnp.where(((lane & (GROUP - 1)) >> 2) == f, 1.0, 0.0) for f in range(FIELDS)]
    even = (lax.axis_index("col") & 1) == 0

    def first(at):
        b, zz = at
        return gather_edges([[state_ref[f, 4 * b + r, zz] for r in range(4)] for f in range(FIELDS)], groups)

    def second(at, owns):
        b, zz = at
        ups = [turn(own, DEPTH * f - 4, 1) for f, own in enumerate(owns)]
        downs = [turn(own, DEPTH * f - 8, 1) for f, own in enumerate(owns)]
        up = functools.reduce(lambda a, b: a + b, [v * m for v, m in zip(ups, slots)])
        down = functools.reduce(lambda a, b: a + b, [v * m for v, m in zip(downs, slots)])
        for f in range(FIELDS):
            own_ref[f, b, zz] = owns[f]
        even_ref[b, zz] = jnp.where(even, up, down)
        odd_ref[b, zz] = jnp.where(even, down, up)

    staged([(b, zz) for b in range(2) for zz in range(OWN)], first, second)


def low_and_high(even_ref, odd_ref):
    even = (lax.axis_index("col") & 1) == 0

    def low(*at):
        return jnp.where(even, odd_ref[at], even_ref[at])

    def high(*at):
        return jnp.where(even, even_ref[at], odd_ref[at])

    return low, high


def layer_edge_kernel(even_ref, odd_ref, inner_ref, out_ref):
    gz = lax.axis_index("gz")
    for i, ref in enumerate((even_ref, odd_ref)):
        for b in range(2):
            out_ref[i, b] = jnp.where(gz == 0, ref[b, OWN - 1], ref[b, 0])


def spread_layers(gz, z_ref, ext_ref):
    for f in range(FIELDS):
        halo = z_ref[f].reshape(DEPTH * ROWS, 128)
        nothing = jnp.zeros_like(halo)
        ext_ref[f, : DEPTH * ROWS] = jnp.where(gz == 0, halo, nothing)
        ext_ref[f, DEPTH * ROWS :] = jnp.where(gz == 0, nothing, halo)


def corner_kernel(row_size, weight_ref, z_ref, even_ref, odd_ref, layer_ref, *rest):
    x_refs, ext_ref = rest[:-1], rest[-1]
    gz = lax.axis_index("gz")
    valid = (iota(0) < 4) == (gz == 0)
    spread_layers(gz, z_ref, ext_ref)
    low, high = low_and_high(even_ref, odd_ref)
    low_z, high_z = low_and_high(layer_ref.at[0], layer_ref.at[1])

    def send(up, slot):
        planes = UP_PLANES if up else DOWN_PLANES

        def tile(i):
            f, x = planes[i]
            return ext_ref[f, pl.ds(x, 8, stride=ROWS), :]

        for i in range(PAIRS):
            pair = tile(i)
            if i + PAIRS < len(planes):
                pair = pair + turn(tile(i + PAIRS), 4, 0)
            x_refs[slot][i] = pair
        b = 1 if up else 0
        for zz in range(OWN):
            x_refs[slot][PAIRS + zz] = low(b, zz)
            x_refs[slot][PAIRS + CHUNK + zz] = high(b, zz)
        x_refs[slot][PAIRS + OWN] = jnp.where(valid, low_z(b), 0.0)
        x_refs[slot][PAIRS + CHUNK + OWN] = jnp.where(valid, high_z(b), 0.0)

    directions(row_size, send)


def turn_sides(low, high):
    lows = [turn(low, 12 - DEPTH * f, 1) for f in range(FIELDS)]
    return lows, [turn(high, 8 - DEPTH * f, 1) for f in range(FIELDS)]


def edge_tiles(owns, sides, place):
    turned = [turn(own, 8, 1) for own in owns]
    out = []
    for own, own_turned, low, high in zip(owns, turned, *sides):
        tile = jnp.where(place < 16, low, own_turned)
        tile = jnp.where(place < 12, high, tile)
        out.append(jnp.where(place < 8, own, tile))
    return out


class Tiles:
    def __init__(self, first, ez_ref, shift):
        self.first, self.ez_ref, self.shift = first, ez_ref, shift
        self.values = {}

    def get(self, f, i, zz):
        value = self.values.get((f, i, zz))
        return self.first(f, i, zz) if value is None else value

    def put(self, f, i, zz, tile):
        self.values[f, i, zz] = tile
        at = i - self.shift
        if f == 2 and zz < OWN and self.ez_ref is not None and 0 <= at < self.ez_ref.shape[0]:
            self.ez_ref[at, zz] = tile


def leapfrog(tiles, exists, h_rows, e_rows, across, h_of, c_of, h_layers, e_layers, skip_hx):
    sub = iota(0)
    every = range(CHUNK)
    blank = [jnp.zeros((8, 128), jnp.float32)] * CHUNK

    def above(values):
        turned = [turn(v, -1, 0) for v in values]
        return [jnp.where(sub == 7, turned[(zz + 1) % CHUNK], turned[zz]) for zz in every]

    def beneath(values):
        turned = [turn(v, 1, 0) for v in values]
        return [jnp.where(sub == 0, turned[zz - 1], turned[zz]) for zz in every]

    def row(f, i):
        return [tiles.get(f, i, zz) for zz in every]

    def load_e(i):
        ey, ez = row(1, i), row(2, i)
        out = dict(ey=ey, ez=ez, ey_x=across.turned(ey, -1), ez_x=across.turned(ez, -1))
        if i in h_rows:
            ex = row(0, i)
            out.update(ex=ex, ex_y=[turn(v, -1, 1) for v in ex], ex_z=above(ex))
            if i not in skip_hx:
                out.update(ez_y=[turn(v, -1, 1) for v in ez], ey_z=above(ey))
        return out

    def work_h(i, loaded):
        e, after, h = loaded[i], loaded.get(i + 1), h_of(i)
        ey_x = across.pick(e["ey_x"], after["ey_x"] if after else blank, -1)
        ez_x = across.pick(e["ez_x"], after["ez_x"] if after else blank, -1)
        new = {}
        for zz in h_layers:
            if i not in skip_hx:
                curl = (e["ez_y"][zz] - e["ez"][zz]) - (e["ey_z"][zz] - e["ey"][zz])
                new[3, zz] = tiles.get(3, i, zz) - h[zz] * curl
            curl = (e["ex_z"][zz] - e["ex"][zz]) - (ez_x[zz] - e["ez"][zz])
            new[4, zz] = tiles.get(4, i, zz) - h[zz] * curl
            curl = (ey_x[zz] - e["ey"][zz]) - (e["ex_y"][zz] - e["ex"][zz])
            new[5, zz] = tiles.get(5, i, zz) - h[zz] * curl
        for (f, zz), tile in new.items():
            tiles.put(f, i, zz, tile)

    def load_h(i):
        hy, hz = row(4, i), row(5, i)
        out = dict(hy=hy, hz=hz, hy_x=across.turned(hy, 1), hz_x=across.turned(hz, 1))
        if i in e_rows:
            hx = row(3, i)
            out.update(hx=hx, hx_y=[turn(v, 1, 1) for v in hx], hz_y=[turn(v, 1, 1) for v in hz])
            out.update(hx_z=beneath(hx), hy_z=beneath(hy))
        return out

    def work_e(i, loaded):
        h, before, c = loaded[i], loaded.get(i - 1), c_of(i)
        hy_x = across.pick(h["hy_x"], before["hy_x"] if before else blank, 1)
        hz_x = across.pick(h["hz_x"], before["hz_x"] if before else blank, 1)
        new = {}
        for zz in e_layers:
            curl = (h["hz"][zz] - h["hz_y"][zz]) - (h["hy"][zz] - h["hy_z"][zz])
            new[0, zz] = tiles.get(0, i, zz) + c[zz] * curl
            curl = (h["hx"][zz] - h["hx_z"][zz]) - (h["hz"][zz] - hz_x[zz])
            new[1, zz] = tiles.get(1, i, zz) + c[zz] * curl
            curl = (h["hy"][zz] - hy_x[zz]) - (h["hx"][zz] - h["hx_y"][zz])
            new[2, zz] = tiles.get(2, i, zz) + c[zz] * curl
        for (f, zz), tile in new.items():
            tiles.put(f, i, zz, tile)

    def items(rows, load, work):
        loaded = {}

        def want(i):
            if i not in loaded and i in exists:
                loaded[i] = load(i)

        def ahead(i):
            for j in (i - 1, i, i + 1):
                if j in rows and j <= i or j == i + (1 if load is load_e else -1):
                    want(j)

        return [(functools.partial(ahead, i), functools.partial(work, i, loaded)) for i in rows]

    return items(h_rows, load_e, work_h), items(e_rows, load_h, work_e)


def pipeline(items):
    if items:
        items[0][0]()
    for at, (_, work) in enumerate(items):
        if at + 1 < len(items):
            items[at + 1][0]()
        work()


def aside(work):
    return lambda: None, work


class Rows:
    def turned(self, values, way):
        return values

    def pick(self, own, other, way):
        return other


class Blocks:
    def __init__(self, groups):
        self.groups = groups

    def turned(self, values, way):
        return [turn(v, way * GROUP, 1) for v in values]

    def pick(self, own, other, way):
        edge = self.groups[3] if way < 0 else self.groups[0]
        return [jnp.where(edge, o, v) for o, v in zip(other, own)]


def spans_inner(n, has_below, has_above):
    last = 7 - n if has_above else 7
    return (n - 1 if has_below else 0, last), (n if has_below else 0, last)


def spans_below(n):
    return (n - 5, n - 2), (n - 4, n - 1)


def spans_above(n):
    return (8 - n, 11 - n), (8 - n, 11 - n)


class Stepper:
    def __init__(self, row_size, main, edge, main_exists, edge_exists, skip_hx):
        gz, row, col = (lax.axis_index(name) for name in ("gz", "row", "col"))
        lane, sub = iota(1), iota(0)
        place, self.group = lane & (GROUP - 1), lane >> 5
        full = jnp.full((8, 128), time_step, jnp.float32)
        self.layer_half = [full] * OWN + [jnp.where((sub >= 4) & (gz == 0), 0.0, full)]
        outside = (place >= 12) & (place < 16) & (col == 0)
        self.edge_half = [jnp.where(outside, 0.0, v) for v in self.layer_half]
        self.lowest = jnp.where(row == 0, 0.0, 1.0) if row_size > 2 else None
        self.main, self.edge, self.skip_hx = main, edge, skip_hx
        self.main_exists, self.edge_exists = main_exists, edge_exists
        self.blocks = Blocks([self.group == r for r in range(4)])

    def masked(self, values, block, span):
        low, high = max(span[0] - 4 * block, 0), min(span[1] - 4 * block, 3)
        if low == 0 and high == 3:
            return values
        mask = (self.group >= low) & (self.group <= high)
        return [jnp.where(mask, v, 0.0) for v in values]

    def main_h(self, i):
        return self.layer_half if self.lowest is None or i >= DEPTH else [v * self.lowest for v in self.layer_half]

    def main_c(self, i):
        return [self.main.get(6, i, zz) for zz in range(CHUNK)]

    def edge_h(self, i, span):
        h = self.edge_half if self.lowest is None or i else [v * self.lowest for v in self.edge_half]
        return self.masked(h, i - 1, span)

    def edge_c(self, i, span):
        return self.masked([self.edge.get(6, i, zz) for zz in range(CHUNK)], i - 1, span)

    def step(self, n, spans, between=None):
        def blocks_of(span):
            return [b + 1 for b in range(-1, 3) if span[0] <= 4 * b + 3 and span[1] >= 4 * b]

        layers = range(CHUNK)
        last = range(OWN) if n == STEPS else layers
        parts = []
        for h_span, e_span in spans:
            h_rows = list(range(DEPTH + h_span[0], DEPTH + h_span[1] + 1))
            e_rows = list(range(DEPTH + e_span[0], DEPTH + e_span[1] + 1))
            skip = h_rows[:1] if self.skip_hx and h_span[0] < e_span[0] else []
            if self.main is not None:
                parts.append(
                    leapfrog(self.main, self.main_exists, h_rows, e_rows, Rows(), self.main_h, self.main_c, layers, last, skip)
                )
            if self.edge is None:
                continue
            h_of, c_of = functools.partial(self.edge_h, span=h_span), functools.partial(self.edge_c, span=e_span)
            parts.append(
                leapfrog(
                    self.edge, self.edge_exists, blocks_of(h_span), blocks_of(e_span), self.blocks, h_of, c_of, layers, last, []
                )
            )
        hs = [item for part in parts for item in part[0]]
        es = [item for part in parts for item in part[1]]
        if between is None and len(hs) < 4:
            between = lambda: None
        return hs + ([aside(between)] if between is not None else []) + es


def rows_cases(row_size, row, run):
    if row_size == 2:
        pl.when(row == 0)(functools.partial(run, False, True))
        pl.when(row == 1)(functools.partial(run, True, False))
    else:
        run(True, True)


def port_sums(n, reached, prow_ref, weight_ref, ez_ref, edge_ref, sum_ref, add_ref):
    for k in range(PORT_TILE):
        at = prow_ref[0, 0, k]
        total = jnp.zeros((8, 128), jnp.float32)
        for zz in range(OWN):
            if ez_ref is not None:
                total = total + ez_ref[at, zz] * weight_ref[k, 0, zz]
            if edge_ref is not None:
                total = total + edge_ref[at >> 2, zz] * weight_ref[k, 1, zz]
        total = jnp.sum(jnp.where(reached(n, at), total, 0.0), axis=0, keepdims=True)
        if add_ref is not None:
            total = total + add_ref[n - 1, k : k + 1, :]
        sum_ref[n - 1, k : k + 1, :] = total


def finish(fields, b, main, edge, write):
    lane = iota(1)
    place = lane & (GROUP - 1)
    sides = (lane < DEPTH) | (lane >= 128 - DEPTH)

    def first(f):
        tiles = [edge.get(f, b + 1, zz) for zz in range(OWN)]
        turned = [turn(tile, -8, 1) for tile in tiles]
        return [jnp.where(place < 8, tile, other) for tile, other in zip(tiles, turned)]

    def second(f, near):
        turned = {(r, zz): turn(near[zz], -(GROUP * r + 8), 1) for r in range(4) for zz in range(OWN)}
        made = {(r, zz): jnp.where(sides, tile, main.get(f, DEPTH + 4 * b + r, zz)) for (r, zz), tile in turned.items()}
        for (r, zz), tile in made.items():
            write(f, r, zz, tile)

    staged(fields, first, second)


def weight_kernel(mode_ref, prow_ref, pcol_ref, pmode_ref, pid_ref, order_ref, weight_ref, strip_ref):
    lane = iota(1)
    for k in range(PORT_TILE):
        strip_ref[k] = jnp.zeros(strip_ref.shape[1:], jnp.float32)
        strip_ref[k, :, 0:PLEN] = mode_ref[pmode_ref[0, 0, k]]
    for k in range(PORT_TILE):
        turned = GROUP * (prow_ref[0, 0, k] & 3)
        at = lane - turned
        for zz in range(OWN):
            tile = pltpu.roll(strip_ref[k, 8 * zz : 8 * zz + 8, :], pcol_ref[0, 0, k], 1)
            weight_ref[k, 0, zz] = jnp.where((lane >= DEPTH) & (lane < 128 - DEPTH), tile, 0.0)
            own = pltpu.roll(tile, turned + 8, 1)
            edge = jnp.where((at >= 4) & (at < 8), own, 0.0)
            weight_ref[k, 1, zz] = jnp.where((at >= 16) & (at < 20), turn(own, 8, 1), edge)


def inner_kernel(
    row_size, elec_ref, magn_ref, mat_ref, z_ref, eps_ref,
    e_ref, h_ref, c_ref, ez_ref, state_ref, plain_ref, ext_ref, halo_ref,
):
    gz, row = lax.axis_index("gz"), lax.axis_index("row")
    spread_layers(gz, z_ref, ext_ref)
    for f in range(FIELDS):
        for x in range(ROWS):
            halo_ref[f, x] = ext_ref[f, pl.ds(x, 8, stride=ROWS), :]
    for z in range(LAYERS):
        plain_ref[z] = coefficient(mat_ref[z], eps_ref)
    for f in range(3):
        rows_outside(elec_ref.reshape(3 * LAYERS * ROWS, 128), f, state_ref, f)
        rows_outside(magn_ref.reshape(3 * LAYERS * ROWS, 128), f, state_ref, f + 3)
    rows_outside(plain_ref.reshape(LAYERS * ROWS, 128), 0, state_ref, 6)

    def first(f, i, zz):
        return halo_ref[f, i - DEPTH] if zz == OWN else state_ref[f, i - DEPTH, zz]

    def run(has_below, has_above):
        main = Tiles(first, None, DEPTH)
        stepper = Stepper(row_size, main, None, range(4, 12), (), False)
        items = []
        for n in range(1, STEPS + 1):
            items.append(aside(functools.partial(setattr, main, "ez_ref", ez_ref.at[n - 1])))
            items += stepper.step(n, [spans_inner(n, has_below, has_above)])
        pipeline(items)
        for i in range(ROWS):
            for zz in range(CHUNK):
                for f in range(6):
                    (e_ref, h_ref)[f // 3][f % 3, i, zz] = main.get(f, DEPTH + i, zz)
                c_ref[i, zz] = main.get(6, DEPTH + i, zz)

    rows_cases(row_size, row, run)


def rim_kernel(
    row_size, z_ref, own_ref, even_ref, odd_ref, layer_ref, e_in, h_in, ez_in, weight_ref, prow_ref,
    edge_e_ref, edge_h_ref, edge_c_ref, done_ref, sum_ref, ext_ref, ez_ref,
):
    gz, row = lax.axis_index("gz"), lax.axis_index("row")
    place = iota(1) & (GROUP - 1)
    groups = lane_groups()
    valid = (iota(0) < 4) == (gz == 0)
    spread_layers(gz, z_ref, ext_ref)
    low_of, high_of = low_and_high(even_ref, odd_ref)
    low_z, high_z = low_and_high(layer_ref.at[0], layer_ref.at[1])
    joined = {}

    def first(at):
        b, zz = at
        if zz < OWN:
            return [own_ref[f, b, zz] for f in range(FIELDS)], turn_sides(low_of(b, zz), high_of(b, zz))
        rows = [[ext_ref[f, pl.ds(4 * b + r, 8, stride=ROWS), :] for r in range(4)] for f in range(FIELDS)]
        sides = turn_sides(*(jnp.where(valid, side(b), 0.0) for side in (low_z, high_z)))
        return gather_edges(rows, groups), sides

    def second(at, made):
        for f, tile in enumerate(edge_tiles(*made, place)):
            joined[f, at[0] + 1, at[1]] = tile

    staged([(b, zz) for b in range(2) for zz in range(CHUNK)], first, second)

    def run(has_below, has_above):
        main = Tiles(lambda f, i, zz: (e_in, h_in)[f // 3][f % 3, i - DEPTH, zz], None, DEPTH)
        edge = Tiles(lambda f, i, zz: joined[f, i, zz], ez_ref, 1)
        stepper = Stepper(row_size, None, edge, (), (1, 2), False)

        def reached(n, at):
            low, high = spans_inner(n, has_below, has_above)[1]
            return (at >= low) & (at <= high)

        items = []
        for n in range(1, STEPS + 1):
            items += stepper.step(n, [spans_inner(n, has_below, has_above)])
            sums = functools.partial(port_sums, n, reached, prow_ref, weight_ref, ez_in.at[n - 1], ez_ref, sum_ref, None)
            items.append(aside(sums))
        pipeline(items)
        for i in range(2):
            for zz in range(CHUNK):
                for f in range(6):
                    (edge_e_ref, edge_h_ref)[f // 3][f % 3, i, zz] = edge.get(f, 1 + i, zz)
                edge_c_ref[i, zz] = edge.get(6, 1 + i, zz)
        if has_below != has_above:

            def write(f, r, zz, tile):
                done_ref[f, r, zz] = tile

            finish(range(6), 0 if has_above else 1, main, edge, write)

    rows_cases(row_size, row, run)


def outer_kernel(
    row_size, ports_each, prow_ref, pid_ref, e_in, h_in, c_in, weight_ref, edge_e_in, edge_h_in, edge_c_in, done_ref, sum_in,
    *rest,
):
    n_x = 1 if row_size == 2 else 2
    x_refs, corner_refs = rest[:n_x], rest[n_x : 2 * n_x]
    eout_hbm, hout_hbm, term_ref, ez_ref, edge_ez_ref, sum_ref, turned_ref, out_ref, sems = rest[2 * n_x :]
    gz, row = lax.axis_index("gz"), lax.axis_index("row")
    lane, sub = iota(1), iota(0)
    place = lane & (GROUP - 1)
    groups = lane_groups()
    valid = (sub < 4) == (gz == 0)
    zeros = jnp.zeros((8, 128), jnp.float32)

    def first_main(f, i, zz):
        if f == 6:
            return c_in[i - DEPTH, zz]
        return e_in[f, i - DEPTH, zz] if f < 3 else h_in[f - 3, i - DEPTH, zz]

    def first_edge(f, i, zz):
        if f == 6:
            return edge_c_in[i - 1, zz]
        return edge_e_in[f, i - 1, zz] if f < 3 else edge_h_in[f - 3, i - 1, zz]

    def write_terms():
        basis = zeros
        for n in range(STEPS):
            for f in range(2 * FREQ):
                basis = jnp.where((sub == n) & (lane == f), float(BASIS[n, f]), basis)
        transform = zeros
        for n in range(STEPS):
            sampled = jnp.sum(sum_ref[n], axis=1, keepdims=True)
            transform = transform + sampled * basis[n : n + 1, :]
        term_ref[...] = jnp.zeros(term_ref.shape, jnp.float32)
        for k in range(PORT_TILE):
            port = pid_ref[0, 0, k]
            term_ref[port // ports_each, pl.ds(port % ports_each, 1), :] = transform[k : k + 1, : 2 * FREQ]

    def run(has_below, has_above):
        main = Tiles(first_main, ez_ref, DEPTH)
        edge = Tiles(first_edge, edge_ez_ref, 1)

        def halo_rows(planes, slot, offset, b):
            got = {}
            for i, (f, x) in enumerate(planes):
                packed = corner_refs[slot][i % PAIRS]
                if i >= PAIRS:
                    packed = turn(packed, 4, 0)
                tiles = [x_refs[slot][i, zz] for zz in range(OWN)]
                tiles.append(jnp.where(valid, packed, 0.0))
                for zz in range(CHUNK):
                    main.put(f, DEPTH + x + offset, zz, tiles[zz])
                    got[f, x + offset - 4 * b, zz] = tiles[zz]

            def first(zz):
                rows = [[got.get((f, r, zz)) for r in range(4)] for f in range(FIELDS)]
                sides = turn_sides(corner_refs[slot][PAIRS + zz], corner_refs[slot][PAIRS + CHUNK + zz])
                return gather_edges(rows, groups), sides

            def second(zz, made):
                for f, tile in enumerate(edge_tiles(*made, place)):
                    edge.put(f, 1 + b, zz, tile)

            staged(range(CHUNK), first, second)

        if has_below:
            halo_rows(UP_PLANES, 0, -ROWS, -1)
        if has_above:
            halo_rows(DOWN_PLANES, n_x - 1, ROWS, 2)

        def reached(n, at):
            out = None
            for wanted, span in ((has_below, spans_below(n)[1]), (has_above, spans_above(n)[1])):
                if wanted:
                    part = (at >= span[0]) & (at <= span[1])
                    out = part if out is None else out | part
            return out

        rows = range(0 if has_below else 4, 16 if has_above else 12)
        blocks = range(0 if has_below else 1, 4 if has_above else 3)
        copies = []

        def hand_out(part):
            fields = range(3 * part, 3 * part + 3)

            def write(f, r, zz, tile, b):
                turned_ref[f, 4 * b + r, 8 * zz : 8 * zz + 8, :] = tile

            for b in range(2):
                put = functools.partial(write, b=b)
                if has_below and has_above or b == (1 if has_above else 0):
                    finish(fields, b, main, edge, put)
                else:
                    for f in fields:
                        for r in range(4):
                            for zz in range(OWN):
                                put(f, r, zz, done_ref[f, r, zz])
            flat = turned_ref.reshape(6 * ROWS * LAYERS, 128)
            for f in fields:
                for z in range(LAYERS):
                    out_ref[f, z] = flat[pl.ds(f * ROWS * LAYERS + z, ROWS, stride=LAYERS), :]
            dest = hout_hbm if part else eout_hbm
            copies.append(pltpu.make_async_copy(out_ref.at[pl.ds(3 * part, 3)], dest, sems.at[part]))
            copies[-1].start()

        stepper = Stepper(row_size, main, edge, rows, blocks, True)
        items = []
        for n in range(1, STEPS + 1):
            spans = ([spans_below(n)] if has_below else []) + ([spans_above(n)] if has_above else [])
            items += stepper.step(n, spans, functools.partial(hand_out, 1) if n == STEPS else None)
            sums = functools.partial(port_sums, n, reached, prow_ref, weight_ref, ez_ref, edge_ez_ref, sum_ref, sum_in)
            items.append(aside(sums))
        pipeline(items)
        hand_out(0)
        write_terms()
        for copy in copies:
            copy.wait()

    rows_cases(row_size, row, run)


def shifted(block, axis, size, distance):
    route = [(i - distance, i) for i in range(size) if 0 <= i - distance < size]
    return lax.ppermute(block, axis, route)


def swapped(block, axis, size, start=0):
    pairs = [(i, i + 1) for i in range(start, size - 1, 2)]
    return lax.ppermute(block, axis, pairs + [(j, i) for i, j in pairs])


def solution(mesh):
    sizes = dict(mesh.shape)
    row_size, col_size, gz_size = sizes["row"], sizes["col"], sizes["gz"]
    n_x = 1 if row_size == 2 else 2

    def across_rows(blocks):
        if row_size == 2:
            return (swapped(blocks[0], "row", 2),)
        return (shifted(blocks[0], "row", row_size, 1), shifted(blocks[1], "row", row_size, -1))

    def per_device(
        electric, magnetic, material, eps_table, mode_table, port_row, port_col, port_mode, port_ids
    ):
        f32 = jnp.float32

        def array(*shape):
            return jax.ShapeDtypeStruct(shape, f32)

        def scratch(*shape):
            return pltpu.VMEM(shape, f32)

        z_send, own, even_send, odd_send, *x_send = pl.pallas_call(
            functools.partial(pack_kernel, row_size),
            out_shape=[
                array(FIELDS, DEPTH, ROWS, 128),
                array(FIELDS, 2, OWN, 8, 128),
                array(2, OWN, 8, 128),
                array(2, OWN, 8, 128),
            ]
            + [array(PLANES, OWN, 8, 128)] * n_x,
            in_specs=[HBM] * 4,
            out_specs=[VMEM] * (4 + n_x),
            scratch_shapes=[
                scratch(FIELDS, ROWS, OWN, 8, 128),
                scratch(FIELDS, LAYERS, ROWS, 128),
                pltpu.SMEM(eps_table.shape, f32),
                pltpu.VMEM(material.shape, jnp.int32),
                pltpu.SemaphoreType.DMA((4,)),
            ],
            name="pack",
        )(eps_table, electric, magnetic, material)
        x_halo = across_rows(x_send)
        even = swapped(even_send, "col", col_size)
        odd = swapped(odd_send, "col", col_size, 1)
        z_halo = swapped(z_send, "gz", gz_size)
        e_now, h_now, c_now, ez_now = pl.pallas_call(
            functools.partial(inner_kernel, row_size),
            out_shape=[
                array(3, ROWS, CHUNK, 8, 128),
                array(3, ROWS, CHUNK, 8, 128),
                array(ROWS, CHUNK, 8, 128),
                array(STEPS, ROWS, OWN, 8, 128),
            ],
            in_specs=[VMEM] * 4 + [SMEM],
            out_specs=[VMEM] * 4,
            scratch_shapes=[
                scratch(FIELDS, ROWS, OWN, 8, 128),
                scratch(LAYERS, ROWS, 128),
                scratch(FIELDS, 8 * ROWS, 128),
                scratch(FIELDS, ROWS, 8, 128),
            ],
            compiler_params=PARAMS,
            cost_estimate=pl.CostEstimate(flops=5_000_000, bytes_accessed=10_000_000, transcendentals=0),
            name="inner",
        )(electric, magnetic, material, z_halo, eps_table)
        layer_send = pl.pallas_call(
            layer_edge_kernel,
            out_shape=array(2, 2, 8, 128),
            in_specs=[VMEM] * 2 + [pl.BlockSpec(memory_space=pl.ANY)],
            out_specs=VMEM,
            compiler_params=PARAMS,
            name="layer_edges",
        )(even, odd, c_now)
        layer_halo = swapped(layer_send, "gz", gz_size)
        weights = pl.pallas_call(
            weight_kernel,
            out_shape=array(PORT_TILE, 2, OWN, 8, 128),
            in_specs=[VMEM] + [SMEM] * 4 + [ANY],
            out_specs=VMEM,
            scratch_shapes=[scratch(PORT_TILE, LAYERS, 128)],
            compiler_params=PARAMS,
            name="weights",
        )(mode_table, port_row, port_col, port_mode, port_ids, layer_send)
        corner_send = pl.pallas_call(
            functools.partial(corner_kernel, row_size),
            out_shape=[array(PAIRS + 2 * CHUNK, 8, 128)] * n_x,
            in_specs=[ANY] + [VMEM] * 4,
            out_specs=[VMEM] * n_x,
            scratch_shapes=[scratch(FIELDS, 8 * ROWS, 128)],
            compiler_params=PARAMS,
            name="corners",
        )(weights, z_halo, even, odd, layer_halo)
        corner = across_rows(corner_send)
        edges = pl.pallas_call(
            functools.partial(rim_kernel, row_size),
            out_shape=[
                array(3, 2, CHUNK, 8, 128),
                array(3, 2, CHUNK, 8, 128),
                array(2, CHUNK, 8, 128),
                array(6, 4, OWN, 8, 128),
                array(STEPS, 8, 128),
            ],
            in_specs=[VMEM] * 9 + [SMEM],
            out_specs=[VMEM] * 5,
            scratch_shapes=[scratch(FIELDS, 8 * ROWS, 128), scratch(2, OWN, 8, 128)],
            compiler_params=PARAMS,
            name="rim",
        )(z_halo, own, even, odd, layer_halo, e_now, h_now, ez_now, weights, port_row)
        devices = col_size * row_size * gz_size
        ports_each = PORT_TILE * col_size * row_size // devices
        electric_out, magnetic_out, term = pl.pallas_call(
            functools.partial(outer_kernel, row_size, ports_each),
            out_shape=[array(3, LAYERS, ROWS, 128)] * 2 + [array(devices, ports_each, 2 * FREQ)],
            in_specs=[SMEM] * 2 + [VMEM] * (9 + 2 * n_x),
            out_specs=[HBM, HBM, VMEM],
            scratch_shapes=[
                scratch(ROWS, OWN, 8, 128),
                scratch(2, OWN, 8, 128),
                scratch(STEPS, 8, 128),
                scratch(6, ROWS, LAYERS, 128),
                scratch(6, LAYERS, ROWS, 128),
                pltpu.SemaphoreType.DMA((2,)),
            ],
            compiler_params=PARAMS,
            name="outer",
        )(port_row, port_ids, e_now, h_now, c_now, weights, *edges, *x_halo, *corner)
        terms = lax.all_to_all(term, ("col", "row", "gz"), 0, 0, tiled=True)
        return (
            electric_out,
            magnetic_out,
            jnp.sum(terms, axis=0),
        )

    in_specs = (
        P(None, "gz", "row", ("grp", "col")),
        P(None, "gz", "row", ("grp", "col")),
        P("gz", "row", ("grp", "col")),
        P(),
        P(None, "gz", None),
        P(("grp", "row"), "col", None),
        P(("grp", "row"), "col", None),
        P(("grp", "row"), "col", None),
        P(("grp", "row"), "col", None),
    )
    out_specs = (
        P(None, "gz", "row", ("grp", "col")),
        P(None, "gz", "row", ("grp", "col")),
        P(("grp", "col", "row", "gz"), None),
    )
    return jax.shard_map(
        per_device, mesh=mesh, in_specs=in_specs, out_specs=out_specs, check_vma=False
    )
```

```python
import functools

import jax
import jax.numpy as jnp
import numpy as np
from jax import lax
from jax.experimental import pallas as pl
from jax.experimental.pallas import tpu as pltpu
from jax.sharding import PartitionSpec as P

STEPS = 4
FREQ = 8
MATS = 8
PLEN = 64
PORT_TILE = 4
FIELDS = 7
DEPTH = STEPS
ROWS = 8
LAYERS = 32
OWN = 4
CHUNK = 5
GROUP = 32

time_step = 0.5

UP_PLANES = [(f, 4) for f in (0, 1, 2, 4, 5)] + [(f, x) for x in (5, 6, 7) for f in range(FIELDS)]
DOWN_PLANES = [(f, x) for x in (0, 1, 2) for f in range(FIELDS)] + [(1, 3), (2, 3)]
PLANES = max(len(UP_PLANES), len(DOWN_PLANES))
PAIRS = (PLANES + 1) // 2

VMEM = pl.BlockSpec(memory_space=pltpu.VMEM)
SMEM = pl.BlockSpec(memory_space=pltpu.SMEM)
HBM = pl.BlockSpec(memory_space=pltpu.HBM)
ANY = pl.BlockSpec(memory_space=pl.ANY)
PARAMS = pltpu.CompilerParams(vmem_limit_bytes=16 * 1024 * 1024)


def dft_basis():
    times = (np.arange(STEPS) + 1.0) * time_step
    omegas = np.pi * (np.arange(FREQ) + 1.0) / FREQ
    angle = times[:, None] * omegas[None, :]
    return np.concatenate([np.cos(angle), -np.sin(angle)], axis=1)


BASIS = dft_basis()


def iota(axis):
    return lax.broadcasted_iota(jnp.int32, (8, 128), axis)


def turn(tile, shift, axis):
    return pltpu.roll(tile, shift % tile.shape[axis], axis)


def directions(row_size, body):
    if row_size == 2:
        row = lax.axis_index("row")
        pl.when(row == 0)(functools.partial(body, True, 0))
        pl.when(row == 1)(functools.partial(body, False, 0))
    else:
        body(True, 0)
        body(False, 1)


def coefficient(material, eps_ref):
    eps = jnp.full((8, 128), eps_ref[0], jnp.float32)
    for which in range(1, MATS):
        eps = jnp.where(material == which, eps_ref[which], eps)
    return time_step * (1.0 / eps)


def rows_outside(flat, f, state_ref, at):
    for x in range(ROWS):
        state_ref[at, x] = flat[pl.ds(f * LAYERS * ROWS + x, LAYERS, stride=ROWS), :].reshape(OWN, 8, 128)


def pack_kernel(row_size, eps_hbm, elec_hbm, magn_hbm, mat_hbm, z_ref, own_ref, even_ref, odd_ref, *rest):
    n_x = 1 if row_size == 2 else 2
    x_hbms, x_refs, (state_ref, main_ref, eps_ref, mat_ref, sems) = rest[:n_x], rest[n_x : 2 * n_x], rest[2 * n_x :]
    copies = [pltpu.make_async_copy(eps_hbm, eps_ref, sems.at[6]), pltpu.make_async_copy(mat_hbm, mat_ref, sems.at[7])]
    for f in range(3):
        copies.append(pltpu.make_async_copy(elec_hbm.at[f], main_ref.at[f], sems.at[f]))
    for f in range(3):
        copies.append(pltpu.make_async_copy(magn_hbm.at[f], main_ref.at[3 + f], sems.at[3 + f]))
    for copy in copies:
        copy.start()
    flat = main_ref.reshape(FIELDS * LAYERS * ROWS, 128)
    copies[0].wait()
    copies[1].wait()
    for z in range(LAYERS):
        main_ref[6, z] = coefficient(mat_ref[z], eps_ref)
    rows_outside(flat, 6, state_ref, 6)
    for f in range(6):
        copies[2 + f].wait()
        rows_outside(flat, f, state_ref, f)

    def send(up, slot):
        for i, (f, x) in enumerate(UP_PLANES if up else DOWN_PLANES):
            x_refs[slot][i] = state_ref[f, x]

    directions(row_size, send)
    outs = [pltpu.make_async_copy(ref, hbm, sems.at[8 + i]) for i, (ref, hbm) in enumerate(zip(x_refs, x_hbms))]
    for out in outs:
        out.start()
    start = jnp.where(lax.axis_index("gz") == 0, LAYERS - DEPTH, 0)
    for f in range(FIELDS):
        z_ref[f] = main_ref[f, pl.ds(start, DEPTH)]
    pack_edges(state_ref, own_ref, even_ref, odd_ref)
    for out in outs:
        out.wait()


def lane_groups():
    group = iota(1) >> 5
    return [jnp.where(group == r, 1.0, 0.0) for r in range(4)]


def gather_edges(rows_of, groups):
    moved = [[tile if tile is None else turn(tile, GROUP * r + 8, 1) for r, tile in enumerate(rows)] for rows in rows_of]
    out = []
    for rows in moved:
        parts = [tile * groups[r] for r, tile in enumerate(rows) if tile is not None]
        out.append(functools.reduce(lambda a, b: a + b, parts) if parts else jnp.zeros((8, 128), jnp.float32))
    return out


def staged(items, first, second):
    waiting = None
    for item in items:
        made = first(item)
        if waiting is not None:
            second(*waiting)
        waiting = (item, made)
    second(*waiting)


def pack_edges(state_ref, own_ref, even_ref, odd_ref):
    lane = iota(1)
    groups = lane_groups()
    slots = [jnp.where(((lane & (GROUP - 1)) >> 2) == f, 1.0, 0.0) for f in range(FIELDS)]
    even = (lax.axis_index("col") & 1) == 0

    def first(at):
        b, zz = at
        return gather_edges([[state_ref[f, 4 * b + r, zz] for r in range(4)] for f in range(FIELDS)], groups)

    def second(at, owns):
        b, zz = at
        ups = [turn(own, DEPTH * f - 4, 1) for f, own in enumerate(owns)]
        downs = [turn(own, DEPTH * f - 8, 1) for f, own in enumerate(owns)]
        up = functools.reduce(lambda a, b: a + b, [v * m for v, m in zip(ups, slots)])
        down = functools.reduce(lambda a, b: a + b, [v * m for v, m in zip(downs, slots)])
        for f in range(FIELDS):
            own_ref[f, b, zz] = owns[f]
        even_ref[b, zz] = jnp.where(even, up, down)
        odd_ref[b, zz] = jnp.where(even, down, up)

    staged([(b, zz) for b in range(2) for zz in range(OWN)], first, second)


def low_and_high(even_ref, odd_ref):
    even = (lax.axis_index("col") & 1) == 0

    def low(*at):
        return jnp.where(even, odd_ref[at], even_ref[at])

    def high(*at):
        return jnp.where(even, even_ref[at], odd_ref[at])

    return low, high


def layer_edge_kernel(even_ref, odd_ref, inner_ref, out_ref):
    gz = lax.axis_index("gz")
    for i, ref in enumerate((even_ref, odd_ref)):
        for b in range(2):
            out_ref[i, b] = jnp.where(gz == 0, ref[b, OWN - 1], ref[b, 0])


def spread_layers(gz, z_ref, ext_ref):
    for f in range(FIELDS):
        halo = z_ref[f].reshape(DEPTH * ROWS, 128)
        nothing = jnp.zeros_like(halo)
        ext_ref[f, : DEPTH * ROWS] = jnp.where(gz == 0, halo, nothing)
        ext_ref[f, DEPTH * ROWS :] = jnp.where(gz == 0, nothing, halo)


def corner_kernel(row_size, weight_ref, z_ref, even_ref, odd_ref, layer_ref, *rest):
    x_refs, ext_ref = rest[:-1], rest[-1]
    gz = lax.axis_index("gz")
    valid = (iota(0) < 4) == (gz == 0)
    spread_layers(gz, z_ref, ext_ref)
    low, high = low_and_high(even_ref, odd_ref)
    low_z, high_z = low_and_high(layer_ref.at[0], layer_ref.at[1])

    def send(up, slot):
        planes = UP_PLANES if up else DOWN_PLANES

        def tile(i):
            f, x = planes[i]
            return ext_ref[f, pl.ds(x, 8, stride=ROWS), :]

        for i in range(PAIRS):
            pair = tile(i)
            if i + PAIRS < len(planes):
                pair = pair + turn(tile(i + PAIRS), 4, 0)
            x_refs[slot][i] = pair
        b = 1 if up else 0
        for zz in range(OWN):
            x_refs[slot][PAIRS + zz] = low(b, zz)
            x_refs[slot][PAIRS + CHUNK + zz] = high(b, zz)
        x_refs[slot][PAIRS + OWN] = jnp.where(valid, low_z(b), 0.0)
        x_refs[slot][PAIRS + CHUNK + OWN] = jnp.where(valid, high_z(b), 0.0)

    directions(row_size, send)


def turn_sides(low, high):
    lows = [turn(low, 12 - DEPTH * f, 1) for f in range(FIELDS)]
    return lows, [turn(high, 8 - DEPTH * f, 1) for f in range(FIELDS)]


def edge_tiles(owns, sides, place):
    turned = [turn(own, 8, 1) for own in owns]
    out = []
    for own, own_turned, low, high in zip(owns, turned, *sides):
        tile = jnp.where(place < 16, low, own_turned)
        tile = jnp.where(place < 12, high, tile)
        out.append(jnp.where(place < 8, own, tile))
    return out


class Tiles:
    def __init__(self, first, ez_ref, shift):
        self.first, self.ez_ref, self.shift = first, ez_ref, shift
        self.values = {}

    def get(self, f, i, zz):
        value = self.values.get((f, i, zz))
        return self.first(f, i, zz) if value is None else value

    def put(self, f, i, zz, tile):
        self.values[f, i, zz] = tile
        at = i - self.shift
        if f == 2 and zz < OWN and self.ez_ref is not None and 0 <= at < self.ez_ref.shape[0]:
            self.ez_ref[at, zz] = tile


def leapfrog(tiles, exists, h_rows, e_rows, across, h_of, c_of, h_layers, e_layers, skip_hx):
    sub = iota(0)
    every = range(CHUNK)
    blank = [jnp.zeros((8, 128), jnp.float32)] * CHUNK

    def above(values):
        turned = [turn(v, -1, 0) for v in values]
        return [jnp.where(sub == 7, turned[(zz + 1) % CHUNK], turned[zz]) for zz in every]

    def beneath(values):
        turned = [turn(v, 1, 0) for v in values]
        return [jnp.where(sub == 0, turned[zz - 1], turned[zz]) for zz in every]

    def row(f, i):
        return [tiles.get(f, i, zz) for zz in every]

    def load_e(i):
        ey, ez = row(1, i), row(2, i)
        out = dict(ey=ey, ez=ez, ey_x=across.turned(ey, -1), ez_x=across.turned(ez, -1))
        if i in h_rows:
            ex = row(0, i)
            out.update(ex=ex, ex_y=[turn(v, -1, 1) for v in ex], ex_z=above(ex))
            if i not in skip_hx:
                out.update(ez_y=[turn(v, -1, 1) for v in ez], ey_z=above(ey))
        return out

    def work_h(i, loaded):
        e, after, h = loaded[i], loaded.get(i + 1), h_of(i)
        ey_x = across.pick(e["ey_x"], after["ey_x"] if after else blank, -1)
        ez_x = across.pick(e["ez_x"], after["ez_x"] if after else blank, -1)
        new = {}
        for zz in h_layers:
            if i not in skip_hx:
                curl = (e["ez_y"][zz] - e["ez"][zz]) - (e["ey_z"][zz] - e["ey"][zz])
                new[3, zz] = tiles.get(3, i, zz) - h[zz] * curl
            curl = (e["ex_z"][zz] - e["ex"][zz]) - (ez_x[zz] - e["ez"][zz])
            new[4, zz] = tiles.get(4, i, zz) - h[zz] * curl
            curl = (ey_x[zz] - e["ey"][zz]) - (e["ex_y"][zz] - e["ex"][zz])
            new[5, zz] = tiles.get(5, i, zz) - h[zz] * curl
        for (f, zz), tile in new.items():
            tiles.put(f, i, zz, tile)

    def load_h(i):
        hy, hz = row(4, i), row(5, i)
        out = dict(hy=hy, hz=hz, hy_x=across.turned(hy, 1), hz_x=across.turned(hz, 1))
        if i in e_rows:
            hx = row(3, i)
            out.update(hx=hx, hx_y=[turn(v, 1, 1) for v in hx], hz_y=[turn(v, 1, 1) for v in hz])
            out.update(hx_z=beneath(hx), hy_z=beneath(hy))
        return out

    def work_e(i, loaded):
        h, before, c = loaded[i], loaded.get(i - 1), c_of(i)
        hy_x = across.pick(h["hy_x"], before["hy_x"] if before else blank, 1)
        hz_x = across.pick(h["hz_x"], before["hz_x"] if before else blank, 1)
        new = {}
        for zz in e_layers:
            curl = (h["hz"][zz] - h["hz_y"][zz]) - (h["hy"][zz] - h["hy_z"][zz])
            new[0, zz] = tiles.get(0, i, zz) + c[zz] * curl
            curl = (h["hx"][zz] - h["hx_z"][zz]) - (h["hz"][zz] - hz_x[zz])
            new[1, zz] = tiles.get(1, i, zz) + c[zz] * curl
            curl = (h["hy"][zz] - hy_x[zz]) - (h["hx"][zz] - h["hx_y"][zz])
            new[2, zz] = tiles.get(2, i, zz) + c[zz] * curl
        for (f, zz), tile in new.items():
            tiles.put(f, i, zz, tile)

    def sweep(rows, load, work):
        loaded = {}

        def want(i):
            if i not in loaded and i in exists:
                loaded[i] = load(i)

        for i in rows:
            for j in (i - 1, i, i + 1):
                if j in rows or j == i + (1 if load is load_e else -1):
                    want(j)
            work(i, loaded)

    sweep(h_rows, load_e, work_h)
    yield
    sweep(e_rows, load_h, work_e)


class Rows:
    def turned(self, values, way):
        return values

    def pick(self, own, other, way):
        return other


class Blocks:
    def __init__(self, groups):
        self.groups = groups

    def turned(self, values, way):
        return [turn(v, way * GROUP, 1) for v in values]

    def pick(self, own, other, way):
        edge = self.groups[3] if way < 0 else self.groups[0]
        return [jnp.where(edge, o, v) for o, v in zip(other, own)]


def spans_inner(n, has_below, has_above):
    last = 7 - n if has_above else 7
    return (n - 1 if has_below else 0, last), (n if has_below else 0, last)


def spans_below(n):
    return (n - 5, n - 2), (n - 4, n - 1)


def spans_above(n):
    return (8 - n, 11 - n), (8 - n, 11 - n)


class Stepper:
    def __init__(self, row_size, main, edge, main_exists, edge_exists, skip_hx):
        gz, row, col = (lax.axis_index(name) for name in ("gz", "row", "col"))
        lane, sub = iota(1), iota(0)
        place, self.group = lane & (GROUP - 1), lane >> 5
        full = jnp.full((8, 128), time_step, jnp.float32)
        self.layer_half = [full] * OWN + [jnp.where((sub >= 4) & (gz == 0), 0.0, full)]
        outside = (place >= 12) & (place < 16) & (col == 0)
        self.edge_half = [jnp.where(outside, 0.0, v) for v in self.layer_half]
        self.lowest = jnp.where(row == 0, 0.0, 1.0) if row_size > 2 else None
        self.main, self.edge, self.skip_hx = main, edge, skip_hx
        self.main_exists, self.edge_exists = main_exists, edge_exists
        self.blocks = Blocks([self.group == r for r in range(4)])

    def masked(self, values, block, span):
        low, high = max(span[0] - 4 * block, 0), min(span[1] - 4 * block, 3)
        if low == 0 and high == 3:
            return values
        mask = (self.group >= low) & (self.group <= high)
        return [jnp.where(mask, v, 0.0) for v in values]

    def main_h(self, i):
        return self.layer_half if self.lowest is None or i >= DEPTH else [v * self.lowest for v in self.layer_half]

    def main_c(self, i):
        return [self.main.get(6, i, zz) for zz in range(CHUNK)]

    def edge_h(self, i, span):
        h = self.edge_half if self.lowest is None or i else [v * self.lowest for v in self.edge_half]
        return self.masked(h, i - 1, span)

    def edge_c(self, i, span):
        return self.masked([self.edge.get(6, i, zz) for zz in range(CHUNK)], i - 1, span)

    def step(self, n, spans, between=None):
        def blocks_of(span):
            return [b + 1 for b in range(-1, 3) if span[0] <= 4 * b + 3 and span[1] >= 4 * b]

        layers = range(CHUNK)
        last = range(OWN) if n == STEPS else layers
        parts = []
        for h_span, e_span in spans:
            h_rows = list(range(DEPTH + h_span[0], DEPTH + h_span[1] + 1))
            e_rows = list(range(DEPTH + e_span[0], DEPTH + e_span[1] + 1))
            skip = h_rows[:1] if self.skip_hx and h_span[0] < e_span[0] else []
            if self.main is not None:
                parts.append(
                    leapfrog(self.main, self.main_exists, h_rows, e_rows, Rows(), self.main_h, self.main_c, layers, last, skip)
                )
            if self.edge is None:
                continue
            h_of, c_of = functools.partial(self.edge_h, span=h_span), functools.partial(self.edge_c, span=e_span)
            parts.append(
                leapfrog(
                    self.edge, self.edge_exists, blocks_of(h_span), blocks_of(e_span), self.blocks, h_of, c_of, layers, last, []
                )
            )
        for part in parts:
            next(part)
        if between is not None:
            between()
        for part in parts:
            next(part, None)


def rows_cases(row_size, row, run):
    if row_size == 2:
        pl.when(row == 0)(functools.partial(run, False, True))
        pl.when(row == 1)(functools.partial(run, True, False))
    else:
        run(True, True)


def port_sums(n, reached, prow_ref, weight_ref, ez_ref, edge_ref, sum_ref, add_ref):
    for k in range(PORT_TILE):
        at = prow_ref[0, 0, k]
        total = jnp.zeros((8, 128), jnp.float32)
        for zz in range(OWN):
            if ez_ref is not None:
                total = total + ez_ref[at, zz] * weight_ref[k, 0, zz]
            if edge_ref is not None:
                total = total + edge_ref[at >> 2, zz] * weight_ref[k, 1, zz]
        total = jnp.sum(jnp.where(reached(n, at), total, 0.0), axis=0, keepdims=True)
        if add_ref is not None:
            total = total + add_ref[n - 1, k : k + 1, :]
        sum_ref[n - 1, k : k + 1, :] = total


def finish(fields, b, main, edge, write):
    lane = iota(1)
    place = lane & (GROUP - 1)
    sides = (lane < DEPTH) | (lane >= 128 - DEPTH)

    def first(f):
        tiles = [edge.get(f, b + 1, zz) for zz in range(OWN)]
        turned = [turn(tile, -8, 1) for tile in tiles]
        return [jnp.where(place < 8, tile, other) for tile, other in zip(tiles, turned)]

    def second(f, near):
        turned = {(r, zz): turn(near[zz], -(GROUP * r + 8), 1) for r in range(4) for zz in range(OWN)}
        made = {(r, zz): jnp.where(sides, tile, main.get(f, DEPTH + 4 * b + r, zz)) for (r, zz), tile in turned.items()}
        for (r, zz), tile in made.items():
            write(f, r, zz, tile)

    staged(fields, first, second)


def weight_kernel(mode_ref, prow_ref, pcol_ref, pmode_ref, pid_ref, order_ref, weight_ref, strip_ref):
    lane = iota(1)
    for k in range(PORT_TILE):
        strip_ref[k] = jnp.zeros(strip_ref.shape[1:], jnp.float32)
        strip_ref[k, :, 0:PLEN] = mode_ref[pmode_ref[0, 0, k]]
    for k in range(PORT_TILE):
        turned = GROUP * (prow_ref[0, 0, k] & 3)
        at = lane - turned
        for zz in range(OWN):
            tile = pltpu.roll(strip_ref[k, 8 * zz : 8 * zz + 8, :], pcol_ref[0, 0, k], 1)
            weight_ref[k, 0, zz] = jnp.where((lane >= DEPTH) & (lane < 128 - DEPTH), tile, 0.0)
            own = pltpu.roll(tile, turned + 8, 1)
            edge = jnp.where((at >= 4) & (at < 8), own, 0.0)
            weight_ref[k, 1, zz] = jnp.where((at >= 16) & (at < 20), turn(own, 8, 1), edge)


def inner_kernel(
    row_size, elec_ref, magn_ref, mat_ref, z_ref, eps_ref,
    e_ref, h_ref, c_ref, ez_ref, state_ref, plain_ref, ext_ref, halo_ref,
):
    gz, row = lax.axis_index("gz"), lax.axis_index("row")
    spread_layers(gz, z_ref, ext_ref)
    for f in range(FIELDS):
        for x in range(ROWS):
            halo_ref[f, x] = ext_ref[f, pl.ds(x, 8, stride=ROWS), :]
    for z in range(LAYERS):
        plain_ref[z] = coefficient(mat_ref[z], eps_ref)
    for f in range(3):
        rows_outside(elec_ref.reshape(3 * LAYERS * ROWS, 128), f, state_ref, f)
        rows_outside(magn_ref.reshape(3 * LAYERS * ROWS, 128), f, state_ref, f + 3)
    rows_outside(plain_ref.reshape(LAYERS * ROWS, 128), 0, state_ref, 6)

    def first(f, i, zz):
        return halo_ref[f, i - DEPTH] if zz == OWN else state_ref[f, i - DEPTH, zz]

    def run(has_below, has_above):
        main = Tiles(first, None, DEPTH)
        stepper = Stepper(row_size, main, None, range(4, 12), (), False)
        for n in range(1, STEPS + 1):
            main.ez_ref = ez_ref.at[n - 1]
            stepper.step(n, [spans_inner(n, has_below, has_above)])
        for i in range(ROWS):
            for zz in range(CHUNK):
                for f in range(6):
                    (e_ref, h_ref)[f // 3][f % 3, i, zz] = main.get(f, DEPTH + i, zz)
                c_ref[i, zz] = main.get(6, DEPTH + i, zz)

    rows_cases(row_size, row, run)


def rim_kernel(
    row_size, z_ref, own_ref, even_ref, odd_ref, layer_ref, e_in, h_in, ez_in, weight_ref, prow_ref,
    edge_e_ref, edge_h_ref, edge_c_ref, done_ref, sum_ref, ext_ref, ez_ref,
):
    gz, row = lax.axis_index("gz"), lax.axis_index("row")
    place = iota(1) & (GROUP - 1)
    groups = lane_groups()
    valid = (iota(0) < 4) == (gz == 0)
    spread_layers(gz, z_ref, ext_ref)
    low_of, high_of = low_and_high(even_ref, odd_ref)
    low_z, high_z = low_and_high(layer_ref.at[0], layer_ref.at[1])
    joined = {}

    def first(at):
        b, zz = at
        if zz < OWN:
            return [own_ref[f, b, zz] for f in range(FIELDS)], turn_sides(low_of(b, zz), high_of(b, zz))
        rows = [[ext_ref[f, pl.ds(4 * b + r, 8, stride=ROWS), :] for r in range(4)] for f in range(FIELDS)]
        sides = turn_sides(*(jnp.where(valid, side(b), 0.0) for side in (low_z, high_z)))
        return gather_edges(rows, groups), sides

    def second(at, made):
        for f, tile in enumerate(edge_tiles(*made, place)):
            joined[f, at[0] + 1, at[1]] = tile

    staged([(b, zz) for b in range(2) for zz in range(CHUNK)], first, second)

    def run(has_below, has_above):
        main = Tiles(lambda f, i, zz: (e_in, h_in)[f // 3][f % 3, i - DEPTH, zz], None, DEPTH)
        edge = Tiles(lambda f, i, zz: joined[f, i, zz], ez_ref, 1)
        stepper = Stepper(row_size, None, edge, (), (1, 2), False)

        def reached(n, at):
            low, high = spans_inner(n, has_below, has_above)[1]
            return (at >= low) & (at <= high)

        for n in range(1, STEPS + 1):
            stepper.step(n, [spans_inner(n, has_below, has_above)])
            port_sums(n, reached, prow_ref, weight_ref, ez_in.at[n - 1], ez_ref, sum_ref, None)
        for i in range(2):
            for zz in range(CHUNK):
                for f in range(6):
                    (edge_e_ref, edge_h_ref)[f // 3][f % 3, i, zz] = edge.get(f, 1 + i, zz)
                edge_c_ref[i, zz] = edge.get(6, 1 + i, zz)
        if has_below != has_above:

            def write(f, r, zz, tile):
                done_ref[f, r, zz] = tile

            finish(range(6), 0 if has_above else 1, main, edge, write)

    rows_cases(row_size, row, run)


def outer_kernel(
    row_size, ports_each, prow_ref, pid_ref, e_in, h_in, c_in, weight_ref, edge_e_in, edge_h_in, edge_c_in, done_ref, sum_in,
    *rest,
):
    n_x = 1 if row_size == 2 else 2
    x_refs, corner_refs = rest[:n_x], rest[n_x : 2 * n_x]
    eout_hbm, hout_hbm, term_ref, ez_ref, edge_ez_ref, sum_ref, turned_ref, out_ref, sems = rest[2 * n_x :]
    gz, row = lax.axis_index("gz"), lax.axis_index("row")
    lane, sub = iota(1), iota(0)
    place = lane & (GROUP - 1)
    groups = lane_groups()
    valid = (sub < 4) == (gz == 0)
    zeros = jnp.zeros((8, 128), jnp.float32)

    def first_main(f, i, zz):
        if f == 6:
            return c_in[i - DEPTH, zz]
        return e_in[f, i - DEPTH, zz] if f < 3 else h_in[f - 3, i - DEPTH, zz]

    def first_edge(f, i, zz):
        if f == 6:
            return edge_c_in[i - 1, zz]
        return edge_e_in[f, i - 1, zz] if f < 3 else edge_h_in[f - 3, i - 1, zz]

    def write_terms():
        basis = zeros
        for n in range(STEPS):
            for f in range(2 * FREQ):
                basis = jnp.where((sub == n) & (lane == f), float(BASIS[n, f]), basis)
        transform = zeros
        for n in range(STEPS):
            sampled = jnp.sum(sum_ref[n], axis=1, keepdims=True)
            transform = transform + sampled * basis[n : n + 1, :]
        term_ref[...] = jnp.zeros(term_ref.shape, jnp.float32)
        for k in range(PORT_TILE):
            port = pid_ref[0, 0, k]
            term_ref[port // ports_each, pl.ds(port % ports_each, 1), :] = transform[k : k + 1, : 2 * FREQ]

    def run(has_below, has_above):
        main = Tiles(first_main, ez_ref, DEPTH)
        edge = Tiles(first_edge, edge_ez_ref, 1)

        def halo_rows(planes, slot, offset, b):
            got = {}
            for i, (f, x) in enumerate(planes):
                packed = corner_refs[slot][i % PAIRS]
                if i >= PAIRS:
                    packed = turn(packed, 4, 0)
                tiles = [x_refs[slot][i, zz] for zz in range(OWN)]
                tiles.append(jnp.where(valid, packed, 0.0))
                for zz in range(CHUNK):
                    main.put(f, DEPTH + x + offset, zz, tiles[zz])
                    got[f, x + offset - 4 * b, zz] = tiles[zz]

            def first(zz):
                rows = [[got.get((f, r, zz)) for r in range(4)] for f in range(FIELDS)]
                sides = turn_sides(corner_refs[slot][PAIRS + zz], corner_refs[slot][PAIRS + CHUNK + zz])
                return gather_edges(rows, groups), sides

            def second(zz, made):
                for f, tile in enumerate(edge_tiles(*made, place)):
                    edge.put(f, 1 + b, zz, tile)

            staged(range(CHUNK), first, second)

        if has_below:
            halo_rows(UP_PLANES, 0, -ROWS, -1)
        if has_above:
            halo_rows(DOWN_PLANES, n_x - 1, ROWS, 2)

        def reached(n, at):
            out = None
            for wanted, span in ((has_below, spans_below(n)[1]), (has_above, spans_above(n)[1])):
                if wanted:
                    part = (at >= span[0]) & (at <= span[1])
                    out = part if out is None else out | part
            return out

        rows = range(0 if has_below else 4, 16 if has_above else 12)
        blocks = range(0 if has_below else 1, 4 if has_above else 3)
        copies = []

        def hand_out(part):
            fields = range(3 * part, 3 * part + 3)

            def write(f, r, zz, tile, b):
                turned_ref[f, 4 * b + r, 8 * zz : 8 * zz + 8, :] = tile

            for b in range(2):
                put = functools.partial(write, b=b)
                if has_below and has_above or b == (1 if has_above else 0):
                    finish(fields, b, main, edge, put)
                else:
                    for f in fields:
                        for r in range(4):
                            for zz in range(OWN):
                                put(f, r, zz, done_ref[f, r, zz])
            flat = turned_ref.reshape(6 * ROWS * LAYERS, 128)
            for f in fields:
                for z in range(LAYERS):
                    out_ref[f, z] = flat[pl.ds(f * ROWS * LAYERS + z, ROWS, stride=LAYERS), :]
            dest = hout_hbm if part else eout_hbm
            copies.append(pltpu.make_async_copy(out_ref.at[pl.ds(3 * part, 3)], dest, sems.at[part]))
            copies[-1].start()

        stepper = Stepper(row_size, main, edge, rows, blocks, True)
        for n in range(1, STEPS + 1):
            spans = ([spans_below(n)] if has_below else []) + ([spans_above(n)] if has_above else [])
            stepper.step(n, spans, functools.partial(hand_out, 1) if n == STEPS else None)
            port_sums(n, reached, prow_ref, weight_ref, ez_ref, edge_ez_ref, sum_ref, sum_in)
        hand_out(0)
        write_terms()
        for copy in copies:
            copy.wait()

    rows_cases(row_size, row, run)


def shifted(block, axis, size, distance):
    route = [(i - distance, i) for i in range(size) if 0 <= i - distance < size]
    return lax.ppermute(block, axis, route)


def swapped(block, axis, size, start=0):
    pairs = [(i, i + 1) for i in range(start, size - 1, 2)]
    return lax.ppermute(block, axis, pairs + [(j, i) for i, j in pairs])


def solution(mesh):
    sizes = dict(mesh.shape)
    row_size, col_size, gz_size = sizes["row"], sizes["col"], sizes["gz"]
    n_x = 1 if row_size == 2 else 2

    def across_rows(blocks):
        if row_size == 2:
            return (swapped(blocks[0], "row", 2),)
        return (shifted(blocks[0], "row", row_size, 1), shifted(blocks[1], "row", row_size, -1))

    def per_device(
        electric, magnetic, material, eps_table, mode_table, port_row, port_col, port_mode, port_ids
    ):
        f32 = jnp.float32

        def array(*shape):
            return jax.ShapeDtypeStruct(shape, f32)

        def scratch(*shape):
            return pltpu.VMEM(shape, f32)

        z_send, own, even_send, odd_send, *x_send = pl.pallas_call(
            functools.partial(pack_kernel, row_size),
            out_shape=[
                array(FIELDS, DEPTH, ROWS, 128),
                array(FIELDS, 2, OWN, 8, 128),
                array(2, OWN, 8, 128),
                array(2, OWN, 8, 128),
            ]
            + [array(PLANES, OWN, 8, 128)] * n_x,
            in_specs=[HBM] * 4,
            out_specs=[VMEM] * 4 + [HBM] * n_x,
            scratch_shapes=[scratch(PLANES, OWN, 8, 128)] * n_x
            + [
                scratch(FIELDS, ROWS, OWN, 8, 128),
                scratch(FIELDS, LAYERS, ROWS, 128),
                pltpu.SMEM(eps_table.shape, f32),
                pltpu.VMEM(material.shape, jnp.int32),
                pltpu.SemaphoreType.DMA((10,)),
            ],
            name="pack",
        )(eps_table, electric, magnetic, material)
        x_halo = across_rows(x_send)
        even = swapped(even_send, "col", col_size)
        odd = swapped(odd_send, "col", col_size, 1)
        z_halo = swapped(z_send, "gz", gz_size)
        e_now, h_now, c_now, ez_now = pl.pallas_call(
            functools.partial(inner_kernel, row_size),
            out_shape=[
                array(3, ROWS, CHUNK, 8, 128),
                array(3, ROWS, CHUNK, 8, 128),
                array(ROWS, CHUNK, 8, 128),
                array(STEPS, ROWS, OWN, 8, 128),
            ],
            in_specs=[VMEM] * 4 + [SMEM],
            out_specs=[VMEM] * 4,
            scratch_shapes=[
                scratch(FIELDS, ROWS, OWN, 8, 128),
                scratch(LAYERS, ROWS, 128),
                scratch(FIELDS, 8 * ROWS, 128),
                scratch(FIELDS, ROWS, 8, 128),
            ],
            compiler_params=PARAMS,
            cost_estimate=pl.CostEstimate(flops=5_000_000, bytes_accessed=10_000_000, transcendentals=0),
            name="inner",
        )(electric, magnetic, material, z_halo, eps_table)
        layer_send = pl.pallas_call(
            layer_edge_kernel,
            out_shape=array(2, 2, 8, 128),
            in_specs=[VMEM] * 2 + [pl.BlockSpec(memory_space=pl.ANY)],
            out_specs=VMEM,
            compiler_params=PARAMS,
            name="layer_edges",
        )(even, odd, c_now)
        layer_halo = swapped(layer_send, "gz", gz_size)
        weights = pl.pallas_call(
            weight_kernel,
            out_shape=array(PORT_TILE, 2, OWN, 8, 128),
            in_specs=[VMEM] + [SMEM] * 4 + [ANY],
            out_specs=VMEM,
            scratch_shapes=[scratch(PORT_TILE, LAYERS, 128)],
            compiler_params=PARAMS,
            name="weights",
        )(mode_table, port_row, port_col, port_mode, port_ids, c_now)
        corner_send = pl.pallas_call(
            functools.partial(corner_kernel, row_size),
            out_shape=[array(PAIRS + 2 * CHUNK, 8, 128)] * n_x,
            in_specs=[ANY] + [VMEM] * 4,
            out_specs=[VMEM] * n_x,
            scratch_shapes=[scratch(FIELDS, 8 * ROWS, 128)],
            compiler_params=PARAMS,
            name="corners",
        )(weights, z_halo, even, odd, layer_halo)
        corner = across_rows(corner_send)
        edges = pl.pallas_call(
            functools.partial(rim_kernel, row_size),
            out_shape=[
                array(3, 2, CHUNK, 8, 128),
                array(3, 2, CHUNK, 8, 128),
                array(2, CHUNK, 8, 128),
                array(6, 4, OWN, 8, 128),
                array(STEPS, 8, 128),
            ],
            in_specs=[VMEM] * 9 + [SMEM],
            out_specs=[VMEM] * 5,
            scratch_shapes=[scratch(FIELDS, 8 * ROWS, 128), scratch(2, OWN, 8, 128)],
            compiler_params=PARAMS,
            name="rim",
        )(z_halo, own, even, odd, layer_halo, e_now, h_now, ez_now, weights, port_row)
        devices = col_size * row_size * gz_size
        ports_each = PORT_TILE * col_size * row_size // devices
        electric_out, magnetic_out, term = pl.pallas_call(
            functools.partial(outer_kernel, row_size, ports_each),
            out_shape=[array(3, LAYERS, ROWS, 128)] * 2 + [array(devices, ports_each, 2 * FREQ)],
            in_specs=[SMEM] * 2 + [VMEM] * (9 + 2 * n_x),
            out_specs=[HBM, HBM, VMEM],
            scratch_shapes=[
                scratch(ROWS, OWN, 8, 128),
                scratch(2, OWN, 8, 128),
                scratch(STEPS, 8, 128),
                scratch(6, ROWS, LAYERS, 128),
                scratch(6, LAYERS, ROWS, 128),
                pltpu.SemaphoreType.DMA((2,)),
            ],
            compiler_params=PARAMS,
            name="outer",
        )(port_row, port_ids, e_now, h_now, c_now, weights, *edges, *x_halo, *corner)
        terms = lax.all_to_all(term, ("col", "row", "gz"), 0, 0, tiled=True)
        return (
            electric_out,
            magnetic_out,
            jnp.sum(terms, axis=0),
        )

    in_specs = (
        P(None, "gz", "row", ("grp", "col")),
        P(None, "gz", "row", ("grp", "col")),
        P("gz", "row", ("grp", "col")),
        P(),
        P(None, "gz", None),
        P(("grp", "row"), "col", None),
        P(("grp", "row"), "col", None),
        P(("grp", "row"), "col", None),
        P(("grp", "row"), "col", None),
    )
    out_specs = (
        P(None, "gz", "row", ("grp", "col")),
        P(None, "gz", "row", ("grp", "col")),
        P(("grp", "col", "row", "gz"), None),
    )
    return jax.shard_map(
        per_device, mesh=mesh, in_specs=in_specs, out_specs=out_specs, check_vma=False
    )
```

```python
import functools

import jax
import jax.numpy as jnp
import numpy as np
from jax import lax
from jax.experimental import pallas as pl
from jax.experimental.pallas import tpu as pltpu
from jax.sharding import PartitionSpec as P

STEPS = 4
FREQ = 8
MATS = 8
PLEN = 64
PORT_TILE = 4
FIELDS = 7
DEPTH = STEPS
ROWS = 8
LAYERS = 32
OWN = 4
CHUNK = 5
GROUP = 32

time_step = 0.5

UP_PLANES = [(f, 4) for f in (0, 1, 2, 4, 5)] + [(f, x) for x in (5, 6, 7) for f in range(FIELDS)]
DOWN_PLANES = [(f, x) for x in (0, 1, 2) for f in range(FIELDS)] + [(1, 3), (2, 3)]
PLANES = max(len(UP_PLANES), len(DOWN_PLANES))
PAIRS = (PLANES + 1) // 2

VMEM = pl.BlockSpec(memory_space=pltpu.VMEM)
SMEM = pl.BlockSpec(memory_space=pltpu.SMEM)
HBM = pl.BlockSpec(memory_space=pltpu.HBM)
ANY = pl.BlockSpec(memory_space=pl.ANY)
PARAMS = pltpu.CompilerParams(vmem_limit_bytes=16 * 1024 * 1024)


def dft_basis():
    times = (np.arange(STEPS) + 1.0) * time_step
    omegas = np.pi * (np.arange(FREQ) + 1.0) / FREQ
    angle = times[:, None] * omegas[None, :]
    return np.concatenate([np.cos(angle), -np.sin(angle)], axis=1)


BASIS = dft_basis()


def iota(axis):
    return lax.broadcasted_iota(jnp.int32, (8, 128), axis)


def turn(tile, shift, axis):
    return pltpu.roll(tile, shift % tile.shape[axis], axis)


def directions(row_size, body):
    if row_size == 2:
        row = lax.axis_index("row")
        pl.when(row == 0)(functools.partial(body, True, 0))
        pl.when(row == 1)(functools.partial(body, False, 0))
    else:
        body(True, 0)
        body(False, 1)


def coefficient(material, eps_ref):
    eps = jnp.full((8, 128), eps_ref[0], jnp.float32)
    for which in range(1, MATS):
        eps = jnp.where(material == which, eps_ref[which], eps)
    return time_step * (1.0 / eps)


def rows_outside(flat, f, state_ref, at):
    for x in range(ROWS):
        state_ref[at, x] = flat[pl.ds(f * LAYERS * ROWS + x, LAYERS, stride=ROWS), :].reshape(OWN, 8, 128)


def pack_kernel(row_size, eps_hbm, elec_hbm, magn_hbm, mat_hbm, z_ref, own_ref, even_ref, odd_ref, *rest):
    x_refs, (state_ref, main_ref, eps_ref, mat_ref, sems) = rest[:-5], rest[-5:]
    copies = [pltpu.make_async_copy(eps_hbm, eps_ref, sems.at[0]), pltpu.make_async_copy(mat_hbm, mat_ref, sems.at[1])]
    copies.append(pltpu.make_async_copy(elec_hbm, main_ref.at[pl.ds(0, 3)], sems.at[2]))
    copies.append(pltpu.make_async_copy(magn_hbm, main_ref.at[pl.ds(3, 3)], sems.at[3]))
    for copy in copies:
        copy.start()
    copies[0].wait()
    copies[1].wait()
    for z in range(LAYERS):
        main_ref[6, z] = coefficient(mat_ref[z], eps_ref)
    copies[2].wait()
    copies[3].wait()
    start = jnp.where(lax.axis_index("gz") == 0, LAYERS - DEPTH, 0)
    for f in range(FIELDS):
        z_ref[f] = main_ref[f, pl.ds(start, DEPTH)]
    flat = main_ref.reshape(FIELDS * LAYERS * ROWS, 128)
    for f in range(FIELDS):
        rows_outside(flat, f, state_ref, f)

    def send(up, slot):
        for i, (f, x) in enumerate(UP_PLANES if up else DOWN_PLANES):
            x_refs[slot][i] = state_ref[f, x]

    directions(row_size, send)
    pack_edges(state_ref, own_ref, even_ref, odd_ref)


def lane_groups():
    group = iota(1) >> 5
    return [jnp.where(group == r, 1.0, 0.0) for r in range(4)]


def gather_edges(rows_of, groups):
    moved = [[tile if tile is None else turn(tile, GROUP * r + 8, 1) for r, tile in enumerate(rows)] for rows in rows_of]
    out = []
    for rows in moved:
        parts = [tile * groups[r] for r, tile in enumerate(rows) if tile is not None]
        out.append(functools.reduce(lambda a, b: a + b, parts) if parts else jnp.zeros((8, 128), jnp.float32))
    return out


def staged(items, first, second):
    waiting = None
    for item in items:
        made = first(item)
        if waiting is not None:
            second(*waiting)
        waiting = (item, made)
    second(*waiting)


def pack_edges(state_ref, own_ref, even_ref, odd_ref):
    lane = iota(1)
    groups = lane_groups()
    slots = [jnp.where(((lane & (GROUP - 1)) >> 2) == f, 1.0, 0.0) for f in range(FIELDS)]
    even = (lax.axis_index("col") & 1) == 0

    def first(at):
        b, zz = at
        return gather_edges([[state_ref[f, 4 * b + r, zz] for r in range(4)] for f in range(FIELDS)], groups)

    def second(at, owns):
        b, zz = at
        ups = [turn(own, DEPTH * f - 4, 1) for f, own in enumerate(owns)]
        downs = [turn(own, DEPTH * f - 8, 1) for f, own in enumerate(owns)]
        up = functools.reduce(lambda a, b: a + b, [v * m for v, m in zip(ups, slots)])
        down = functools.reduce(lambda a, b: a + b, [v * m for v, m in zip(downs, slots)])
        for f in range(FIELDS):
            own_ref[f, b, zz] = owns[f]
        even_ref[b, zz] = jnp.where(even, up, down)
        odd_ref[b, zz] = jnp.where(even, down, up)

    staged([(b, zz) for b in range(2) for zz in range(OWN)], first, second)


def low_and_high(even_ref, odd_ref):
    even = (lax.axis_index("col") & 1) == 0

    def low(*at):
        return jnp.where(even, odd_ref[at], even_ref[at])

    def high(*at):
        return jnp.where(even, even_ref[at], odd_ref[at])

    return low, high


def layer_edge_kernel(even_ref, odd_ref, inner_ref, out_ref):
    gz = lax.axis_index("gz")
    for i, ref in enumerate((even_ref, odd_ref)):
        for b in range(2):
            out_ref[i, b] = jnp.where(gz == 0, ref[b, OWN - 1], ref[b, 0])


def spread_layers(gz, z_ref, ext_ref):
    for f in range(FIELDS):
        halo = z_ref[f].reshape(DEPTH * ROWS, 128)
        nothing = jnp.zeros_like(halo)
        ext_ref[f, : DEPTH * ROWS] = jnp.where(gz == 0, halo, nothing)
        ext_ref[f, DEPTH * ROWS :] = jnp.where(gz == 0, nothing, halo)


def corner_kernel(row_size, weight_ref, z_ref, even_ref, odd_ref, layer_ref, *rest):
    x_refs, ext_ref = rest[:-1], rest[-1]
    gz = lax.axis_index("gz")
    valid = (iota(0) < 4) == (gz == 0)
    spread_layers(gz, z_ref, ext_ref)
    low, high = low_and_high(even_ref, odd_ref)
    low_z, high_z = low_and_high(layer_ref.at[0], layer_ref.at[1])

    def send(up, slot):
        planes = UP_PLANES if up else DOWN_PLANES

        def tile(i):
            f, x = planes[i]
            return ext_ref[f, pl.ds(x, 8, stride=ROWS), :]

        for i in range(PAIRS):
            pair = tile(i)
            if i + PAIRS < len(planes):
                pair = pair + turn(tile(i + PAIRS), 4, 0)
            x_refs[slot][i] = pair
        b = 1 if up else 0
        for zz in range(OWN):
            x_refs[slot][PAIRS + zz] = low(b, zz)
            x_refs[slot][PAIRS + CHUNK + zz] = high(b, zz)
        x_refs[slot][PAIRS + OWN] = jnp.where(valid, low_z(b), 0.0)
        x_refs[slot][PAIRS + CHUNK + OWN] = jnp.where(valid, high_z(b), 0.0)

    directions(row_size, send)


def turn_sides(low, high):
    lows = [turn(low, 12 - DEPTH * f, 1) for f in range(FIELDS)]
    return lows, [turn(high, 8 - DEPTH * f, 1) for f in range(FIELDS)]


def edge_tiles(owns, sides, place):
    turned = [turn(own, 8, 1) for own in owns]
    out = []
    for own, own_turned, low, high in zip(owns, turned, *sides):
        tile = jnp.where(place < 16, low, own_turned)
        tile = jnp.where(place < 12, high, tile)
        out.append(jnp.where(place < 8, own, tile))
    return out


class Tiles:
    def __init__(self, first, ez_ref, shift):
        self.first, self.ez_ref, self.shift = first, ez_ref, shift
        self.values = {}

    def get(self, f, i, zz):
        value = self.values.get((f, i, zz))
        return self.first(f, i, zz) if value is None else value

    def put(self, f, i, zz, tile):
        self.values[f, i, zz] = tile
        at = i - self.shift
        if f == 2 and zz < OWN and self.ez_ref is not None and 0 <= at < self.ez_ref.shape[0]:
            self.ez_ref[at, zz] = tile


def leapfrog(tiles, exists, h_rows, e_rows, across, h_of, c_of, h_layers, e_layers, skip_hx):
    sub = iota(0)
    every = range(CHUNK)
    blank = [jnp.zeros((8, 128), jnp.float32)] * CHUNK

    def above(values):
        turned = [turn(v, -1, 0) for v in values]
        return [jnp.where(sub == 7, turned[(zz + 1) % CHUNK], turned[zz]) for zz in every]

    def beneath(values):
        turned = [turn(v, 1, 0) for v in values]
        return [jnp.where(sub == 0, turned[zz - 1], turned[zz]) for zz in every]

    def row(f, i):
        return [tiles.get(f, i, zz) for zz in every]

    def load_e(i):
        ey, ez = row(1, i), row(2, i)
        out = dict(ey=ey, ez=ez, ey_x=across.turned(ey, -1), ez_x=across.turned(ez, -1))
        if i in h_rows:
            ex = row(0, i)
            out.update(ex=ex, ex_y=[turn(v, -1, 1) for v in ex], ex_z=above(ex))
            if i not in skip_hx:
                out.update(ez_y=[turn(v, -1, 1) for v in ez], ey_z=above(ey))
        return out

    def work_h(i, loaded):
        e, after, h = loaded[i], loaded.get(i + 1), h_of(i)
        ey_x = across.pick(e["ey_x"], after["ey_x"] if after else blank, -1)
        ez_x = across.pick(e["ez_x"], after["ez_x"] if after else blank, -1)
        new = {}
        for zz in h_layers:
            if i not in skip_hx:
                curl = (e["ez_y"][zz] - e["ez"][zz]) - (e["ey_z"][zz] - e["ey"][zz])
                new[3, zz] = tiles.get(3, i, zz) - h[zz] * curl
            curl = (e["ex_z"][zz] - e["ex"][zz]) - (ez_x[zz] - e["ez"][zz])
            new[4, zz] = tiles.get(4, i, zz) - h[zz] * curl
            curl = (ey_x[zz] - e["ey"][zz]) - (e["ex_y"][zz] - e["ex"][zz])
            new[5, zz] = tiles.get(5, i, zz) - h[zz] * curl
        for (f, zz), tile in new.items():
            tiles.put(f, i, zz, tile)

    def load_h(i):
        hy, hz = row(4, i), row(5, i)
        out = dict(hy=hy, hz=hz, hy_x=across.turned(hy, 1), hz_x=across.turned(hz, 1))
        if i in e_rows:
            hx = row(3, i)
            out.update(hx=hx, hx_y=[turn(v, 1, 1) for v in hx], hz_y=[turn(v, 1, 1) for v in hz])
            out.update(hx_z=beneath(hx), hy_z=beneath(hy))
        return out

    def work_e(i, loaded):
        h, before, c = loaded[i], loaded.get(i - 1), c_of(i)
        hy_x = across.pick(h["hy_x"], before["hy_x"] if before else blank, 1)
        hz_x = across.pick(h["hz_x"], before["hz_x"] if before else blank, 1)
        new = {}
        for zz in e_layers:
            curl = (h["hz"][zz] - h["hz_y"][zz]) - (h["hy"][zz] - h["hy_z"][zz])
            new[0, zz] = tiles.get(0, i, zz) + c[zz] * curl
            curl = (h["hx"][zz] - h["hx_z"][zz]) - (h["hz"][zz] - hz_x[zz])
            new[1, zz] = tiles.get(1, i, zz) + c[zz] * curl
            curl = (h["hy"][zz] - hy_x[zz]) - (h["hx"][zz] - h["hx_y"][zz])
            new[2, zz] = tiles.get(2, i, zz) + c[zz] * curl
        for (f, zz), tile in new.items():
            tiles.put(f, i, zz, tile)

    def sweep(rows, load, work):
        loaded = {}

        def want(i):
            if i not in loaded and i in exists:
                loaded[i] = load(i)

        for i in rows:
            for j in (i - 1, i, i + 1):
                if j in rows or j == i + (1 if load is load_e else -1):
                    want(j)
            work(i, loaded)

    sweep(h_rows, load_e, work_h)
    yield
    sweep(e_rows, load_h, work_e)


class Rows:
    def turned(self, values, way):
        return values

    def pick(self, own, other, way):
        return other


class Blocks:
    def __init__(self, groups):
        self.groups = groups

    def turned(self, values, way):
        return [turn(v, way * GROUP, 1) for v in values]

    def pick(self, own, other, way):
        edge = self.groups[3] if way < 0 else self.groups[0]
        return [jnp.where(edge, o, v) for o, v in zip(other, own)]


def spans_inner(n, has_below, has_above):
    last = 7 - n if has_above else 7
    return (n - 1 if has_below else 0, last), (n if has_below else 0, last)


def spans_below(n):
    return (n - 5, n - 2), (n - 4, n - 1)


def spans_above(n):
    return (8 - n, 11 - n), (8 - n, 11 - n)


class Stepper:
    def __init__(self, row_size, main, edge, main_exists, edge_exists, skip_hx):
        gz, row, col = (lax.axis_index(name) for name in ("gz", "row", "col"))
        lane, sub = iota(1), iota(0)
        place, self.group = lane & (GROUP - 1), lane >> 5
        full = jnp.full((8, 128), time_step, jnp.float32)
        self.layer_half = [full] * OWN + [jnp.where((sub >= 4) & (gz == 0), 0.0, full)]
        outside = (place >= 12) & (place < 16) & (col == 0)
        self.edge_half = [jnp.where(outside, 0.0, v) for v in self.layer_half]
        self.lowest = jnp.where(row == 0, 0.0, 1.0) if row_size > 2 else None
        self.main, self.edge, self.skip_hx = main, edge, skip_hx
        self.main_exists, self.edge_exists = main_exists, edge_exists
        self.blocks = Blocks([self.group == r for r in range(4)])

    def masked(self, values, block, span):
        low, high = max(span[0] - 4 * block, 0), min(span[1] - 4 * block, 3)
        if low == 0 and high == 3:
            return values
        mask = (self.group >= low) & (self.group <= high)
        return [jnp.where(mask, v, 0.0) for v in values]

    def main_h(self, i):
        return self.layer_half if self.lowest is None or i >= DEPTH else [v * self.lowest for v in self.layer_half]

    def main_c(self, i):
        return [self.main.get(6, i, zz) for zz in range(CHUNK)]

    def edge_h(self, i, span):
        h = self.edge_half if self.lowest is None or i else [v * self.lowest for v in self.edge_half]
        return self.masked(h, i - 1, span)

    def edge_c(self, i, span):
        return self.masked([self.edge.get(6, i, zz) for zz in range(CHUNK)], i - 1, span)

    def step(self, n, spans, between=None):
        def blocks_of(span):
            return [b + 1 for b in range(-1, 3) if span[0] <= 4 * b + 3 and span[1] >= 4 * b]

        layers = range(CHUNK)
        last = range(OWN) if n == STEPS else layers
        parts = []
        for h_span, e_span in spans:
            h_rows = list(range(DEPTH + h_span[0], DEPTH + h_span[1] + 1))
            e_rows = list(range(DEPTH + e_span[0], DEPTH + e_span[1] + 1))
            skip = h_rows[:1] if self.skip_hx and h_span[0] < e_span[0] else []
            if self.main is not None:
                parts.append(
                    leapfrog(self.main, self.main_exists, h_rows, e_rows, Rows(), self.main_h, self.main_c, layers, last, skip)
                )
            if self.edge is None:
                continue
            h_of, c_of = functools.partial(self.edge_h, span=h_span), functools.partial(self.edge_c, span=e_span)
            parts.append(
                leapfrog(
                    self.edge, self.edge_exists, blocks_of(h_span), blocks_of(e_span), self.blocks, h_of, c_of, layers, last, []
                )
            )
        for part in parts:
            next(part)
        if between is not None:
            between()
        for part in parts:
            next(part, None)


def rows_cases(row_size, row, run):
    if row_size == 2:
        pl.when(row == 0)(functools.partial(run, False, True))
        pl.when(row == 1)(functools.partial(run, True, False))
    else:
        run(True, True)


def port_sums(n, reached, prow_ref, weight_ref, ez_ref, edge_ref, sum_ref, add_ref):
    for k in range(PORT_TILE):
        at = prow_ref[0, 0, k]
        total = jnp.zeros((8, 128), jnp.float32)
        for zz in range(OWN):
            if ez_ref is not None:
                total = total + ez_ref[at, zz] * weight_ref[k, 0, zz]
            if edge_ref is not None:
                total = total + edge_ref[at >> 2, zz] * weight_ref[k, 1, zz]
        total = jnp.sum(jnp.where(reached(n, at), total, 0.0), axis=0, keepdims=True)
        if add_ref is not None:
            total = total + add_ref[n - 1, k : k + 1, :]
        sum_ref[n - 1, k : k + 1, :] = total


def finish(fields, b, main, edge, write):
    lane = iota(1)
    place = lane & (GROUP - 1)
    sides = (lane < DEPTH) | (lane >= 128 - DEPTH)

    def first(f):
        tiles = [edge.get(f, b + 1, zz) for zz in range(OWN)]
        turned = [turn(tile, -8, 1) for tile in tiles]
        return [jnp.where(place < 8, tile, other) for tile, other in zip(tiles, turned)]

    def second(f, near):
        turned = {(r, zz): turn(near[zz], -(GROUP * r + 8), 1) for r in range(4) for zz in range(OWN)}
        made = {(r, zz): jnp.where(sides, tile, main.get(f, DEPTH + 4 * b + r, zz)) for (r, zz), tile in turned.items()}
        for (r, zz), tile in made.items():
            write(f, r, zz, tile)

    staged(fields, first, second)


def weight_kernel(mode_ref, prow_ref, pcol_ref, pmode_ref, pid_ref, order_ref, weight_ref, strip_ref):
    lane = iota(1)
    for k in range(PORT_TILE):
        strip_ref[k] = jnp.zeros(strip_ref.shape[1:], jnp.float32)
        strip_ref[k, :, 0:PLEN] = mode_ref[pmode_ref[0, 0, k]]
    for k in range(PORT_TILE):
        turned = GROUP * (prow_ref[0, 0, k] & 3)
        at = lane - turned
        for zz in range(OWN):
            tile = pltpu.roll(strip_ref[k, 8 * zz : 8 * zz + 8, :], pcol_ref[0, 0, k], 1)
            weight_ref[k, 0, zz] = jnp.where((lane >= DEPTH) & (lane < 128 - DEPTH), tile, 0.0)
            own = pltpu.roll(tile, turned + 8, 1)
            edge = jnp.where((at >= 4) & (at < 8), own, 0.0)
            weight_ref[k, 1, zz] = jnp.where((at >= 16) & (at < 20), turn(own, 8, 1), edge)


def inner_kernel(
    row_size, elec_ref, magn_ref, mat_ref, z_ref, eps_ref,
    e_ref, h_ref, c_ref, ez_ref, state_ref, plain_ref, ext_ref, halo_ref,
):
    gz, row = lax.axis_index("gz"), lax.axis_index("row")
    spread_layers(gz, z_ref, ext_ref)
    for f in range(FIELDS):
        for x in range(ROWS):
            halo_ref[f, x] = ext_ref[f, pl.ds(x, 8, stride=ROWS), :]
    for z in range(LAYERS):
        plain_ref[z] = coefficient(mat_ref[z], eps_ref)
    for f in range(3):
        rows_outside(elec_ref.reshape(3 * LAYERS * ROWS, 128), f, state_ref, f)
        rows_outside(magn_ref.reshape(3 * LAYERS * ROWS, 128), f, state_ref, f + 3)
    rows_outside(plain_ref.reshape(LAYERS * ROWS, 128), 0, state_ref, 6)

    def first(f, i, zz):
        return halo_ref[f, i - DEPTH] if zz == OWN else state_ref[f, i - DEPTH, zz]

    def run(has_below, has_above):
        main = Tiles(first, None, DEPTH)
        stepper = Stepper(row_size, main, None, range(4, 12), (), False)
        for n in range(1, STEPS + 1):
            main.ez_ref = ez_ref.at[n - 1]
            stepper.step(n, [spans_inner(n, has_below, has_above)])
        for i in range(ROWS):
            for zz in range(CHUNK):
                for f in range(6):
                    (e_ref, h_ref)[f // 3][f % 3, i, zz] = main.get(f, DEPTH + i, zz)
                c_ref[i, zz] = main.get(6, DEPTH + i, zz)

    rows_cases(row_size, row, run)


def rim_kernel(
    row_size, z_ref, own_ref, even_ref, odd_ref, layer_ref, e_in, h_in, ez_in, weight_ref, prow_ref,
    edge_e_ref, edge_h_ref, edge_c_ref, done_ref, sum_ref, ext_ref, ez_ref,
):
    gz, row = lax.axis_index("gz"), lax.axis_index("row")
    place = iota(1) & (GROUP - 1)
    groups = lane_groups()
    valid = (iota(0) < 4) == (gz == 0)
    spread_layers(gz, z_ref, ext_ref)
    low_of, high_of = low_and_high(even_ref, odd_ref)
    low_z, high_z = low_and_high(layer_ref.at[0], layer_ref.at[1])
    joined = {}

    def first(at):
        b, zz = at
        if zz < OWN:
            return [own_ref[f, b, zz] for f in range(FIELDS)], turn_sides(low_of(b, zz), high_of(b, zz))
        rows = [[ext_ref[f, pl.ds(4 * b + r, 8, stride=ROWS), :] for r in range(4)] for f in range(FIELDS)]
        sides = turn_sides(*(jnp.where(valid, side(b), 0.0) for side in (low_z, high_z)))
        return gather_edges(rows, groups), sides

    def second(at, made):
        for f, tile in enumerate(edge_tiles(*made, place)):
            joined[f, at[0] + 1, at[1]] = tile

    staged([(b, zz) for b in range(2) for zz in range(CHUNK)], first, second)

    def run(has_below, has_above):
        main = Tiles(lambda f, i, zz: (e_in, h_in)[f // 3][f % 3, i - DEPTH, zz], None, DEPTH)
        edge = Tiles(lambda f, i, zz: joined[f, i, zz], ez_ref, 1)
        stepper = Stepper(row_size, None, edge, (), (1, 2), False)

        def reached(n, at):
            low, high = spans_inner(n, has_below, has_above)[1]
            return (at >= low) & (at <= high)

        for n in range(1, STEPS + 1):
            stepper.step(n, [spans_inner(n, has_below, has_above)])
            port_sums(n, reached, prow_ref, weight_ref, ez_in.at[n - 1], ez_ref, sum_ref, None)
        for i in range(2):
            for zz in range(CHUNK):
                for f in range(6):
                    (edge_e_ref, edge_h_ref)[f // 3][f % 3, i, zz] = edge.get(f, 1 + i, zz)
                edge_c_ref[i, zz] = edge.get(6, 1 + i, zz)
        if has_below != has_above:

            def write(f, r, zz, tile):
                done_ref[f, r, zz] = tile

            finish(range(6), 0 if has_above else 1, main, edge, write)

    rows_cases(row_size, row, run)


def outer_kernel(
    row_size, ports_each, prow_ref, pid_ref, e_in, h_in, c_in, weight_ref, edge_e_in, edge_h_in, edge_c_in, done_ref, sum_in,
    *rest,
):
    n_x = 1 if row_size == 2 else 2
    x_refs, corner_refs = rest[:n_x], rest[n_x : 2 * n_x]
    eout_hbm, hout_hbm, term_ref, ez_ref, edge_ez_ref, sum_ref, turned_ref, out_ref, sems = rest[2 * n_x :]
    gz, row = lax.axis_index("gz"), lax.axis_index("row")
    lane, sub = iota(1), iota(0)
    place = lane & (GROUP - 1)
    groups = lane_groups()
    valid = (sub < 4) == (gz == 0)
    zeros = jnp.zeros((8, 128), jnp.float32)

    def first_main(f, i, zz):
        if f == 6:
            return c_in[i - DEPTH, zz]
        return e_in[f, i - DEPTH, zz] if f < 3 else h_in[f - 3, i - DEPTH, zz]

    def first_edge(f, i, zz):
        if f == 6:
            return edge_c_in[i - 1, zz]
        return edge_e_in[f, i - 1, zz] if f < 3 else edge_h_in[f - 3, i - 1, zz]

    def write_terms():
        basis = zeros
        for n in range(STEPS):
            for f in range(2 * FREQ):
                basis = jnp.where((sub == n) & (lane == f), float(BASIS[n, f]), basis)
        transform = zeros
        for n in range(STEPS):
            sampled = jnp.sum(sum_ref[n], axis=1, keepdims=True)
            transform = transform + sampled * basis[n : n + 1, :]
        term_ref[...] = jnp.zeros(term_ref.shape, jnp.float32)
        for k in range(PORT_TILE):
            port = pid_ref[0, 0, k]
            term_ref[port // ports_each, pl.ds(port % ports_each, 1), :] = transform[k : k + 1, : 2 * FREQ]

    def run(has_below, has_above):
        main = Tiles(first_main, ez_ref, DEPTH)
        edge = Tiles(first_edge, edge_ez_ref, 1)

        def halo_rows(planes, slot, offset, b):
            got = {}
            for i, (f, x) in enumerate(planes):
                packed = corner_refs[slot][i % PAIRS]
                if i >= PAIRS:
                    packed = turn(packed, 4, 0)
                tiles = [x_refs[slot][i, zz] for zz in range(OWN)]
                tiles.append(jnp.where(valid, packed, 0.0))
                for zz in range(CHUNK):
                    main.put(f, DEPTH + x + offset, zz, tiles[zz])
                    got[f, x + offset - 4 * b, zz] = tiles[zz]

            def first(zz):
                rows = [[got.get((f, r, zz)) for r in range(4)] for f in range(FIELDS)]
                sides = turn_sides(corner_refs[slot][PAIRS + zz], corner_refs[slot][PAIRS + CHUNK + zz])
                return gather_edges(rows, groups), sides

            def second(zz, made):
                for f, tile in enumerate(edge_tiles(*made, place)):
                    edge.put(f, 1 + b, zz, tile)

            staged(range(CHUNK), first, second)

        if has_below:
            halo_rows(UP_PLANES, 0, -ROWS, -1)
        if has_above:
            halo_rows(DOWN_PLANES, n_x - 1, ROWS, 2)

        def reached(n, at):
            out = None
            for wanted, span in ((has_below, spans_below(n)[1]), (has_above, spans_above(n)[1])):
                if wanted:
                    part = (at >= span[0]) & (at <= span[1])
                    out = part if out is None else out | part
            return out

        rows = range(0 if has_below else 4, 16 if has_above else 12)
        blocks = range(0 if has_below else 1, 4 if has_above else 3)
        copies = []

        def hand_out(part):
            fields = range(3 * part, 3 * part + 3)

            def write(f, r, zz, tile, b):
                turned_ref[f, 4 * b + r, 8 * zz : 8 * zz + 8, :] = tile

            for b in range(2):
                put = functools.partial(write, b=b)
                if has_below and has_above or b == (1 if has_above else 0):
                    finish(fields, b, main, edge, put)
                else:
                    for f in fields:
                        for r in range(4):
                            for zz in range(OWN):
                                put(f, r, zz, done_ref[f, r, zz])
            flat = turned_ref.reshape(6 * ROWS * LAYERS, 128)
            for f in fields:
                for z in range(LAYERS):
                    out_ref[f, z] = flat[pl.ds(f * ROWS * LAYERS + z, ROWS, stride=LAYERS), :]
            dest = hout_hbm if part else eout_hbm
            copies.append(pltpu.make_async_copy(out_ref.at[pl.ds(3 * part, 3)], dest, sems.at[part]))
            copies[-1].start()

        stepper = Stepper(row_size, main, edge, rows, blocks, True)
        for n in range(1, STEPS + 1):
            spans = ([spans_below(n)] if has_below else []) + ([spans_above(n)] if has_above else [])
            stepper.step(n, spans, functools.partial(hand_out, 1) if n == STEPS else None)
            port_sums(n, reached, prow_ref, weight_ref, ez_ref, edge_ez_ref, sum_ref, sum_in)
        hand_out(0)
        write_terms()
        for copy in copies:
            copy.wait()

    rows_cases(row_size, row, run)


def shifted(block, axis, size, distance):
    route = [(i - distance, i) for i in range(size) if 0 <= i - distance < size]
    return lax.ppermute(block, axis, route)


def swapped(block, axis, size, start=0):
    pairs = [(i, i + 1) for i in range(start, size - 1, 2)]
    return lax.ppermute(block, axis, pairs + [(j, i) for i, j in pairs])


def solution(mesh):
    sizes = dict(mesh.shape)
    row_size, col_size, gz_size = sizes["row"], sizes["col"], sizes["gz"]
    n_x = 1 if row_size == 2 else 2

    def across_rows(blocks):
        if row_size == 2:
            return (swapped(blocks[0], "row", 2),)
        return (shifted(blocks[0], "row", row_size, 1), shifted(blocks[1], "row", row_size, -1))

    def per_device(
        electric, magnetic, material, eps_table, mode_table, port_row, port_col, port_mode, port_ids
    ):
        f32 = jnp.float32

        def array(*shape):
            return jax.ShapeDtypeStruct(shape, f32)

        def scratch(*shape):
            return pltpu.VMEM(shape, f32)

        z_send, own, even_send, odd_send, *x_send = pl.pallas_call(
            functools.partial(pack_kernel, row_size),
            out_shape=[
                array(FIELDS, DEPTH, ROWS, 128),
                array(FIELDS, 2, OWN, 8, 128),
                array(2, OWN, 8, 128),
                array(2, OWN, 8, 128),
            ]
            + [array(PLANES, OWN, 8, 128)] * n_x,
            in_specs=[HBM] * 4,
            out_specs=[VMEM] * (4 + n_x),
            scratch_shapes=[
                scratch(FIELDS, ROWS, OWN, 8, 128),
                scratch(FIELDS, LAYERS, ROWS, 128),
                pltpu.SMEM(eps_table.shape, f32),
                pltpu.VMEM(material.shape, jnp.int32),
                pltpu.SemaphoreType.DMA((4,)),
            ],
            compiler_params=pltpu.CompilerParams(vmem_limit_bytes=62_500_000),
            name="pack",
        )(eps_table, electric, magnetic, material)
        x_halo = across_rows(x_send)
        even = swapped(even_send, "col", col_size)
        odd = swapped(odd_send, "col", col_size, 1)
        z_halo = swapped(z_send, "gz", gz_size)
        e_now, h_now, c_now, ez_now = pl.pallas_call(
            functools.partial(inner_kernel, row_size),
            out_shape=[
                array(3, ROWS, CHUNK, 8, 128),
                array(3, ROWS, CHUNK, 8, 128),
                array(ROWS, CHUNK, 8, 128),
                array(STEPS, ROWS, OWN, 8, 128),
            ],
            in_specs=[VMEM] * 4 + [SMEM],
            out_specs=[VMEM] * 4,
            scratch_shapes=[
                scratch(FIELDS, ROWS, OWN, 8, 128),
                scratch(LAYERS, ROWS, 128),
                scratch(FIELDS, 8 * ROWS, 128),
                scratch(FIELDS, ROWS, 8, 128),
            ],
            compiler_params=PARAMS,
            cost_estimate=pl.CostEstimate(flops=5_000_000, bytes_accessed=10_000_000, transcendentals=0),
            name="inner",
        )(electric, magnetic, material, z_halo, eps_table)
        layer_send = pl.pallas_call(
            layer_edge_kernel,
            out_shape=array(2, 2, 8, 128),
            in_specs=[VMEM] * 2 + [pl.BlockSpec(memory_space=pl.ANY)],
            out_specs=VMEM,
            compiler_params=PARAMS,
            name="layer_edges",
        )(even, odd, c_now)
        layer_halo = swapped(layer_send, "gz", gz_size)
        weights = pl.pallas_call(
            weight_kernel,
            out_shape=array(PORT_TILE, 2, OWN, 8, 128),
            in_specs=[VMEM] + [SMEM] * 4 + [ANY],
            out_specs=VMEM,
            scratch_shapes=[scratch(PORT_TILE, LAYERS, 128)],
            compiler_params=PARAMS,
            name="weights",
        )(mode_table, port_row, port_col, port_mode, port_ids, layer_send)
        corner_send = pl.pallas_call(
            functools.partial(corner_kernel, row_size),
            out_shape=[array(PAIRS + 2 * CHUNK, 8, 128)] * n_x,
            in_specs=[ANY] + [VMEM] * 4,
            out_specs=[VMEM] * n_x,
            scratch_shapes=[scratch(FIELDS, 8 * ROWS, 128)],
            compiler_params=PARAMS,
            name="corners",
        )(weights, z_halo, even, odd, layer_halo)
        corner = across_rows(corner_send)
        edges = pl.pallas_call(
            functools.partial(rim_kernel, row_size),
            out_shape=[
                array(3, 2, CHUNK, 8, 128),
                array(3, 2, CHUNK, 8, 128),
                array(2, CHUNK, 8, 128),
                array(6, 4, OWN, 8, 128),
                array(STEPS, 8, 128),
            ],
            in_specs=[VMEM] * 9 + [SMEM],
            out_specs=[VMEM] * 5,
            scratch_shapes=[scratch(FIELDS, 8 * ROWS, 128), scratch(2, OWN, 8, 128)],
            compiler_params=PARAMS,
            name="rim",
        )(z_halo, own, even, odd, layer_halo, e_now, h_now, ez_now, weights, port_row)
        devices = col_size * row_size * gz_size
        ports_each = PORT_TILE * col_size * row_size // devices
        electric_out, magnetic_out, term = pl.pallas_call(
            functools.partial(outer_kernel, row_size, ports_each),
            out_shape=[array(3, LAYERS, ROWS, 128)] * 2 + [array(devices, ports_each, 2 * FREQ)],
            in_specs=[SMEM] * 2 + [VMEM] * (9 + 2 * n_x),
            out_specs=[HBM, HBM, VMEM],
            scratch_shapes=[
                scratch(ROWS, OWN, 8, 128),
                scratch(2, OWN, 8, 128),
                scratch(STEPS, 8, 128),
                scratch(6, ROWS, LAYERS, 128),
                scratch(6, LAYERS, ROWS, 128),
                pltpu.SemaphoreType.DMA((2,)),
            ],
            compiler_params=PARAMS,
            name="outer",
        )(port_row, port_ids, e_now, h_now, c_now, weights, *edges, *x_halo, *corner)
        terms = lax.all_to_all(term, ("col", "row", "gz"), 0, 0, tiled=True)
        return (
            electric_out,
            magnetic_out,
            jnp.sum(terms, axis=0),
        )

    in_specs = (
        P(None, "gz", "row", ("grp", "col")),
        P(None, "gz", "row", ("grp", "col")),
        P("gz", "row", ("grp", "col")),
        P(),
        P(None, "gz", None),
        P(("grp", "row"), "col", None),
        P(("grp", "row"), "col", None),
        P(("grp", "row"), "col", None),
        P(("grp", "row"), "col", None),
    )
    out_specs = (
        P(None, "gz", "row", ("grp", "col")),
        P(None, "gz", "row", ("grp", "col")),
        P(("grp", "col", "row", "gz"), None),
    )
    return jax.shard_map(
        per_device, mesh=mesh, in_specs=in_specs, out_specs=out_specs, check_vma=False
    )
```

```python
import functools

import jax
import jax.numpy as jnp
import numpy as np
from jax import lax
from jax.experimental import pallas as pl
from jax.experimental.pallas import tpu as pltpu
from jax.sharding import PartitionSpec as P

STEPS = 4
FREQ = 8
MATS = 8
PLEN = 64
PORT_TILE = 4
FIELDS = 7
DEPTH = STEPS
ROWS = 8
LAYERS = 32
OWN = 4
CHUNK = 5
GROUP = 32

time_step = 0.5

UP_PLANES = [(f, 4) for f in (0, 1, 2, 4, 5)] + [(f, x) for x in (5, 6, 7) for f in range(FIELDS)]
DOWN_PLANES = [(f, x) for x in (0, 1, 2) for f in range(FIELDS)] + [(1, 3), (2, 3)]
PLANES = max(len(UP_PLANES), len(DOWN_PLANES))
PAIRS = (PLANES + 1) // 2

VMEM = pl.BlockSpec(memory_space=pltpu.VMEM)
SMEM = pl.BlockSpec(memory_space=pltpu.SMEM)
HBM = pl.BlockSpec(memory_space=pltpu.HBM)
ANY = pl.BlockSpec(memory_space=pl.ANY)
PARAMS = pltpu.CompilerParams(vmem_limit_bytes=16 * 1024 * 1024)


def dft_basis():
    times = (np.arange(STEPS) + 1.0) * time_step
    omegas = np.pi * (np.arange(FREQ) + 1.0) / FREQ
    angle = times[:, None] * omegas[None, :]
    return np.concatenate([np.cos(angle), -np.sin(angle)], axis=1)


BASIS = dft_basis()


def iota(axis):
    return lax.broadcasted_iota(jnp.int32, (8, 128), axis)


def turn(tile, shift, axis):
    return pltpu.roll(tile, shift % tile.shape[axis], axis)


def directions(row_size, body):
    if row_size == 2:
        row = lax.axis_index("row")
        pl.when(row == 0)(functools.partial(body, True, 0))
        pl.when(row == 1)(functools.partial(body, False, 0))
    else:
        body(True, 0)
        body(False, 1)


def coefficient(material, eps_ref):
    eps = jnp.full((8, 128), eps_ref[0], jnp.float32)
    for which in range(1, MATS):
        eps = jnp.where(material == which, eps_ref[which], eps)
    return time_step * (1.0 / eps)


def rows_outside(flat, f, state_ref, at):
    for x in range(ROWS):
        state_ref[at, x] = flat[pl.ds(f * LAYERS * ROWS + x, LAYERS, stride=ROWS), :].reshape(OWN, 8, 128)


def pack_kernel(row_size, eps_hbm, elec_hbm, magn_hbm, mat_hbm, z_ref, own_ref, even_ref, odd_ref, *rest):
    x_refs, (state_ref, main_ref, eps_ref, mat_ref, sems) = rest[:-5], rest[-5:]
    copies = [pltpu.make_async_copy(eps_hbm, eps_ref, sems.at[0]), pltpu.make_async_copy(mat_hbm, mat_ref, sems.at[1])]
    copies.append(pltpu.make_async_copy(elec_hbm, main_ref.at[pl.ds(0, 3)], sems.at[2]))
    copies.append(pltpu.make_async_copy(magn_hbm, main_ref.at[pl.ds(3, 3)], sems.at[3]))
    for copy in copies:
        copy.start()
    copies[0].wait()
    copies[1].wait()
    for z in range(LAYERS):
        main_ref[6, z] = coefficient(mat_ref[z], eps_ref)
    copies[2].wait()
    copies[3].wait()
    start = jnp.where(lax.axis_index("gz") == 0, LAYERS - DEPTH, 0)
    for f in range(FIELDS):
        z_ref[f] = main_ref[f, pl.ds(start, DEPTH)]
    flat = main_ref.reshape(FIELDS * LAYERS * ROWS, 128)
    for f in range(FIELDS):
        rows_outside(flat, f, state_ref, f)

    def send(up, slot):
        for i, (f, x) in enumerate(UP_PLANES if up else DOWN_PLANES):
            x_refs[slot][i] = state_ref[f, x]

    directions(row_size, send)
    pack_edges(state_ref, own_ref, even_ref, odd_ref)


def lane_groups():
    group = iota(1) >> 5
    return [jnp.where(group == r, 1.0, 0.0) for r in range(4)]


def gather_edges(rows_of, groups):
    moved = [[tile if tile is None else turn(tile, GROUP * r + 8, 1) for r, tile in enumerate(rows)] for rows in rows_of]
    out = []
    for rows in moved:
        parts = [tile * groups[r] for r, tile in enumerate(rows) if tile is not None]
        out.append(functools.reduce(lambda a, b: a + b, parts) if parts else jnp.zeros((8, 128), jnp.float32))
    return out


def staged(items, first, second):
    waiting = None
    for item in items:
        made = first(item)
        if waiting is not None:
            second(*waiting)
        waiting = (item, made)
    second(*waiting)


def pack_edges(state_ref, own_ref, even_ref, odd_ref):
    lane = iota(1)
    groups = lane_groups()
    slots = [jnp.where(((lane & (GROUP - 1)) >> 2) == f, 1.0, 0.0) for f in range(FIELDS)]
    even = (lax.axis_index("col") & 1) == 0

    def first(at):
        b, zz = at
        return gather_edges([[state_ref[f, 4 * b + r, zz] for r in range(4)] for f in range(FIELDS)], groups)

    def second(at, owns):
        b, zz = at
        ups = [turn(own, DEPTH * f - 4, 1) for f, own in enumerate(owns)]
        downs = [turn(own, DEPTH * f - 8, 1) for f, own in enumerate(owns)]
        up = functools.reduce(lambda a, b: a + b, [v * m for v, m in zip(ups, slots)])
        down = functools.reduce(lambda a, b: a + b, [v * m for v, m in zip(downs, slots)])
        for f in range(FIELDS):
            own_ref[f, b, zz] = owns[f]
        even_ref[b, zz] = jnp.where(even, up, down)
        odd_ref[b, zz] = jnp.where(even, down, up)

    staged([(b, zz) for b in range(2) for zz in range(OWN)], first, second)


def low_and_high(even_ref, odd_ref):
    even = (lax.axis_index("col") & 1) == 0

    def low(*at):
        return jnp.where(even, odd_ref[at], even_ref[at])

    def high(*at):
        return jnp.where(even, even_ref[at], odd_ref[at])

    return low, high


def layer_edge_kernel(even_ref, odd_ref, inner_ref, out_ref):
    gz = lax.axis_index("gz")
    for i, ref in enumerate((even_ref, odd_ref)):
        for b in range(2):
            out_ref[i, b] = jnp.where(gz == 0, ref[b, OWN - 1], ref[b, 0])


def spread_layers(gz, z_ref, ext_ref):
    for f in range(FIELDS):
        halo = z_ref[f].reshape(DEPTH * ROWS, 128)
        nothing = jnp.zeros_like(halo)
        ext_ref[f, : DEPTH * ROWS] = jnp.where(gz == 0, halo, nothing)
        ext_ref[f, DEPTH * ROWS :] = jnp.where(gz == 0, nothing, halo)


def corner_kernel(row_size, weight_ref, z_ref, even_ref, odd_ref, layer_ref, *rest):
    x_refs, ext_ref = rest[:-1], rest[-1]
    gz = lax.axis_index("gz")
    valid = (iota(0) < 4) == (gz == 0)
    spread_layers(gz, z_ref, ext_ref)
    low, high = low_and_high(even_ref, odd_ref)
    low_z, high_z = low_and_high(layer_ref.at[0], layer_ref.at[1])

    def send(up, slot):
        planes = UP_PLANES if up else DOWN_PLANES

        def tile(i):
            f, x = planes[i]
            return ext_ref[f, pl.ds(x, 8, stride=ROWS), :]

        for i in range(PAIRS):
            pair = tile(i)
            if i + PAIRS < len(planes):
                pair = pair + turn(tile(i + PAIRS), 4, 0)
            x_refs[slot][i] = pair
        b = 1 if up else 0
        for zz in range(OWN):
            x_refs[slot][PAIRS + zz] = low(b, zz)
            x_refs[slot][PAIRS + CHUNK + zz] = high(b, zz)
        x_refs[slot][PAIRS + OWN] = jnp.where(valid, low_z(b), 0.0)
        x_refs[slot][PAIRS + CHUNK + OWN] = jnp.where(valid, high_z(b), 0.0)

    directions(row_size, send)


def turn_sides(low, high):
    lows = [turn(low, 12 - DEPTH * f, 1) for f in range(FIELDS)]
    return lows, [turn(high, 8 - DEPTH * f, 1) for f in range(FIELDS)]


def edge_tiles(owns, sides, place):
    turned = [turn(own, 8, 1) for own in owns]
    out = []
    for own, own_turned, low, high in zip(owns, turned, *sides):
        tile = jnp.where(place < 16, low, own_turned)
        tile = jnp.where(place < 12, high, tile)
        out.append(jnp.where(place < 8, own, tile))
    return out


class Tiles:
    def __init__(self, first, ez_ref, shift):
        self.first, self.ez_ref, self.shift = first, ez_ref, shift
        self.values = {}

    def get(self, f, i, zz):
        value = self.values.get((f, i, zz))
        return self.first(f, i, zz) if value is None else value

    def put(self, f, i, zz, tile):
        self.values[f, i, zz] = tile
        at = i - self.shift
        if f == 2 and zz < OWN and self.ez_ref is not None and 0 <= at < self.ez_ref.shape[0]:
            self.ez_ref[at, zz] = tile


def leapfrog(tiles, exists, h_rows, e_rows, across, h_of, c_of, h_layers, e_layers, skip_hx):
    sub = iota(0)
    every = range(CHUNK)
    blank = [jnp.zeros((8, 128), jnp.float32)] * CHUNK

    def above(values):
        turned = [turn(v, -1, 0) for v in values]
        return [jnp.where(sub == 7, turned[(zz + 1) % CHUNK], turned[zz]) for zz in every]

    def beneath(values):
        turned = [turn(v, 1, 0) for v in values]
        return [jnp.where(sub == 0, turned[zz - 1], turned[zz]) for zz in every]

    def row(f, i):
        return [tiles.get(f, i, zz) for zz in every]

    def load_e(i):
        ey, ez = row(1, i), row(2, i)
        out = dict(ey=ey, ez=ez, ey_x=across.turned(ey, -1), ez_x=across.turned(ez, -1))
        if i in h_rows:
            ex = row(0, i)
            out.update(ex=ex, ex_y=[turn(v, -1, 1) for v in ex], ex_z=above(ex))
            if i not in skip_hx:
                out.update(ez_y=[turn(v, -1, 1) for v in ez], ey_z=above(ey))
        return out

    def work_h(i, loaded):
        e, after, h = loaded[i], loaded.get(i + 1), h_of(i)
        ey_x = across.pick(e["ey_x"], after["ey_x"] if after else blank, -1)
        ez_x = across.pick(e["ez_x"], after["ez_x"] if after else blank, -1)
        new = {}
        for zz in h_layers:
            if i not in skip_hx:
                curl = (e["ez_y"][zz] - e["ez"][zz]) - (e["ey_z"][zz] - e["ey"][zz])
                new[3, zz] = tiles.get(3, i, zz) - h[zz] * curl
            curl = (e["ex_z"][zz] - e["ex"][zz]) - (ez_x[zz] - e["ez"][zz])
            new[4, zz] = tiles.get(4, i, zz) - h[zz] * curl
            curl = (ey_x[zz] - e["ey"][zz]) - (e["ex_y"][zz] - e["ex"][zz])
            new[5, zz] = tiles.get(5, i, zz) - h[zz] * curl
        for (f, zz), tile in new.items():
            tiles.put(f, i, zz, tile)

    def load_h(i):
        hy, hz = row(4, i), row(5, i)
        out = dict(hy=hy, hz=hz, hy_x=across.turned(hy, 1), hz_x=across.turned(hz, 1))
        if i in e_rows:
            hx = row(3, i)
            out.update(hx=hx, hx_y=[turn(v, 1, 1) for v in hx], hz_y=[turn(v, 1, 1) for v in hz])
            out.update(hx_z=beneath(hx), hy_z=beneath(hy))
        return out

    def work_e(i, loaded):
        h, before, c = loaded[i], loaded.get(i - 1), c_of(i)
        hy_x = across.pick(h["hy_x"], before["hy_x"] if before else blank, 1)
        hz_x = across.pick(h["hz_x"], before["hz_x"] if before else blank, 1)
        new = {}
        for zz in e_layers:
            curl = (h["hz"][zz] - h["hz_y"][zz]) - (h["hy"][zz] - h["hy_z"][zz])
            new[0, zz] = tiles.get(0, i, zz) + c[zz] * curl
            curl = (h["hx"][zz] - h["hx_z"][zz]) - (h["hz"][zz] - hz_x[zz])
            new[1, zz] = tiles.get(1, i, zz) + c[zz] * curl
            curl = (h["hy"][zz] - hy_x[zz]) - (h["hx"][zz] - h["hx_y"][zz])
            new[2, zz] = tiles.get(2, i, zz) + c[zz] * curl
        for (f, zz), tile in new.items():
            tiles.put(f, i, zz, tile)

    def sweep(rows, load, work):
        loaded = {}

        def want(i):
            if i not in loaded and i in exists:
                loaded[i] = load(i)

        for i in rows:
            for j in (i - 1, i, i + 1):
                if j in rows or j == i + (1 if load is load_e else -1):
                    want(j)
            work(i, loaded)

    sweep(h_rows, load_e, work_h)
    yield
    sweep(e_rows, load_h, work_e)


class Rows:
    def turned(self, values, way):
        return values

    def pick(self, own, other, way):
        return other


class Blocks:
    def __init__(self, groups):
        self.groups = groups

    def turned(self, values, way):
        return [turn(v, way * GROUP, 1) for v in values]

    def pick(self, own, other, way):
        edge = self.groups[3] if way < 0 else self.groups[0]
        return [jnp.where(edge, o, v) for o, v in zip(other, own)]


def spans_inner(n, has_below, has_above):
    last = 7 - n if has_above else 7
    return (n - 1 if has_below else 0, last), (n if has_below else 0, last)


def spans_below(n):
    return (n - 5, n - 2), (n - 4, n - 1)


def spans_above(n):
    return (8 - n, 11 - n), (8 - n, 11 - n)


class Stepper:
    def __init__(self, row_size, main, edge, main_exists, edge_exists, skip_hx):
        gz, row, col = (lax.axis_index(name) for name in ("gz", "row", "col"))
        lane, sub = iota(1), iota(0)
        place, self.group = lane & (GROUP - 1), lane >> 5
        full = jnp.full((8, 128), time_step, jnp.float32)
        self.layer_half = [full] * OWN + [jnp.where((sub >= 4) & (gz == 0), 0.0, full)]
        outside = (place >= 12) & (place < 16) & (col == 0)
        self.edge_half = [jnp.where(outside, 0.0, v) for v in self.layer_half]
        self.lowest = jnp.where(row == 0, 0.0, 1.0) if row_size > 2 else None
        self.main, self.edge, self.skip_hx = main, edge, skip_hx
        self.main_exists, self.edge_exists = main_exists, edge_exists
        self.blocks = Blocks([self.group == r for r in range(4)])

    def masked(self, values, block, span):
        low, high = max(span[0] - 4 * block, 0), min(span[1] - 4 * block, 3)
        if low == 0 and high == 3:
            return values
        mask = (self.group >= low) & (self.group <= high)
        return [jnp.where(mask, v, 0.0) for v in values]

    def main_h(self, i):
        return self.layer_half if self.lowest is None or i >= DEPTH else [v * self.lowest for v in self.layer_half]

    def main_c(self, i):
        return [self.main.get(6, i, zz) for zz in range(CHUNK)]

    def edge_h(self, i, span):
        h = self.edge_half if self.lowest is None or i else [v * self.lowest for v in self.edge_half]
        return self.masked(h, i - 1, span)

    def edge_c(self, i, span):
        return self.masked([self.edge.get(6, i, zz) for zz in range(CHUNK)], i - 1, span)

    def step(self, n, spans, between=None):
        def blocks_of(span):
            return [b + 1 for b in range(-1, 3) if span[0] <= 4 * b + 3 and span[1] >= 4 * b]

        layers = range(CHUNK)
        last = range(OWN) if n == STEPS else layers
        parts = []
        for h_span, e_span in spans:
            h_rows = list(range(DEPTH + h_span[0], DEPTH + h_span[1] + 1))
            e_rows = list(range(DEPTH + e_span[0], DEPTH + e_span[1] + 1))
            skip = h_rows[:1] if self.skip_hx and h_span[0] < e_span[0] else []
            if self.main is not None:
                parts.append(
                    leapfrog(self.main, self.main_exists, h_rows, e_rows, Rows(), self.main_h, self.main_c, layers, last, skip)
                )
            if self.edge is None:
                continue
            h_of, c_of = functools.partial(self.edge_h, span=h_span), functools.partial(self.edge_c, span=e_span)
            parts.append(
                leapfrog(
                    self.edge, self.edge_exists, blocks_of(h_span), blocks_of(e_span), self.blocks, h_of, c_of, layers, last, []
                )
            )
        for part in parts:
            next(part)
        if between is not None:
            between()
        for part in parts:
            next(part, None)


def rows_cases(row_size, row, run):
    if row_size == 2:
        pl.when(row == 0)(functools.partial(run, False, True))
        pl.when(row == 1)(functools.partial(run, True, False))
    else:
        run(True, True)


def port_sums(n, reached, prow_ref, weight_ref, ez_ref, edge_ref, sum_ref, add_ref):
    for k in range(PORT_TILE):
        at = prow_ref[0, 0, k]
        total = jnp.zeros((8, 128), jnp.float32)
        for zz in range(OWN):
            if ez_ref is not None:
                total = total + ez_ref[at, zz] * weight_ref[k, 0, zz]
            if edge_ref is not None:
                total = total + edge_ref[at >> 2, zz] * weight_ref[k, 1, zz]
        total = jnp.sum(jnp.where(reached(n, at), total, 0.0), axis=0, keepdims=True)
        if add_ref is not None:
            total = total + add_ref[n - 1, k : k + 1, :]
        sum_ref[n - 1, k : k + 1, :] = total


def finish(fields, b, main, edge, write):
    lane = iota(1)
    place = lane & (GROUP - 1)
    sides = (lane < DEPTH) | (lane >= 128 - DEPTH)

    def first(f):
        tiles = [edge.get(f, b + 1, zz) for zz in range(OWN)]
        turned = [turn(tile, -8, 1) for tile in tiles]
        return [jnp.where(place < 8, tile, other) for tile, other in zip(tiles, turned)]

    def second(f, near):
        turned = {(r, zz): turn(near[zz], -(GROUP * r + 8), 1) for r in range(4) for zz in range(OWN)}
        made = {(r, zz): jnp.where(sides, tile, main.get(f, DEPTH + 4 * b + r, zz)) for (r, zz), tile in turned.items()}
        for (r, zz), tile in made.items():
            write(f, r, zz, tile)

    staged(fields, first, second)


def weight_kernel(mode_ref, prow_ref, pcol_ref, pmode_ref, pid_ref, order_ref, weight_ref, strip_ref):
    lane = iota(1)
    for k in range(PORT_TILE):
        strip_ref[k] = jnp.zeros(strip_ref.shape[1:], jnp.float32)
        strip_ref[k, :, 0:PLEN] = mode_ref[pmode_ref[0, 0, k]]
    for k in range(PORT_TILE):
        turned = GROUP * (prow_ref[0, 0, k] & 3)
        at = lane - turned
        for zz in range(OWN):
            tile = pltpu.roll(strip_ref[k, 8 * zz : 8 * zz + 8, :], pcol_ref[0, 0, k], 1)
            weight_ref[k, 0, zz] = jnp.where((lane >= DEPTH) & (lane < 128 - DEPTH), tile, 0.0)
            own = pltpu.roll(tile, turned + 8, 1)
            edge = jnp.where((at >= 4) & (at < 8), own, 0.0)
            weight_ref[k, 1, zz] = jnp.where((at >= 16) & (at < 20), turn(own, 8, 1), edge)


def inner_kernel(
    row_size, elec_ref, magn_ref, mat_ref, z_ref, eps_ref,
    e_ref, h_ref, c_ref, ez_ref, state_ref, plain_ref, ext_ref, halo_ref,
):
    gz, row = lax.axis_index("gz"), lax.axis_index("row")
    spread_layers(gz, z_ref, ext_ref)
    for f in range(FIELDS):
        for x in range(ROWS):
            halo_ref[f, x] = ext_ref[f, pl.ds(x, 8, stride=ROWS), :]
    for z in range(LAYERS):
        plain_ref[z] = coefficient(mat_ref[z], eps_ref)
    for f in range(3):
        rows_outside(elec_ref.reshape(3 * LAYERS * ROWS, 128), f, state_ref, f)
        rows_outside(magn_ref.reshape(3 * LAYERS * ROWS, 128), f, state_ref, f + 3)
    rows_outside(plain_ref.reshape(LAYERS * ROWS, 128), 0, state_ref, 6)

    def first(f, i, zz):
        return halo_ref[f, i - DEPTH] if zz == OWN else state_ref[f, i - DEPTH, zz]

    def run(has_below, has_above):
        main = Tiles(first, None, DEPTH)
        stepper = Stepper(row_size, main, None, range(4, 12), (), False)
        for n in range(1, STEPS + 1):
            main.ez_ref = ez_ref.at[n - 1]
            stepper.step(n, [spans_inner(n, has_below, has_above)])
        for i in range(ROWS):
            for zz in range(CHUNK):
                for f in range(6):
                    (e_ref, h_ref)[f // 3][f % 3, i, zz] = main.get(f, DEPTH + i, zz)
                c_ref[i, zz] = main.get(6, DEPTH + i, zz)

    rows_cases(row_size, row, run)


def rim_kernel(
    row_size, z_ref, own_ref, even_ref, odd_ref, layer_ref, e_in, h_in, ez_in, weight_ref, prow_ref,
    edge_e_ref, edge_h_ref, edge_c_ref, done_ref, sum_ref, ext_ref, ez_ref,
):
    gz, row = lax.axis_index("gz"), lax.axis_index("row")
    place = iota(1) & (GROUP - 1)
    groups = lane_groups()
    valid = (iota(0) < 4) == (gz == 0)
    spread_layers(gz, z_ref, ext_ref)
    low_of, high_of = low_and_high(even_ref, odd_ref)
    low_z, high_z = low_and_high(layer_ref.at[0], layer_ref.at[1])
    joined = {}

    def first(at):
        b, zz = at
        if zz < OWN:
            return [own_ref[f, b, zz] for f in range(FIELDS)], turn_sides(low_of(b, zz), high_of(b, zz))
        rows = [[ext_ref[f, pl.ds(4 * b + r, 8, stride=ROWS), :] for r in range(4)] for f in range(FIELDS)]
        sides = turn_sides(*(jnp.where(valid, side(b), 0.0) for side in (low_z, high_z)))
        return gather_edges(rows, groups), sides

    def second(at, made):
        for f, tile in enumerate(edge_tiles(*made, place)):
            joined[f, at[0] + 1, at[1]] = tile

    staged([(b, zz) for b in range(2) for zz in range(CHUNK)], first, second)

    def run(has_below, has_above):
        main = Tiles(lambda f, i, zz: (e_in, h_in)[f // 3][f % 3, i - DEPTH, zz], None, DEPTH)
        edge = Tiles(lambda f, i, zz: joined[f, i, zz], ez_ref, 1)
        stepper = Stepper(row_size, None, edge, (), (1, 2), False)

        def reached(n, at):
            low, high = spans_inner(n, has_below, has_above)[1]
            return (at >= low) & (at <= high)

        for n in range(1, STEPS + 1):
            stepper.step(n, [spans_inner(n, has_below, has_above)])
            port_sums(n, reached, prow_ref, weight_ref, ez_in.at[n - 1], ez_ref, sum_ref, None)
        for i in range(2):
            for zz in range(CHUNK):
                for f in range(6):
                    (edge_e_ref, edge_h_ref)[f // 3][f % 3, i, zz] = edge.get(f, 1 + i, zz)
                edge_c_ref[i, zz] = edge.get(6, 1 + i, zz)
        if has_below != has_above:

            def write(f, r, zz, tile):
                done_ref[f, r, zz] = tile

            finish(range(6), 0 if has_above else 1, main, edge, write)

    rows_cases(row_size, row, run)


def outer_kernel(
    row_size, ports_each, prow_ref, pid_ref, e_in, h_in, c_in, weight_ref, edge_e_in, edge_h_in, edge_c_in, done_ref, sum_in,
    *rest,
):
    n_x = 1 if row_size == 2 else 2
    x_refs, corner_refs = rest[:n_x], rest[n_x : 2 * n_x]
    eout_hbm, hout_hbm, term_ref, ez_ref, edge_ez_ref, sum_ref, turned_ref, out_ref, sems = rest[2 * n_x :]
    gz, row = lax.axis_index("gz"), lax.axis_index("row")
    lane, sub = iota(1), iota(0)
    place = lane & (GROUP - 1)
    groups = lane_groups()
    valid = (sub < 4) == (gz == 0)
    zeros = jnp.zeros((8, 128), jnp.float32)

    def first_main(f, i, zz):
        if f == 6:
            return c_in[i - DEPTH, zz]
        return e_in[f, i - DEPTH, zz] if f < 3 else h_in[f - 3, i - DEPTH, zz]

    def first_edge(f, i, zz):
        if f == 6:
            return edge_c_in[i - 1, zz]
        return edge_e_in[f, i - 1, zz] if f < 3 else edge_h_in[f - 3, i - 1, zz]

    def write_terms():
        basis = zeros
        for n in range(STEPS):
            for f in range(2 * FREQ):
                basis = jnp.where((sub == n) & (lane == f), float(BASIS[n, f]), basis)
        transform = zeros
        for n in range(STEPS):
            sampled = jnp.sum(sum_ref[n], axis=1, keepdims=True)
            transform = transform + sampled * basis[n : n + 1, :]
        term_ref[...] = jnp.zeros(term_ref.shape, jnp.float32)
        for k in range(PORT_TILE):
            port = pid_ref[0, 0, k]
            term_ref[port // ports_each, pl.ds(port % ports_each, 1), :] = transform[k : k + 1, : 2 * FREQ]

    def run(has_below, has_above):
        main = Tiles(first_main, ez_ref, DEPTH)
        edge = Tiles(first_edge, edge_ez_ref, 1)

        def halo_rows(planes, slot, offset, b):
            got = {}
            for i, (f, x) in enumerate(planes):
                packed = corner_refs[slot][i % PAIRS]
                if i >= PAIRS:
                    packed = turn(packed, 4, 0)
                tiles = [x_refs[slot][i, zz] for zz in range(OWN)]
                tiles.append(jnp.where(valid, packed, 0.0))
                for zz in range(CHUNK):
                    main.put(f, DEPTH + x + offset, zz, tiles[zz])
                    got[f, x + offset - 4 * b, zz] = tiles[zz]

            def first(zz):
                rows = [[got.get((f, r, zz)) for r in range(4)] for f in range(FIELDS)]
                sides = turn_sides(corner_refs[slot][PAIRS + zz], corner_refs[slot][PAIRS + CHUNK + zz])
                return gather_edges(rows, groups), sides

            def second(zz, made):
                for f, tile in enumerate(edge_tiles(*made, place)):
                    edge.put(f, 1 + b, zz, tile)

            staged(range(CHUNK), first, second)

        if has_below:
            halo_rows(UP_PLANES, 0, -ROWS, -1)
        if has_above:
            halo_rows(DOWN_PLANES, n_x - 1, ROWS, 2)

        def reached(n, at):
            out = None
            for wanted, span in ((has_below, spans_below(n)[1]), (has_above, spans_above(n)[1])):
                if wanted:
                    part = (at >= span[0]) & (at <= span[1])
                    out = part if out is None else out | part
            return out

        rows = range(0 if has_below else 4, 16 if has_above else 12)
        blocks = range(0 if has_below else 1, 4 if has_above else 3)
        copies = []

        def hand_out(part):
            for f in range(3 * part, 3 * part + 3):
                hand_out_field(part, f)

        def hand_out_field(part, field):
            fields = range(field, field + 1)

            def write(f, r, zz, tile, b):
                turned_ref[f, 4 * b + r, 8 * zz : 8 * zz + 8, :] = tile

            for b in range(2):
                put = functools.partial(write, b=b)
                if has_below and has_above or b == (1 if has_above else 0):
                    finish(fields, b, main, edge, put)
                else:
                    for f in fields:
                        for r in range(4):
                            for zz in range(OWN):
                                put(f, r, zz, done_ref[f, r, zz])
            flat = turned_ref.reshape(6 * ROWS * LAYERS, 128)
            for f in fields:
                for z in range(LAYERS):
                    out_ref[f, z] = flat[pl.ds(f * ROWS * LAYERS + z, ROWS, stride=LAYERS), :]
            dest = hout_hbm if part else eout_hbm
            copies.append(pltpu.make_async_copy(out_ref.at[field], dest.at[field % 3], sems.at[field]))
            copies[-1].start()

        stepper = Stepper(row_size, main, edge, rows, blocks, True)
        for n in range(1, STEPS + 1):
            spans = ([spans_below(n)] if has_below else []) + ([spans_above(n)] if has_above else [])
            stepper.step(n, spans, functools.partial(hand_out, 1) if n == STEPS else None)
            port_sums(n, reached, prow_ref, weight_ref, ez_ref, edge_ez_ref, sum_ref, sum_in)
        hand_out(0)
        write_terms()
        for copy in copies:
            copy.wait()

    rows_cases(row_size, row, run)


def shifted(block, axis, size, distance):
    route = [(i - distance, i) for i in range(size) if 0 <= i - distance < size]
    return lax.ppermute(block, axis, route)


def swapped(block, axis, size, start=0):
    pairs = [(i, i + 1) for i in range(start, size - 1, 2)]
    return lax.ppermute(block, axis, pairs + [(j, i) for i, j in pairs])


def solution(mesh):
    sizes = dict(mesh.shape)
    row_size, col_size, gz_size = sizes["row"], sizes["col"], sizes["gz"]
    n_x = 1 if row_size == 2 else 2

    def across_rows(blocks):
        if row_size == 2:
            return (swapped(blocks[0], "row", 2),)
        return (shifted(blocks[0], "row", row_size, 1), shifted(blocks[1], "row", row_size, -1))

    def per_device(
        electric, magnetic, material, eps_table, mode_table, port_row, port_col, port_mode, port_ids
    ):
        f32 = jnp.float32

        def array(*shape):
            return jax.ShapeDtypeStruct(shape, f32)

        def scratch(*shape):
            return pltpu.VMEM(shape, f32)

        z_send, own, even_send, odd_send, *x_send = pl.pallas_call(
            functools.partial(pack_kernel, row_size),
            out_shape=[
                array(FIELDS, DEPTH, ROWS, 128),
                array(FIELDS, 2, OWN, 8, 128),
                array(2, OWN, 8, 128),
                array(2, OWN, 8, 128),
            ]
            + [array(PLANES, OWN, 8, 128)] * n_x,
            in_specs=[HBM] * 4,
            out_specs=[VMEM] * (4 + n_x),
            scratch_shapes=[
                scratch(FIELDS, ROWS, OWN, 8, 128),
                scratch(FIELDS, LAYERS, ROWS, 128),
                pltpu.SMEM(eps_table.shape, f32),
                pltpu.VMEM(material.shape, jnp.int32),
                pltpu.SemaphoreType.DMA((4,)),
            ],
            name="pack",
        )(eps_table, electric, magnetic, material)
        x_halo = across_rows(x_send)
        even = swapped(even_send, "col", col_size)
        odd = swapped(odd_send, "col", col_size, 1)
        z_halo = swapped(z_send, "gz", gz_size)
        e_now, h_now, c_now, ez_now = pl.pallas_call(
            functools.partial(inner_kernel, row_size),
            out_shape=[
                array(3, ROWS, CHUNK, 8, 128),
                array(3, ROWS, CHUNK, 8, 128),
                array(ROWS, CHUNK, 8, 128),
                array(STEPS, ROWS, OWN, 8, 128),
            ],
            in_specs=[VMEM] * 4 + [SMEM],
            out_specs=[VMEM] * 4,
            scratch_shapes=[
                scratch(FIELDS, ROWS, OWN, 8, 128),
                scratch(LAYERS, ROWS, 128),
                scratch(FIELDS, 8 * ROWS, 128),
                scratch(FIELDS, ROWS, 8, 128),
            ],
            compiler_params=PARAMS,
            cost_estimate=pl.CostEstimate(flops=5_000_000, bytes_accessed=10_000_000, transcendentals=0),
            name="inner",
        )(electric, magnetic, material, z_halo, eps_table)
        layer_send = pl.pallas_call(
            layer_edge_kernel,
            out_shape=array(2, 2, 8, 128),
            in_specs=[VMEM] * 2 + [pl.BlockSpec(memory_space=pl.ANY)],
            out_specs=VMEM,
            compiler_params=PARAMS,
            name="layer_edges",
        )(even, odd, c_now)
        layer_halo = swapped(layer_send, "gz", gz_size)
        weights = pl.pallas_call(
            weight_kernel,
            out_shape=array(PORT_TILE, 2, OWN, 8, 128),
            in_specs=[VMEM] + [SMEM] * 4 + [ANY],
            out_specs=VMEM,
            scratch_shapes=[scratch(PORT_TILE, LAYERS, 128)],
            compiler_params=PARAMS,
            name="weights",
        )(mode_table, port_row, port_col, port_mode, port_ids, layer_send)
        corner_send = pl.pallas_call(
            functools.partial(corner_kernel, row_size),
            out_shape=[array(PAIRS + 2 * CHUNK, 8, 128)] * n_x,
            in_specs=[ANY] + [VMEM] * 4,
            out_specs=[VMEM] * n_x,
            scratch_shapes=[scratch(FIELDS, 8 * ROWS, 128)],
            compiler_params=PARAMS,
            name="corners",
        )(weights, z_halo, even, odd, layer_halo)
        corner = across_rows(corner_send)
        edges = pl.pallas_call(
            functools.partial(rim_kernel, row_size),
            out_shape=[
                array(3, 2, CHUNK, 8, 128),
                array(3, 2, CHUNK, 8, 128),
                array(2, CHUNK, 8, 128),
                array(6, 4, OWN, 8, 128),
                array(STEPS, 8, 128),
            ],
            in_specs=[VMEM] * 9 + [SMEM],
            out_specs=[VMEM] * 5,
            scratch_shapes=[scratch(FIELDS, 8 * ROWS, 128), scratch(2, OWN, 8, 128)],
            compiler_params=PARAMS,
            name="rim",
        )(z_halo, own, even, odd, layer_halo, e_now, h_now, ez_now, weights, port_row)
        devices = col_size * row_size * gz_size
        ports_each = PORT_TILE * col_size * row_size // devices
        electric_out, magnetic_out, term = pl.pallas_call(
            functools.partial(outer_kernel, row_size, ports_each),
            out_shape=[array(3, LAYERS, ROWS, 128)] * 2 + [array(devices, ports_each, 2 * FREQ)],
            in_specs=[SMEM] * 2 + [VMEM] * (9 + 2 * n_x),
            out_specs=[HBM, HBM, VMEM],
            scratch_shapes=[
                scratch(ROWS, OWN, 8, 128),
                scratch(2, OWN, 8, 128),
                scratch(STEPS, 8, 128),
                scratch(6, ROWS, LAYERS, 128),
                scratch(6, LAYERS, ROWS, 128),
                pltpu.SemaphoreType.DMA((6,)),
            ],
            compiler_params=PARAMS,
            name="outer",
        )(port_row, port_ids, e_now, h_now, c_now, weights, *edges, *x_halo, *corner)
        terms = lax.all_to_all(term, ("col", "row", "gz"), 0, 0, tiled=True)
        return (
            electric_out,
            magnetic_out,
            jnp.sum(terms, axis=0),
        )

    in_specs = (
        P(None, "gz", "row", ("grp", "col")),
        P(None, "gz", "row", ("grp", "col")),
        P("gz", "row", ("grp", "col")),
        P(),
        P(None, "gz", None),
        P(("grp", "row"), "col", None),
        P(("grp", "row"), "col", None),
        P(("grp", "row"), "col", None),
        P(("grp", "row"), "col", None),
    )
    out_specs = (
        P(None, "gz", "row", ("grp", "col")),
        P(None, "gz", "row", ("grp", "col")),
        P(("grp", "col", "row", "gz"), None),
    )
    return jax.shard_map(
        per_device, mesh=mesh, in_specs=in_specs, out_specs=out_specs, check_vma=False
    )
```
